32 devices in a mesh: dp: 8 (over z, x), mp: 4 (over y, core).
Axes of the slice: x: 2, y: 2, z: 4, core: 2. Of those that a mesh axis runs over, the one named last changes fastest.
Arguments:
- tokens: bfloat16 [8192, 768], P('dp'), may hold values from -6 to 6
- routes: int32 [8192, 1], P('dp'), may hold values from 0 to 7
- lengths: int32 [4], replicated, may hold values from 512 to 2048, as said below
- cotangent: bfloat16 [8192, 768], P('dp'), may hold values from -6 to 6
- first_gain: bfloat16 [768], replicated, may hold values from 0.5 to 1.5
- mixer_in: bfloat16 [768, 2, 1536], P(None, None, 'mp'), may hold values from -0.21875 to 0.21875
- conv_weight: bfloat16 [4, 1536], P(None, 'mp'), may hold values from -3 to 3
- conv_bias: bfloat16 [1536], P('mp'), may hold values from -1.5 to 1.5
- select_weight: bfloat16 [1536, 80], P('mp'), may hold values from -0.15625 to 0.15625
- step_weight: bfloat16 [48, 1536], P(None, 'mp'), may hold values from -0.875 to 0.875
- step_bias: bfloat16 [1536], P('mp'), may hold values from -4.5 to -1.5
- decay_log: bfloat16 [16, 1536], P(None, 'mp'), may hold values from -7 to 2
- skip_gain: bfloat16 [1536], P('mp'), may hold values from 0.5 to 1.5
- mixer_out: bfloat16 [1536, 768], P('mp'), may hold values from -0.15625 to 0.15625
- second_gain: bfloat16 [768], replicated, may hold values from 0.5 to 1.5
- router_weight: bfloat16 [768, 8], replicated, may hold values from -0.109375 to 0.109375
- expert_up: bfloat16 [8, 768, 3072], P('dp', None, 'mp'), may hold values from -0.21875 to 0.21875
- up_bias: bfloat16 [8, 3072], P('dp', 'mp'), may hold values from -0.59765625 to 0.59765625
- expert_down: bfloat16 [8, 3072, 768], P('dp', 'mp'), may hold values from -2 to 2
- down_bias: bfloat16 [8, 768], P('dp'), may hold values from -2.65625 to 2.65625
Outputs:
- block_out: bfloat16 [8192, 768], P('dp')
- token_grad: float32 [8192, 768], P('dp')
- first_gain_grad: float32 [768], replicated
- mixer_in_grad: float32 [768, 2, 1536], P(None, None, 'mp')
- conv_weight_grad: float32 [4, 1536], P(None, 'mp')
- conv_bias_grad: float32 [1536], P('mp')
- select_weight_grad: float32 [1536, 80], P('mp')
- step_weight_grad: float32 [48, 1536], P(None, 'mp')
- step_bias_grad: float32 [1536], P('mp')
- decay_log_grad: float32 [16, 1536], P(None, 'mp')
- skip_gain_grad: float32 [1536], P('mp')
- mixer_out_grad: float32 [1536, 768], P('mp')
- second_gain_grad: float32 [768], replicated
- router_weight_grad: float32 [768, 8], replicated
- expert_up_grad: float32 [8, 768, 3072], P('dp', None, 'mp')
- up_bias_grad: float32 [8, 3072], P('dp', 'mp')
- expert_down_grad: float32 [8, 3072, 768], P('dp', 'mp')
- down_bias_grad: float32 [8, 768], P('dp')
The draws below stay inside these ranges and needn't reach their ends.
Inputs may be any that keep to these rules, and one draw needn't show every extreme that they name: `lengths`: each entry is a sequence's valid places, counted from place 0; at least one sequence has all 2048.
All inputs are finite; a program needn't handle non-finite values.
Results may differ from the reference program's by a relative error of at most 0.017.
Values may be sent and summed in bfloat16 or wider, within the bound.
A program may use at most 448 MiB of HBM per device.

```python
import jax
import jax.numpy as jnp
from jax import lax

D = 768
DI = 1536
STATE = 16
DT_RANK = 48
KC = 4
FF = 3072
TOK_DEV = 1024
SLOT_DEV = 256
BLOCK = 256
EXPERTS = 8
CAP = 160
TOKENS = 8192
NSEQ = 4
SEQ = 2048
N_DP = 8


def draw_lengths(key, part):
    first_key = jax.random.fold_in(key, 11)
    second_key = jax.random.fold_in(key, 23)
    drawn = jax.random.randint(first_key, (NSEQ,), SEQ // 4, SEQ + 1)
    longest = jax.random.randint(second_key, (), 0, NSEQ)
    return jnp.where(jnp.arange(NSEQ) == longest, SEQ, drawn).astype(jnp.int32)


def levels(rng, dims, split, least, top_value):
    def one(dim, blocks):
        draws = jax.random.uniform(jax.random.fold_in(jax.random.fold_in(rng, 6), dim), (blocks,), jnp.float32, least / len(split), top_value / len(split))
        return jnp.repeat(jnp.exp(draws), dims[dim] // blocks).reshape((-1,) + (1,) * (len(dims) - dim - 1))

    factor_of = one(*split[0])
    for cut in split[1:]:
        factor_of = factor_of * one(*cut)
    return factor_of


def different_ones(own_key, rows, number_of, top, lift):
    sequence = jax.random.permutation(jax.random.fold_in(own_key, 1), number_of)
    favour = sequence
    for power in range(3):
        favour = favour * favour // number_of
    favour = favour * lift // number_of
    chance = jax.random.randint(jax.random.fold_in(own_key, 2), (rows, number_of), 0, 4096) + favour
    fixed_rows = jax.random.permutation(jax.random.fold_in(own_key, 3), rows)[jnp.arange(number_of) % rows]
    chance = jnp.where(jnp.arange(rows)[:, None] == fixed_rows[None, :], 1 << 14, chance)
    score = chance * number_of + jnp.arange(number_of)
    return lax.top_k(score.astype(jnp.int32), top)[1].astype(jnp.int32)


def normal_values(own_key, dims, scale, limit, cuts=(), held_as=jnp.bfloat16):
    values = jax.random.normal(own_key, dims, jnp.float32) * scale
    if len(cuts) > 0:
        values = levels(own_key, dims, cuts, -0.22, 0.18) * values
    return jnp.clip(values, min=-limit, max=limit).astype(held_as)


def setup_inputs(seed: int = 0) -> dict:
    key_list = jax.random.split(jax.random.key(seed), 21)
    return {
        "tokens": normal_values(key_list[0], (TOKENS, D), 1.0, 6.0, ((0, 8),)),
        "routes": different_ones(key_list[1], TOKENS, EXPERTS, 1, 1024),
        "lengths": draw_lengths(jax.random.fold_in(key_list[20], 71), 0),
        "cotangent": normal_values(key_list[3], (TOKENS, D), 1.0, 6.0, ((0, 8),)),
        "first_gain": jnp.clip(1.0 + 0.1 * jax.random.normal(key_list[4], (D,), jnp.float32), 0.5, 1.5).astype(jnp.bfloat16),
        "mixer_in": normal_values(key_list[5], (D, 2, DI), D ** -0.5, 0.21875, ((2, 4),)),
        "conv_weight": normal_values(key_list[6], (KC, DI), KC ** -0.5, 3.0, ((1, 4),)),
        "conv_bias": normal_values(key_list[7], (DI,), 0.3, 1.5, ((0, 4),)),
        "select_weight": normal_values(key_list[8], (DI, DT_RANK + 2 * STATE), DI ** -0.5, 0.15625, ((0, 4),)),
        "step_weight": normal_values(key_list[9], (DT_RANK, DI), DT_RANK ** -0.5, 0.875, ((1, 4),)),
        "step_bias": jnp.clip(-4.5 + 3.0 * jax.random.uniform(key_list[10], (DI,), jnp.float32) ** levels(key_list[10], (DI,), ((0, 4),), -0.2, 0.2), -4.5, -1.5).astype(jnp.bfloat16),
        "decay_log": jnp.clip(-7.0 + 9.0 * jax.random.uniform(key_list[11], (STATE, DI), jnp.float32) ** levels(key_list[11], (STATE, DI), ((1, 4),), -0.2, 0.2), -7.0, 2.0).astype(jnp.bfloat16),
        "skip_gain": jnp.clip(0.5 + 1.0 * jax.random.uniform(key_list[12], (DI,), jnp.float32) ** levels(key_list[12], (DI,), ((0, 4),), -0.2, 0.2), 0.5, 1.5).astype(jnp.bfloat16),
        "mixer_out": normal_values(key_list[13], (DI, D), DI ** -0.5, 0.15625, ((0, 4),)),
        "second_gain": jnp.clip(1.0 + 0.1 * jax.random.normal(key_list[14], (D,), jnp.float32), 0.5, 1.5).astype(jnp.bfloat16),
        "router_weight": normal_values(key_list[15], (D, EXPERTS), (4 * D) ** -0.5, 0.109375),
        "expert_up": normal_values(key_list[16], (EXPERTS, D, FF), D ** -0.5, 0.21875, ((0, 8), (2, 4))),
        "up_bias": normal_values(key_list[17], (EXPERTS, FF), 0.1, 0.59765625, ((0, 8), (1, 4))),
        "expert_down": normal_values(key_list[18], (EXPERTS, FF, D), (max(1, 512 // (EXPERTS * EXPERTS))) ** -0.5, 2.0, ((0, 8), (1, 4))),
        "down_bias": normal_values(key_list[19], (EXPERTS, D), (EXPERTS / 16), 2.65625, ((0, 8),)),
    }


@jax.custom_vjp
def low(v):
    return lax.optimization_barrier(v.astype(jnp.bfloat16)).astype(jnp.float32)

@jax.custom_vjp
def low_back(v):
    return v

def low_keep(v):
    return (low(v), None)

def low_pass(kept, grad):
    return (grad,)

def back_keep(v):
    return (v, None)

def back_low(kept, grad):
    return (low(grad),)
low.defvjp(low_keep, low_pass)
low_back.defvjp(back_keep, back_low)
hp_level = lax.Precision.HIGHEST
norm_eps = 1e-05

def rms_scale(values, norm_gain):
    return values * lax.rsqrt(lax.optimization_barrier(jnp.mean(values * values, axis=-1, keepdims=True)) + norm_eps) * norm_gain

def to_seq(values):
    width = values.shape[-1]
    return values.reshape(N_DP, NSEQ, SLOT_DEV, width).transpose(1, 0, 2, 3).reshape(NSEQ * SEQ, width)

def from_seq(values):
    width = values.shape[-1]
    return values.reshape(NSEQ, N_DP, SLOT_DEV, width).transpose(1, 0, 2, 3).reshape(TOKENS, width)

def to_blocks(values):
    width = values.shape[-1]
    return to_seq(values).reshape(NSEQ, SEQ // BLOCK, BLOCK, width).transpose(1, 0, 2, 3)

def pair_step(earlier_pair, later_pair):
    return (earlier_pair[0] * later_pair[0], later_pair[0] * earlier_pair[1] + later_pair[1])

def scan_piece(scan_carry, pieces):
    decay_rates, carry_state = scan_carry
    step_vals, input_vals, bin_vals, cout_vals = pieces
    decays = jnp.exp(step_vals[:, :, :, None] * decay_rates[None, None])
    drives = (step_vals * input_vals)[:, :, :, None] * bin_vals[:, :, None, :]
    cum_decay, local_state = lax.associative_scan(pair_step, (decays, drives), axis=1)
    states = local_state + cum_decay * carry_state[:, None]
    outputs = jnp.einsum('stcn,stn->stc', states, cout_vals, precision=hp_level)
    return ((decay_rates, states[:, -1]), outputs)

def reference(tokens, routes, lengths, cotangent, first_gain, mixer_in, conv_weight, conv_bias, select_weight, step_weight, step_bias, decay_log, skip_gain, mixer_out, second_gain, router_weight, expert_up, up_bias, expert_down, down_bias):
    positions = jnp.arange(TOKENS, dtype=jnp.int32)
    group_of = positions // TOK_DEV
    inside = positions % TOK_DEV
    seq_of = inside // SLOT_DEV
    place_of = group_of * SLOT_DEV + inside % SLOT_DEV
    valid_mask = (place_of < lengths[seq_of]).astype(jnp.float32)
    route_ids = routes[:, 0].astype(jnp.int32)
    expert_iota = jnp.arange(EXPERTS, dtype=jnp.int32)
    route_match = route_ids[:, None] == expert_iota[None]
    route_hot = route_match.astype(jnp.float32)
    live_hot = (route_match & (valid_mask[:, None] > 0.5)).astype(jnp.int32)
    blocked = live_hot.reshape(N_DP, TOK_DEV, EXPERTS)
    earlier = jnp.cumsum(blocked, axis=1).astype(jnp.int32) - blocked
    position = lax.optimization_barrier(jnp.sum(earlier * blocked, axis=2)).astype(jnp.int32)
    kept_mask = (valid_mask.reshape(N_DP, TOK_DEV) > 0.5) & (position < CAP)
    slot_ids = route_ids.reshape(N_DP, TOK_DEV) * CAP + position
    slot_iota = jnp.arange(EXPERTS * CAP, dtype=jnp.int32)
    dispatch = ((slot_ids[:, None, :] == slot_iota[None, :, None]) & kept_mask[:, None, :]).astype(jnp.float32)

    def forward(tok_vals, gain_first, proj_in, conv_taps, conv_shift, proj_sel, proj_step, step_shift, rate_log, skip_vals, proj_out, gain_second, proj_route, up_mats, up_shift, down_mats, down_shift):
        normed_in = low(rms_scale(tok_vals, gain_first))
        both_in = low(low_back(jnp.einsum('td,dkc->tkc', normed_in, proj_in, precision=hp_level)))
        u_in = both_in[:, 0, :]
        gate_pre = both_in[:, 1, :]
        grouped = to_seq(u_in).reshape(NSEQ, SEQ, DI)
        padded = jnp.pad(grouped, ((0, 0), (KC - 1, 0), (0, 0)))
        conv_pre = jnp.zeros((NSEQ, SEQ, DI), jnp.float32) + conv_shift
        for offset in range(KC):
            conv_pre = conv_pre + conv_taps[offset] * padded[:, offset:offset + SEQ]
        conv_pre = from_seq(conv_pre.reshape(NSEQ * SEQ, DI))
        u_vals = low(jax.nn.silu(conv_pre))
        projected = low_back(jnp.dot(u_vals, proj_sel, precision=hp_level))
        dt_low = projected[:, :DT_RANK]
        bin_vals = projected[:, DT_RANK:DT_RANK + STATE]
        cout_vals = projected[:, DT_RANK + STATE:]
        step_vals = valid_mask[:, None] * jax.nn.softplus(jnp.dot(dt_low, proj_step, precision=hp_level) + step_shift)
        decay_rates = -jnp.exp(rate_log).T
        pieces = (to_blocks(step_vals), to_blocks(u_vals), to_blocks(bin_vals), to_blocks(cout_vals))
        final_carry, scan_vals = lax.scan(jax.checkpoint(scan_piece), (decay_rates, jnp.zeros((NSEQ, DI, STATE), jnp.float32)), pieces)
        scan_seq = scan_vals.transpose(1, 0, 2, 3).reshape(NSEQ * SEQ, DI)
        scan_out = from_seq(scan_seq) + skip_vals * u_vals
        gated_vals = low(scan_out * jax.nn.silu(gate_pre))
        mixer_vals = low_back(jnp.dot(gated_vals, proj_out, precision=hp_level))
        residual = tok_vals + valid_mask[:, None] * mixer_vals
        normed_out = low(rms_scale(residual, gain_second))
        logits = low_back(jnp.dot(normed_out, proj_route, precision=hp_level))
        route_probs = jax.nn.softmax(logits, axis=-1)
        gate_prob = lax.optimization_barrier(jnp.sum(route_probs * route_hot, axis=-1))
        sent_rows = low_back(jnp.einsum('bst,btd->bsd', dispatch, normed_out.reshape(N_DP, TOK_DEV, D), precision=hp_level))
        expert_rows = sent_rows.reshape(N_DP, EXPERTS, CAP, D).transpose(1, 0, 2, 3).reshape(EXPERTS, N_DP * CAP, D)
        hidden_pre = low_back(jnp.einsum('emd,edf->emf', expert_rows, up_mats, precision=hp_level) + up_shift[:, None, :])
        hidden_act = low(jax.nn.gelu(hidden_pre, approximate=True))
        expert_result = low(low_back(jnp.einsum('emf,efd->emd', hidden_act, down_mats, precision=hp_level) + down_shift[:, None, :]))
        returned = expert_result.reshape(EXPERTS, N_DP, CAP, D).transpose(1, 0, 2, 3).reshape(N_DP, EXPERTS * CAP, D)
        tok_result = jnp.einsum('bst,bsd->btd', dispatch, returned, precision=hp_level).reshape(TOKENS, D)
        return residual + gate_prob[:, None] * tok_result
    floats = [value.astype(jnp.float32) for value in (tokens, first_gain, mixer_in, conv_weight, conv_bias, select_weight, step_weight, step_bias, decay_log, skip_gain, mixer_out, second_gain, router_weight, expert_up, up_bias, expert_down, down_bias)]
    block_vals, pullback = jax.vjp(forward, *floats)
    gradients = pullback(cotangent.astype(jnp.float32))
    return (block_vals.astype(jnp.bfloat16), gradients[0], gradients[1], gradients[2], gradients[3], gradients[4], gradients[5], gradients[6], gradients[7], gradients[8], gradients[9], gradients[10], gradients[11], gradients[12], gradients[13], gradients[14], gradients[15], gradients[16])
```

```python
import functools

import jax
import jax.numpy as jnp
from jax import lax
from jax.experimental import pallas as pl
from jax.experimental.pallas import tpu as pltpu
from jax.sharding import PartitionSpec as P

F32 = jnp.float32
BF16 = jnp.bfloat16
SLOT_DEV = 256
LANES = 128
SUB = 8
LOG2E = 1.4426950408889634
LN2 = 0.6931471805599453
VMEM = 48 * 2**20
norm_eps = 1e-05


def lane(col):
    return jnp.broadcast_to(col, (SUB, LANES))


def row(ref, n, cs):
    return jnp.broadcast_to(ref[n : n + 1, cs], (SUB, LANES))


def tiles(count):
    return [slice(ct * LANES, (ct + 1) * LANES) for ct in range(count // LANES)]


def whole(*dims):
    return pl.BlockSpec(dims, lambda i: (0,) * len(dims))


def local_forward_kernel(step_ref, x_ref, bin_ref, rates_ref, out_ref):
    places, chans = step_ref.shape[0], step_ref.shape[2]
    states, half = rates_ref.shape[0], 8
    cols = tiles(chans)
    for nh in range(states // half):
        ns = [nh * half + n for n in range(half)]

        def body(i, st):
            st = list(st)
            b = bin_ref[i]
            bb = [lane(b[:, n : n + 1]) for n in ns]
            for ct, cs in enumerate(cols):
                s = step_ref[i, :, cs]
                x = x_ref[i, :, cs]
                for n in range(half):
                    k = n * len(cols) + ct
                    e = jnp.exp2(s * row(rates_ref, ns[n], cs))
                    st[k] = e * st[k] + x * bb[n]
            return tuple(st)

        zero = tuple(jnp.zeros((SUB, LANES), F32) for _ in range(half * len(cols)))
        st = lax.fori_loop(0, places, body, zero, unroll=8)
        for n in range(half):
            for ct, cs in enumerate(cols):
                out_ref[ns[n], :, cs] = st[n * len(cols) + ct]


def local_forward(step, x, bin_vals, rates):
    return pl.pallas_call(
        local_forward_kernel,
        out_shape=jax.ShapeDtypeStruct((rates.shape[0], SUB, step.shape[2]), F32),
        compiler_params=pltpu.CompilerParams(vmem_limit_bytes=VMEM),
    )(step, x, bin_vals, rates)


def forward_kernel(
    step_ref, x_ref, bin_ref, cout_ref, rates_ref, h0_ref, y_ref, hb_ref, hf_ref, st_ref
):
    places, chans = step_ref.shape[0], step_ref.shape[2]
    states, half = rates_ref.shape[0], 8
    cols = tiles(chans)

    @pl.when(pl.program_id(0) == 0)
    def _():
        st_ref[...] = h0_ref[...]

    for nh in range(states // half):
        ns = [nh * half + n for n in range(half)]

        def body(i, st):
            st = list(st)
            b = bin_ref[i]
            c = cout_ref[i]
            bb = [lane(b[:, n : n + 1]) for n in ns]
            cc = [lane(c[:, n : n + 1]) for n in ns]
            for ct, cs in enumerate(cols):
                s = step_ref[i, :, cs]
                x = x_ref[i, :, cs]
                y = y_ref[i, :, cs] if nh else jnp.zeros((SUB, LANES), F32)
                for n in range(half):
                    k = n * len(cols) + ct
                    hb_ref[i, ns[n], :, cs] = st[k].astype(hb_ref.dtype)
                    e = jnp.exp2(s * row(rates_ref, ns[n], cs))
                    st[k] = e * st[k] + x * bb[n]
                    y = y + cc[n] * st[k]
                y_ref[i, :, cs] = y
            return tuple(st)

        st = tuple(st_ref[n, :, cs] for n in ns for cs in cols)
        st = lax.fori_loop(0, places, body, st, unroll=8)
        for n in range(half):
            for ct, cs in enumerate(cols):
                st_ref[ns[n], :, cs] = st[n * len(cols) + ct]
    hf_ref[...] = st_ref[...]


def forward(step, x, bin_vals, cout, rates, h0, block=16):
    places, _, chans = step.shape
    states = rates.shape[0]
    part = lambda width: pl.BlockSpec((block, SUB, width), lambda i: (i, 0, 0))
    return pl.pallas_call(
        forward_kernel,
        grid=(places // block,),
        in_specs=[
            part(chans),
            part(chans),
            part(states),
            part(states),
            whole(states, chans),
            whole(states, SUB, chans),
        ],
        out_specs=[
            part(chans),
            pl.BlockSpec((block, states, SUB, chans), lambda i: (i, 0, 0, 0)),
            whole(states, SUB, chans),
        ],
        out_shape=[
            jax.ShapeDtypeStruct((places, SUB, chans), F32),
            jax.ShapeDtypeStruct((places, states, SUB, chans), BF16),
            jax.ShapeDtypeStruct((states, SUB, chans), F32),
        ],
        scratch_shapes=[pltpu.VMEM((states, SUB, chans), F32)],
        compiler_params=pltpu.CompilerParams(vmem_limit_bytes=VMEM),
    )(step, x, bin_vals, cout, rates, h0)


def local_backward_kernel(step_ref, gs_ref, cout_ref, rates_ref, out_ref):
    places, chans = step_ref.shape[0], step_ref.shape[2]
    states, half = rates_ref.shape[0], 8
    cols = tiles(chans)
    for nh in range(states // half):
        ns = [nh * half + n for n in range(half)]

        def body(lap, st):
            i = places - 1 - lap
            st = list(st)
            c = cout_ref[i]
            cc = [lane(c[:, n : n + 1]) for n in ns]
            for ct, cs in enumerate(cols):
                s = step_ref[i, :, cs]
                g = gs_ref[i, :, cs]
                for n in range(half):
                    k = n * len(cols) + ct
                    e = jnp.exp2(s * row(rates_ref, ns[n], cs))
                    st[k] = e * (st[k] + g * cc[n])
            return tuple(st)

        zero = tuple(jnp.zeros((SUB, LANES), F32) for _ in range(half * len(cols)))
        st = lax.fori_loop(0, places, body, zero, unroll=8)
        for n in range(half):
            for ct, cs in enumerate(cols):
                out_ref[ns[n], :, cs] = st[n * len(cols) + ct]


def local_backward(step, gs, cout, rates):
    return pl.pallas_call(
        local_backward_kernel,
        out_shape=jax.ShapeDtypeStruct((rates.shape[0], SUB, step.shape[2]), F32),
        compiler_params=pltpu.CompilerParams(vmem_limit_bytes=VMEM),
    )(step, gs, cout, rates)


def backward_kernel(
    step_ref,
    x_ref,
    gs_ref,
    gp_ref,
    bin_ref,
    cout_ref,
    rates_ref,
    g0_ref,
    hb_ref,
    sg_ref,
    sb_ref,
    qb_ref,
    qc_ref,
    rt_out,
    gst_ref,
    rt_ref,
    q_ref,
    p_ref,
):
    places, chans = step_ref.shape[0], step_ref.shape[2]
    states, some = rates_ref.shape[0], 4
    cols = tiles(chans)

    @pl.when(pl.program_id(0) == 0)
    def _():
        gst_ref[...] = g0_ref[...]
        rt_ref[...] = jnp.zeros_like(rt_ref)

    for nq in range(states // some):
        ns = [nq * some + n for n in range(some)]
        size = some * len(cols)

        def body(lap, carry):
            i = places - 1 - lap
            st, rt = list(carry[:size]), list(carry[size:])
            b = bin_ref[i]
            c = cout_ref[i]
            bb = [lane(b[:, n : n + 1]) for n in ns]
            cc = [lane(c[:, n : n + 1]) for n in ns]
            qb, qc = [None] * some, [None] * some
            for ct, cs in enumerate(cols):
                s = step_ref[i, :, cs]
                x = x_ref[i, :, cs]
                g = gs_ref[i, :, cs]
                gp = gp_ref[i, :, cs]
                sg = sg_ref[i, :, cs] if nq else jnp.zeros((SUB, LANES), F32)
                sb = sb_ref[i, :, cs] if nq else jnp.zeros((SUB, LANES), F32)
                for n in range(some):
                    k = n * len(cols) + ct
                    rate = row(rates_ref, ns[n], cs)
                    e = jnp.exp2(s * rate)
                    h = hb_ref[i, ns[n], :, cs].astype(F32)
                    grad = st[k] + g * cc[n]
                    st[k] = e * grad
                    dg = st[k] * h
                    sg = sg + dg * rate
                    rt[k] = rt[k] + dg * s
                    sb = sb + grad * bb[n]
                    qb[n] = grad * x if ct == 0 else qb[n] + grad * x
                    qc[n] = gp * h if ct == 0 else qc[n] + gp * h
                sg_ref[i, :, cs] = sg
                sb_ref[i, :, cs] = sb
            rows = pl.ds(pl.multiple_of(i * SUB, SUB), SUB)
            for n in range(some):
                q_ref[rows, ns[n] * LANES : (ns[n] + 1) * LANES] = qb[n]
                p_ref[rows, ns[n] * LANES : (ns[n] + 1) * LANES] = qc[n]
            return tuple(st) + tuple(rt)

        at = [(ns[n], slice(None), cs) for n in range(some) for cs in cols]
        init = tuple(gst_ref[a] for a in at) + tuple(rt_ref[a] for a in at)
        out = lax.fori_loop(0, places, body, init, unroll=8)
        for j, a in enumerate(at):
            gst_ref[a] = out[j]
            rt_ref[a] = out[size + j]
    dims = (states * LANES, states)
    sel = lax.broadcasted_iota(jnp.int32, dims, 0) // LANES == lax.broadcasted_iota(
        jnp.int32, dims, 1
    )
    sel = sel.astype(BF16)
    qb_ref[...] = jnp.dot(q_ref[...].astype(BF16), sel, preferred_element_type=F32)
    qc_ref[...] = jnp.dot(p_ref[...].astype(BF16), sel, preferred_element_type=F32)
    rt_out[...] = rt_ref[...]


def backward(step, x, gs, gp, bin_vals, cout, rates, g0, hb, block=16):
    places, _, chans = step.shape
    states = rates.shape[0]
    count = places // block
    part = lambda width: pl.BlockSpec((block, SUB, width), lambda i: (count - 1 - i, 0, 0))
    flat = pl.BlockSpec((block * SUB, states), lambda i: (count - 1 - i, 0))
    return pl.pallas_call(
        backward_kernel,
        grid=(count,),
        in_specs=[
            part(chans),
            part(chans),
            part(chans),
            part(chans),
            part(states),
            part(states),
            whole(states, chans),
            whole(states, SUB, chans),
            pl.BlockSpec((block, states, SUB, chans), lambda i: (count - 1 - i, 0, 0, 0)),
        ],
        out_specs=[part(chans), part(chans), flat, flat, whole(states, SUB, chans)],
        out_shape=[
            jax.ShapeDtypeStruct((places, SUB, chans), F32),
            jax.ShapeDtypeStruct((places, SUB, chans), F32),
            jax.ShapeDtypeStruct((places * SUB, states), F32),
            jax.ShapeDtypeStruct((places * SUB, states), F32),
            jax.ShapeDtypeStruct((states, SUB, chans), F32),
        ],
        scratch_shapes=[
            pltpu.VMEM((states, SUB, chans), F32),
            pltpu.VMEM((states, SUB, chans), F32),
            pltpu.VMEM((block * SUB, states * LANES), F32),
            pltpu.VMEM((block * SUB, states * LANES), F32),
        ],
        compiler_params=pltpu.CompilerParams(vmem_limit_bytes=VMEM),
    )(step, x, gs, gp, bin_vals, cout, rates, g0, hb)


def passed_along(block, axis, distance):
    devices = range(lax.axis_size(axis))
    route = [(i - distance, i) for i in devices if i - distance in devices]
    return lax.ppermute(block, axis, route)


def sum_mp(block):
    return lax.psum(block, "mp")


def entering_states(total, part, rates, reverse):
    count = lax.axis_size("dp")
    place = lax.axis_index("dp")
    ahead = count - 1 - place if reverse else place
    totals = lax.all_gather(total, "dp")
    parts = lax.all_gather(part.astype(BF16), "dp")

    def one(lap, state):
        source = count - 1 - lap if reverse else lap
        decay = jnp.exp2(
            rates[:, None, :] * lax.dynamic_index_in_dim(totals, source, 0, False)[None]
        )
        return decay * state + lax.dynamic_index_in_dim(parts, source, 0, False).astype(F32)

    return lax.fori_loop(0, ahead, one, jnp.zeros(part.shape, F32))


def silu_slope(values):
    sigmoid_vals = jax.nn.sigmoid(values)
    return sigmoid_vals * (1.0 + values * (1.0 - sigmoid_vals))


def gelu_tanh(values):
    return jax.nn.gelu(values, approximate=True)


def norm_back(grad_norm, normed, inverse, norm_gain):
    scaled = grad_norm * norm_gain
    return inverse * (scaled - normed * jnp.mean(scaled * normed, axis=-1, keepdims=True))


def dot(a, b, dims):
    return lax.dot_general(a, b, (dims, ((), ())), preferred_element_type=F32)


NN = ((1,), (0,))
NT = ((1,), (1,))
TN = ((0,), (0,))


def per_device(
    tokens,
    routes,
    lengths,
    cotangent,
    first_gain,
    mixer_in,
    conv_weight,
    conv_bias,
    select_weight,
    step_weight,
    step_bias,
    decay_log,
    skip_gain,
    mixer_out,
    second_gain,
    router_weight,
    expert_up,
    up_bias,
    expert_down,
    down_bias,
):
    tok_count, model_width = tokens.shape
    kernel, chan_count = conv_weight.shape
    rank_size = step_weight.shape[0]
    state_size = decay_log.shape[0]
    expert_total = router_weight.shape[1]
    capacity = max(2, (5 * tok_count + 4 * expert_total - 1) // (4 * expert_total))
    slot_dev = SLOT_DEV
    seq_count = tok_count // slot_dev
    chunks = SUB // seq_count
    places_dev = slot_dev // chunks
    edge = kernel - 1
    device = lax.axis_index("dp")
    last = lax.axis_size("dp") - 1

    def reorder(values):
        width = values.shape[-1]
        return values.reshape(SUB, places_dev, width).transpose(1, 0, 2).reshape(tok_count, width)

    def restore(values):
        width = values.shape[-1]
        return values.reshape(places_dev, SUB, width).transpose(1, 0, 2).reshape(tok_count, width)

    rows = jnp.arange(tok_count)
    sub_ids = rows % SUB
    seq_ids = sub_ids // chunks
    local_place = (sub_ids % chunks) * places_dev + rows // SUB
    original = seq_ids * slot_dev + local_place
    places = device * slot_dev + local_place
    seq_length = jnp.sum(
        jnp.where(seq_ids[:, None] == jnp.arange(lengths.shape[0])[None], lengths[None], 0), axis=1
    )
    valid_mask = (places < seq_length).astype(F32)
    valid_col = valid_mask[:, None]
    even = (jnp.arange(SUB) % chunks == 0)[None, :, None]
    odd = (jnp.arange(SUB) % chunks == chunks - 1)[None, :, None]

    tok_vals = reorder(tokens).astype(F32)
    cot_low = reorder(cotangent)
    cot_vals = cot_low.astype(F32)
    route_ids = reorder(routes)[:, 0]

    expert_iota = jnp.arange(expert_total, dtype=jnp.int32)
    route_match = route_ids[:, None] == expert_iota[None]
    route_hot = route_match.astype(F32)
    live_hot = route_hot * valid_col
    before = (original[None, :] < original[:, None]).astype(BF16)
    earlier = dot(before, live_hot.astype(BF16), NN)
    position = jnp.sum(earlier * live_hot, axis=1).astype(jnp.int32)
    kept_mask = (valid_mask > 0.5) & (position < capacity)
    slot_ids = jnp.where(kept_mask, route_ids * capacity + position, -1)
    slot_iota = jnp.arange(expert_total * capacity, dtype=jnp.int32)
    dispatch = (slot_ids[None, :] == slot_iota[:, None]).astype(BF16)

    def to_experts(values):
        sent = dot(dispatch, values, NN).astype(BF16).reshape(expert_total, capacity, model_width)
        return lax.all_to_all(sent, "dp", split_axis=0, concat_axis=1, tiled=True)[0]

    def from_experts(values):
        back = lax.all_to_all(values[None], "dp", split_axis=1, concat_axis=0, tiled=True)
        return dot(dispatch, back.reshape(expert_total * capacity, model_width), TN)

    cot_rows = to_experts(cot_low)

    inverse_one = lax.rsqrt(jnp.mean(tok_vals * tok_vals, axis=-1, keepdims=True) + norm_eps)
    normed_one = tok_vals * inverse_one
    first_vals = first_gain.astype(F32)
    normed_in = (normed_one * first_vals).astype(BF16)
    mixer_in_flat = mixer_in.reshape(model_width, 2 * chan_count)
    both_in = dot(normed_in, mixer_in_flat, NN).astype(BF16)
    gate_pre = both_in[:, chan_count:].astype(F32)
    conv_seq = both_in[:, :chan_count].astype(F32).reshape(places_dev, SUB, chan_count)
    tail = conv_seq[places_dev - edge :]
    other_tail = passed_along(tail.astype(BF16), "dp", 1).astype(F32)
    lead_rows = jnp.where(even, jnp.roll(other_tail, 1 - chunks, axis=1), jnp.roll(tail, 1, axis=1))
    extended = jnp.concatenate([lead_rows, conv_seq], axis=0)
    conv_taps = conv_weight.astype(F32)
    conv_pre = jnp.zeros(conv_seq.shape, F32) + conv_bias.astype(F32)
    for offset in range(kernel):
        conv_pre = conv_pre + conv_taps[offset] * extended[offset : offset + places_dev]
    conv_pre = conv_pre.reshape(tok_count, chan_count)
    inner_vals = jax.nn.silu(conv_pre).astype(BF16)
    inner_f = inner_vals.astype(F32)
    projected = sum_mp(dot(inner_vals, select_weight, NN))
    low_rank = projected[:, :rank_size]
    bin_vals = projected[:, rank_size : rank_size + state_size]
    cout_vals = projected[:, rank_size + state_size :]
    low_high = low_rank.astype(BF16)
    low_rest = (low_rank - low_high.astype(F32)).astype(BF16)
    step_pre = dot(
        jnp.concatenate([low_high, low_rest], axis=1),
        jnp.concatenate([step_weight, step_weight], axis=0),
        NN,
    ) + step_bias.astype(F32)
    step_vals = valid_col * jax.nn.softplus(step_pre)
    decay_rates = -jnp.exp(decay_log.astype(F32))
    rates = decay_rates * LOG2E

    by_place = lambda values: values.reshape(places_dev, SUB, values.shape[-1])
    drive = step_vals * inner_f
    step_p, drive_p, bin_p, cout_p = map(by_place, (step_vals, drive, bin_vals, cout_vals))
    chunk_state = local_forward(step_p, drive_p, bin_p, rates)
    chunk_steps = jnp.sum(step_p, axis=0)
    chunk_decay = jnp.exp2(rates[:, None, :] * chunk_steps[None])
    split = lambda values: [values[..., k::chunks, :] for k in range(chunks)]
    joined = lambda parts: jnp.stack(parts, axis=2).reshape(parts[0].shape[0], SUB, chan_count)
    states, decays = split(chunk_state), split(chunk_decay)
    total = jnp.sum(chunk_steps.reshape(seq_count, chunks, chan_count), axis=1)
    summary = jnp.zeros_like(states[0])
    for k in range(chunks):
        summary = decays[k] * summary + states[k]
    state_in = [entering_states(total, summary, rates, False)]
    for k in range(chunks - 1):
        state_in.append(decays[k] * state_in[k] + states[k])
    scan_sum, states_before, last_states = forward(
        step_p, drive_p, bin_p, cout_p, rates, joined(state_in)
    )
    skip_vals = skip_gain.astype(F32)
    scan_out = scan_sum.reshape(tok_count, chan_count) + skip_vals * inner_f
    gate_act = jax.nn.silu(gate_pre)
    gated_vals = (scan_out * gate_act).astype(BF16)
    mixer_vals = sum_mp(dot(gated_vals, mixer_out, NN))
    residual = tok_vals + valid_col * mixer_vals
    inverse_two = lax.rsqrt(jnp.mean(residual * residual, axis=-1, keepdims=True) + norm_eps)
    normed_two = residual * inverse_two
    second_vals = second_gain.astype(F32)
    normed_out = (normed_two * second_vals).astype(BF16)
    logits = dot(normed_out, router_weight, NN)
    route_probs = jax.nn.softmax(logits, axis=-1)
    gate_prob = jnp.sum(route_probs * route_hot, axis=-1)

    expert_rows = to_experts(normed_out)
    own_hot = (expert_iota == device).astype(F32)
    row_probs = jnp.sum(
        jax.nn.softmax(dot(expert_rows, router_weight, NN), axis=-1) * own_hot, axis=-1
    )
    expert_grad = (row_probs[:, None] * cot_rows.astype(F32)).astype(BF16)
    up_mat, down_mat = expert_up[0], expert_down[0]
    hidden_pre = dot(expert_rows, up_mat, NN) + up_bias.astype(F32)
    hidden_act, gelu_pull = jax.vjp(gelu_tanh, hidden_pre)
    hidden_low = hidden_act.astype(BF16)
    result_part = dot(hidden_low, down_mat, NN)
    expert_result = (sum_mp(result_part) + down_bias.astype(F32)).astype(BF16)
    tok_result = from_experts(expert_result)
    block_out = (residual + gate_prob[:, None] * tok_result).astype(BF16)
    grad_down_bias = jnp.sum(expert_grad.astype(F32), axis=0)[None]
    grad_down = dot(hidden_low, expert_grad, TN)[None]
    grad_hidden = dot(expert_grad, down_mat, NT)
    grad_pre = gelu_pull(grad_hidden)[0].astype(BF16)
    grad_up_bias = jnp.sum(grad_pre.astype(F32), axis=0)[None]
    grad_up = dot(expert_rows, grad_pre, TN)[None]
    grad_rows = sum_mp(dot(grad_pre, up_mat, NT)).astype(BF16)
    grad_experts = from_experts(grad_rows)
    grad_gate = jnp.sum(cot_vals * tok_result, axis=-1)
    grad_logits = (grad_gate[:, None] * route_probs * (route_hot - gate_prob[:, None])).astype(BF16)
    grad_router = dot(normed_out, grad_logits, TN)
    grad_normed = grad_experts + dot(grad_logits, router_weight, NT)
    grad_second = jnp.sum(grad_normed * normed_two, axis=0)
    grad_resid = cot_vals + norm_back(grad_normed, normed_two, inverse_two, second_vals)
    grad_mixed = (valid_col * grad_resid).astype(BF16)
    grad_mixer_out = dot(gated_vals, grad_mixed, TN)
    grad_gated = dot(grad_mixed, mixer_out, NT)
    grad_scan = grad_gated * gate_act
    grad_gate_pre = grad_gated * scan_out * silu_slope(gate_pre)
    grad_skip = jnp.sum(grad_scan * inner_f, axis=0)

    gs_p = by_place(grad_scan)
    chunk_grad = split(local_backward(step_p, gs_p, cout_p, rates))
    back = jnp.zeros_like(chunk_grad[0])
    for k in reversed(range(chunks)):
        back = decays[k] * back + chunk_grad[k]
    grad_in = [entering_states(total, back, rates, True)]
    for k in reversed(range(1, chunks)):
        grad_in.insert(0, decays[k] * grad_in[0] + chunk_grad[k])
    gp_p = jnp.concatenate([jnp.zeros_like(gs_p[:1]), gs_p[:-1]], axis=0)
    rate_sum, state_bin, grad_bin, cout_shift, rate_parts = backward(
        step_p, drive_p, gs_p, gp_p, bin_p, cout_p, rates, joined(grad_in), states_before
    )
    rate_sum = rate_sum.reshape(tok_count, chan_count) * LN2
    state_bin = state_bin.reshape(tok_count, chan_count)
    last_cout = jnp.sum(gs_p[places_dev - 1][None] * last_states, axis=-1).T
    grad_cout = jnp.concatenate([cout_shift[SUB:], last_cout], axis=0)
    grad_decay_log = jnp.sum(rate_parts, axis=1) * decay_rates
    grad_step = rate_sum + inner_f * state_bin
    grad_inner = grad_scan * skip_vals + step_vals * state_bin
    grad_step_pre = grad_step * valid_col * jax.nn.sigmoid(step_pre)
    grad_step_bias = jnp.sum(grad_step_pre, axis=0)
    step_pre_low = grad_step_pre.astype(BF16)
    grad_step_weight = dot(low_high, step_pre_low, TN)
    grad_low_part = dot(step_pre_low, step_weight, NT)
    proj_part = jnp.concatenate([grad_low_part, grad_bin, grad_cout], axis=1)
    grad_proj = sum_mp(proj_part).astype(BF16)
    grad_select = dot(inner_vals, grad_proj, TN)
    grad_inner = grad_inner + dot(grad_proj, select_weight, NT)
    grad_conv = grad_inner * silu_slope(conv_pre)
    grad_conv_bias = jnp.sum(grad_conv, axis=0)
    grad_conv_seq = by_place(grad_conv)
    grad_taps = jnp.stack(
        [
            jnp.sum(grad_conv_seq * extended[offset : offset + places_dev], axis=(0, 1))
            for offset in range(kernel)
        ],
        axis=0,
    )
    head = grad_conv_seq[:edge]
    other_head = passed_along(head, "dp", -1)
    tail_rows = jnp.where(odd, jnp.roll(other_head, chunks - 1, axis=1), jnp.roll(head, -1, axis=1))
    grad_tail = jnp.concatenate([grad_conv_seq, tail_rows], axis=0)
    grad_conv_in = jnp.zeros(grad_conv_seq.shape, F32)
    for offset in range(kernel):
        lead = edge - offset
        grad_conv_in = grad_conv_in + conv_taps[offset] * grad_tail[lead : lead + places_dev]
    grad_both = jnp.concatenate(
        [grad_conv_in.reshape(tok_count, chan_count), grad_gate_pre], axis=1
    ).astype(BF16)
    grad_mixer_in = dot(normed_in, grad_both, TN)
    input_part = dot(grad_both, mixer_in_flat, NT)
    grad_normed_in = sum_mp(input_part.astype(BF16)).astype(F32)
    grad_first = jnp.sum(grad_normed_in * normed_one, axis=0)
    token_grad = grad_resid + norm_back(grad_normed_in, normed_one, inverse_one, first_vals)
    summed = lax.psum(
        (
            grad_first,
            grad_mixer_in,
            grad_taps,
            grad_conv_bias,
            grad_select,
            grad_step_weight,
            grad_step_bias,
            grad_decay_log,
            grad_skip,
            grad_mixer_out,
            grad_second,
            grad_router,
        ),
        "dp",
    )
    return (
        restore(block_out),
        restore(token_grad),
        summed[0],
        summed[1].reshape(mixer_in.shape),
        *summed[2:],
        grad_up,
        grad_up_bias,
        grad_down,
        grad_down_bias,
    )


def solution(mesh):
    return jax.shard_map(
        per_device,
        mesh=mesh,
        in_specs=(
            P("dp", None),
            P("dp", None),
            P(),
            P("dp", None),
            P(),
            P(None, None, "mp"),
            P(None, "mp"),
            P("mp"),
            P("mp", None),
            P(None, "mp"),
            P("mp"),
            P(None, "mp"),
            P("mp"),
            P("mp", None),
            P(),
            P(),
            P("dp", None, "mp"),
            P("dp", "mp"),
            P("dp", "mp", None),
            P("dp", None),
        ),
        out_specs=(
            P("dp", None),
            P("dp", None),
            P(),
            P(None, None, "mp"),
            P(None, "mp"),
            P("mp"),
            P("mp", None),
            P(None, "mp"),
            P("mp"),
            P(None, "mp"),
            P("mp"),
            P("mp", None),
            P(),
            P(),
            P("dp", None, "mp"),
            P("dp", "mp"),
            P("dp", "mp", None),
            P("dp", None),
        ),
        check_vma=False,
    )
```

```python
import functools

import jax
import jax.numpy as jnp
from jax import lax
from jax.experimental import pallas as pl
from jax.experimental.pallas import tpu as pltpu
from jax.sharding import PartitionSpec as P

F32 = jnp.float32
BF16 = jnp.bfloat16
SLOT_DEV = 256
LANES = 128
SUB = 8
LOG2E = 1.4426950408889634
LN2 = 0.6931471805599453
VMEM = 48 * 2**20
norm_eps = 1e-05
MESH = pl.DeviceIdType.MESH


NN = ((1,), (0,))
NT = ((1,), (1,))
TN = ((0,), (0,))


def dot(a, b, dims):
    return lax.dot_general(a, b, (dims, ((), ())), preferred_element_type=F32)


def lane(col):
    return jnp.broadcast_to(col, (SUB, LANES))


def row(ref, n, cs):
    return jnp.broadcast_to(ref[n : n + 1, cs], (SUB, LANES))


def tiles(count):
    return [slice(ct * LANES, (ct + 1) * LANES) for ct in range(count // LANES)]


def whole(*dims):
    return pl.BlockSpec(dims, lambda i: (0,) * len(dims))


def local_forward_kernel(step_ref, x_ref, bin_ref, rates_ref, out_ref):
    places, chans = step_ref.shape[0], step_ref.shape[2]
    states, half = rates_ref.shape[0], 8
    cols = tiles(chans)
    for nh in range(states // half):
        ns = [nh * half + n for n in range(half)]

        def body(i, st):
            st = list(st)
            b = bin_ref[i]
            bb = [lane(b[:, n : n + 1]) for n in ns]
            for ct, cs in enumerate(cols):
                s = step_ref[i, :, cs]
                x = x_ref[i, :, cs]
                for n in range(half):
                    k = n * len(cols) + ct
                    e = jnp.exp2(s * row(rates_ref, ns[n], cs))
                    st[k] = e * st[k] + x * bb[n]
            return tuple(st)

        zero = tuple(jnp.zeros((SUB, LANES), F32) for _ in range(half * len(cols)))
        st = lax.fori_loop(0, places, body, zero, unroll=8)
        for n in range(half):
            for ct, cs in enumerate(cols):
                out_ref[ns[n], :, cs] = st[n * len(cols) + ct]


def local_forward(step, x, bin_vals, rates):
    return pl.pallas_call(
        local_forward_kernel,
        out_shape=jax.ShapeDtypeStruct((rates.shape[0], SUB, step.shape[2]), F32),
        compiler_params=pltpu.CompilerParams(vmem_limit_bytes=VMEM),
    )(step, x, bin_vals, rates)


def forward_kernel(
    step_ref, x_ref, bin_ref, cout_ref, rates_ref, h0_ref, y_ref, hb_ref, hf_ref, st_ref
):
    places, chans = step_ref.shape[0], step_ref.shape[2]
    states, half = rates_ref.shape[0], 8
    cols = tiles(chans)

    @pl.when(pl.program_id(0) == 0)
    def _():
        st_ref[...] = h0_ref[...]

    for nh in range(states // half):
        ns = [nh * half + n for n in range(half)]

        def body(i, st):
            st = list(st)
            b = bin_ref[i]
            c = cout_ref[i]
            bb = [lane(b[:, n : n + 1]) for n in ns]
            cc = [lane(c[:, n : n + 1]) for n in ns]
            for ct, cs in enumerate(cols):
                s = step_ref[i, :, cs]
                x = x_ref[i, :, cs]
                y = y_ref[i, :, cs] if nh else jnp.zeros((SUB, LANES), F32)
                for n in range(half):
                    k = n * len(cols) + ct
                    hb_ref[i, ns[n], :, cs] = st[k].astype(hb_ref.dtype)
                    e = jnp.exp2(s * row(rates_ref, ns[n], cs))
                    st[k] = e * st[k] + x * bb[n]
                    y = y + cc[n] * st[k]
                y_ref[i, :, cs] = y
            return tuple(st)

        st = tuple(st_ref[n, :, cs] for n in ns for cs in cols)
        st = lax.fori_loop(0, places, body, st, unroll=8)
        for n in range(half):
            for ct, cs in enumerate(cols):
                st_ref[ns[n], :, cs] = st[n * len(cols) + ct]
    hf_ref[...] = st_ref[...]


def forward(step, x, bin_vals, cout, rates, h0, block=16):
    places, _, chans = step.shape
    states = rates.shape[0]
    part = lambda width: pl.BlockSpec((block, SUB, width), lambda i: (i, 0, 0))
    return pl.pallas_call(
        forward_kernel,
        grid=(places // block,),
        in_specs=[
            part(chans),
            part(chans),
            part(states),
            part(states),
            whole(states, chans),
            whole(states, SUB, chans),
        ],
        out_specs=[
            part(chans),
            pl.BlockSpec((block, states, SUB, chans), lambda i: (i, 0, 0, 0)),
            whole(states, SUB, chans),
        ],
        out_shape=[
            jax.ShapeDtypeStruct((places, SUB, chans), F32),
            jax.ShapeDtypeStruct((places, states, SUB, chans), BF16),
            jax.ShapeDtypeStruct((states, SUB, chans), F32),
        ],
        scratch_shapes=[pltpu.VMEM((states, SUB, chans), F32)],
        compiler_params=pltpu.CompilerParams(vmem_limit_bytes=VMEM),
    )(step, x, bin_vals, cout, rates, h0)


def local_backward_kernel(step_ref, gs_ref, cout_ref, rates_ref, out_ref):
    places, chans = step_ref.shape[0], step_ref.shape[2]
    states, half = rates_ref.shape[0], 8
    cols = tiles(chans)
    for nh in range(states // half):
        ns = [nh * half + n for n in range(half)]

        def body(lap, st):
            i = places - 1 - lap
            st = list(st)
            c = cout_ref[i]
            cc = [lane(c[:, n : n + 1]) for n in ns]
            for ct, cs in enumerate(cols):
                s = step_ref[i, :, cs]
                g = gs_ref[i, :, cs]
                for n in range(half):
                    k = n * len(cols) + ct
                    e = jnp.exp2(s * row(rates_ref, ns[n], cs))
                    st[k] = e * (st[k] + g * cc[n])
            return tuple(st)

        zero = tuple(jnp.zeros((SUB, LANES), F32) for _ in range(half * len(cols)))
        st = lax.fori_loop(0, places, body, zero, unroll=8)
        for n in range(half):
            for ct, cs in enumerate(cols):
                out_ref[ns[n], :, cs] = st[n * len(cols) + ct]


def local_backward(step, gs, cout, rates):
    return pl.pallas_call(
        local_backward_kernel,
        out_shape=jax.ShapeDtypeStruct((rates.shape[0], SUB, step.shape[2]), F32),
        compiler_params=pltpu.CompilerParams(vmem_limit_bytes=VMEM),
    )(step, gs, cout, rates)


def backward_kernel(
    step_ref,
    x_ref,
    gs_ref,
    gp_ref,
    bin_ref,
    cout_ref,
    rates_ref,
    g0_ref,
    hb_ref,
    inner_ref,
    slope_ref,
    low_ref,
    weight_ref,
    skip_ref,
    base_ref,
    low_out,
    qb_ref,
    qc_ref,
    rt_out,
    sw_ref,
    sbias_ref,
    gst_ref,
    rt_ref,
    q_ref,
    p_ref,
    sg_ref,
    sb_ref,
):
    places, chans = step_ref.shape[0], step_ref.shape[2]
    states, some = rates_ref.shape[0], 4
    cols = tiles(chans)

    @pl.when(pl.program_id(0) == 0)
    def _():
        gst_ref[...] = g0_ref[...]
        rt_ref[...] = jnp.zeros_like(rt_ref)
        sw_ref[...] = jnp.zeros_like(sw_ref)
        sbias_ref[...] = jnp.zeros_like(sbias_ref)

    for nq in range(states // some):
        ns = [nq * some + n for n in range(some)]
        size = some * len(cols)

        def body(lap, carry):
            i = places - 1 - lap
            st, rt = list(carry[:size]), list(carry[size:])
            b = bin_ref[i]
            c = cout_ref[i]
            bb = [lane(b[:, n : n + 1]) for n in ns]
            cc = [lane(c[:, n : n + 1]) for n in ns]
            qb, qc = [None] * some, [None] * some
            for ct, cs in enumerate(cols):
                s = step_ref[i, :, cs]
                x = x_ref[i, :, cs]
                g = gs_ref[i, :, cs]
                gp = gp_ref[i, :, cs]
                sg = sg_ref[i, :, cs] if nq else jnp.zeros((SUB, LANES), F32)
                sb = sb_ref[i, :, cs] if nq else jnp.zeros((SUB, LANES), F32)
                for n in range(some):
                    k = n * len(cols) + ct
                    rate = row(rates_ref, ns[n], cs)
                    e = jnp.exp2(s * rate)
                    h = hb_ref[i, ns[n], :, cs].astype(F32)
                    grad = st[k] + g * cc[n]
                    st[k] = e * grad
                    dg = st[k] * h
                    sg = sg + dg * rate
                    rt[k] = rt[k] + dg * s
                    sb = sb + grad * bb[n]
                    qb[n] = grad * x if ct == 0 else qb[n] + grad * x
                    qc[n] = gp * h if ct == 0 else qc[n] + gp * h
                sg_ref[i, :, cs] = sg
                sb_ref[i, :, cs] = sb
            rows = pl.ds(pl.multiple_of(i * SUB, SUB), SUB)
            for n in range(some):
                q_ref[rows, ns[n] * LANES : (ns[n] + 1) * LANES] = qb[n]
                p_ref[rows, ns[n] * LANES : (ns[n] + 1) * LANES] = qc[n]
            return tuple(st) + tuple(rt)

        at = [(ns[n], slice(None), cs) for n in range(some) for cs in cols]
        init = tuple(gst_ref[a] for a in at) + tuple(rt_ref[a] for a in at)
        out = lax.fori_loop(0, places, body, init, unroll=8)
        for j, a in enumerate(at):
            gst_ref[a] = out[j]
            rt_ref[a] = out[size + j]
    dims = (states * LANES, states)
    sel = lax.broadcasted_iota(jnp.int32, dims, 0) // LANES == lax.broadcasted_iota(
        jnp.int32, dims, 1
    )
    sel = sel.astype(BF16)
    qb_ref[...] = jnp.dot(q_ref[...].astype(BF16), sel, preferred_element_type=F32)
    qc_ref[...] = jnp.dot(p_ref[...].astype(BF16), sel, preferred_element_type=F32)
    rt_out[...] = rt_ref[...]
    flat = lambda ref: ref[...].reshape(places * SUB, chans)
    sb = flat(sb_ref)
    base_ref[...] = flat(gs_ref) * skip_ref[...] + flat(step_ref) * sb
    pre = (flat(sg_ref) * LN2 + inner_ref[...].astype(F32) * sb) * slope_ref[...]
    sbias_ref[...] += jnp.sum(pre.reshape(places, SUB, chans), axis=0)
    pre = pre.astype(BF16)
    sw_ref[...] += dot(low_ref[...], pre, TN)
    low_out[...] = dot(pre, weight_ref[...], NT)


def backward(
    step, x, gs, gp, bin_vals, cout, rates, g0, hb, inner, slope, low, weight, skip, block=16
):
    places, _, chans = step.shape
    states = rates.shape[0]
    rank = weight.shape[0]
    count = places // block
    part = lambda width: pl.BlockSpec((block, SUB, width), lambda i: (count - 1 - i, 0, 0))
    flat = lambda width: pl.BlockSpec((block * SUB, width), lambda i: (count - 1 - i, 0))
    rows = places * SUB
    return pl.pallas_call(
        backward_kernel,
        grid=(count,),
        in_specs=[
            part(chans),
            part(chans),
            part(chans),
            part(chans),
            part(states),
            part(states),
            whole(states, chans),
            whole(states, SUB, chans),
            pl.BlockSpec((block, states, SUB, chans), lambda i: (count - 1 - i, 0, 0, 0)),
            flat(chans),
            flat(chans),
            flat(rank),
            whole(rank, chans),
            whole(1, chans),
        ],
        out_specs=[
            flat(chans),
            flat(rank),
            flat(states),
            flat(states),
            whole(states, SUB, chans),
            whole(rank, chans),
            whole(SUB, chans),
        ],
        out_shape=[
            jax.ShapeDtypeStruct((rows, chans), F32),
            jax.ShapeDtypeStruct((rows, rank), F32),
            jax.ShapeDtypeStruct((rows, states), F32),
            jax.ShapeDtypeStruct((rows, states), F32),
            jax.ShapeDtypeStruct((states, SUB, chans), F32),
            jax.ShapeDtypeStruct((rank, chans), F32),
            jax.ShapeDtypeStruct((SUB, chans), F32),
        ],
        scratch_shapes=[
            pltpu.VMEM((states, SUB, chans), F32),
            pltpu.VMEM((states, SUB, chans), F32),
            pltpu.VMEM((block * SUB, states * LANES), F32),
            pltpu.VMEM((block * SUB, states * LANES), F32),
            pltpu.VMEM((block, SUB, chans), F32),
            pltpu.VMEM((block, SUB, chans), F32),
        ],
        compiler_params=pltpu.CompilerParams(vmem_limit_bytes=VMEM),
    )(step, x, gs, gp, bin_vals, cout, rates, g0, hb, inner, slope, low, weight, skip)


def passed_along(block, axis, distance):
    devices = range(lax.axis_size(axis))
    route = [(i - distance, i) for i in devices if i - distance in devices]
    return lax.ppermute(block, axis, route)


def mp_pair():
    j = lax.axis_index("mp")
    return j, j + 1 - 2 * (j % 2), (j + 2) % 4


def greet(others):
    barrier = pltpu.get_barrier_semaphore()
    for other in others:
        pl.semaphore_signal(barrier, inc=1, device_id=other, device_id_type=MESH)
    pl.semaphore_wait(barrier, len(others))


def sending(src, dst, send, recv, device):
    copy = pltpu.make_async_remote_copy(
        src_ref=src, dst_ref=dst, send_sem=send, recv_sem=recv, device_id=device, device_id_type=MESH
    )
    copy.start()
    return copy


def vmem_call(kernel, out_shape, scratch, collective_id, *args, cost=0):
    space = pl.BlockSpec(memory_space=pltpu.VMEM)
    return pl.pallas_call(
        kernel,
        out_shape=out_shape,
        in_specs=[space] * len(args),
        out_specs=jax.tree.map(lambda _: space, out_shape),
        scratch_shapes=scratch,
        compiler_params=pltpu.CompilerParams(
            collective_id=collective_id, has_side_effects=True, vmem_limit_bytes=VMEM
        ),
    )(*args)


def sum_kernel(count, x_ref, out_ref, ra, sb, rb, send, recv):
    j, near, far = mp_pair()
    near, far = {"mp": near}, {"mp": far}
    half = x_ref.shape[0] // 2
    size = half // count
    own = pl.multiple_of((j % 2) * half, half)
    other = pl.multiple_of((1 - j % 2) * half, half)
    greet([near, far])
    first = [
        sending(x_ref.at[pl.ds(other + k * size, size)], ra.at[k], send.at[0, k], recv.at[0, k], near)
        for k in range(count)
    ]
    second, third = [], []
    for k in range(count):
        first[k].wait_recv()
        mine = x_ref[pl.ds(own + k * size, size), :].astype(F32)
        sb[k] = (mine + ra[k].astype(F32)).astype(sb.dtype)
        second.append(sending(sb.at[k], rb.at[k], send.at[1, k], recv.at[1, k], far))
    for k in range(count):
        second[k].wait_recv()
        rows = pl.ds(own + k * size, size)
        out_ref[rows, :] = (sb[k].astype(F32) + rb[k].astype(F32)).astype(out_ref.dtype)
        third.append(
            sending(out_ref.at[rows], out_ref.at[rows], send.at[2, k], recv.at[2, k], near)
        )
    for k in range(count):
        third[k].wait_recv()
    for copy in first + second + third:
        copy.wait_send()


def sum_mp(x, collective_id, count=4):
    rows, width = x.shape
    slots = pltpu.VMEM((count, rows // 2 // count, width), x.dtype)
    sems = pltpu.SemaphoreType.DMA((3, count))
    return vmem_call(
        functools.partial(sum_kernel, count),
        jax.ShapeDtypeStruct(x.shape, x.dtype),
        [slots, slots, slots, sems, sems],
        collective_id,
        x,
    )


def half_turn(tile):
    return pltpu.roll(tile, SUB // 2, 0)


def exchange_kernel(n, reverse, part_ref, total_ref, rates_ref, packed_ref, *refs):
    if reverse:
        all_ref, out_ref, sbuf, rbuf, send, recv = refs
    else:
        out_ref, all_ref, sbuf, rbuf, send, recv = refs
    g = lax.axis_index("dp")
    states, chans = rates_ref.shape
    pairs = states // 2
    greet([{"dp": (g + k) % n} for k in range(1, n)])
    upper = lax.broadcasted_iota(jnp.int32, (SUB, chans), 0) >= SUB // 2
    total = total_ref[...]
    copies = []
    if not reverse:
        all_ref[0] = total + half_turn(total)
        copies += [
            sending(all_ref.at[0], all_ref.at[k], send.at[1, k], recv.at[1, k], {"dp": (g + k) % n})
            for k in range(1, n)
        ]
    decay = lambda m: jnp.exp2(jnp.broadcast_to(rates_ref[m : m + 1, :], (SUB, chans)) * total)

    def summary(m):
        part = part_ref[m]
        return part + decay(m) * half_turn(part)

    def packed(p):
        low, high = summary(p), summary(p + pairs)
        if reverse:
            return jnp.where(upper, half_turn(high), low)
        return jnp.where(upper, high, half_turn(low))

    for p in range(0, pairs, 2):
        sbuf[p * SUB : (p + 2) * SUB, :] = jnp.concatenate([packed(p), packed(p + 1)], axis=0).astype(BF16)
    copies += [
        sending(sbuf, rbuf.at[k], send.at[0, k], recv.at[0, k], {"dp": (g + k) % n})
        for k in range(1, n)
    ]
    for copy in copies:
        copy.wait_recv()

    def one(lap, held):
        away = n - 1 - lap
        slot = n - away if reverse else away
        use = (g + away < n) if reverse else (away <= g)
        steps = all_ref[slot]
        new = []
        for p in range(0, pairs, 2):
            got = rbuf[slot, p * SUB : (p + 2) * SUB, :].astype(F32)
            for q in (p, p + 1):
                fall = jnp.exp2(packed_ref[q] * steps)
                value = fall * held[q] + got[(q - p) * SUB : (q - p + 1) * SUB]
                new.append(jnp.where(use, value, held[q]))
        return tuple(new)

    zero = tuple(jnp.zeros((SUB, chans), F32) for _ in range(pairs))
    held = lax.fori_loop(0, n - 1, one, zero)
    for m in range(states):
        state = held[m % pairs]
        if (m >= pairs) != reverse:
            state = half_turn(state)
        later = half_turn(decay(m) * state + part_ref[m])
        out_ref[m] = jnp.where(upper, state, later) if reverse else jnp.where(upper, later, state)
    for copy in copies:
        copy.wait_send()


def exchange(n, reverse, collective_id, part, total, rates, *held):
    states, chans = rates.shape
    pairs = states // 2
    wide = lambda r: jnp.broadcast_to(r[:, None, :], (pairs, SUB // 2, chans))
    packed = jnp.concatenate([wide(rates[:pairs]), wide(rates[pairs:])], axis=1)
    entering = jax.ShapeDtypeStruct((states, SUB, chans), F32)
    totals = jax.ShapeDtypeStruct((n, SUB, chans), F32)
    sems = pltpu.SemaphoreType.DMA((2, n))
    return vmem_call(
        functools.partial(exchange_kernel, n, reverse),
        entering if reverse else [entering, totals],
        [pltpu.VMEM((pairs * SUB, chans), BF16), pltpu.VMEM((n, pairs * SUB, chans), BF16), sems, sems],
        collective_id,
        part, total, rates, packed, *held,
    )


def spread(out_ref, n, g, y, c, near, far, arrived, send, recv):
    hr, hc = out_ref.shape[1] // 2, out_ref.shape[2] // 2
    at = lambda s, u: out_ref.at[s, pl.ds(pl.multiple_of(u * hr, hr), hr), pl.ds(pl.multiple_of(c * hc, hc), hc)]
    outs, mids, ends = [], [], []

    def first(k):
        arrived(k)
        s = (g + n - k) % n
        mids.append(sending(at(s, y), at(s, y), send.at[1, k], recv.at[1, k], far))
        outs.append(sending(at(s, y), at(s, y), send.at[2, k], recv.at[2, k], near))

    def second(k):
        s = (g + n - k) % n
        mids[k].wait_recv()
        ends.append(sending(at(s, 1 - y), at(s, 1 - y), send.at[3, k], recv.at[3, k], near))

    def finish():
        for copy in outs + ends:
            copy.wait_recv()
        for copy in outs + mids + ends:
            copy.wait_send()

    return first, second, finish


def dispatch_kernel(n, x_ref, out_ref, send, recv, local):
    g = lax.axis_index("dp")
    j, near, far = mp_pair()
    near, far = {"mp": near}, {"mp": far}
    y, c = j // 2, j % 2
    hr, hc = out_ref.shape[1] // 2, out_ref.shape[2] // 2
    greet([near, far] + [{"dp": (g + k) % n} for k in range(1, n)])
    rows = pl.ds(pl.multiple_of(y * hr, hr), hr)
    place = out_ref.at[g, rows, pl.ds(pl.multiple_of(c * hc, hc), hc)]
    own = pltpu.make_async_copy(x_ref.at[g], place, local)
    own.start()
    copies = [own] + [
        sending(x_ref.at[(g + k) % n], place, send.at[0, k], recv.at[0, k], {"dp": (g + k) % n})
        for k in range(1, n)
    ]
    arrived = lambda k: copies[k].wait_recv() if k else own.wait()
    first, second, finish = spread(out_ref, n, g, y, c, near, far, arrived, send, recv)
    for k in range(n + 1):
        if k < n:
            first(k)
        if k >= 1:
            second(k - 1)
    finish()
    for copy in copies[1:]:
        copy.wait_send()


def dispatch_rows(n, collective_id, x):
    sems = pltpu.SemaphoreType.DMA((4, n))
    return vmem_call(
        functools.partial(dispatch_kernel, n),
        jax.ShapeDtypeStruct((n, 2 * x.shape[1], 2 * x.shape[2]), x.dtype),
        [sems, sems, pltpu.SemaphoreType.DMA],
        collective_id, x,
    )


def return_kernel(n, count, bias_ref, *refs):
    parts, refs = refs[:count], refs[count:]
    outs, refs = refs[:count], refs[count:]
    ra, sb, rb, qb, send, recv = refs
    g = lax.axis_index("dp")
    j, near, far = mp_pair()
    near, far = {"mp": near}, {"mp": far}
    y, c = j // 2, j % 2
    rows, hr, hc = outs[0].shape[1], outs[0].shape[1] // 2, outs[0].shape[2] // 2
    greet([near, far] + [{"dp": (g + k) % n} for k in range(1, n)])
    mine = pl.ds(pl.multiple_of(c * hc, hc), hc)
    theirs = pl.ds(pl.multiple_of((1 - c) * hc, hc), hc)
    up = pl.ds(pl.multiple_of(y * hr, hr), hr)
    down = pl.ds(pl.multiple_of((1 - y) * hr, hr), hr)
    total = count * n
    near_copies, far_copies, back_copies = [], [], []
    for t in range(total):
        a, k = t // n, t % n
        to = (g + k) % n
        near_copies.append(
            sending(parts[a].at[to, :, theirs], ra.at[t], send.at[4, t], recv.at[4, t], near)
        )

    def pair_sum(t):
        a, k = t // n, t % n
        near_copies[t].wait_recv()
        sb[t] = (parts[a][(g + k) % n, :, mine].astype(F32) + ra[t].astype(F32)).astype(BF16)
        far_copies.append(sending(sb.at[t, down], rb.at[t], send.at[5, t], recv.at[5, t], far))

    def full_sum(t):
        a, k = t // n, t % n
        far_copies[t].wait_recv()
        value = sb[t, up, :].astype(F32) + rb[t].astype(F32)
        if a == 0:
            value = value + bias_ref[:, mine]
        if k == 0:
            outs[a][g, up, mine] = value.astype(BF16)
            back_copies.append(None)
        else:
            to = (g + k) % n
            qb[t] = value.astype(BF16)
            back_copies.append(
                sending(qb.at[t], outs[a].at[g, up, mine], send.at[0, t], recv.at[0, t], {"dp": to})
            )

    spreads = []
    for a in range(count):
        arrived = lambda k, a=a: back_copies[a * n + k].wait_recv() if k else None
        spreads.append(
            spread(outs[a], n, g, y, c, near, far, arrived, send.at[:, pl.ds(a * n, n)], recv.at[:, pl.ds(a * n, n)])
        )
    for t in range(total + 5):
        if t < total:
            pair_sum(t)
        if 0 <= t - 1 < total:
            full_sum(t - 1)
        if 0 <= t - 3 < total:
            spreads[(t - 3) // n][0]((t - 3) % n)
        if 0 <= t - 5 < total:
            spreads[(t - 5) // n][1]((t - 5) % n)
    for _, _, finish in spreads:
        finish()
    for copy in near_copies + far_copies + [b for b in back_copies if b is not None]:
        copy.wait_send()


def return_rows(n, collective_id, bias, *parts):
    _, rows, width = parts[0].shape
    count = len(parts)
    sems = pltpu.SemaphoreType.DMA((6, count * n))
    return vmem_call(
        functools.partial(return_kernel, n, count),
        [jax.ShapeDtypeStruct(p.shape, BF16) for p in parts],
        [
            pltpu.VMEM((count * n, rows, width // 2), BF16),
            pltpu.VMEM((count * n, rows, width // 2), BF16),
            pltpu.VMEM((count * n, rows // 2, width // 2), BF16),
            pltpu.VMEM((count * n, rows // 2, width // 2), BF16),
            sems, sems,
        ],
        collective_id, bias, *parts,
    )


def total_kernel(n, x_ref, out_ref, ra, sb, rc, send, recv):
    g = lax.axis_index("dp")
    odd = g % 2
    pair = {"dp": g + 1 - 2 * odd}
    m = n // 2
    z = g // 2
    like = [{"dp": 2 * ((z + k) % m) + odd} for k in range(1, m)]
    greet([pair] + like)
    order = [(z + k) % m for k in range(1, m)] + [z]
    first = [
        sending(x_ref.at[2 * order[k] + 1 - odd], ra.at[k], send.at[0, k], recv.at[0, k], pair)
        for k in range(m)
    ]
    second = []
    for k in range(m):
        first[k].wait_recv()
        sb[k] = (x_ref[2 * order[k] + odd].astype(F32) + ra[k].astype(F32)).astype(BF16)
        if k < m - 1:
            second.append(sending(sb.at[k], rc.at[k], send.at[1, k], recv.at[1, k], like[k]))
    value = sb[m - 1].astype(F32)
    for copy in second:
        copy.wait_recv()
    for k in range(m - 1):
        value = value + rc[k].astype(F32)
    out_ref[g] = value.astype(BF16)
    third = [
        sending(out_ref.at[g], out_ref.at[g], send.at[2, k], recv.at[2, k], like[k]) for k in range(m - 1)
    ]
    fourth = [sending(out_ref.at[g], out_ref.at[g], send.at[3, 0], recv.at[3, 0], pair)]
    for k in range(m - 1):
        third[k].wait_recv()
        b = 2 * ((z + m - 1 - k) % m) + odd
        fourth.append(sending(out_ref.at[b], out_ref.at[b], send.at[3, k + 1], recv.at[3, k + 1], pair))
    for copy in fourth:
        copy.wait_recv()
    for copy in first + second + third + fourth:
        copy.wait_send()


def total_dp(n, collective_id, x):
    _, rows, width = x.shape
    m = n // 2
    slots = lambda count: pltpu.VMEM((count, rows, width), BF16)
    sems = pltpu.SemaphoreType.DMA((4, m))
    return vmem_call(
        functools.partial(total_kernel, n),
        jax.ShapeDtypeStruct(x.shape, BF16),
        [slots(m), slots(m), slots(m), sems, sems],
        collective_id, x,
    )


def ds(start, size):
    return pl.ds(pl.multiple_of(start, size), size)


def mixer_back_kernel(
    n,
    proj_ref,
    select_ref,
    inner_ref,
    base_ref,
    pre_ref,
    both_ref,
    lead_ref,
    gate_ref,
    normed_ref,
    weight_ref,
    taps_ref,
    gsel_ref,
    sums_ref,
    gin_ref,
    part_ref,
    conv_s,
    ext_s,
    both_s,
    got,
    send,
    recv,
):
    g = lax.axis_index("dp")
    rows, chans = inner_ref.shape
    kernel = taps_ref.shape[0]
    edge = (kernel - 1) * SUB
    before, after = {"dp": (g + n - 1) % n}, {"dp": (g + 1) % n}
    greet([before, after])
    size = 256
    sums_ref[...] = jnp.zeros_like(sums_ref)
    ext_s[0:edge, :] = lead_ref[...]

    def conv_block(b):
        at = ds(b * size, size)
        grad = base_ref[at, :] + dot(proj_ref[at, :], select_ref[...], NT)
        grad = grad * silu_slope(pre_ref[at, :])
        conv_s[at, :] = grad
        ext_s[pl.ds(pl.multiple_of(b * size + edge, SUB), size), :] = both_ref[at, 0:chans].astype(F32)

    conv_block(0)
    copy = sending(conv_s.at[0:edge], got, send, recv, before)

    def rest(b, _):
        conv_block(b)
        return 0

    lax.fori_loop(1, rows // size, rest, 0)
    gsel_ref[...] = dot(proj_ref[...], inner_ref[...], TN)

    def taps(b, _):
        grad = conv_s[ds(b * size, size), :]
        folded = lambda v: jnp.sum(v.reshape(size // SUB, SUB, chans), axis=0)
        for k in range(kernel):
            past = ext_s[pl.ds(pl.multiple_of(b * size + k * SUB, SUB), size), :]
            sums_ref[k] += folded(grad * past)
        sums_ref[kernel] += folded(grad)
        return 0

    lax.fori_loop(0, rows // size, taps, 0)
    copy.wait_recv()
    upper = lax.broadcasted_iota(jnp.int32, (SUB, chans), 0) >= SUB // 2
    some = jnp.where(g < n - 1, 1.0, 0.0)
    for k in range(kernel - 1):
        at = slice(k * SUB, (k + 1) * SUB)
        tail = half_turn(jnp.where(upper, conv_s[at, :], got[at, :] * some))
        conv_s[rows + k * SUB : rows + (k + 1) * SUB, :] = tail

    def back(b, _):
        at = ds(b * size, size)
        total = jnp.zeros((size, chans), F32)
        for k in range(kernel):
            later = conv_s[pl.ds(pl.multiple_of(b * size + (kernel - 1 - k) * SUB, SUB), size), :]
            total = total + taps_ref[k : k + 1, :] * later
        both_s[at, 0:chans] = total.astype(BF16)
        both_s[at, chans : 2 * chans] = gate_ref[at, :]
        part_ref[at, :] = dot(both_s[at, :], weight_ref[...], NT).astype(BF16)
        return 0

    lax.fori_loop(0, rows // size, back, 0)

    def weights(b, _):
        at = ds(b * size, size)
        gin_ref[:, at] = dot(normed_ref[...], both_s[:, at], TN).astype(BF16)
        return 0

    lax.fori_loop(0, 2 * chans // size, weights, 0)
    copy.wait_send()


def mixer_back(n, collective_id, proj, select, inner, base, pre, both, lead, gate, normed, weight, taps):
    rows, chans = inner.shape
    width = normed.shape[1]
    kernel = taps.shape[0]
    edge = (kernel - 1) * SUB
    shape = jax.ShapeDtypeStruct
    return vmem_call(
        functools.partial(mixer_back_kernel, n),
        [
            shape((select.shape[1], chans), F32),
            shape((kernel + 1, SUB, chans), F32),
            shape((width, 2 * chans), BF16),
            shape((rows, width), BF16),
        ],
        [
            pltpu.VMEM((rows + edge, chans), F32),
            pltpu.VMEM((rows + edge, chans), F32),
            pltpu.VMEM((rows, 2 * chans), BF16),
            pltpu.VMEM((edge, chans), F32),
            pltpu.SemaphoreType.DMA,
            pltpu.SemaphoreType.DMA,
        ],
        collective_id, proj, select, inner, base, pre, both, lead, gate, normed, weight, taps,
    )


def token_back_kernel(
    cuts,
    slot_ref,
    result_ref,
    rows_ref,
    residual_ref,
    probs_ref,
    hot_ref,
    normed_ref,
    cot_ref,
    valid_ref,
    gain_ref,
    router_ref,
    gated_ref,
    out_ref,
    scan_ref,
    both_ref,
    inner_ref,
    block_ref,
    resid_ref,
    gs_ref,
    gate_ref,
    router_out,
    second_ref,
    mixer_ref,
    skip_ref,
    mixed_s,
    block_s,
):
    rows, width = residual_ref.shape
    chans = inner_ref.shape[1]
    slots = result_ref.shape[0]
    size = 256
    router_out[...] = jnp.zeros_like(router_out)
    second_ref[...] = jnp.zeros_like(second_ref)
    skip_ref[...] = jnp.zeros_like(skip_ref)

    def body(b, _):
        at = ds(b * size, size)
        folded = lambda v: jnp.sum(v.reshape(size // SUB, SUB, v.shape[1]), axis=0)
        iota = lax.broadcasted_iota(jnp.int32, (size, slots), 1)
        pick = jnp.where(iota == slot_ref[at, :], 1.0, 0.0).astype(BF16)
        result = dot(pick, result_ref[...], NN)
        grad = dot(pick, rows_ref[...], NN)
        probs, hot = probs_ref[at, :], hot_ref[at, :]
        chosen = jnp.sum(probs * hot, axis=1, keepdims=True)
        residual = residual_ref[at, :]
        block = residual + chosen * result
        for ct in range(width // LANES):
            block_s[ct, at, :] = block[:, ct * LANES : (ct + 1) * LANES]
        cot = cot_ref[at, :].astype(F32)
        gate = jnp.sum(cot * result, axis=1, keepdims=True)
        logit = (gate * probs * (hot - chosen)).astype(BF16)
        router_out[...] += dot(logit, normed_ref[at, :], TN)
        grad = grad + dot(logit, router_ref[...], NT)
        inverse = lax.rsqrt(jnp.mean(residual * residual, axis=1, keepdims=True) + norm_eps)
        normed = residual * inverse
        second_ref[...] += folded(grad * normed)
        scaled = grad * gain_ref[...]
        mean = jnp.mean(scaled * normed, axis=1, keepdims=True)
        resid = cot + inverse * (scaled - normed * mean)
        resid_ref[at, :] = resid
        mixed = (valid_ref[at, :] * resid).astype(BF16)
        mixed_s[at, :] = mixed
        grad_gated = dot(mixed, out_ref[...], NT)
        pre = both_ref[at, chans : 2 * chans].astype(F32)
        sig = jax.nn.sigmoid(pre)
        act = pre * sig
        gs = grad_gated * act
        gs_ref[at, :] = gs
        skip_ref[...] += folded(gs * inner_ref[at, :].astype(F32))
        gate_ref[at, :] = (grad_gated * scan_ref[at, :] * (sig * (1.0 + pre * (1.0 - sig)))).astype(BF16)
        return 0

    lax.fori_loop(0, rows // size, body, 0)
    mixer_ref[...] = dot(gated_ref[...], mixed_s[...], TN)
    restore(cuts, block_s, block_ref)


def restore(cuts, tile_ref, out_ref):
    seqs, chunks, places = cuts
    for ct in range(tile_ref.shape[0]):
        for q in range(seqs):
            for k in range(chunks):
                picked = tile_ref[ct, pl.ds(k * seqs + q, places, stride=SUB), :]
                start = (q * chunks + k) * places
                out_ref[start : start + places, ct * LANES : (ct + 1) * LANES] = picked.astype(out_ref.dtype)


def token_back(cuts, *args):
    (slot, result, _, residual, probs, _, _, _, _, _, router, gated, _, scan, both, inner) = args
    rows, width = residual.shape
    chans = inner.shape[1]
    shape = jax.ShapeDtypeStruct
    return pl.pallas_call(
        functools.partial(token_back_kernel, cuts),
        out_shape=[
            shape((rows, width), BF16),
            shape((rows, width), F32),
            shape((rows, chans), F32),
            shape((rows, chans), BF16),
            shape((router.shape[1], width), F32),
            shape((SUB, width), F32),
            shape((chans, width), F32),
            shape((SUB, chans), F32),
        ],
        scratch_shapes=[
            pltpu.VMEM((rows, width), BF16),
            pltpu.VMEM((width // LANES, rows, LANES), F32),
        ],
        compiler_params=pltpu.CompilerParams(vmem_limit_bytes=VMEM),
    )(*args)


def last_kernel(
    n, count, cuts, x_ref, blocks_ref, tok_ref, resid_ref, gain_ref, grad_ref, out_ref, first_ref,
    sum_s, ra, sb, rb, pa, ps, pc, tile_s, firsts, send, recv,
):
    g = lax.axis_index("dp")
    j, near, far = mp_pair()
    near, far = {"mp": near}, {"mp": far}
    odd, z, m = g % 2, g // 2, n // 2
    pair = {"dp": g + 1 - 2 * odd}
    like = [{"dp": 2 * ((z + k) % m) + odd} for k in range(1, m)]
    others = [{"dp": (g + k) % n} for k in range(1, n)]
    greet([near, far] + others)
    rows, width = x_ref.shape
    half = rows // 2
    size = half // count
    own = (j % 2) * half
    other = (1 - j % 2) * half
    one = [
        sending(x_ref.at[ds(other + k * size, size)], ra.at[k], send.at[0, k], recv.at[0, k], near)
        for k in range(count)
    ]
    order = [(z + k) % m for k in range(1, m)] + [z]
    first = [
        sending(blocks_ref.at[2 * order[k] + 1 - odd], pa.at[k], send.at[3, k], recv.at[3, k], pair)
        for k in range(m)
    ]
    two, three, second = [], [], []

    def pair_sum(k):
        first[k].wait_recv()
        ps[k] = (blocks_ref[2 * order[k] + odd].astype(F32) + pa[k].astype(F32)).astype(BF16)
        if k < m - 1:
            second.append(sending(ps.at[k], pc.at[k], send.at[4, k], recv.at[4, k], like[k]))

    for k in range(max(count, m)):
        if k < count:
            one[k].wait_recv()
            mine = x_ref[ds(own + k * size, size), :].astype(F32)
            sb[k] = (mine + ra[k].astype(F32)).astype(BF16)
            two.append(sending(sb.at[k], rb.at[k], send.at[1, k], recv.at[1, k], far))
        if k < m:
            pair_sum(k)
    firsts[0] = jnp.zeros(firsts.shape[1:], F32)
    gain = gain_ref[...]

    def norm_rows(start):
        at = ds(start, size)
        grad = sum_s[at, :].astype(F32)
        tok = tok_ref[at, :].astype(F32)
        inverse = lax.rsqrt(jnp.mean(tok * tok, axis=1, keepdims=True) + norm_eps)
        normed = tok * inverse
        firsts[0] += jnp.sum((grad * normed).reshape(size // SUB, SUB, width), axis=0)
        scaled = grad * gain
        mean = jnp.mean(scaled * normed, axis=1, keepdims=True)
        value = resid_ref[at, :] + inverse * (scaled - normed * mean)
        for ct in range(width // LANES):
            tile_s[ct, at, :] = value[:, ct * LANES : (ct + 1) * LANES]

    for k in range(count):
        two[k].wait_recv()
        at = ds(own + k * size, size)
        sum_s[at, :] = (sb[k].astype(F32) + rb[k].astype(F32)).astype(BF16)
        three.append(sending(sum_s.at[at], sum_s.at[at], send.at[2, k], recv.at[2, k], near))
    value = ps[m - 1].astype(F32)
    for copy in second:
        copy.wait_recv()
    for k in range(m - 1):
        value = value + pc[k].astype(F32)
    out_ref[g] = value.astype(BF16)
    third = [
        sending(out_ref.at[g], out_ref.at[g], send.at[5, k], recv.at[5, k], like[k]) for k in range(m - 1)
    ]
    fourth = [sending(out_ref.at[g], out_ref.at[g], send.at[6, 0], recv.at[6, 0], pair)]
    for k in range(count):
        norm_rows(own + k * size)
    for k in range(count):
        three[k].wait_recv()
        norm_rows(other + k * size)
    spread_first = [
        sending(firsts.at[0], firsts.at[k], send.at[7, k], recv.at[7, k], others[k - 1]) for k in range(1, n)
    ]
    for k in range(m - 1):
        third[k].wait_recv()
        b = 2 * ((z + m - 1 - k) % m) + odd
        fourth.append(sending(out_ref.at[b], out_ref.at[b], send.at[6, k + 1], recv.at[6, k + 1], pair))
    restore(cuts, tile_s, grad_ref)
    for copy in spread_first:
        copy.wait_recv()

    def one_first(d, total):
        return total + firsts[(g + n - d) % n]

    first_ref[...] = lax.fori_loop(0, n, one_first, jnp.zeros(first_ref.shape, F32))
    for copy in fourth:
        copy.wait_recv()
    for copy in one + two + three + first + second + third + fourth + spread_first:
        copy.wait_send()


def last_sums(n, collective_id, cuts, x, blocks, tok, resid, gain, count=4):
    rows, width = x.shape
    m = n // 2
    height = blocks.shape[1]
    slots = pltpu.VMEM((count, rows // 2 // count, width), BF16)
    parts = pltpu.VMEM((m, height, width), BF16)
    sems = pltpu.SemaphoreType.DMA((8, max(n, count)))
    shape = jax.ShapeDtypeStruct
    return vmem_call(
        functools.partial(last_kernel, n, count, cuts),
        [shape((rows, width), F32), shape(blocks.shape, BF16), shape((SUB, width), F32)],
        [
            pltpu.VMEM((rows, width), BF16),
            slots,
            slots,
            slots,
            parts,
            parts,
            parts,
            pltpu.VMEM((width // LANES, rows, LANES), F32),
            pltpu.VMEM((n, SUB, width), F32),
            sems,
            sems,
        ],
        collective_id, x, blocks, tok, resid, gain,
    )


def round_kernel(x_ref, out_ref):
    out_ref[...] = x_ref[...].astype(BF16)


def rounded(x):
    return pl.pallas_call(round_kernel, out_shape=jax.ShapeDtypeStruct(x.shape, BF16))(x)


def silu_slope(values):
    sigmoid_vals = jax.nn.sigmoid(values)
    return sigmoid_vals * (1.0 + values * (1.0 - sigmoid_vals))


def gelu_tanh(values):
    return jax.nn.gelu(values, approximate=True)


def norm_back(grad_norm, normed, inverse, norm_gain):
    scaled = grad_norm * norm_gain
    return inverse * (scaled - normed * jnp.mean(scaled * normed, axis=-1, keepdims=True))


def per_device(
    tokens,
    routes,
    lengths,
    cotangent,
    first_gain,
    mixer_in,
    conv_weight,
    conv_bias,
    select_weight,
    step_weight,
    step_bias,
    decay_log,
    skip_gain,
    mixer_out,
    second_gain,
    router_weight,
    expert_up,
    up_bias,
    expert_down,
    down_bias,
):
    tok_count, model_width = tokens.shape
    kernel, chan_count = conv_weight.shape
    rank_size = step_weight.shape[0]
    state_size = decay_log.shape[0]
    expert_total = router_weight.shape[1]
    capacity = max(2, (5 * tok_count + 4 * expert_total - 1) // (4 * expert_total))
    slot_dev = SLOT_DEV
    seq_count = tok_count // slot_dev
    chunks = SUB // seq_count
    places_dev = slot_dev // chunks
    edge = kernel - 1
    device = lax.axis_index("dp")
    dp_count = lax.axis_size("dp")

    def reorder(values):
        width = values.shape[-1]
        cut = values.reshape(seq_count, chunks, places_dev, width)
        return cut.transpose(2, 1, 0, 3).reshape(tok_count, width)

    rows = jnp.arange(tok_count)
    sub_ids = rows % SUB
    seq_ids = sub_ids % seq_count
    local_place = (sub_ids // seq_count) * places_dev + rows // SUB
    original = seq_ids * slot_dev + local_place
    places = device * slot_dev + local_place
    seq_length = jnp.sum(
        jnp.where(seq_ids[:, None] == jnp.arange(lengths.shape[0])[None], lengths[None], 0), axis=1
    )
    valid_mask = (places < seq_length).astype(F32)
    valid_col = valid_mask[:, None]
    opening = (jnp.arange(SUB) < seq_count)[None, :, None]

    tok_low = reorder(tokens)
    tok_vals = tok_low.astype(F32)
    cot_low = reorder(cotangent)
    route_ids = reorder(routes)[:, 0]

    expert_iota = jnp.arange(expert_total, dtype=jnp.int32)
    route_match = route_ids[:, None] == expert_iota[None]
    route_hot = route_match.astype(F32)
    live_hot = route_hot * valid_col
    before = (original[None, :] < original[:, None]).astype(BF16)
    earlier = dot(before, live_hot.astype(BF16), NN)
    position = jnp.sum(earlier * live_hot, axis=1).astype(jnp.int32)
    kept_mask = (valid_mask > 0.5) & (position < capacity)
    room = (capacity + 31) // 32 * 32
    slot_ids = jnp.where(kept_mask, route_ids * room + position, -1)
    half_rows, half_cols = room // 2, model_width // 2
    place_mp = lax.axis_index("mp")
    quarter_iota = (
        jnp.arange(expert_total)[:, None] * room
        + (place_mp // 2) * half_rows
        + jnp.arange(half_rows)[None]
    ).reshape(-1, 1)
    quarter = (slot_ids[None, :] == quarter_iota).astype(BF16)

    def to_experts(values, collective_id):
        part = lax.dynamic_slice_in_dim(values, (place_mp % 2) * half_cols, half_cols, 1)
        sent = dot(quarter, part, NN).astype(BF16).reshape(expert_total, half_rows, half_cols)
        return dispatch_rows(dp_count, collective_id, sent).reshape(dp_count * room, model_width)

    cot_rows = to_experts(cot_low, 0)

    inverse_one = lax.rsqrt(jnp.mean(tok_vals * tok_vals, axis=-1, keepdims=True) + norm_eps)
    normed_one = tok_vals * inverse_one
    first_vals = first_gain.astype(F32)
    normed_in = (normed_one * first_vals).astype(BF16)
    mixer_in_flat = mixer_in.reshape(model_width, 2 * chan_count)
    both_in = dot(normed_in, mixer_in_flat, NN).astype(BF16)
    gate_pre = both_in[:, chan_count:].astype(F32)
    conv_seq = both_in[:, :chan_count].astype(F32).reshape(places_dev, SUB, chan_count)
    tail = conv_seq[places_dev - edge :]
    other_tail = passed_along(tail.astype(BF16), "dp", 1).astype(F32)
    lead_rows = jnp.roll(jnp.where(opening, tail, other_tail), seq_count, axis=1)
    extended = jnp.concatenate([lead_rows, conv_seq], axis=0)
    conv_taps = conv_weight.astype(F32)
    conv_pre = jnp.zeros(conv_seq.shape, F32) + conv_bias.astype(F32)
    for offset in range(kernel):
        conv_pre = conv_pre + conv_taps[offset] * extended[offset : offset + places_dev]
    conv_pre = conv_pre.reshape(tok_count, chan_count)
    inner_vals = jax.nn.silu(conv_pre).astype(BF16)
    inner_f = inner_vals.astype(F32)
    projected = sum_mp(dot(inner_vals, select_weight, NN), 1, 2)
    low_rank = projected[:, :rank_size]
    bin_vals = projected[:, rank_size : rank_size + state_size]
    cout_vals = projected[:, rank_size + state_size :]
    low_high = low_rank.astype(BF16)
    low_rest = (low_rank - low_high.astype(F32)).astype(BF16)
    step_pre = dot(
        jnp.concatenate([low_high, low_rest], axis=1),
        jnp.concatenate([step_weight, step_weight], axis=0),
        NN,
    ) + step_bias.astype(F32)
    step_vals = valid_col * jax.nn.softplus(step_pre)
    step_slope = valid_col * jax.nn.sigmoid(step_pre)
    decay_rates = -jnp.exp(decay_log.astype(F32))
    rates = decay_rates * LOG2E

    by_place = lambda values: values.reshape(places_dev, SUB, values.shape[-1])
    drive = step_vals * inner_f
    step_p, drive_p, bin_p, cout_p = map(by_place, (step_vals, drive, bin_vals, cout_vals))
    chunk_state = local_forward(step_p, drive_p, bin_p, rates)
    chunk_steps = jnp.sum(step_p, axis=0)
    state_in, totals = exchange(dp_count, False, 2, chunk_state, chunk_steps, rates)
    scan_sum, states_before, last_states = forward(
        step_p, drive_p, bin_p, cout_p, rates, state_in
    )
    skip_vals = skip_gain.astype(F32)
    scan_out = scan_sum.reshape(tok_count, chan_count) + skip_vals * inner_f
    gate_act = jax.nn.silu(gate_pre)
    gated_vals = (scan_out * gate_act).astype(BF16)
    mixer_vals = sum_mp(dot(gated_vals, mixer_out, NN).astype(BF16), 3).astype(F32)
    residual = tok_vals + valid_col * mixer_vals
    inverse_two = lax.rsqrt(jnp.mean(residual * residual, axis=-1, keepdims=True) + norm_eps)
    normed_two = residual * inverse_two
    second_vals = second_gain.astype(F32)
    normed_out = (normed_two * second_vals).astype(BF16)
    logits = dot(normed_out, router_weight, NN)
    route_probs = jax.nn.softmax(logits, axis=-1)
    gate_prob = jnp.sum(route_probs * route_hot, axis=-1)

    expert_rows = to_experts(normed_out, 4)
    own_hot = (expert_iota == device).astype(F32)
    row_probs = jnp.sum(
        jax.nn.softmax(dot(expert_rows, router_weight, NN), axis=-1) * own_hot, axis=-1
    )
    expert_grad = (row_probs[:, None] * cot_rows.astype(F32)).astype(BF16)
    up_mat, down_mat = expert_up[0], expert_down[0]
    hidden_pre = dot(expert_rows, up_mat, NN) + up_bias.astype(F32)
    hidden_act, gelu_pull = jax.vjp(gelu_tanh, hidden_pre)
    hidden_low = hidden_act.astype(BF16)
    result_part = dot(hidden_low, down_mat, NN).astype(BF16)
    grad_down_bias = jnp.sum(expert_grad.astype(F32), axis=0)[None]
    grad_down = dot(hidden_low, expert_grad, TN)[None]
    grad_hidden = dot(expert_grad, down_mat, NT)
    grad_pre = gelu_pull(grad_hidden)[0].astype(BF16)
    grad_up_bias = jnp.sum(grad_pre.astype(F32), axis=0)[None]
    grad_up = dot(expert_rows, grad_pre, TN)[None]
    rows_part = dot(grad_pre, up_mat, NT).astype(BF16)
    by_group = lambda values: values.reshape(dp_count, room, model_width)
    returned = return_rows(
        dp_count, 5, down_bias.astype(F32), by_group(result_part), by_group(rows_part)
    )
    cuts = (seq_count, chunks, places_dev)
    (
        block_out,
        grad_resid,
        grad_scan,
        grad_gate_low,
        grad_router,
        grad_second,
        grad_mixer_out,
        grad_skip,
    ) = token_back(
        cuts,
        slot_ids[:, None],
        *[back.reshape(expert_total * room, model_width) for back in returned],
        residual,
        route_probs,
        route_hot,
        normed_out,
        cot_low,
        valid_col,
        second_vals[None],
        router_weight,
        gated_vals,
        mixer_out,
        scan_out,
        both_in,
        inner_vals,
    )

    gs_p = by_place(grad_scan)
    chunk_grad = local_backward(step_p, gs_p, cout_p, rates)
    grad_in = exchange(dp_count, True, 6, chunk_grad, chunk_steps, rates, totals)
    gp_p = jnp.concatenate([jnp.zeros_like(gs_p[:1]), gs_p[:-1]], axis=0)
    grad_base, grad_low_part, grad_bin, cout_shift, rate_parts, grad_step_weight, grad_step_bias = backward(
        step_p,
        drive_p,
        gs_p,
        gp_p,
        bin_p,
        cout_p,
        rates,
        grad_in,
        states_before,
        inner_vals,
        step_slope,
        low_high,
        step_weight,
        skip_vals[None],
    )
    last_cout = jnp.sum(gs_p[places_dev - 1][None] * last_states, axis=-1).T
    grad_cout = jnp.concatenate([cout_shift[SUB:], last_cout], axis=0)
    grad_decay_log = jnp.sum(rate_parts, axis=1) * decay_rates
    proj_part = jnp.concatenate([grad_low_part, grad_bin, grad_cout], axis=1)
    grad_proj = sum_mp(proj_part.astype(BF16), 7, 2)
    grad_select, conv_sums, grad_mixer_in, input_part = mixer_back(
        dp_count,
        8,
        grad_proj,
        select_weight,
        inner_vals,
        grad_base,
        conv_pre,
        both_in,
        lead_rows.reshape(edge * SUB, chan_count),
        grad_gate_low,
        normed_in,
        mixer_in_flat,
        conv_taps,
    )
    conv_sums = jnp.sum(conv_sums, axis=1)
    grad_taps, grad_conv_bias = conv_sums[:kernel], conv_sums[kernel]
    shared = (
        grad_mixer_in,
        grad_mixer_out,
        grad_select,
        grad_step_weight,
        grad_taps,
        grad_conv_bias,
        jnp.sum(grad_step_bias, axis=0),
        grad_decay_log,
        jnp.sum(grad_skip, axis=0),
        jnp.sum(grad_second, axis=0),
        grad_router,
    )
    flat = [part.reshape(-1) for part in shared[2:]]
    rest = sum(part.size for part in flat)
    height = (shared[0].size + shared[1].size + rest + model_width - 1) // model_width
    height = (height + 16 * dp_count - 1) // (16 * dp_count) * (16 * dp_count)
    pad = height * model_width - shared[0].size - shared[1].size - rest
    small = jnp.concatenate(flat + [jnp.zeros((pad,), F32)]).reshape(-1, model_width)
    stacked = jnp.concatenate([shared[0], rounded(jnp.concatenate([shared[1], small], axis=0))], axis=0)
    token_grad, stacked, grad_first = last_sums(
        dp_count,
        9,
        cuts,
        input_part,
        stacked.reshape(dp_count, -1, model_width),
        tok_low,
        grad_resid,
        first_vals[None],
    )
    stacked = stacked.reshape(height, model_width).astype(F32)
    first_rows, next_rows = shared[0].shape[0], shared[0].shape[0] + shared[1].shape[0]
    tail_flat = stacked[next_rows:].reshape(-1)
    summed, start = [stacked[:first_rows], stacked[first_rows:next_rows]], 0
    for part in shared[2:]:
        summed.append(tail_flat[start : start + part.size].reshape(part.shape))
        start += part.size
    return (
        block_out,
        token_grad,
        jnp.sum(grad_first, axis=0),
        summed[0].reshape(mixer_in.shape),
        summed[4],
        summed[5],
        summed[2].T,
        summed[3],
        summed[6],
        summed[7],
        summed[8],
        summed[1],
        summed[9],
        summed[10].T,
        grad_up,
        grad_up_bias,
        grad_down,
        grad_down_bias,
    )


def solution(mesh):
    return jax.shard_map(
        per_device,
        mesh=mesh,
        in_specs=(
            P("dp", None),
            P("dp", None),
            P(),
            P("dp", None),
            P(),
            P(None, None, "mp"),
            P(None, "mp"),
            P("mp"),
            P("mp", None),
            P(None, "mp"),
            P("mp"),
            P(None, "mp"),
            P("mp"),
            P("mp", None),
            P(),
            P(),
            P("dp", None, "mp"),
            P("dp", "mp"),
            P("dp", "mp", None),
            P("dp", None),
        ),
        out_specs=(
            P("dp", None),
            P("dp", None),
            P(),
            P(None, None, "mp"),
            P(None, "mp"),
            P("mp"),
            P("mp", None),
            P(None, "mp"),
            P("mp"),
            P(None, "mp"),
            P("mp"),
            P("mp", None),
            P(),
            P(),
            P("dp", None, "mp"),
            P("dp", "mp"),
            P("dp", "mp", None),
            P("dp", None),
        ),
        check_vma=False,
    )
```

```python
import functools

import jax
import jax.numpy as jnp
from jax import lax
from jax.experimental import pallas as pl
from jax.experimental.pallas import tpu as pltpu
from jax.sharding import PartitionSpec as P

F32 = jnp.float32
BF16 = jnp.bfloat16
SLOT_DEV = 256
LANES = 128
SUB = 8
LOG2E = 1.4426950408889634
LN2 = 0.6931471805599453
VMEM = 48 * 2**20
norm_eps = 1e-05
MESH = pl.DeviceIdType.MESH


NN = ((1,), (0,))
NT = ((1,), (1,))
TN = ((0,), (0,))


def dot(a, b, dims):
    return lax.dot_general(a, b, (dims, ((), ())), preferred_element_type=F32)


def lane(col):
    return jnp.broadcast_to(col, (SUB, LANES))


def row(ref, n, cs):
    return jnp.broadcast_to(ref[n : n + 1, cs], (SUB, LANES))


def tiles(count):
    return [slice(ct * LANES, (ct + 1) * LANES) for ct in range(count // LANES)]


def whole(*dims):
    return pl.BlockSpec(dims, lambda i: (0,) * len(dims))


def local_scan(step_ref, in_ref, map_ref, rates_ref, out_ref, nh, half, reverse):
    places, chans = step_ref.shape[0], step_ref.shape[2]
    cols = tiles(chans)
    ns = [nh * half + n for n in range(half)]

    def body(lap, st):
        i = places - 1 - lap if reverse else lap
        st = list(st)
        m = map_ref[i]
        mm = [lane(m[:, n : n + 1]) for n in ns]
        for ct, cs in enumerate(cols):
            s = step_ref[i, :, cs]
            x = in_ref[i, :, cs]
            for n in range(half):
                k = n * len(cols) + ct
                e = jnp.exp2(s * row(rates_ref, ns[n], cs))
                st[k] = e * (st[k] + x * mm[n]) if reverse else e * st[k] + x * mm[n]
        return tuple(st)

    zero = tuple(jnp.zeros((SUB, LANES), F32) for _ in range(half * len(cols)))
    st = lax.fori_loop(0, places, body, zero, unroll=8)
    for n in range(half):
        for ct, cs in enumerate(cols):
            out_ref[ns[n], :, cs] = st[n * len(cols) + ct]


def forward_kernel(
    step_ref,
    x_ref,
    bin_ref,
    cout_ref,
    rates_ref,
    h0_ref,
    inner_ref,
    gate_ref,
    skip_ref,
    weight_ref,
    scan_ref,
    gated_ref,
    part_ref,
    hb_ref,
    hf_ref,
    st_ref,
    y_ref,
):
    places, chans = step_ref.shape[0], step_ref.shape[2]
    states, half = rates_ref.shape[0], 8
    cols = tiles(chans)

    @pl.when(pl.program_id(0) == 0)
    def _():
        st_ref[...] = h0_ref[...]

    for nh in range(states // half):
        ns = [nh * half + n for n in range(half)]

        def body(i, st):
            st = list(st)
            b = bin_ref[i]
            c = cout_ref[i]
            bb = [lane(b[:, n : n + 1]) for n in ns]
            cc = [lane(c[:, n : n + 1]) for n in ns]
            for ct, cs in enumerate(cols):
                s = step_ref[i, :, cs]
                x = x_ref[i, :, cs]
                y = y_ref[i, :, cs] if nh else jnp.zeros((SUB, LANES), F32)
                for n in range(half):
                    k = n * len(cols) + ct
                    hb_ref[i, ns[n], :, cs] = st[k].astype(hb_ref.dtype)
                    e = jnp.exp2(s * row(rates_ref, ns[n], cs))
                    st[k] = e * st[k] + x * bb[n]
                    y = y + cc[n] * st[k]
                y_ref[i, :, cs] = y
            return tuple(st)

        st = tuple(st_ref[n, :, cs] for n in ns for cs in cols)
        st = lax.fori_loop(0, places, body, st, unroll=8)
        for n in range(half):
            for ct, cs in enumerate(cols):
                st_ref[ns[n], :, cs] = st[n * len(cols) + ct]
    hf_ref[...] = st_ref[...]
    scan = y_ref[...].reshape(places * SUB, chans) + skip_ref[...] * inner_ref[...].astype(F32)
    scan_ref[...] = scan
    gate = gate_ref[...].astype(F32)
    gated = (scan * (gate * jax.nn.sigmoid(gate))).astype(BF16)
    gated_ref[...] = gated
    part_ref[...] = dot(gated, weight_ref[...], NN).astype(BF16)


def forward(step, x, bin_vals, cout, rates, h0, inner, both, skip, weight, block=16):
    places, _, chans = step.shape
    states = rates.shape[0]
    width = weight.shape[1]
    rows = places * SUB
    part = lambda size: pl.BlockSpec((block, SUB, size), lambda i: (i, 0, 0))
    flat = lambda size, col=0: pl.BlockSpec((block * SUB, size), lambda i: (i, col))
    shape = jax.ShapeDtypeStruct
    return pl.pallas_call(
        forward_kernel,
        grid=(places // block,),
        in_specs=[
            part(chans),
            part(chans),
            part(states),
            part(states),
            whole(states, chans),
            whole(states, SUB, chans),
            flat(chans),
            flat(chans, 1),
            whole(1, chans),
            whole(chans, width),
        ],
        out_specs=[
            flat(chans),
            flat(chans),
            flat(width),
            pl.BlockSpec((block, states, SUB, chans), lambda i: (i, 0, 0, 0)),
            whole(states, SUB, chans),
        ],
        out_shape=[
            shape((rows, chans), F32),
            shape((rows, chans), BF16),
            shape((rows, width), BF16),
            shape((places, states, SUB, chans), BF16),
            shape((states, SUB, chans), F32),
        ],
        scratch_shapes=[
            pltpu.VMEM((states, SUB, chans), F32),
            pltpu.VMEM((block, SUB, chans), F32),
        ],
        compiler_params=pltpu.CompilerParams(vmem_limit_bytes=VMEM),
    )(step, x, bin_vals, cout, rates, h0, inner, both, skip, weight)


def backward_kernel(
    n,
    step_ref,
    x_ref,
    gs_ref,
    past_ref,
    bin_ref,
    cout_ref,
    rates_ref,
    g0_ref,
    hf_ref,
    hb_ref,
    inner_ref,
    slope_ref,
    low_ref,
    weight_ref,
    skip_ref,
    early_ref,
    base_ref,
    low_out,
    qb_ref,
    qc_ref,
    rt_out,
    sw_ref,
    sbias_ref,
    gin_ref,
    gout_ref,
    few_ref,
    last_ref,
    gst_ref,
    rt_ref,
    q_ref,
    p_ref,
    sg_ref,
    sb_ref,
    gp_ref,
    sums,
    send,
    recv,
):
    places, chans = step_ref.shape[0], step_ref.shape[2]
    states, some = rates_ref.shape[0], 4
    cols = tiles(chans)
    g, _, pair, like = dp_pairs(n)
    start, middle, end = gathering(n, sums, send, recv)

    @pl.when(pl.program_id(0) == 0)
    def _():
        greet([pair] + like)
        sums[g] = early_ref[...]
        start()

    @pl.when(pl.program_id(0) == pl.num_programs(0) // 2)
    def _():
        middle()

    @pl.when(pl.program_id(0) == 0)
    def _():
        gst_ref[...] = g0_ref[...]
        rt_ref[...] = jnp.zeros_like(rt_ref)
        sw_ref[...] = jnp.zeros_like(sw_ref)
        sbias_ref[...] = jnp.zeros_like(sbias_ref)

    gp_ref[0] = past_ref[0]
    gp_ref[1:places] = gs_ref[0 : places - 1]

    for nq in range(states // some):
        ns = [nq * some + n for n in range(some)]
        size = some * len(cols)

        def body(lap, carry):
            i = places - 1 - lap
            st, rt = list(carry[:size]), list(carry[size:])
            b = bin_ref[i]
            c = cout_ref[i]
            bb = [lane(b[:, n : n + 1]) for n in ns]
            cc = [lane(c[:, n : n + 1]) for n in ns]
            qb, qc = [None] * some, [None] * some
            for ct, cs in enumerate(cols):
                s = step_ref[i, :, cs]
                x = x_ref[i, :, cs]
                g = gs_ref[i, :, cs]
                gp = gp_ref[i, :, cs]
                sg = sg_ref[i, :, cs] if nq else jnp.zeros((SUB, LANES), F32)
                sb = sb_ref[i, :, cs] if nq else jnp.zeros((SUB, LANES), F32)
                for n in range(some):
                    k = n * len(cols) + ct
                    rate = row(rates_ref, ns[n], cs)
                    e = jnp.exp2(s * rate)
                    h = hb_ref[i, ns[n], :, cs].astype(F32)
                    grad = st[k] + g * cc[n]
                    st[k] = e * grad
                    dg = st[k] * h
                    sg = sg + dg * rate
                    rt[k] = rt[k] + dg * s
                    sb = sb + grad * bb[n]
                    qb[n] = grad * x if ct == 0 else qb[n] + grad * x
                    qc[n] = gp * h if ct == 0 else qc[n] + gp * h
                sg_ref[i, :, cs] = sg
                sb_ref[i, :, cs] = sb
            rows = pl.ds(pl.multiple_of(i * SUB, SUB), SUB)
            for n in range(some):
                q_ref[rows, ns[n] * LANES : (ns[n] + 1) * LANES] = qb[n]
                p_ref[rows, ns[n] * LANES : (ns[n] + 1) * LANES] = qc[n]
            return tuple(st) + tuple(rt)

        at = [(ns[n], slice(None), cs) for n in range(some) for cs in cols]
        init = tuple(gst_ref[a] for a in at) + tuple(rt_ref[a] for a in at)
        out = lax.fori_loop(0, places, body, init, unroll=8)
        for j, a in enumerate(at):
            gst_ref[a] = out[j]
            rt_ref[a] = out[size + j]
    dims = (states * LANES, states)
    sel = lax.broadcasted_iota(jnp.int32, dims, 0) // LANES == lax.broadcasted_iota(
        jnp.int32, dims, 1
    )
    sel = sel.astype(BF16)
    qb_ref[...] = jnp.dot(q_ref[...].astype(BF16), sel, preferred_element_type=F32)
    qc_ref[...] = jnp.dot(p_ref[...].astype(BF16), sel, preferred_element_type=F32)
    rt_out[...] = rt_ref[...]

    @pl.when(pl.program_id(0) == 0)
    def _():
        for n_ in range(states):
            value = hf_ref[n_, :, cols[0]] * gs_ref[places - 1, :, cols[0]]
            for cs in cols[1:]:
                value = value + hf_ref[n_, :, cs] * gs_ref[places - 1, :, cs]
            p_ref[0:SUB, n_ * LANES : (n_ + 1) * LANES] = value
        last_ref[...] = jnp.dot(p_ref[0:SUB, :].astype(BF16), sel, preferred_element_type=F32)

    flat = lambda ref: ref[...].reshape(places * SUB, chans)
    sb = flat(sb_ref)
    base_ref[...] = flat(gs_ref) * skip_ref[...] + flat(step_ref) * sb
    pre = (flat(sg_ref) * LN2 + inner_ref[...].astype(F32) * sb) * slope_ref[...]
    sbias_ref[...] += jnp.sum(pre.reshape(places, SUB, chans), axis=0)
    pre = pre.astype(BF16)
    sw_ref[...] += dot(low_ref[...], pre, TN)
    low_out[...] = dot(pre, weight_ref[...], NT)

    @pl.when(pl.program_id(0) == pl.num_programs(0) - 1)
    def _():
        end()
        mh = gin_ref.shape[0] // n
        sh = few_ref.shape[0] // n
        for b in range(n):
            few_ref[b * sh : (b + 1) * sh, :] = sums[b, 2 * mh : 2 * mh + sh, :].astype(F32)
            gin_ref[b * mh : (b + 1) * mh, :] = sums[b, 0:mh, :].astype(F32)
            gout_ref[b * mh : (b + 1) * mh, :] = sums[b, mh : 2 * mh, :].astype(F32)


def backward(
    n, collective_id, mh, step, x, gs, bin_vals, cout, rates, g0, hf, hb, inner, slope, low, weight, skip, early, block=16
):
    places, _, chans = step.shape
    states = rates.shape[0]
    rank = weight.shape[0]
    count = places // block
    part = lambda width: pl.BlockSpec((block, SUB, width), lambda i: (count - 1 - i, 0, 0))
    flat = lambda width: pl.BlockSpec((block * SUB, width), lambda i: (count - 1 - i, 0))
    rows = places * SUB
    tall = n * mh
    few = n * (early.shape[0] - 2 * mh)
    sems = pltpu.SemaphoreType.DMA((2, n // 2))
    return pl.pallas_call(
        functools.partial(backward_kernel, n),
        grid=(count,),
        in_specs=[
            part(chans),
            part(chans),
            part(chans),
            pl.BlockSpec((1, SUB, chans), lambda i: (jnp.maximum((count - 1 - i) * block - 1, 0), 0, 0)),
            part(states),
            part(states),
            whole(states, chans),
            whole(states, SUB, chans),
            whole(states, SUB, chans),
            pl.BlockSpec((block, states, SUB, chans), lambda i: (count - 1 - i, 0, 0, 0)),
            flat(chans),
            flat(chans),
            flat(rank),
            whole(rank, chans),
            whole(1, chans),
            whole(*early.shape),
        ],
        out_specs=[
            flat(chans),
            flat(rank),
            flat(states),
            flat(states),
            whole(states, SUB, chans),
            whole(rank, chans),
            whole(SUB, chans),
            whole(tall, chans),
            whole(tall, chans),
            whole(few, chans),
            whole(SUB, states),
        ],
        out_shape=[
            jax.ShapeDtypeStruct((rows, chans), F32),
            jax.ShapeDtypeStruct((rows, rank), F32),
            jax.ShapeDtypeStruct((rows, states), F32),
            jax.ShapeDtypeStruct((rows, states), F32),
            jax.ShapeDtypeStruct((states, SUB, chans), F32),
            jax.ShapeDtypeStruct((rank, chans), F32),
            jax.ShapeDtypeStruct((SUB, chans), F32),
            jax.ShapeDtypeStruct((tall, chans), F32),
            jax.ShapeDtypeStruct((tall, chans), F32),
            jax.ShapeDtypeStruct((few, chans), F32),
            jax.ShapeDtypeStruct((SUB, states), F32),
        ],
        scratch_shapes=[
            pltpu.VMEM((states, SUB, chans), F32),
            pltpu.VMEM((states, SUB, chans), F32),
            pltpu.VMEM((block * SUB, states * LANES), F32),
            pltpu.VMEM((block * SUB, states * LANES), F32),
            pltpu.VMEM((block, SUB, chans), F32),
            pltpu.VMEM((block, SUB, chans), F32),
            pltpu.VMEM((block, SUB, chans), F32),
            pltpu.VMEM((n, *early.shape), BF16),
            sems,
            sems,
        ],
        compiler_params=pltpu.CompilerParams(
            collective_id=collective_id, has_side_effects=True, vmem_limit_bytes=VMEM
        ),
    )(step, x, gs, gs, bin_vals, cout, rates, g0, hf, hb, inner, slope, low, weight, skip, early)


def mp_pair():
    j = lax.axis_index("mp")
    return j, j + 1 - 2 * (j % 2), (j + 2) % 4


def ds(start, size):
    return pl.ds(pl.multiple_of(start, size), size)


def greet(others):
    barrier = pltpu.get_barrier_semaphore()
    for other in others:
        pl.semaphore_signal(barrier, inc=1, device_id=other, device_id_type=MESH)
    pl.semaphore_wait(barrier, len(others))


def sending(src, dst, send, recv, device):
    copy = pltpu.make_async_remote_copy(
        src_ref=src, dst_ref=dst, send_sem=send, recv_sem=recv, device_id=device, device_id_type=MESH
    )
    copy.start()
    return copy


def vmem_call(kernel, out_shape, scratch, collective_id, *args, cost=0):
    space = pl.BlockSpec(memory_space=pltpu.VMEM)
    return pl.pallas_call(
        kernel,
        out_shape=out_shape,
        in_specs=[space] * len(args),
        out_specs=jax.tree.map(lambda _: space, out_shape),
        scratch_shapes=scratch,
        compiler_params=pltpu.CompilerParams(
            collective_id=collective_id, has_side_effects=True, vmem_limit_bytes=VMEM
        ),
    )(*args)


def sum_kernel(count, x_ref, out_ref, ra, sb, rb, send, recv):
    j, near, far = mp_pair()
    near, far = {"mp": near}, {"mp": far}
    half = x_ref.shape[0] // 2
    size = half // count
    own = pl.multiple_of((j % 2) * half, half)
    other = pl.multiple_of((1 - j % 2) * half, half)
    greet([near, far])
    first = [
        sending(x_ref.at[pl.ds(other + k * size, size)], ra.at[k], send.at[0, k], recv.at[0, k], near)
        for k in range(count)
    ]
    second, third = [], []
    for k in range(count):
        first[k].wait_recv()
        mine = x_ref[pl.ds(own + k * size, size), :].astype(F32)
        sb[k] = (mine + ra[k].astype(F32)).astype(sb.dtype)
        second.append(sending(sb.at[k], rb.at[k], send.at[1, k], recv.at[1, k], far))
    for k in range(count):
        second[k].wait_recv()
        rows = pl.ds(own + k * size, size)
        out_ref[rows, :] = (sb[k].astype(F32) + rb[k].astype(F32)).astype(out_ref.dtype)
        third.append(
            sending(out_ref.at[rows], out_ref.at[rows], send.at[2, k], recv.at[2, k], near)
        )
    for k in range(count):
        third[k].wait_recv()
    for copy in first + second + third:
        copy.wait_send()


def sum_mp(x, collective_id, count=4):
    rows, width = x.shape
    slots = pltpu.VMEM((count, rows // 2 // count, width), x.dtype)
    sems = pltpu.SemaphoreType.DMA((3, count))
    return vmem_call(
        functools.partial(sum_kernel, count),
        jax.ShapeDtypeStruct(x.shape, x.dtype),
        [slots, slots, slots, sems, sems],
        collective_id,
        x,
    )


def half_turn(tile):
    return pltpu.roll(tile, SUB // 2, 0)


def exchange_body(n, reverse, part_ref, total_ref, rates_ref, packed_ref, all_ref, out_ref, sbuf, rbuf, send, recv):
    g = lax.axis_index("dp")
    states, chans = rates_ref.shape
    pairs = states // 2
    upper = lax.broadcasted_iota(jnp.int32, (SUB, chans), 0) >= SUB // 2
    total = total_ref[...]
    copies = []
    if not reverse:
        all_ref[0] = total + half_turn(total)
        copies += [
            sending(all_ref.at[0], all_ref.at[k], send.at[1, k], recv.at[1, k], {"dp": (g + k) % n})
            for k in range(1, n)
        ]
    decay = lambda m: jnp.exp2(jnp.broadcast_to(rates_ref[m : m + 1, :], (SUB, chans)) * total)

    def summary(m):
        part = part_ref[m]
        return part + decay(m) * half_turn(part)

    def packed(p):
        low, high = summary(p), summary(p + pairs)
        if reverse:
            return jnp.where(upper, half_turn(high), low)
        return jnp.where(upper, high, half_turn(low))

    for p in range(0, pairs, 2):
        sbuf[p * SUB : (p + 2) * SUB, :] = jnp.concatenate([packed(p), packed(p + 1)], axis=0).astype(BF16)
    copies += [
        sending(sbuf, rbuf.at[k], send.at[0, k], recv.at[0, k], {"dp": (g + k) % n})
        for k in range(1, n)
    ]
    for copy in copies:
        copy.wait_recv()

    def one(lap, held):
        away = n - 1 - lap
        slot = n - away if reverse else away
        use = (g + away < n) if reverse else (away <= g)
        steps = all_ref[slot]
        new = []
        for p in range(0, pairs, 2):
            got = rbuf[slot, p * SUB : (p + 2) * SUB, :].astype(F32)
            for q in (p, p + 1):
                fall = jnp.exp2(packed_ref[q] * steps)
                value = fall * held[q] + got[(q - p) * SUB : (q - p + 1) * SUB]
                new.append(jnp.where(use, value, held[q]))
        return tuple(new)

    zero = tuple(jnp.zeros((SUB, chans), F32) for _ in range(pairs))
    held = lax.fori_loop(0, n - 1, one, zero)
    for m in range(states):
        state = held[m % pairs]
        if (m >= pairs) != reverse:
            state = half_turn(state)
        later = half_turn(decay(m) * state + part_ref[m])
        out_ref[m] = jnp.where(upper, state, later) if reverse else jnp.where(upper, later, state)
    for copy in copies:
        copy.wait_send()


def packed_rates(rates):
    states, chans = rates.shape
    pairs = states // 2
    wide = lambda r: jnp.broadcast_to(r[:, None, :], (pairs, SUB // 2, chans))
    return jnp.concatenate([wide(rates[:pairs]), wide(rates[pairs:])], axis=1)


def enter_forward_kernel(
    n, proj_ref, weight_ref, bias_ref, inner_ref, valid_ref, rates_ref, packed_ref,
    step_ref, drive_ref, slope_ref, bin_ref, cout_ref, low_ref, total_ref, h0_ref, all_ref,
    part, sbuf, rbuf, send, recv,
):
    places, _, chans = step_ref.shape
    states = rates_ref.shape[0]
    rank = weight_ref.shape[0]
    g = lax.axis_index("dp")
    greet([{"dp": (g + k) % n} for k in range(1, n)])
    size = 256
    total_ref[...] = jnp.zeros_like(total_ref)

    def block(b, _):
        at = ds(b * size, size)
        here = pl.ds(pl.multiple_of(b * (size // SUB), size // SUB), size // SUB)
        by_place = lambda v: v.reshape(size // SUB, SUB, v.shape[1])
        proj = proj_ref[at, :]
        low = proj[:, 0:rank]
        high = low.astype(BF16)
        rest = (low - high.astype(F32)).astype(BF16)
        low_ref[at, :] = high
        pre = dot(high, weight_ref[...], NN) + dot(rest, weight_ref[...], NN) + bias_ref[...]
        valid = valid_ref[at, :]
        steps = valid * (jnp.maximum(pre, 0.0) + jnp.log1p(jnp.exp(-jnp.abs(pre))))
        slope_ref[at, :] = valid * jax.nn.sigmoid(pre)
        step_ref[here] = by_place(steps)
        drive_ref[here] = by_place(steps * inner_ref[at, :].astype(F32))
        total_ref[...] += jnp.sum(by_place(steps), axis=0)
        bin_ref[here] = by_place(proj[:, rank : rank + states])
        cout_ref[here] = by_place(proj[:, rank + states : rank + 2 * states])
        return 0

    lax.fori_loop(0, places * SUB // size, block, 0)
    half = 8
    for nh in range(states // half):
        local_scan(step_ref, drive_ref, bin_ref, rates_ref, part, nh, half, False)
    exchange_body(n, False, part, total_ref, rates_ref, packed_ref, all_ref, h0_ref, sbuf, rbuf, send, recv)


def enter_forward(n, collective_id, proj, weight, bias, inner, valid, rates):
    rows, chans = inner.shape
    states = rates.shape[0]
    rank = weight.shape[0]
    shape = jax.ShapeDtypeStruct
    places = rows // SUB
    entering = shape((states, SUB, chans), F32)
    sems = pltpu.SemaphoreType.DMA((2, n))
    return vmem_call(
        functools.partial(enter_forward_kernel, n),
        [
            shape((places, SUB, chans), F32),
            shape((places, SUB, chans), F32),
            shape((rows, chans), F32),
            shape((places, SUB, states), F32),
            shape((places, SUB, states), F32),
            shape((rows, rank), BF16),
            shape((SUB, chans), F32),
            entering,
            shape((n, SUB, chans), F32),
        ],
        [
            pltpu.VMEM((states, SUB, chans), F32),
            pltpu.VMEM((states * SUB // 2, chans), BF16),
            pltpu.VMEM((n, states * SUB // 2, chans), BF16),
            sems,
            sems,
        ],
        collective_id, proj, weight, bias, inner, valid, rates, packed_rates(rates),
    )


def dp_pairs(n):
    g = lax.axis_index("dp")
    odd, z, m = g % 2, g // 2, n // 2
    return g, odd, {"dp": g + 1 - 2 * odd}, [{"dp": 2 * ((z + k) % m) + odd} for k in range(1, m)]


def gathering(n, sums, send, recv):
    g, odd, pair, like = dp_pairs(n)
    z, m = g // 2, n // 2

    def copy(kind, k, b, to):
        return pltpu.make_async_remote_copy(
            src_ref=sums.at[b],
            dst_ref=sums.at[b],
            send_sem=send.at[kind, k],
            recv_sem=recv.at[kind, k],
            device_id=to,
            device_id_type=MESH,
        )

    third = lambda k: copy(0, k, g, like[k])
    fourth = lambda k: copy(1, k, 2 * ((z + m - k) % m) + odd, pair)

    def start():
        for k in range(m - 1):
            third(k).start()
        fourth(0).start()

    def middle():
        for k in range(m - 1):
            third(k).wait_recv()
            fourth(k + 1).start()

    def end():
        for k in range(m):
            fourth(k).wait_recv()
        for k in range(m - 1):
            third(k).wait_send()
        for k in range(m):
            fourth(k).wait_send()

    return start, middle, end


def enter_backward_kernel(
    n, step_ref, gs_ref, cout_ref, total_ref, rates_ref, packed_ref, all_ref, blocks_ref,
    g0_ref, own_ref, part, sbuf, rbuf, pa, ps, pc, send, recv, pair_send, pair_recv,
):
    states = rates_ref.shape[0]
    g, odd, pair, like = dp_pairs(n)
    z, m = g // 2, n // 2
    greet([{"dp": (g + k) % n} for k in range(1, n)])
    order = [(z + k) % m for k in range(1, m)] + [z]
    first = [
        sending(blocks_ref.at[2 * order[k] + 1 - odd], pa.at[k], pair_send.at[0, k], pair_recv.at[0, k], pair)
        for k in range(m)
    ]
    half = 8
    second = []
    for nh in range(states // half):
        local_scan(step_ref, gs_ref, cout_ref, rates_ref, part, nh, half, True)
        if nh == 0:
            few = range(0, m // 2)
        else:
            few = range(m // 2, m)
        for k in few:
            first[k].wait_recv()
            ps[k] = (blocks_ref[2 * order[k] + odd].astype(F32) + pa[k].astype(F32)).astype(BF16)
            if k < m - 1:
                second.append(sending(ps.at[k], pc.at[k], pair_send.at[1, k], pair_recv.at[1, k], like[k]))
    exchange_body(n, True, part, total_ref, rates_ref, packed_ref, all_ref, g0_ref, sbuf, rbuf, send, recv)
    value = ps[m - 1].astype(F32)
    for copy in second:
        copy.wait_recv()
    for k in range(m - 1):
        value = value + pc[k].astype(F32)
    own_ref[...] = value.astype(BF16)
    for copy in first + second:
        copy.wait_send()


def enter_backward(n, collective_id, step, gs, cout, total, rates, totals, blocks):
    _, _, chans = step.shape
    states = rates.shape[0]
    shape = jax.ShapeDtypeStruct
    m = n // 2
    sems = pltpu.SemaphoreType.DMA((2, n))
    some = pltpu.VMEM((m, *blocks.shape[1:]), BF16)
    return vmem_call(
        functools.partial(enter_backward_kernel, n),
        [shape((states, SUB, chans), F32), shape(blocks.shape[1:], BF16)],
        [
            pltpu.VMEM((states, SUB, chans), F32),
            pltpu.VMEM((states * SUB // 2, chans), BF16),
            pltpu.VMEM((n, states * SUB // 2, chans), BF16),
            some,
            some,
            some,
            sems,
            sems,
            sems,
            sems,
        ],
        collective_id, step, gs, cout, total, rates, packed_rates(rates), totals, blocks,
    )


def half_pick(ids, slots):
    iota = lax.broadcasted_iota(jnp.int32, (ids.shape[0], slots), 1)
    return jnp.where(iota == ids, 1.0, 0.0).astype(BF16)


def dispatching(n, x_ref, out_ref, send, recv, local):
    g = lax.axis_index("dp")
    j, near, _ = mp_pair()
    hc = x_ref.shape[2]
    cols = ds((j % 2) * hc, hc)

    def leave(k):
        return pltpu.make_async_remote_copy(
            src_ref=x_ref.at[(g + k) % n],
            dst_ref=out_ref.at[g, :, cols],
            send_sem=send.at[0, k],
            recv_sem=recv.at[0, k],
            device_id={"dp": (g + k) % n},
            device_id_type=MESH,
        )

    def share(k):
        place = out_ref.at[(g + n - k) % n, :, cols]
        return pltpu.make_async_remote_copy(
            src_ref=place,
            dst_ref=place,
            send_sem=send.at[1, k],
            recv_sem=recv.at[1, k],
            device_id={"mp": near},
            device_id_type=MESH,
        )

    own = pltpu.make_async_copy(x_ref.at[g], out_ref.at[g, :, cols], local)

    def start():
        own.start()
        for k in range(1, n):
            leave(k).start()

    def middle():
        for k in range(n):
            if k:
                leave(k).wait_recv()
            else:
                own.wait()
            share(k).start()

    def end():
        for k in range(n):
            share(k).wait_recv()
        for k in range(n):
            if k:
                leave(k).wait_send()
            share(k).wait_send()

    return start, middle, end


def arrange(cuts, in_ref, tile_ref):
    seqs, chunks, places = cuts
    for ct in range(tile_ref.shape[0]):
        for q in range(seqs):
            for k in range(chunks):
                start = (q * chunks + k) * places
                value = in_ref[start : start + places, ct * LANES : (ct + 1) * LANES]
                tile_ref[ct, pl.ds(k * seqs + q, places, stride=SUB), :] = value.astype(F32)


def front_kernel(
    n,
    cuts,
    capacity,
    tokens_ref,
    cot_ref,
    routes_ref,
    lengths_ref,
    gain_ref,
    weight_ref,
    taps_ref,
    bias_ref,
    select_ref,
    tok_ref,
    cot_low_ref,
    normed_ref,
    both_ref,
    pre_ref,
    inner_ref,
    lead_ref,
    proj_ref,
    rows_ref,
    slot_ref,
    half_ref,
    valid_ref,
    hot_ref,
    tile_s,
    ext_s,
    live_s,
    quarter,
    got,
    part_s,
    ra,
    sb,
    rb,
    send,
    recv,
    dsend,
    drecv,
    local,
):
    seqs, chunks, places = cuts
    g = lax.axis_index("dp")
    j, near, far = mp_pair()
    y, c = j // 2, j % 2
    near, far = {"mp": near}, {"mp": far}
    rows, width = tok_ref.shape
    chans = inner_ref.shape[1]
    kernel = taps_ref.shape[0]
    edge = (kernel - 1) * SUB
    slot_dev = chunks * places
    experts_all = hot_ref.shape[1]
    hr, hc = rows_ref.shape[1], width // 2
    size = 256
    greet([near, far] + [{"dp": (g + k) % n} for k in range(1, n)])

    arrange(cuts, tokens_ref, tile_s)

    def first(b, _):
        at = ds(b * size, size)
        tok = jnp.concatenate([tile_s[ct, at, :] for ct in range(width // LANES)], axis=1)
        tok_ref[at, :] = tok.astype(BF16)
        inverse = lax.rsqrt(jnp.mean(tok * tok, axis=1, keepdims=True) + norm_eps)
        normed = (tok * inverse * gain_ref[...]).astype(BF16)
        normed_ref[at, :] = normed
        both = dot(normed, weight_ref[...], NN).astype(BF16)
        both_ref[at, :] = both
        ext_s[pl.ds(pl.multiple_of(b * size + edge, SUB), size), :] = both[:, 0:chans].astype(F32)
        return 0

    lax.fori_loop(0, rows // size, first, 0)
    ends = sending(
        both_ref.at[rows - 32 : rows, 0:chans], got, send.at[3, 0], recv.at[3, 0], {"dp": (g + 1) % n}
    )

    at_row = lax.broadcasted_iota(jnp.int32, (rows, 1), 0)
    sub = at_row % SUB
    seq = sub % seqs
    local_place = (sub // seqs) * places + at_row // SUB
    limit = jnp.zeros((rows, 1), jnp.int32)
    for q in range(seqs):
        limit = jnp.where(seq == q, lengths_ref[0:1, q : q + 1], limit)
    valid = jnp.where(g * slot_dev + local_place < limit, 1.0, 0.0)
    valid_ref[...] = valid
    route = routes_ref[...]
    hot = jnp.where(lax.broadcasted_iota(jnp.int32, (rows, experts_all), 1) == route, 1.0, 0.0)
    hot_ref[...] = hot
    live_s[...] = hot * valid
    col = lax.broadcasted_iota(jnp.int32, (1, rows), 1)
    col_sub = col % SUB
    original = (col_sub % seqs) * slot_dev + (col_sub // seqs) * places + col // SUB
    room = 2 * hr

    def position(b, _):
        at = ds(b * size, size)
        here = b * size + lax.broadcasted_iota(jnp.int32, (size, 1), 0)
        here_sub = here % SUB
        mine = (here_sub % seqs) * slot_dev + (here_sub // seqs) * places + here // SUB
        before = jnp.where(original < mine, 1.0, 0.0).astype(BF16)
        live = live_s[at, :]
        earlier = dot(before, live_s[...].astype(BF16), NN)
        pos = jnp.sum(earlier * live, axis=1, keepdims=True)
        kept = jnp.where(pos < capacity, jnp.sum(live, axis=1, keepdims=True), 0.0) > 0.5
        pos = pos.astype(jnp.int32)
        to = routes_ref[at, :]
        slot_ref[at, :] = jnp.where(kept, to * room + pos, -1)
        lower = pos - y * hr
        inside = jnp.where(lower >= 0, 1, 0) * jnp.where(lower < hr, 1, 0)
        half_ref[at, :] = jnp.where(kept, jnp.where(inside > 0, to * hr + lower, -1), -1)
        return 0

    lax.fori_loop(0, rows // size, position, 0)

    ends.wait_recv()
    upper = lax.broadcasted_iota(jnp.int32, (SUB, chans), 0) >= SUB // 2
    some = jnp.where(g > 0, 1.0, 0.0)
    tails = got[...].astype(F32) * some
    for k in range(kernel - 1):
        at = slice(k * SUB, (k + 1) * SUB)
        tail = ext_s[rows + k * SUB : rows + (k + 1) * SUB, :]
        other_tail = tails[32 - edge + k * SUB : 32 - edge + (k + 1) * SUB, :]
        lead = half_turn(jnp.where(upper, other_tail, tail))
        ext_s[at, :] = lead
        lead_ref[at, :] = lead

    half = rows // 2
    count = half // size
    own = c * half
    other = (1 - c) * half

    def conv(start):
        at = ds(start, size)
        pre = jnp.broadcast_to(bias_ref[...], (size, chans))
        for k in range(kernel):
            past = ext_s[pl.ds(pl.multiple_of(start + k * SUB, SUB), size), :]
            pre = pre + taps_ref[k : k + 1, :] * past
        pre_ref[at, :] = pre
        inner = (pre * jax.nn.sigmoid(pre)).astype(BF16)
        inner_ref[at, :] = inner
        part_s[at, :] = dot(inner, select_ref[...], NN)

    one, two, three = [], [], []
    for k in range(count):
        conv(other + k * size)
        at = ds(other + k * size, size)
        one.append(sending(part_s.at[at], ra.at[k], send.at[0, k], recv.at[0, k], near))
    for k in range(count):
        conv(own + k * size)
        one[k].wait_recv()
        sb[k] = part_s[ds(own + k * size, size), :] + ra[k]
        two.append(sending(sb.at[k], rb.at[k], send.at[1, k], recv.at[1, k], far))

    arrange(cuts, cot_ref, tile_s)

    def second(b, _):
        at = ds(b * size, size)
        cot = jnp.concatenate([tile_s[ct, at, :] for ct in range(width // LANES)], axis=1)
        cot_low_ref[at, :] = cot.astype(BF16)
        return 0

    lax.fori_loop(0, rows // size, second, 0)
    pick = half_pick(half_ref[...], n * hr)
    sent = dot(pick, cot_low_ref[:, ds(c * hc, hc)], TN).astype(BF16)
    quarter[...] = sent.reshape(n, hr, hc)
    start, middle, end = dispatching(n, quarter, rows_ref, dsend, drecv, local)
    start()
    for k in range(count):
        two[k].wait_recv()
        at = ds(own + k * size, size)
        proj_ref[at, :] = sb[k] + rb[k]
        three.append(sending(proj_ref.at[at], proj_ref.at[at], send.at[2, k], recv.at[2, k], near))
    for copy in three:
        copy.wait_recv()
    middle()
    end()
    for copy in [ends] + one + two + three:
        copy.wait_send()


def front(n, collective_id, cuts, capacity, hr, experts_all, *args):
    tokens, taps, select = args[0], args[6], args[8]
    rows, width = tokens.shape
    kernel, chans = taps.shape
    edge = (kernel - 1) * SUB
    wide = select.shape[1]
    count = rows // 512
    shape = jax.ShapeDtypeStruct
    sems = pltpu.SemaphoreType.DMA((4, count))
    dsems = pltpu.SemaphoreType.DMA((2, n))
    sums = pltpu.VMEM((count, 256, wide), F32)
    return vmem_call(
        functools.partial(front_kernel, n, cuts, capacity),
        [
            shape((rows, width), BF16),
            shape((rows, width), BF16),
            shape((rows, width), BF16),
            shape((rows, 2 * chans), BF16),
            shape((rows, chans), F32),
            shape((rows, chans), BF16),
            shape((edge, chans), F32),
            shape((rows, wide), F32),
            shape((n, hr, width), BF16),
            shape((rows, 1), jnp.int32),
            shape((rows, 1), jnp.int32),
            shape((rows, 1), F32),
            shape((rows, experts_all), F32),
        ],
        [
            pltpu.VMEM((width // LANES, rows, LANES), F32),
            pltpu.VMEM((rows + edge, chans), F32),
            pltpu.VMEM((rows, experts_all), F32),
            pltpu.VMEM((n, hr, width // 2), BF16),
            pltpu.VMEM((32, chans), BF16),
            pltpu.VMEM((rows, wide), F32),
            sums,
            sums,
            sums,
            sems,
            sems,
            dsems,
            dsems,
            pltpu.SemaphoreType.DMA,
        ],
        collective_id, *args,
    )


def middle_kernel(
    n,
    count,
    part_ref,
    tok_ref,
    valid_ref,
    gain_ref,
    half_ref,
    resid_ref,
    rows_ref,
    sum_s,
    normed_s,
    quarter,
    ra,
    sb,
    rb,
    send,
    recv,
    dsend,
    drecv,
    local,
):
    g = lax.axis_index("dp")
    j, near, far = mp_pair()
    c = j % 2
    near, far = {"mp": near}, {"mp": far}
    rows, width = tok_ref.shape
    hr, hc = rows_ref.shape[1], width // 2
    half = rows // 2
    size = half // count
    own, other = c * half, (1 - c) * half
    greet([near, far] + [{"dp": (g + k) % n} for k in range(1, n)])
    one = [
        sending(part_ref.at[ds(other + k * size, size)], ra.at[k], send.at[0, k], recv.at[0, k], near)
        for k in range(count)
    ]
    two, three = [], []
    for k in range(count):
        one[k].wait_recv()
        mine = part_ref[ds(own + k * size, size), :].astype(F32)
        sb[k] = (mine + ra[k].astype(F32)).astype(BF16)
        two.append(sending(sb.at[k], rb.at[k], send.at[1, k], recv.at[1, k], far))

    def norm(start):
        at = ds(start, size)
        resid = tok_ref[at, :].astype(F32) + valid_ref[at, :] * sum_s[at, :].astype(F32)
        resid_ref[at, :] = resid
        inverse = lax.rsqrt(jnp.mean(resid * resid, axis=1, keepdims=True) + norm_eps)
        normed_s[at, :] = (resid * inverse * gain_ref[...]).astype(BF16)

    for k in range(count):
        two[k].wait_recv()
        at = ds(own + k * size, size)
        sum_s[at, :] = (sb[k].astype(F32) + rb[k].astype(F32)).astype(BF16)
        three.append(sending(sum_s.at[at], sum_s.at[at], send.at[2, k], recv.at[2, k], near))
        norm(own + k * size)
    for k in range(count):
        three[k].wait_recv()
        norm(other + k * size)
    pick = half_pick(half_ref[...], n * hr)
    sent = dot(pick, normed_s[:, ds(c * hc, hc)], TN).astype(BF16)
    quarter[...] = sent.reshape(n, hr, hc)
    start, middle, end = dispatching(n, quarter, rows_ref, dsend, drecv, local)
    start()
    middle()
    end()
    for copy in one + two + three:
        copy.wait_send()


def mixer_to_experts(n, collective_id, hr, part, tok, valid, gain, half_slots, count=4):
    rows, width = tok.shape
    shape = jax.ShapeDtypeStruct
    sems = pltpu.SemaphoreType.DMA((3, count))
    dsems = pltpu.SemaphoreType.DMA((2, n))
    slots = pltpu.VMEM((count, rows // 2 // count, width), BF16)
    whole_rows = pltpu.VMEM((rows, width), BF16)
    return vmem_call(
        functools.partial(middle_kernel, n, count),
        [shape((rows, width), F32), shape((n, hr, width), BF16)],
        [
            whole_rows,
            whole_rows,
            pltpu.VMEM((n, hr, width // 2), BF16),
            slots,
            slots,
            slots,
            sems,
            sems,
            dsems,
            dsems,
            pltpu.SemaphoreType.DMA,
        ],
        collective_id, part, tok, valid, gain, half_slots,
    )


def expert_kernel(
    n,
    rows_ref,
    cot_ref,
    up_ref,
    ub_ref,
    down_ref,
    other_ref,
    ub2_ref,
    db_ref,
    router_ref,
    hot_ref,
    out_ref,
    gown_ref,
    gother_ref,
    gub_ref,
    gdb_ref,
    part,
    hid,
    slope,
    pre,
    grad,
    ra,
    qb,
    send,
    recv,
):
    g = lax.axis_index("dp")
    j, near, far = mp_pair()
    near, far = {"mp": near}, {"mp": far}
    y, c = j // 2, j % 2
    hr, width = rows_ref.shape[1], rows_ref.shape[2]
    hidden = up_ref.shape[1]
    hc = width // 2
    half, total, window = n // 2, 2 * n, min(n, 6)
    size = half * hr
    greet([near, far] + [{"dp": (g + k) % n} for k in range(1, n)])
    mine, theirs = ds(c * hc, hc), ds((1 - c) * hc, hc)
    up, down = ds(y * hr, hr), ds((1 - y) * hr, hr)
    gub_ref[...] = jnp.zeros_like(gub_ref)
    gdb_ref[...] = jnp.zeros_like(gdb_ref)
    folded = lambda v: jnp.sum(v.reshape(v.shape[0] // SUB, SUB, v.shape[1]), axis=0)
    ups = (up_ref, other_ref.at[0:width])
    downs = (down_ref, other_ref.at[width : width + hidden])
    biases = (ub_ref, ub2_ref)

    def copy(kind, there, here, src, dst, to):
        return pltpu.make_async_remote_copy(
            src_ref=src,
            dst_ref=dst,
            send_sem=send.at[kind, here],
            recv_sem=recv.at[kind, there],
            device_id=to,
            device_id_type=MESH,
        )

    def target(t):
        return (g + t) % n

    def source(t):
        return (g + 2 * n - t) % n

    def near_copy(t):
        at = part.at[t // n, target(t)]
        return copy(0, t, t, at.at[:, theirs], ra.at[t], near)

    def back_copy(t, arriving):
        a = t // n * n
        there = a + source(t) if arriving else a + g
        return copy(1, there, t, qb.at[t], out_ref.at[t // n, g, up, mine], {"dp": target(t)})

    def place(t, rows):
        return out_ref.at[t // n, source(t), rows, mine]

    def pass_far(t):
        return copy(2, t, t, place(t, up), place(t, up), far)

    def pass_near(t):
        return copy(3, t, t, place(t, up), place(t, up), near)

    def pass_on(t):
        return copy(4, t, t, place(t, down), place(t, down), near)

    def wide(ref, base):
        return ref[pl.ds(base, half)].reshape(size, ref.shape[2])

    def ahead(base):
        rows = wide(rows_ref, base)
        total_part = None
        for k in range(2):
            v = dot(rows, ups[k][...], NN) + biases[k][...]
            sq = v * v
            th = jnp.tanh(v * (GELU_A + GELU_A * GELU_B * sq))
            at = pl.ds(pl.multiple_of(base * hr, size), size)
            act = (0.5 * v * (1.0 + th)).astype(BF16)
            hid[k, at, :] = act
            slope[k, at, :] = 0.5 * (1.0 + th) + 0.5 * v * (1.0 - th * th) * (
                GELU_A + 3.0 * GELU_A * GELU_B * sq
            )
            term = dot(act, downs[k][...], NN)
            total_part = term if k == 0 else total_part + term
        part[0, pl.ds(base, half)] = total_part.astype(BF16).reshape(half, hr, width)

    def behind(base):
        at = pl.ds(pl.multiple_of(base * hr, size), size)
        probs = jax.nn.softmax(dot(wide(rows_ref, base), router_ref[...], NN), axis=-1)
        chosen = jnp.sum(probs * hot_ref[...], axis=1, keepdims=True)
        scaled = (chosen * wide(cot_ref, base).astype(F32)).astype(BF16)
        grad[at, :] = scaled
        gdb_ref[...] += folded(scaled.astype(F32))
        total_part = None
        for k in range(2):
            value = (dot(scaled, downs[k][...], NT) * slope[k, at, :]).astype(BF16)
            pre[k, at, :] = value
            gub_ref[k] += folded(value.astype(F32))
            term = dot(value, ups[k][...], NT)
            total_part = term if k == 0 else total_part + term
        part[1, pl.ds(base, half)] = total_part.astype(BF16).reshape(half, hr, width)

    def pair_sum(t):
        near_copy(t).wait_recv()
        value = part[t // n, target(t), :, mine].astype(F32) + ra[t].astype(F32)
        qb[t] = (value + jnp.where(t < n, 1.0, 0.0) * db_ref[:, mine]).astype(BF16)

        @pl.when(t % n == 0)
        def _():
            out_ref[t // n, g, up, mine] = qb[t]

    def leave(t):
        @pl.when(t % n != 0)
        def _():
            back_copy(t, False).start()

    def arrived(t):
        @pl.when(t % n != 0)
        def _():
            back_copy(t, True).wait_recv()

        pass_far(t).start()
        pass_near(t).start()

    def passed(t):
        pass_far(t).wait_recv()
        pass_on(t).start()

    cut = 256
    pieces = width // cut

    def weights(q):
        at = ds(q % pieces * cut, cut)
        for kind in range(2):
            for k in range(2):

                @pl.when(q // pieces == 2 * kind + 1 - k)
                def _(kind=kind, k=k):
                    if kind == 0:
                        value = dot(hid[k], grad[:, at], TN)
                    else:
                        value = dot(rows_ref[...].reshape(n * hr, width), pre[k, :, at], TN)
                    if k == 0:
                        gown_ref[kind, :, at] = value
                    else:
                        gother_ref[kind, :, at] = value.astype(BF16)

    def each(act, start, count):
        def one(i, _):
            act(start + i)
            return 0

        lax.fori_loop(0, count, one, 0)

    for kind, work in enumerate((ahead, behind)):
        work(0)
        work(half)
        each(lambda t: near_copy(t).start(), kind * n, n)
        each(pair_sum, kind * n, n)
        if kind == 0:
            each(leave, 0, window)

    lag = 2

    def step(i, _):
        @pl.when(i < 4 * pieces)
        def _():
            weights(i)

        @pl.when(i + window < total)
        def _():
            leave(i + window)

        @pl.when(i < total)
        def _():
            arrived(i)

        @pl.when((i >= lag) & (i < total + lag))
        def _():
            passed(i - lag)

        return 0

    lax.fori_loop(0, max(4 * pieces, total + lag), step, 0)

    def finish_one(t, _):
        pass_near(t).wait_recv()
        pass_on(t).wait_recv()
        for made in (near_copy, pass_far, pass_near, pass_on):
            made(t).wait_send()

        @pl.when(t % n != 0)
        def _():
            back_copy(t, False).wait_send()

        return 0

    lax.fori_loop(0, total, finish_one, 0)


GELU_A = 0.7978845608028654
GELU_B = 0.044715


def experts(n, collective_id, rows, cot, up, up_bias, down, other, other_bias, down_bias, router, hot):
    _, hr, width = rows.shape
    hidden = up.shape[1]
    shape = jax.ShapeDtypeStruct
    sems = pltpu.SemaphoreType.DMA((5, 2 * n))
    quarters = pltpu.VMEM((2 * n, hr, width // 2), BF16)
    return vmem_call(
        functools.partial(expert_kernel, n),
        [
            shape((2, n, 2 * hr, width), BF16),
            shape((2, width, hidden), F32),
            shape((2, width, hidden), BF16),
            shape((2, SUB, hidden), F32),
            shape((SUB, width), F32),
        ],
        [
            pltpu.VMEM((2, n, hr, width), BF16),
            pltpu.VMEM((2, n * hr, hidden), BF16),
            pltpu.VMEM((2, n * hr, hidden), F32),
            pltpu.VMEM((2, n * hr, hidden), BF16),
            pltpu.VMEM((n * hr, width), BF16),
            quarters,
            quarters,
            sems,
            sems,
        ],
        collective_id, rows, cot, up, up_bias, down, other, other_bias, down_bias, router, hot,
    )


def finish_kernel(
    n,
    count,
    cuts,
    layout,
    proj_ref,
    select_ref,
    inner_ref,
    base_ref,
    pre_ref,
    both_ref,
    lead_ref,
    gate_ref,
    normed_ref,
    weight_ref,
    taps_ref,
    given_ref,
    tok_ref,
    resid_ref,
    gain_ref,
    grad_ref,
    gin_ref,
    small_ref,
    first_ref,
    conv_s,
    ext_s,
    both_s,
    got,
    part_s,
    sum_s,
    ra,
    sb,
    rb,
    blocks,
    pa,
    ps,
    pc,
    outs,
    tile_s,
    firsts,
    rows_s,
    fold_s,
    send,
    recv,
):
    mh, sh = layout
    g = lax.axis_index("dp")
    j, near, far = mp_pair()
    near, far = {"mp": near}, {"mp": far}
    odd, z, m = g % 2, g // 2, n // 2
    pair = {"dp": g + 1 - 2 * odd}
    like = [{"dp": 2 * ((z + k) % m) + odd} for k in range(1, m)]
    others = [{"dp": (g + k) % n} for k in range(1, n)]
    greet([near, far] + others)
    rows, chans = inner_ref.shape
    width = normed_ref.shape[1]
    kernel = taps_ref.shape[0]
    edge = (kernel - 1) * SUB
    block = 256
    ext_s[0:edge, :] = lead_ref[...]

    def conv_block(b):
        at = ds(b * block, block)
        grad = base_ref[at, :] + dot(proj_ref[at, :], select_ref[...], NT)
        conv_s[at, :] = grad * silu_slope(pre_ref[at, :])
        ext_s[pl.ds(pl.multiple_of(b * block + edge, SUB), block), :] = both_ref[at, 0:chans].astype(F32)

    conv_block(0)
    head = sending(conv_s.at[0:edge], got, send.at[8, 0], recv.at[8, 0], {"dp": (g + n - 1) % n})

    def rest(b, _):
        conv_block(b)
        return 0

    lax.fori_loop(1, rows // block, rest, 0)
    head.wait_recv()
    upper = lax.broadcasted_iota(jnp.int32, (SUB, chans), 0) >= SUB // 2
    some = jnp.where(g < n - 1, 1.0, 0.0)
    for k in range(kernel - 1):
        at = slice(k * SUB, (k + 1) * SUB)
        tail = half_turn(jnp.where(upper, conv_s[at, :], got[at, :] * some))
        conv_s[rows + k * SUB : rows + (k + 1) * SUB, :] = tail

    half = rows // 2
    size = half // count
    own = (j % 2) * half
    other = (1 - j % 2) * half

    def back(start):
        at = ds(start, size)
        total = jnp.zeros((size, chans), F32)
        for k in range(kernel):
            later = conv_s[pl.ds(pl.multiple_of(start + (kernel - 1 - k) * SUB, SUB), size), :]
            total = total + taps_ref[k : k + 1, :] * later
        both_s[at, 0:chans] = total.astype(BF16)
        both_s[at, chans : 2 * chans] = gate_ref[at, :]
        part_s[at, :] = dot(both_s[at, :], weight_ref[...], NT).astype(BF16)

    one, two, three, first, second = [], [], [], [], []
    for k in range(count):
        back(other + k * size)
        at = ds(other + k * size, size)
        one.append(sending(part_s.at[at], ra.at[k], send.at[0, k], recv.at[0, k], near))
    for k in range(count):
        back(own + k * size)
        one[k].wait_recv()
        mine = part_s[ds(own + k * size, size), :].astype(F32)
        sb[k] = (mine + ra[k].astype(F32)).astype(BF16)
        two.append(sending(sb.at[k], rb.at[k], send.at[1, k], recv.at[1, k], far))

    rows_s[0:width, :] = dot(normed_ref[...], both_s[:, 0:chans], TN)
    given = given_ref.shape[0]
    selects = select_ref.shape[1]
    rest_at = given + selects
    fold_s[0:given, :] = given_ref[...]
    fold_s[given:rest_at, :] = dot(proj_ref[...], inner_ref[...], TN)
    folded = lambda v: jnp.sum(v.reshape(block // SUB, SUB, chans), axis=0)

    def taps(b, sums):
        grad = conv_s[ds(b * block, block), :]
        past = [ext_s[pl.ds(pl.multiple_of(b * block + k * SUB, SUB), block), :] for k in range(kernel)]
        return tuple(v + folded(grad * p) for v, p in zip(sums, past)) + (sums[kernel] + folded(grad),)

    zero = tuple(jnp.zeros((SUB, chans), F32) for _ in range(kernel + 1))
    sums = lax.fori_loop(0, rows // block, taps, zero)
    for k in range(kernel + 1):
        fold_s[rest_at + k : rest_at + k + 1, :] = jnp.sum(sums[k], axis=0, keepdims=True)
    for b in range(n):
        blocks[b, 0:mh, :] = rows_s[b * mh : (b + 1) * mh, :].astype(BF16)
        blocks[b, mh : mh + sh, :] = fold_s[b * sh : (b + 1) * sh, :].astype(BF16)
    order = [(z + k) % m for k in range(1, m)] + [z]
    first = [
        sending(blocks.at[2 * order[k] + 1 - odd], pa.at[k], send.at[3, k], recv.at[3, k], pair)
        for k in range(m)
    ]
    for k in range(max(count, m)):
        if k < m:
            first[k].wait_recv()
            ps[k] = (blocks[2 * order[k] + odd].astype(F32) + pa[k].astype(F32)).astype(BF16)
            if k < m - 1:
                second.append(sending(ps.at[k], pc.at[k], send.at[4, k], recv.at[4, k], like[k]))
        if k < count:
            two[k].wait_recv()
            at = ds(own + k * size, size)
            sum_s[at, :] = (sb[k].astype(F32) + rb[k].astype(F32)).astype(BF16)
            three.append(sending(sum_s.at[at], sum_s.at[at], send.at[2, k], recv.at[2, k], near))
    value = ps[m - 1].astype(F32)
    for copy in second:
        copy.wait_recv()
    for k in range(m - 1):
        value = value + pc[k].astype(F32)
    outs[g] = value.astype(BF16)
    third = [sending(outs.at[g], outs.at[g], send.at[5, k], recv.at[5, k], like[k]) for k in range(m - 1)]
    fourth = [sending(outs.at[g], outs.at[g], send.at[6, 0], recv.at[6, 0], pair)]
    firsts[0] = jnp.zeros(firsts.shape[1:], F32)
    gain = gain_ref[...]

    def norm_rows(start):
        at = ds(start, size)
        grad = sum_s[at, :].astype(F32)
        tok = tok_ref[at, :].astype(F32)
        inverse = lax.rsqrt(jnp.mean(tok * tok, axis=1, keepdims=True) + norm_eps)
        normed = tok * inverse
        firsts[0] += jnp.sum((grad * normed).reshape(size // SUB, SUB, width), axis=0)
        scaled = grad * gain
        mean = jnp.mean(scaled * normed, axis=1, keepdims=True)
        value = resid_ref[at, :] + inverse * (scaled - normed * mean)
        for ct in range(width // LANES):
            tile_s[ct, at, :] = value[:, ct * LANES : (ct + 1) * LANES]

    for k in range(count):
        norm_rows(own + k * size)
    for k in range(count):
        three[k].wait_recv()
        norm_rows(other + k * size)
    spread_first = [
        sending(firsts.at[0], firsts.at[k], send.at[7, k], recv.at[7, k], others[k - 1]) for k in range(1, n)
    ]
    for k in range(m - 1):
        third[k].wait_recv()
        b = 2 * ((z + m - 1 - k) % m) + odd
        fourth.append(sending(outs.at[b], outs.at[b], send.at[6, k + 1], recv.at[6, k + 1], pair))
    restore(cuts, tile_s, grad_ref)
    for copy in spread_first:
        copy.wait_recv()

    def one_first(d, total):
        return total + firsts[(g + n - d) % n]

    first_ref[...] = lax.fori_loop(0, n, one_first, jnp.zeros(first_ref.shape, F32))
    for copy in fourth:
        copy.wait_recv()
    for b in range(n):
        gin_ref[b * mh : (b + 1) * mh, :] = outs[b, 0:mh, :].astype(F32)
        small_ref[b * sh : (b + 1) * sh, :] = outs[b, mh : mh + sh, :].astype(F32)
    for copy in [head] + one + two + three + first + second + third + fourth + spread_first:
        copy.wait_send()


def finish(n, collective_id, cuts, *args, count=4):
    proj, select, inner, normed, taps, given = args[0], args[1], args[2], args[8], args[10], args[11]
    rows, chans = inner.shape
    width = normed.shape[1]
    kernel = taps.shape[0]
    edge = (kernel - 1) * SUB
    m = n // 2
    over = lambda size: (size + 16 * n - 1) // (16 * n) * 16
    mh, sh = over(width), over(given.shape[0] + select.shape[1] + kernel + 1)
    slots = pltpu.VMEM((count, rows // 2 // count, width), BF16)
    part = lambda k: pltpu.VMEM((k, mh + sh, chans), BF16)
    sems = pltpu.SemaphoreType.DMA((9, max(n, count)))
    shape = jax.ShapeDtypeStruct
    return vmem_call(
        functools.partial(finish_kernel, n, count, cuts, (mh, sh)),
        [
            shape((rows, width), F32),
            shape((n * mh, chans), F32),
            shape((n * sh, chans), F32),
            shape((SUB, width), F32),
        ],
        [
            pltpu.VMEM((rows + edge, chans), F32),
            pltpu.VMEM((rows + edge, chans), F32),
            pltpu.VMEM((rows, 2 * chans), BF16),
            pltpu.VMEM((edge, chans), F32),
            pltpu.VMEM((rows, width), BF16),
            pltpu.VMEM((rows, width), BF16),
            slots,
            slots,
            slots,
            part(n),
            part(m),
            part(m),
            part(m),
            part(n),
            pltpu.VMEM((width // LANES, rows, LANES), F32),
            pltpu.VMEM((n, SUB, width), F32),
            pltpu.VMEM((n * mh, chans), F32),
            pltpu.VMEM((n * sh, chans), F32),
            sems,
            sems,
        ],
        collective_id, *args,
    )


def token_back_kernel(
    cuts,
    slot_ref,
    back_ref,
    residual_ref,
    hot_ref,
    cot_ref,
    valid_ref,
    gain_ref,
    router_ref,
    gated_ref,
    out_ref,
    scan_ref,
    both_ref,
    inner_ref,
    normed_in_ref,
    block_ref,
    resid_ref,
    gs_ref,
    gate_ref,
    early_ref,
    mixed_s,
    block_s,
    early_s,
    small_s,
    router_out,
    second_ref,
    skip_ref,
):
    rows, width = residual_ref.shape
    chans = inner_ref.shape[1]
    slots = back_ref.shape[1] * back_ref.shape[2]
    size = 256
    router_out[...] = jnp.zeros_like(router_out)
    second_ref[...] = jnp.zeros_like(second_ref)
    skip_ref[...] = jnp.zeros_like(skip_ref)

    def body(b, _):
        at = ds(b * size, size)
        folded = lambda v: jnp.sum(v.reshape(size // SUB, SUB, v.shape[1]), axis=0)
        iota = lax.broadcasted_iota(jnp.int32, (size, slots), 1)
        pick = jnp.where(iota == slot_ref[at, :], 1.0, 0.0).astype(BF16)
        result = dot(pick, back_ref[0].reshape(slots, width), NN)
        grad = dot(pick, back_ref[1].reshape(slots, width), NN)
        residual = residual_ref[at, :]
        inverse = lax.rsqrt(jnp.mean(residual * residual, axis=1, keepdims=True) + norm_eps)
        normed = residual * inverse
        normed_low = (normed * gain_ref[...]).astype(BF16)
        hot = hot_ref[at, :]
        probs = jax.nn.softmax(dot(normed_low, router_ref[...], NN), axis=-1)
        chosen = jnp.sum(probs * hot, axis=1, keepdims=True)
        block = residual + chosen * result
        for ct in range(width // LANES):
            block_s[ct, at, :] = block[:, ct * LANES : (ct + 1) * LANES]
        cot = cot_ref[at, :].astype(F32)
        gate = jnp.sum(cot * result, axis=1, keepdims=True)
        logit = (gate * probs * (hot - chosen)).astype(BF16)
        router_out[...] += dot(logit, normed_low, TN)
        grad = grad + dot(logit, router_ref[...], NT)
        second_ref[...] += folded(grad * normed)
        scaled = grad * gain_ref[...]
        mean = jnp.mean(scaled * normed, axis=1, keepdims=True)
        resid = cot + inverse * (scaled - normed * mean)
        resid_ref[at, :] = resid
        mixed = (valid_ref[at, :] * resid).astype(BF16)
        mixed_s[at, :] = mixed
        grad_gated = dot(mixed, out_ref[...], NT)
        pre = both_ref[at, chans : 2 * chans].astype(F32)
        sig = jax.nn.sigmoid(pre)
        act = pre * sig
        gs = grad_gated * act
        gs_ref[at, :] = gs
        skip_ref[...] += folded(gs * inner_ref[at, :].astype(F32))
        gate_ref[at, :] = (grad_gated * scan_ref[at, :] * (sig * (1.0 + pre * (1.0 - sig)))).astype(BF16)
        return 0

    lax.fori_loop(0, rows // size, body, 0)
    n, mh = early_ref.shape[0], early_s.shape[1] // early_ref.shape[0]
    sh = early_ref.shape[1] - 2 * mh
    some = router_out.shape[0]
    for k in range(width // chans):
        at = slice(k * chans, (k + 1) * chans)
        small_s[k * some : (k + 1) * some, :] = router_out[:, at]
        line = 2 * some + k
        small_s[line : line + 1, :] = jnp.sum(second_ref[:, at], axis=0, keepdims=True)
    small_s[2 * some + 2 : 2 * some + 3, :] = jnp.sum(skip_ref[...], axis=0, keepdims=True)
    early_s[0, 0:width, :] = dot(normed_in_ref[...], gate_ref[...], TN)
    value = dot(gated_ref[...], mixed_s[...], TN)
    for k in range(width // chans):
        early_s[1, k * chans : (k + 1) * chans, :] = value[:, k * chans : (k + 1) * chans]
    for b in range(n):
        for k in range(2):
            early_ref[b, k * mh : (k + 1) * mh, :] = early_s[k, b * mh : (b + 1) * mh, :].astype(BF16)
        early_ref[b, 2 * mh : 2 * mh + sh, :] = small_s[b * sh : (b + 1) * sh, :].astype(BF16)
    restore(cuts, block_s, block_ref)


def restore(cuts, tile_ref, out_ref):
    seqs, chunks, places = cuts
    for ct in range(tile_ref.shape[0]):
        for q in range(seqs):
            for k in range(chunks):
                picked = tile_ref[ct, pl.ds(k * seqs + q, places, stride=SUB), :]
                start = (q * chunks + k) * places
                out_ref[start : start + places, ct * LANES : (ct + 1) * LANES] = picked.astype(out_ref.dtype)


def token_back(n, cuts, *args):
    residual, router, inner = args[2], args[7], args[12]
    over = lambda size: (size + 16 * n - 1) // (16 * n) * 16
    mh, sh = over(residual.shape[1]), over(2 * router.shape[1] + 3)
    rows, width = residual.shape
    chans = inner.shape[1]
    shape = jax.ShapeDtypeStruct
    return pl.pallas_call(
        functools.partial(token_back_kernel, cuts),
        out_shape=[
            shape((rows, width), BF16),
            shape((rows, width), F32),
            shape((rows, chans), F32),
            shape((rows, chans), BF16),
            shape((n, 2 * mh + sh, chans), BF16),
        ],
        scratch_shapes=[
            pltpu.VMEM((rows, width), BF16),
            pltpu.VMEM((width // LANES, rows, LANES), F32),
            pltpu.VMEM((2, n * mh, chans), F32),
            pltpu.VMEM((n * sh, chans), F32),
            pltpu.VMEM((router.shape[1], width), F32),
            pltpu.VMEM((SUB, width), F32),
            pltpu.VMEM((SUB, chans), F32),
        ],
        compiler_params=pltpu.CompilerParams(vmem_limit_bytes=VMEM),
    )(*args)


def silu_slope(values):
    sigmoid_vals = jax.nn.sigmoid(values)
    return sigmoid_vals * (1.0 + values * (1.0 - sigmoid_vals))


def per_device(
    tokens,
    routes,
    lengths,
    cotangent,
    first_gain,
    mixer_in,
    conv_weight,
    conv_bias,
    select_weight,
    step_weight,
    step_bias,
    decay_log,
    skip_gain,
    mixer_out,
    second_gain,
    router_weight,
    expert_up,
    up_bias,
    expert_down,
    down_bias,
):
    tok_count, model_width = tokens.shape
    kernel, chan_count = conv_weight.shape
    rank_size = step_weight.shape[0]
    state_size = decay_log.shape[0]
    expert_total = router_weight.shape[1]
    capacity = max(2, (5 * tok_count + 4 * expert_total - 1) // (4 * expert_total))
    room = (capacity + 31) // 32 * 32
    slot_dev = SLOT_DEV
    seq_count = tok_count // slot_dev
    chunks = SUB // seq_count
    places_dev = slot_dev // chunks
    cuts = (seq_count, chunks, places_dev)
    device = lax.axis_index("dp")
    dp_count = lax.axis_size("dp")

    mp_count = lax.axis_size("mp")
    to_far = [(i, (i + mp_count // 2) % mp_count) for i in range(mp_count)]
    swap_far = lambda values: lax.ppermute(values, "mp", to_far)
    own_bias = jnp.broadcast_to(up_bias, (16, up_bias.shape[1]))
    other_weights = swap_far(jnp.concatenate([expert_up[0], expert_down[0], own_bias], axis=0))

    first_vals = first_gain.astype(F32)
    second_vals = second_gain.astype(F32)
    mixer_in_flat = mixer_in.reshape(model_width, 2 * chan_count)
    conv_taps = conv_weight.astype(F32)
    routes_cut = routes.reshape(seq_count, chunks, places_dev).transpose(2, 1, 0)
    (
        tok_low,
        cot_low,
        normed_in,
        both_in,
        conv_pre,
        inner_vals,
        lead_rows,
        projected,
        cot_rows,
        slot_ids,
        half_slots,
        valid_col,
        route_hot,
    ) = front(
        dp_count,
        0,
        cuts,
        capacity,
        room // 2,
        expert_total,
        tokens,
        cotangent,
        routes_cut.reshape(tok_count, 1),
        lengths[None],
        first_vals[None],
        mixer_in_flat,
        conv_taps,
        conv_bias.astype(F32)[None],
        select_weight,
    )
    decay_rates = -jnp.exp(decay_log.astype(F32))
    rates = decay_rates * LOG2E

    step_p, drive_p, step_slope, bin_p, cout_p, low_high, chunk_steps, state_in, totals = enter_forward(
        dp_count,
        2,
        projected,
        step_weight,
        step_bias.astype(F32)[None],
        inner_vals,
        valid_col,
        rates,
    )
    skip_vals = skip_gain.astype(F32)
    scan_out, gated_vals, mixer_part, states_before, last_states = forward(
        step_p,
        drive_p,
        bin_p,
        cout_p,
        rates,
        state_in,
        inner_vals,
        both_in,
        skip_vals[None],
        mixer_out,
    )
    residual, expert_rows = mixer_to_experts(
        dp_count, 3, room // 2, mixer_part, tok_low, valid_col, second_vals[None], half_slots
    )

    own_hot = (jnp.arange(expert_total) == device).astype(F32)[None]
    returned, grad_own, grad_other, up_bias_parts, down_bias_part = experts(
        dp_count,
        5,
        expert_rows,
        cot_rows,
        expert_up[0],
        up_bias.astype(F32),
        expert_down[0],
        other_weights,
        other_weights[-16:-15].astype(F32),
        down_bias.astype(F32),
        router_weight,
        own_hot,
    )
    down_bias_part = down_bias_part.astype(BF16)
    bias_rows = jnp.concatenate([up_bias_parts[1].astype(BF16), down_bias_part], axis=0)
    from_far = swap_far((grad_other, bias_rows))
    grad_down = grad_own[0] + from_far[0][0].astype(F32)
    grad_up = grad_own[1] + from_far[0][1].astype(F32)
    grad_up_bias = up_bias_parts[0] + from_far[1][:SUB].astype(F32)
    grad_down_bias = down_bias_part.astype(F32) + from_far[1][SUB:].astype(F32)
    (
        block_out,
        grad_resid,
        grad_scan,
        grad_gate_low,
        early,
    ) = token_back(
        dp_count,
        cuts,
        slot_ids,
        returned,
        residual,
        route_hot,
        cot_low,
        valid_col,
        second_vals[None],
        router_weight,
        gated_vals,
        mixer_out,
        scan_out,
        both_in,
        inner_vals,
        normed_in,
    )
    gs_p = grad_scan.reshape(places_dev, SUB, chan_count)
    grad_in, early = enter_backward(
        dp_count, 6, step_p, gs_p, cout_p, chunk_steps, rates, totals, early
    )
    (
        grad_base,
        grad_low_part,
        grad_bin,
        cout_shift,
        rate_parts,
        grad_step_weight,
        grad_step_bias,
        grad_gate_in,
        grad_mixer_out,
        few,
        last_cout,
    ) = backward(
        dp_count,
        9,
        (model_width + 16 * dp_count - 1) // (16 * dp_count) * 16,
        step_p,
        drive_p,
        gs_p,
        bin_p,
        cout_p,
        rates,
        grad_in,
        last_states,
        states_before,
        inner_vals,
        step_slope,
        low_high,
        step_weight,
        skip_vals[None],
        early,
    )
    grad_cout = jnp.concatenate([cout_shift[SUB:], last_cout], axis=0)
    grad_decay_log = jnp.sum(rate_parts, axis=1) * decay_rates
    proj_part = jnp.concatenate([grad_low_part, grad_bin, grad_cout], axis=1)
    grad_proj = sum_mp(proj_part.astype(BF16), 7, 2)
    given = jnp.concatenate(
        [grad_step_weight, grad_decay_log, jnp.sum(grad_step_bias, axis=0, keepdims=True)], axis=0
    )
    given = jnp.pad(given, ((0, -given.shape[0] % SUB), (0, 0)))
    token_grad, grad_conv_half, small, grad_first = finish(
        dp_count,
        8,
        cuts,
        grad_proj,
        select_weight,
        inner_vals,
        grad_base,
        conv_pre,
        both_in,
        lead_rows,
        grad_gate_low,
        normed_in,
        mixer_in_flat,
        conv_taps,
        given,
        tok_low,
        grad_resid,
        first_vals[None],
    )
    select_at = given.shape[0]
    taps_at = select_at + select_weight.shape[1]
    rest = rank_size + state_size
    second_at = 2 * expert_total
    return (
        block_out,
        token_grad,
        jnp.sum(grad_first, axis=0),
        jnp.stack([grad_conv_half[:model_width], grad_gate_in[:model_width]], axis=1),
        small[taps_at : taps_at + kernel],
        small[taps_at + kernel],
        small[select_at:taps_at].T,
        small[:rank_size],
        small[rest],
        small[rank_size:rest],
        few[second_at + 2],
        jnp.concatenate([grad_mixer_out[:chan_count], grad_mixer_out[chan_count : 2 * chan_count]], axis=1),
        few[second_at : second_at + 2].reshape(model_width),
        jnp.concatenate([few[:expert_total], few[expert_total:second_at]], axis=1).T,
        grad_up[None],
        jnp.sum(grad_up_bias, axis=0)[None],
        grad_down[None],
        jnp.sum(grad_down_bias, axis=0)[None],
    )


def solution(mesh):
    return jax.shard_map(
        per_device,
        mesh=mesh,
        in_specs=(
            P("dp", None),
            P("dp", None),
            P(),
            P("dp", None),
            P(),
            P(None, None, "mp"),
            P(None, "mp"),
            P("mp"),
            P("mp", None),
            P(None, "mp"),
            P("mp"),
            P(None, "mp"),
            P("mp"),
            P("mp", None),
            P(),
            P(),
            P("dp", None, "mp"),
            P("dp", "mp"),
            P("dp", "mp", None),
            P("dp", None),
        ),
        out_specs=(
            P("dp", None),
            P("dp", None),
            P(),
            P(None, None, "mp"),
            P(None, "mp"),
            P("mp"),
            P("mp", None),
            P(None, "mp"),
            P("mp"),
            P(None, "mp"),
            P("mp"),
            P("mp", None),
            P(),
            P(),
            P("dp", None, "mp"),
            P("dp", "mp"),
            P("dp", "mp", None),
            P("dp", None),
        ),
        check_vma=False,
    )
```

```python
import functools

import jax
import jax.numpy as jnp
from jax import lax
from jax.experimental import pallas as pl
from jax.experimental.pallas import tpu as pltpu
from jax.sharding import PartitionSpec as P

F32 = jnp.float32
BF16 = jnp.bfloat16
SLOT_DEV = 256
LANES = 128
SUB = 8
LOG2E = 1.4426950408889634
LN2 = 0.6931471805599453
VMEM = 48 * 2**20
norm_eps = 1e-05
MESH = pl.DeviceIdType.MESH


NN = ((1,), (0,))
NT = ((1,), (1,))
TN = ((0,), (0,))


def dot(a, b, dims):
    return lax.dot_general(a, b, (dims, ((), ())), preferred_element_type=F32)


def lane(col):
    return jnp.broadcast_to(col, (SUB, LANES))


def row(ref, n, cs):
    return jnp.broadcast_to(ref[n : n + 1, cs], (SUB, LANES))


def tiles(count):
    return [slice(ct * LANES, (ct + 1) * LANES) for ct in range(count // LANES)]


def whole(*dims):
    return pl.BlockSpec(dims, lambda i: (0,) * len(dims))


def local_scan(step_ref, in_ref, map_ref, rates_ref, out_ref, nh, half, reverse):
    places, chans = step_ref.shape[0], step_ref.shape[2]
    cols = tiles(chans)
    ns = [nh * half + n for n in range(half)]

    def body(lap, st):
        i = places - 1 - lap if reverse else lap
        st = list(st)
        m = map_ref[i]
        mm = [lane(m[:, n : n + 1]) for n in ns]
        for ct, cs in enumerate(cols):
            s = step_ref[i, :, cs]
            x = in_ref[i, :, cs]
            for n in range(half):
                k = n * len(cols) + ct
                e = jnp.exp2(s * row(rates_ref, ns[n], cs))
                st[k] = e * (st[k] + x * mm[n]) if reverse else e * st[k] + x * mm[n]
        return tuple(st)

    zero = tuple(jnp.zeros((SUB, LANES), F32) for _ in range(half * len(cols)))
    st = lax.fori_loop(0, places, body, zero, unroll=8)
    for n in range(half):
        for ct, cs in enumerate(cols):
            out_ref[ns[n], :, cs] = st[n * len(cols) + ct]


def forward_kernel(
    step_ref,
    x_ref,
    bin_ref,
    cout_ref,
    rates_ref,
    h0_ref,
    inner_ref,
    gate_ref,
    skip_ref,
    weight_ref,
    scan_ref,
    gated_ref,
    part_ref,
    hb_ref,
    hf_ref,
    st_ref,
    y_ref,
):
    places, chans = step_ref.shape[0], step_ref.shape[2]
    states, half = rates_ref.shape[0], 8
    cols = tiles(chans)

    @pl.when(pl.program_id(0) == 0)
    def _():
        st_ref[...] = h0_ref[...]

    for nh in range(states // half):
        ns = [nh * half + n for n in range(half)]

        def body(i, st):
            st = list(st)
            b = bin_ref[i]
            c = cout_ref[i]
            bb = [lane(b[:, n : n + 1]) for n in ns]
            cc = [lane(c[:, n : n + 1]) for n in ns]
            for ct, cs in enumerate(cols):
                s = step_ref[i, :, cs]
                x = x_ref[i, :, cs]
                y = y_ref[i, :, cs] if nh else jnp.zeros((SUB, LANES), F32)
                for n in range(half):
                    k = n * len(cols) + ct
                    hb_ref[i, ns[n], :, cs] = st[k].astype(hb_ref.dtype)
                    e = jnp.exp2(s * row(rates_ref, ns[n], cs))
                    st[k] = e * st[k] + x * bb[n]
                    y = y + cc[n] * st[k]
                y_ref[i, :, cs] = y
            return tuple(st)

        st = tuple(st_ref[n, :, cs] for n in ns for cs in cols)
        st = lax.fori_loop(0, places, body, st, unroll=8)
        for n in range(half):
            for ct, cs in enumerate(cols):
                st_ref[ns[n], :, cs] = st[n * len(cols) + ct]
    hf_ref[...] = st_ref[...]
    scan = y_ref[...].reshape(places * SUB, chans) + skip_ref[...] * inner_ref[...].astype(F32)
    scan_ref[...] = scan
    gate = gate_ref[...].astype(F32)
    gated = (scan * (gate * jax.nn.sigmoid(gate))).astype(BF16)
    gated_ref[...] = gated
    part_ref[...] = dot(gated, weight_ref[...], NN).astype(BF16)


def forward(step, x, bin_vals, cout, rates, h0, inner, both, skip, weight, block=16):
    places, _, chans = step.shape
    states = rates.shape[0]
    width = weight.shape[1]
    rows = places * SUB
    part = lambda size: pl.BlockSpec((block, SUB, size), lambda i: (i, 0, 0))
    flat = lambda size, col=0: pl.BlockSpec((block * SUB, size), lambda i: (i, col))
    shape = jax.ShapeDtypeStruct
    return pl.pallas_call(
        forward_kernel,
        grid=(places // block,),
        in_specs=[
            part(chans),
            part(chans),
            part(states),
            part(states),
            whole(states, chans),
            whole(states, SUB, chans),
            flat(chans),
            flat(chans, 1),
            whole(1, chans),
            whole(chans, width),
        ],
        out_specs=[
            flat(chans),
            flat(chans),
            flat(width),
            pl.BlockSpec((block, states, SUB, chans), lambda i: (i, 0, 0, 0)),
            whole(states, SUB, chans),
        ],
        out_shape=[
            shape((rows, chans), F32),
            shape((rows, chans), BF16),
            shape((rows, width), BF16),
            shape((places, states, SUB, chans), BF16),
            shape((states, SUB, chans), F32),
        ],
        scratch_shapes=[
            pltpu.VMEM((states, SUB, chans), F32),
            pltpu.VMEM((block, SUB, chans), F32),
        ],
        compiler_params=pltpu.CompilerParams(vmem_limit_bytes=VMEM),
    )(step, x, bin_vals, cout, rates, h0, inner, both, skip, weight)


def backward_kernel(
    n,
    step_ref,
    x_ref,
    gs_ref,
    past_ref,
    bin_ref,
    cout_ref,
    rates_ref,
    g0_ref,
    hf_ref,
    hb_ref,
    inner_ref,
    slope_ref,
    low_ref,
    weight_ref,
    skip_ref,
    early_ref,
    base_ref,
    proj_ref,
    given_ref,
    gin_ref,
    gout_ref,
    few_ref,
    sbias_ref,
    gst_ref,
    rt_ref,
    q_ref,
    p_ref,
    sg_ref,
    sb_ref,
    gp_ref,
    sums,
    send,
    recv,
):
    places, chans = step_ref.shape[0], step_ref.shape[2]
    states, some = rates_ref.shape[0], 4
    cols = tiles(chans)
    g, _, pair, like = dp_pairs(n)
    start, middle, end = gathering(n, sums, send, recv)

    @pl.when(pl.program_id(0) == 0)
    def _():
        greet([pair] + like)
        sums[g] = early_ref[...]
        start()

    @pl.when(pl.program_id(0) == pl.num_programs(0) // 2)
    def _():
        middle()

    @pl.when(pl.program_id(0) == 0)
    def _():
        gst_ref[...] = g0_ref[...]
        rt_ref[...] = jnp.zeros_like(rt_ref)
        given_ref[...] = jnp.zeros_like(given_ref)
        proj_ref[...] = jnp.zeros_like(proj_ref)
        sbias_ref[...] = jnp.zeros_like(sbias_ref)

    gp_ref[0] = past_ref[0]
    gp_ref[1:places] = gs_ref[0 : places - 1]

    for nq in range(states // some):
        ns = [nq * some + n for n in range(some)]
        size = some * len(cols)

        def body(lap, carry):
            i = places - 1 - lap
            st, rt = list(carry[:size]), list(carry[size:])
            b = bin_ref[i]
            c = cout_ref[i]
            bb = [lane(b[:, n : n + 1]) for n in ns]
            cc = [lane(c[:, n : n + 1]) for n in ns]
            qb, qc = [None] * some, [None] * some
            for ct, cs in enumerate(cols):
                s = step_ref[i, :, cs]
                x = x_ref[i, :, cs]
                g = gs_ref[i, :, cs]
                gp = gp_ref[i, :, cs]
                sg = sg_ref[i, :, cs] if nq else jnp.zeros((SUB, LANES), F32)
                sb = sb_ref[i, :, cs] if nq else jnp.zeros((SUB, LANES), F32)
                for n in range(some):
                    k = n * len(cols) + ct
                    rate = row(rates_ref, ns[n], cs)
                    e = jnp.exp2(s * rate)
                    h = hb_ref[i, ns[n], :, cs].astype(F32)
                    grad = st[k] + g * cc[n]
                    st[k] = e * grad
                    dg = st[k] * h
                    sg = sg + dg * rate
                    rt[k] = rt[k] + dg * s
                    sb = sb + grad * bb[n]
                    qb[n] = grad * x if ct == 0 else qb[n] + grad * x
                    qc[n] = gp * h if ct == 0 else qc[n] + gp * h
                sg_ref[i, :, cs] = sg
                sb_ref[i, :, cs] = sb
            rows = pl.ds(pl.multiple_of(i * SUB, SUB), SUB)
            for n in range(some):
                q_ref[rows, ns[n] * LANES : (ns[n] + 1) * LANES] = qb[n]
                p_ref[rows, ns[n] * LANES : (ns[n] + 1) * LANES] = qc[n]
            return tuple(st) + tuple(rt)

        at = [(ns[n], slice(None), cs) for n in range(some) for cs in cols]
        init = tuple(gst_ref[a] for a in at) + tuple(rt_ref[a] for a in at)
        out = lax.fori_loop(0, places, body, init, unroll=8)
        for j, a in enumerate(at):
            gst_ref[a] = out[j]
            rt_ref[a] = out[size + j]
    rank = low_ref.shape[1]
    wide = proj_ref.shape[1]
    dims = (states * LANES, wide)
    state = lax.broadcasted_iota(jnp.int32, dims, 0) // LANES
    column = lax.broadcasted_iota(jnp.int32, dims, 1)
    to_bin = jnp.where(column == state + rank, 1.0, 0.0).astype(BF16)
    to_cout = jnp.where(column == state + rank + states, 1.0, 0.0).astype(BF16)
    block_rows = places * SUB
    base = (pl.num_programs(0) - 1 - pl.program_id(0)) * block_rows
    here = pl.ds(pl.multiple_of(base + SUB, SUB), block_rows)
    late = pl.ds(pl.multiple_of(base, SUB), block_rows)

    @pl.when(pl.program_id(0) == 0)
    def _():
        end_rows = pl.ds(pl.multiple_of(base + block_rows, SUB), SUB)
        total_ = None
        for n_ in range(states):
            value = hf_ref[n_, :, cols[0]] * gs_ref[places - 1, :, cols[0]]
            for cs in cols[1:]:
                value = value + hf_ref[n_, :, cs] * gs_ref[places - 1, :, cs]
            term = jnp.dot(
                value.astype(BF16), to_cout[n_ * LANES : (n_ + 1) * LANES], preferred_element_type=F32
            )
            total_ = term if total_ is None else total_ + term
        proj_ref[end_rows, :] += total_

    proj_ref[late, :] += jnp.dot(p_ref[...].astype(BF16), to_cout, preferred_element_type=F32)
    flat = lambda ref: ref[...].reshape(places * SUB, chans)
    sb = flat(sb_ref)
    base_ref[...] = flat(gs_ref) * skip_ref[...] + flat(step_ref) * sb
    pre = (flat(sg_ref) * LN2 + inner_ref[...].astype(F32) * sb) * slope_ref[...]
    sbias_ref[...] += jnp.sum(pre.reshape(places, SUB, chans), axis=0)
    pre = pre.astype(BF16)
    given_ref[0:rank, :] += dot(low_ref[...], pre, TN)
    proj_ref[here, :] += dot(pre, weight_ref[...], NT) + jnp.dot(
        q_ref[...].astype(BF16), to_bin, preferred_element_type=F32
    )

    @pl.when(pl.program_id(0) == pl.num_programs(0) - 1)
    def _():
        end()
        for n_ in range(states):
            line = rank + n_
            total_ = jnp.sum(rt_ref[n_], axis=0, keepdims=True)
            given_ref[line : line + 1, :] = total_ * rates_ref[n_ : n_ + 1, :] * LN2
        line = rank + states
        given_ref[line : line + 1, :] = jnp.sum(sbias_ref[...], axis=0, keepdims=True)
        mh = gin_ref.shape[0] // n
        sh = few_ref.shape[0] // n
        for b in range(n):
            few_ref[b * sh : (b + 1) * sh, :] = sums[b, 2 * mh : 2 * mh + sh, :].astype(F32)
            gin_ref[b * mh : (b + 1) * mh, :] = sums[b, 0:mh, :].astype(F32)
            gout_ref[b * mh : (b + 1) * mh, :] = sums[b, mh : 2 * mh, :].astype(F32)


def backward(
    n, collective_id, mh, step, x, gs, bin_vals, cout, rates, g0, hf, hb, inner, slope, low, weight, skip, early, block=16
):
    places, _, chans = step.shape
    states = rates.shape[0]
    rank, wide = low.shape[1], weight.shape[0]
    extra = (rank + states + SUB) // SUB * SUB
    count = places // block
    part = lambda width: pl.BlockSpec((block, SUB, width), lambda i: (count - 1 - i, 0, 0))
    flat = lambda width: pl.BlockSpec((block * SUB, width), lambda i: (count - 1 - i, 0))
    rows = places * SUB
    tall = n * mh
    few = n * (early.shape[0] - 2 * mh)
    sems = pltpu.SemaphoreType.DMA((2, n // 2))
    return pl.pallas_call(
        functools.partial(backward_kernel, n),
        grid=(count,),
        in_specs=[
            part(chans),
            part(chans),
            part(chans),
            pl.BlockSpec((1, SUB, chans), lambda i: (jnp.maximum((count - 1 - i) * block - 1, 0), 0, 0)),
            part(states),
            part(states),
            whole(states, chans),
            whole(states, SUB, chans),
            whole(states, SUB, chans),
            pl.BlockSpec((block, states, SUB, chans), lambda i: (count - 1 - i, 0, 0, 0)),
            flat(chans),
            flat(chans),
            flat(rank),
            whole(wide, chans),
            whole(1, chans),
            whole(*early.shape),
        ],
        out_specs=[
            flat(chans),
            whole(rows + SUB, wide),
            whole(extra, chans),
            whole(tall, chans),
            whole(tall, chans),
            whole(few, chans),
        ],
        out_shape=[
            jax.ShapeDtypeStruct((rows, chans), F32),
            jax.ShapeDtypeStruct((rows + SUB, wide), F32),
            jax.ShapeDtypeStruct((extra, chans), F32),
            jax.ShapeDtypeStruct((tall, chans), F32),
            jax.ShapeDtypeStruct((tall, chans), F32),
            jax.ShapeDtypeStruct((few, chans), F32),
        ],
        scratch_shapes=[
            pltpu.VMEM((SUB, chans), F32),
            pltpu.VMEM((states, SUB, chans), F32),
            pltpu.VMEM((states, SUB, chans), F32),
            pltpu.VMEM((block * SUB, states * LANES), F32),
            pltpu.VMEM((block * SUB, states * LANES), F32),
            pltpu.VMEM((block, SUB, chans), F32),
            pltpu.VMEM((block, SUB, chans), F32),
            pltpu.VMEM((block, SUB, chans), F32),
            pltpu.VMEM((n, *early.shape), BF16),
            sems,
            sems,
        ],
        compiler_params=pltpu.CompilerParams(
            collective_id=collective_id, has_side_effects=True, vmem_limit_bytes=VMEM
        ),
    )(step, x, gs, gs, bin_vals, cout, rates, g0, hf, hb, inner, slope, low, weight, skip, early)


def mp_pair():
    j = lax.axis_index("mp")
    return j, j + 1 - 2 * (j % 2), (j + 2) % 4


def ds(start, size):
    return pl.ds(pl.multiple_of(start, size), size)


def greet(others):
    barrier = pltpu.get_barrier_semaphore()
    for other in others:
        pl.semaphore_signal(barrier, inc=1, device_id=other, device_id_type=MESH)
    pl.semaphore_wait(barrier, len(others))


def sending(src, dst, send, recv, device):
    copy = pltpu.make_async_remote_copy(
        src_ref=src, dst_ref=dst, send_sem=send, recv_sem=recv, device_id=device, device_id_type=MESH
    )
    copy.start()
    return copy


def vmem_call(kernel, out_shape, scratch, collective_id, *args, cost=0):
    space = pl.BlockSpec(memory_space=pltpu.VMEM)
    return pl.pallas_call(
        kernel,
        out_shape=out_shape,
        in_specs=[space] * len(args),
        out_specs=jax.tree.map(lambda _: space, out_shape),
        scratch_shapes=scratch,
        compiler_params=pltpu.CompilerParams(
            collective_id=collective_id, has_side_effects=True, vmem_limit_bytes=VMEM
        ),
    )(*args)


def half_turn(tile):
    return pltpu.roll(tile, SUB // 2, 0)


def send_totals(n, total_ref, all_ref, send, recv):
    g = lax.axis_index("dp")
    all_ref[0] = total_ref[...] + half_turn(total_ref[...])
    return [
        sending(all_ref.at[0], all_ref.at[k], send.at[1, k], recv.at[1, k], {"dp": (g + k) % n})
        for k in range(1, n)
    ]


def exchange_body(
    n, reverse, copies, part_ref, total_ref, rates_ref, packed_ref, all_ref, out_ref, sbuf, rbuf, send, recv
):
    g = lax.axis_index("dp")
    states, chans = rates_ref.shape
    pairs = states // 2
    upper = lax.broadcasted_iota(jnp.int32, (SUB, chans), 0) >= SUB // 2
    total = total_ref[...]
    decay = lambda m: jnp.exp2(jnp.broadcast_to(rates_ref[m : m + 1, :], (SUB, chans)) * total)

    def summary(m):
        part = part_ref[m]
        return part + decay(m) * half_turn(part)

    def packed(p):
        low, high = summary(p), summary(p + pairs)
        if reverse:
            return jnp.where(upper, half_turn(high), low)
        return jnp.where(upper, high, half_turn(low))

    for p in range(0, pairs, 2):
        sbuf[p * SUB : (p + 2) * SUB, :] = jnp.concatenate([packed(p), packed(p + 1)], axis=0).astype(BF16)
    copies = copies + [
        sending(sbuf, rbuf.at[k], send.at[0, k], recv.at[0, k], {"dp": (g + k) % n})
        for k in range(1, n)
    ]
    for copy in copies:
        copy.wait_recv()

    def one(lap, held):
        away = n - 1 - lap
        slot = n - away if reverse else away
        use = (g + away < n) if reverse else (away <= g)
        steps = all_ref[slot]
        new = []
        for p in range(0, pairs, 2):
            got = rbuf[slot, p * SUB : (p + 2) * SUB, :].astype(F32)
            for q in (p, p + 1):
                fall = jnp.exp2(packed_ref[q] * steps)
                value = fall * held[q] + got[(q - p) * SUB : (q - p + 1) * SUB]
                new.append(jnp.where(use, value, held[q]))
        return tuple(new)

    zero = tuple(jnp.zeros((SUB, chans), F32) for _ in range(pairs))
    held = lax.fori_loop(0, n - 1, one, zero)
    for m in range(states):
        state = held[m % pairs]
        if (m >= pairs) != reverse:
            state = half_turn(state)
        later = half_turn(decay(m) * state + part_ref[m])
        out_ref[m] = jnp.where(upper, state, later) if reverse else jnp.where(upper, later, state)
    for copy in copies:
        copy.wait_send()


def packed_rates(rates):
    states, chans = rates.shape
    pairs = states // 2
    wide = lambda r: jnp.broadcast_to(r[:, None, :], (pairs, SUB // 2, chans))
    return jnp.concatenate([wide(rates[:pairs]), wide(rates[pairs:])], axis=1)


def enter_forward_kernel(
    n, proj_ref, weight_ref, bias_ref, inner_ref, valid_ref, rates_ref, packed_ref,
    step_ref, drive_ref, slope_ref, bin_ref, cout_ref, low_ref, total_ref, h0_ref, all_ref,
    part, sbuf, rbuf, send, recv,
):
    places, _, chans = step_ref.shape
    states = rates_ref.shape[0]
    rank = weight_ref.shape[0]
    g = lax.axis_index("dp")
    greet([{"dp": (g + k) % n} for k in range(1, n)])
    size = 256
    total_ref[...] = jnp.zeros_like(total_ref)

    def block(b, _):
        at = ds(b * size, size)
        here = pl.ds(pl.multiple_of(b * (size // SUB), size // SUB), size // SUB)
        by_place = lambda v: v.reshape(size // SUB, SUB, v.shape[1])
        proj = proj_ref[at, :]
        low = proj[:, 0:rank]
        high = low.astype(BF16)
        rest = (low - high.astype(F32)).astype(BF16)
        low_ref[at, :] = high
        pre = dot(high, weight_ref[...], NN) + dot(rest, weight_ref[...], NN) + bias_ref[...]
        valid = valid_ref[at, :]
        steps = valid * (jnp.maximum(pre, 0.0) + jnp.log1p(jnp.exp(-jnp.abs(pre))))
        slope_ref[at, :] = valid * jax.nn.sigmoid(pre)
        step_ref[here] = by_place(steps)
        drive_ref[here] = by_place(steps * inner_ref[at, :].astype(F32))
        total_ref[...] += jnp.sum(by_place(steps), axis=0)
        bin_ref[here] = by_place(proj[:, rank : rank + states])
        cout_ref[here] = by_place(proj[:, rank + states : rank + 2 * states])
        return 0

    lax.fori_loop(0, places * SUB // size, block, 0)
    copies = send_totals(n, total_ref, all_ref, send, recv)
    half = 8
    for nh in range(states // half):
        local_scan(step_ref, drive_ref, bin_ref, rates_ref, part, nh, half, False)
    exchange_body(n, False, copies, part, total_ref, rates_ref, packed_ref, all_ref, h0_ref, sbuf, rbuf, send, recv)


def enter_forward(n, collective_id, proj, weight, bias, inner, valid, rates):
    rows, chans = inner.shape
    states = rates.shape[0]
    rank = weight.shape[0]
    shape = jax.ShapeDtypeStruct
    places = rows // SUB
    entering = shape((states, SUB, chans), F32)
    sems = pltpu.SemaphoreType.DMA((2, n))
    return vmem_call(
        functools.partial(enter_forward_kernel, n),
        [
            shape((places, SUB, chans), F32),
            shape((places, SUB, chans), F32),
            shape((rows, chans), F32),
            shape((places, SUB, states), F32),
            shape((places, SUB, states), F32),
            shape((rows, rank), BF16),
            shape((SUB, chans), F32),
            entering,
            shape((n, SUB, chans), F32),
        ],
        [
            pltpu.VMEM((states, SUB, chans), F32),
            pltpu.VMEM((states * SUB // 2, chans), BF16),
            pltpu.VMEM((n, states * SUB // 2, chans), BF16),
            sems,
            sems,
        ],
        collective_id, proj, weight, bias, inner, valid, rates, packed_rates(rates),
    )


def dp_pairs(n):
    g = lax.axis_index("dp")
    odd, z, m = g % 2, g // 2, n // 2
    return g, odd, {"dp": g + 1 - 2 * odd}, [{"dp": 2 * ((z + k) % m) + odd} for k in range(1, m)]


def gathering(n, sums, send, recv):
    g, odd, pair, like = dp_pairs(n)
    z, m = g // 2, n // 2

    def copy(kind, k, b, to):
        return pltpu.make_async_remote_copy(
            src_ref=sums.at[b],
            dst_ref=sums.at[b],
            send_sem=send.at[kind, k],
            recv_sem=recv.at[kind, k],
            device_id=to,
            device_id_type=MESH,
        )

    third = lambda k: copy(0, k, g, like[k])
    fourth = lambda k: copy(1, k, 2 * ((z + m - k) % m) + odd, pair)

    def start():
        for k in range(m - 1):
            third(k).start()
        fourth(0).start()

    def middle():
        for k in range(m - 1):
            third(k).wait_recv()
            fourth(k + 1).start()

    def end():
        for k in range(m):
            fourth(k).wait_recv()
        for k in range(m - 1):
            third(k).wait_send()
        for k in range(m):
            fourth(k).wait_send()

    return start, middle, end


def enter_backward_kernel(
    n, step_ref, gs_ref, cout_ref, total_ref, rates_ref, packed_ref, all_ref, blocks_ref,
    g0_ref, own_ref, part, sbuf, rbuf, pa, ps, pc, send, recv, pair_send, pair_recv,
):
    states = rates_ref.shape[0]
    g, odd, pair, like = dp_pairs(n)
    z, m = g // 2, n // 2
    greet([{"dp": (g + k) % n} for k in range(1, n)])
    order = [(z + k) % m for k in range(1, m)] + [z]
    first = [
        sending(blocks_ref.at[2 * order[k] + 1 - odd], pa.at[k], pair_send.at[0, k], pair_recv.at[0, k], pair)
        for k in range(m)
    ]
    half = 8
    second = []
    for nh in range(states // half):
        local_scan(step_ref, gs_ref, cout_ref, rates_ref, part, nh, half, True)
        if nh == 0:
            few = range(0, m // 2)
        else:
            few = range(m // 2, m)
        for k in few:
            first[k].wait_recv()
            ps[k] = (blocks_ref[2 * order[k] + odd].astype(F32) + pa[k].astype(F32)).astype(BF16)
            if k < m - 1:
                second.append(sending(ps.at[k], pc.at[k], pair_send.at[1, k], pair_recv.at[1, k], like[k]))
    exchange_body(n, True, [], part, total_ref, rates_ref, packed_ref, all_ref, g0_ref, sbuf, rbuf, send, recv)
    value = ps[m - 1].astype(F32)
    for copy in second:
        copy.wait_recv()
    for k in range(m - 1):
        value = value + pc[k].astype(F32)
    own_ref[...] = value.astype(BF16)
    for copy in first + second:
        copy.wait_send()


def enter_backward(n, collective_id, step, gs, cout, total, rates, totals, blocks):
    _, _, chans = step.shape
    states = rates.shape[0]
    shape = jax.ShapeDtypeStruct
    m = n // 2
    sems = pltpu.SemaphoreType.DMA((2, n))
    some = pltpu.VMEM((m, *blocks.shape[1:]), BF16)
    return vmem_call(
        functools.partial(enter_backward_kernel, n),
        [shape((states, SUB, chans), F32), shape(blocks.shape[1:], BF16)],
        [
            pltpu.VMEM((states, SUB, chans), F32),
            pltpu.VMEM((states * SUB // 2, chans), BF16),
            pltpu.VMEM((n, states * SUB // 2, chans), BF16),
            some,
            some,
            some,
            sems,
            sems,
            sems,
            sems,
        ],
        collective_id, step, gs, cout, total, rates, packed_rates(rates), totals, blocks,
    )


def half_pick(ids, slots):
    iota = lax.broadcasted_iota(jnp.int32, (ids.shape[0], slots), 1)
    return jnp.where(iota == ids, 1.0, 0.0).astype(BF16)


def dispatching(n, x_ref, out_ref, send, recv, local):
    g = lax.axis_index("dp")
    j, near, _ = mp_pair()
    hc = x_ref.shape[2]
    cols = ds((j % 2) * hc, hc)

    def leave(k):
        return pltpu.make_async_remote_copy(
            src_ref=x_ref.at[(g + k) % n],
            dst_ref=out_ref.at[g, :, cols],
            send_sem=send.at[0, k],
            recv_sem=recv.at[0, k],
            device_id={"dp": (g + k) % n},
            device_id_type=MESH,
        )

    def share(k):
        place = out_ref.at[(g + n - k) % n, :, cols]
        return pltpu.make_async_remote_copy(
            src_ref=place,
            dst_ref=place,
            send_sem=send.at[1, k],
            recv_sem=recv.at[1, k],
            device_id={"mp": near},
            device_id_type=MESH,
        )

    own = pltpu.make_async_copy(x_ref.at[g], out_ref.at[g, :, cols], local)

    def start():
        own.start()
        for k in range(1, n):
            leave(k).start()

    def middle():
        for k in range(n):
            if k:
                leave(k).wait_recv()
            else:
                own.wait()
            share(k).start()

    def end():
        for k in range(n):
            share(k).wait_recv()
        for k in range(n):
            if k:
                leave(k).wait_send()
            share(k).wait_send()

    return start, middle, end


def arrange(cuts, in_ref, tile_ref):
    seqs, chunks, places = cuts
    for ct in range(tile_ref.shape[0]):
        for q in range(seqs):
            for k in range(chunks):
                start = (q * chunks + k) * places
                value = in_ref[start : start + places, ct * LANES : (ct + 1) * LANES]
                tile_ref[ct, pl.ds(k * seqs + q, places, stride=SUB), :] = value.astype(F32)


def front_kernel(
    n,
    cuts,
    capacity,
    tokens_ref,
    cot_ref,
    routes_ref,
    lengths_ref,
    gain_ref,
    weight_ref,
    taps_ref,
    bias_ref,
    select_ref,
    tok_ref,
    cot_low_ref,
    normed_ref,
    both_ref,
    pre_ref,
    inner_ref,
    lead_ref,
    proj_ref,
    rows_ref,
    slot_ref,
    half_ref,
    valid_ref,
    hot_ref,
    tile_s,
    ext_s,
    live_s,
    quarter,
    got,
    part_s,
    ra,
    sb,
    rb,
    send,
    recv,
    dsend,
    drecv,
    local,
):
    seqs, chunks, places = cuts
    g = lax.axis_index("dp")
    j, near, far = mp_pair()
    y, c = j // 2, j % 2
    near, far = {"mp": near}, {"mp": far}
    rows, width = tok_ref.shape
    chans = inner_ref.shape[1]
    kernel = taps_ref.shape[0]
    edge = (kernel - 1) * SUB
    slot_dev = chunks * places
    experts_all = hot_ref.shape[1]
    hr, hc = rows_ref.shape[1], width // 2
    size = 256
    greet([near, far] + [{"dp": (g + k) % n} for k in range(1, n)])

    arrange(cuts, tokens_ref, tile_s)

    def first(b, _):
        at = ds(b * size, size)
        tok = jnp.concatenate([tile_s[ct, at, :] for ct in range(width // LANES)], axis=1)
        tok_ref[at, :] = tok.astype(BF16)
        inverse = lax.rsqrt(jnp.mean(tok * tok, axis=1, keepdims=True) + norm_eps)
        normed = (tok * inverse * gain_ref[...]).astype(BF16)
        normed_ref[at, :] = normed
        both = dot(normed, weight_ref[...], NN).astype(BF16)
        both_ref[at, :] = both
        ext_s[pl.ds(pl.multiple_of(b * size + edge, SUB), size), :] = both[:, 0:chans].astype(F32)
        return 0

    lax.fori_loop(0, rows // size, first, 0)
    ends = sending(
        both_ref.at[rows - 32 : rows, 0:chans], got, send.at[3, 0], recv.at[3, 0], {"dp": (g + 1) % n}
    )

    at_row = lax.broadcasted_iota(jnp.int32, (rows, 1), 0)
    sub = at_row % SUB
    seq = sub % seqs
    local_place = (sub // seqs) * places + at_row // SUB
    limit = jnp.zeros((rows, 1), jnp.int32)
    for q in range(seqs):
        limit = jnp.where(seq == q, lengths_ref[0:1, q : q + 1], limit)
    valid = jnp.where(g * slot_dev + local_place < limit, 1.0, 0.0)
    valid_ref[...] = valid
    route = routes_ref[...]
    hot = jnp.where(lax.broadcasted_iota(jnp.int32, (rows, experts_all), 1) == route, 1.0, 0.0)
    hot_ref[...] = hot
    live_s[...] = hot * valid
    col = lax.broadcasted_iota(jnp.int32, (1, rows), 1)
    col_sub = col % SUB
    original = (col_sub % seqs) * slot_dev + (col_sub // seqs) * places + col // SUB
    room = 2 * hr

    def position(b, _):
        at = ds(b * size, size)
        here = b * size + lax.broadcasted_iota(jnp.int32, (size, 1), 0)
        here_sub = here % SUB
        mine = (here_sub % seqs) * slot_dev + (here_sub // seqs) * places + here // SUB
        before = jnp.where(original < mine, 1.0, 0.0).astype(BF16)
        live = live_s[at, :]
        earlier = dot(before, live_s[...].astype(BF16), NN)
        pos = jnp.sum(earlier * live, axis=1, keepdims=True)
        kept = jnp.where(pos < capacity, jnp.sum(live, axis=1, keepdims=True), 0.0) > 0.5
        pos = pos.astype(jnp.int32)
        to = routes_ref[at, :]
        slot_ref[at, :] = jnp.where(kept, to * room + pos, -1)
        lower = pos - y * hr
        inside = jnp.where(lower >= 0, 1, 0) * jnp.where(lower < hr, 1, 0)
        half_ref[at, :] = jnp.where(kept, jnp.where(inside > 0, to * hr + lower, -1), -1)
        return 0

    lax.fori_loop(0, rows // size, position, 0)

    ends.wait_recv()
    upper = lax.broadcasted_iota(jnp.int32, (SUB, chans), 0) >= SUB // 2
    some = jnp.where(g > 0, 1.0, 0.0)
    tails = got[...].astype(F32) * some
    for k in range(kernel - 1):
        at = slice(k * SUB, (k + 1) * SUB)
        tail = ext_s[rows + k * SUB : rows + (k + 1) * SUB, :]
        other_tail = tails[32 - edge + k * SUB : 32 - edge + (k + 1) * SUB, :]
        lead = half_turn(jnp.where(upper, other_tail, tail))
        ext_s[at, :] = lead
        lead_ref[at, :] = lead

    half = rows // 2
    count = half // size
    own = c * half
    other = (1 - c) * half

    def conv(start):
        at = ds(start, size)
        pre = jnp.broadcast_to(bias_ref[...], (size, chans))
        for k in range(kernel):
            past = ext_s[pl.ds(pl.multiple_of(start + k * SUB, SUB), size), :]
            pre = pre + taps_ref[k : k + 1, :] * past
        pre_ref[at, :] = pre
        inner = (pre * jax.nn.sigmoid(pre)).astype(BF16)
        inner_ref[at, :] = inner
        part_s[at, :] = dot(inner, select_ref[...], NN)

    one, two, three = [], [], []
    for k in range(count):
        conv(other + k * size)
        at = ds(other + k * size, size)
        one.append(sending(part_s.at[at], ra.at[k], send.at[0, k], recv.at[0, k], near))
    for k in range(count):
        conv(own + k * size)
        one[k].wait_recv()
        sb[k] = part_s[ds(own + k * size, size), :] + ra[k]
        two.append(sending(sb.at[k], rb.at[k], send.at[1, k], recv.at[1, k], far))

    arrange(cuts, cot_ref, tile_s)

    def second(b, _):
        at = ds(b * size, size)
        cot = jnp.concatenate([tile_s[ct, at, :] for ct in range(width // LANES)], axis=1)
        cot_low_ref[at, :] = cot.astype(BF16)
        return 0

    lax.fori_loop(0, rows // size, second, 0)
    pick = half_pick(half_ref[...], n * hr)
    sent = dot(pick, cot_low_ref[:, ds(c * hc, hc)], TN).astype(BF16)
    quarter[...] = sent.reshape(n, hr, hc)
    start, middle, end = dispatching(n, quarter, rows_ref, dsend, drecv, local)
    start()
    for k in range(count):
        two[k].wait_recv()
        at = ds(own + k * size, size)
        proj_ref[at, :] = sb[k] + rb[k]
        three.append(sending(proj_ref.at[at], proj_ref.at[at], send.at[2, k], recv.at[2, k], near))
    for copy in three:
        copy.wait_recv()
    middle()
    end()
    for copy in [ends] + one + two + three:
        copy.wait_send()


def front(n, collective_id, cuts, capacity, hr, experts_all, *args):
    tokens, taps, select = args[0], args[6], args[8]
    rows, width = tokens.shape
    kernel, chans = taps.shape
    edge = (kernel - 1) * SUB
    wide = select.shape[1]
    count = rows // 512
    shape = jax.ShapeDtypeStruct
    sems = pltpu.SemaphoreType.DMA((4, count))
    dsems = pltpu.SemaphoreType.DMA((2, n))
    sums = pltpu.VMEM((count, 256, wide), F32)
    return vmem_call(
        functools.partial(front_kernel, n, cuts, capacity),
        [
            shape((rows, width), BF16),
            shape((rows, width), BF16),
            shape((rows, width), BF16),
            shape((rows, 2 * chans), BF16),
            shape((rows, chans), F32),
            shape((rows, chans), BF16),
            shape((edge, chans), F32),
            shape((rows, wide), F32),
            shape((n, hr, width), BF16),
            shape((rows, 1), jnp.int32),
            shape((rows, 1), jnp.int32),
            shape((rows, 1), F32),
            shape((rows, experts_all), F32),
        ],
        [
            pltpu.VMEM((width // LANES, rows, LANES), F32),
            pltpu.VMEM((rows + edge, chans), F32),
            pltpu.VMEM((rows, experts_all), F32),
            pltpu.VMEM((n, hr, width // 2), BF16),
            pltpu.VMEM((32, chans), BF16),
            pltpu.VMEM((rows, wide), F32),
            sums,
            sums,
            sums,
            sems,
            sems,
            dsems,
            dsems,
            pltpu.SemaphoreType.DMA,
        ],
        collective_id, *args,
    )


def middle_kernel(
    n,
    count,
    part_ref,
    tok_ref,
    valid_ref,
    gain_ref,
    half_ref,
    resid_ref,
    rows_ref,
    sum_s,
    normed_s,
    quarter,
    ra,
    sb,
    rb,
    send,
    recv,
    dsend,
    drecv,
    local,
):
    g = lax.axis_index("dp")
    j, near, far = mp_pair()
    c = j % 2
    near, far = {"mp": near}, {"mp": far}
    rows, width = tok_ref.shape
    hr, hc = rows_ref.shape[1], width // 2
    half = rows // 2
    size = half // count
    own, other = c * half, (1 - c) * half
    greet([near, far] + [{"dp": (g + k) % n} for k in range(1, n)])
    one = [
        sending(part_ref.at[ds(other + k * size, size)], ra.at[k], send.at[0, k], recv.at[0, k], near)
        for k in range(count)
    ]
    two, three = [], []
    for k in range(count):
        one[k].wait_recv()
        mine = part_ref[ds(own + k * size, size), :].astype(F32)
        sb[k] = (mine + ra[k].astype(F32)).astype(BF16)
        two.append(sending(sb.at[k], rb.at[k], send.at[1, k], recv.at[1, k], far))

    def norm(start):
        at = ds(start, size)
        resid = tok_ref[at, :].astype(F32) + valid_ref[at, :] * sum_s[at, :].astype(F32)
        resid_ref[at, :] = resid
        inverse = lax.rsqrt(jnp.mean(resid * resid, axis=1, keepdims=True) + norm_eps)
        normed_s[at, :] = (resid * inverse * gain_ref[...]).astype(BF16)

    for k in range(count):
        two[k].wait_recv()
        at = ds(own + k * size, size)
        sum_s[at, :] = (sb[k].astype(F32) + rb[k].astype(F32)).astype(BF16)
        three.append(sending(sum_s.at[at], sum_s.at[at], send.at[2, k], recv.at[2, k], near))
        norm(own + k * size)
    for k in range(count):
        three[k].wait_recv()
        norm(other + k * size)
    pick = half_pick(half_ref[...], n * hr)
    sent = dot(pick, normed_s[:, ds(c * hc, hc)], TN).astype(BF16)
    quarter[...] = sent.reshape(n, hr, hc)
    start, middle, end = dispatching(n, quarter, rows_ref, dsend, drecv, local)
    start()
    middle()
    end()
    for copy in one + two + three:
        copy.wait_send()


def mixer_to_experts(n, collective_id, hr, part, tok, valid, gain, half_slots, count=4):
    rows, width = tok.shape
    shape = jax.ShapeDtypeStruct
    sems = pltpu.SemaphoreType.DMA((3, count))
    dsems = pltpu.SemaphoreType.DMA((2, n))
    slots = pltpu.VMEM((count, rows // 2 // count, width), BF16)
    whole_rows = pltpu.VMEM((rows, width), BF16)
    return vmem_call(
        functools.partial(middle_kernel, n, count),
        [shape((rows, width), F32), shape((n, hr, width), BF16)],
        [
            whole_rows,
            whole_rows,
            pltpu.VMEM((n, hr, width // 2), BF16),
            slots,
            slots,
            slots,
            sems,
            sems,
            dsems,
            dsems,
            pltpu.SemaphoreType.DMA,
        ],
        collective_id, part, tok, valid, gain, half_slots,
    )


def expert_kernel(
    n,
    rows_ref,
    cot_ref,
    up_ref,
    ub_ref,
    down_ref,
    other_ref,
    ub2_ref,
    db_ref,
    router_ref,
    hot_ref,
    out_ref,
    gown_ref,
    gother_ref,
    gub_ref,
    gdb_ref,
    part,
    hid,
    slope,
    pre,
    grad,
    ra,
    qb,
    send,
    recv,
):
    g = lax.axis_index("dp")
    j, near, far = mp_pair()
    near, far = {"mp": near}, {"mp": far}
    y, c = j // 2, j % 2
    hr, width = rows_ref.shape[1], rows_ref.shape[2]
    hidden = up_ref.shape[1]
    hc = width // 2
    half, total, window = n // 2, 2 * n, min(n, 6)
    size = half * hr
    greet([near, far] + [{"dp": (g + k) % n} for k in range(1, n)])
    mine, theirs = ds(c * hc, hc), ds((1 - c) * hc, hc)
    up, down = ds(y * hr, hr), ds((1 - y) * hr, hr)
    gub_ref[...] = jnp.zeros_like(gub_ref)
    gdb_ref[...] = jnp.zeros_like(gdb_ref)
    folded = lambda v: jnp.sum(v.reshape(v.shape[0] // SUB, SUB, v.shape[1]), axis=0)
    ups = (up_ref, other_ref.at[0:width])
    downs = (down_ref, other_ref.at[width : width + hidden])
    biases = (ub_ref, ub2_ref)

    def copy(kind, there, here, src, dst, to):
        return pltpu.make_async_remote_copy(
            src_ref=src,
            dst_ref=dst,
            send_sem=send.at[kind, here],
            recv_sem=recv.at[kind, there],
            device_id=to,
            device_id_type=MESH,
        )

    def target(t):
        return (g + t) % n

    def source(t):
        return (g + 2 * n - t) % n

    def near_copy(t):
        at = part.at[t // n, target(t)]
        return copy(0, t, t, at.at[:, theirs], ra.at[t], near)

    def back_copy(t, arriving):
        a = t // n * n
        there = a + source(t) if arriving else a + g
        return copy(1, there, t, qb.at[t], out_ref.at[t // n, g, up, mine], {"dp": target(t)})

    def place(t, rows):
        return out_ref.at[t // n, source(t), rows, mine]

    def pass_far(t):
        return copy(2, t, t, place(t, up), place(t, up), far)

    def pass_near(t):
        return copy(3, t, t, place(t, up), place(t, up), near)

    def pass_on(t):
        return copy(4, t, t, place(t, down), place(t, down), near)

    def wide(ref, base):
        return ref[pl.ds(base, half)].reshape(size, ref.shape[2])

    def ahead(base):
        rows = wide(rows_ref, base)
        total_part = None
        for k in range(2):
            v = dot(rows, ups[k][...], NN) + biases[k][...]
            sq = v * v
            th = jnp.tanh(v * (GELU_A + GELU_A * GELU_B * sq))
            at = pl.ds(pl.multiple_of(base * hr, size), size)
            act = (0.5 * v * (1.0 + th)).astype(BF16)
            hid[k, at, :] = act
            slope[k, at, :] = 0.5 * (1.0 + th) + 0.5 * v * (1.0 - th * th) * (
                GELU_A + 3.0 * GELU_A * GELU_B * sq
            )
            term = dot(act, downs[k][...], NN)
            total_part = term if k == 0 else total_part + term
        part[0, pl.ds(base, half)] = total_part.astype(BF16).reshape(half, hr, width)

    def behind(base):
        at = pl.ds(pl.multiple_of(base * hr, size), size)
        probs = jax.nn.softmax(dot(wide(rows_ref, base), router_ref[...], NN), axis=-1)
        chosen = jnp.sum(probs * hot_ref[...], axis=1, keepdims=True)
        scaled = (chosen * wide(cot_ref, base).astype(F32)).astype(BF16)
        grad[at, :] = scaled
        gdb_ref[...] += folded(scaled.astype(F32))
        total_part = None
        for k in range(2):
            value = (dot(scaled, downs[k][...], NT) * slope[k, at, :]).astype(BF16)
            pre[k, at, :] = value
            gub_ref[k] += folded(value.astype(F32))
            term = dot(value, ups[k][...], NT)
            total_part = term if k == 0 else total_part + term
        part[1, pl.ds(base, half)] = total_part.astype(BF16).reshape(half, hr, width)

    def pair_sum(t):
        near_copy(t).wait_recv()
        value = part[t // n, target(t), :, mine].astype(F32) + ra[t].astype(F32)
        qb[t] = (value + jnp.where(t < n, 1.0, 0.0) * db_ref[:, mine]).astype(BF16)

        @pl.when(t % n == 0)
        def _():
            out_ref[t // n, g, up, mine] = qb[t]

    def leave(t):
        @pl.when(t % n != 0)
        def _():
            back_copy(t, False).start()

    def arrived(t):
        @pl.when(t % n != 0)
        def _():
            back_copy(t, True).wait_recv()

        pass_far(t).start()
        pass_near(t).start()

    def passed(t):
        pass_far(t).wait_recv()
        pass_on(t).start()

    cut = 256
    pieces = width // cut

    def weights(q):
        at = ds(q % pieces * cut, cut)
        for kind in range(2):
            for k in range(2):

                @pl.when(q // pieces == 2 * kind + 1 - k)
                def _(kind=kind, k=k):
                    if kind == 0:
                        value = dot(hid[k], grad[:, at], TN)
                    else:
                        value = dot(rows_ref[...].reshape(n * hr, width), pre[k, :, at], TN)
                    if k == 0:
                        gown_ref[kind, :, at] = value
                    else:
                        gother_ref[kind, :, at] = value.astype(BF16)

    def each(act, start, count):
        def one(i, _):
            act(start + i)
            return 0

        lax.fori_loop(0, count, one, 0)

    for kind, work in enumerate((ahead, behind)):
        work(0)
        work(half)
        each(lambda t: near_copy(t).start(), kind * n, n)
        each(pair_sum, kind * n, n)
        if kind == 0:
            each(leave, 0, window)

    lag = 2

    def step(i, _):
        @pl.when(i < 4 * pieces)
        def _():
            weights(i)

        @pl.when(i + window < total)
        def _():
            leave(i + window)

        @pl.when(i < total)
        def _():
            arrived(i)

        @pl.when((i >= lag) & (i < total + lag))
        def _():
            passed(i - lag)

        return 0

    lax.fori_loop(0, max(4 * pieces, total + lag), step, 0)

    def finish_one(t, _):
        pass_near(t).wait_recv()
        pass_on(t).wait_recv()
        for made in (near_copy, pass_far, pass_near, pass_on):
            made(t).wait_send()

        @pl.when(t % n != 0)
        def _():
            back_copy(t, False).wait_send()

        return 0

    lax.fori_loop(0, total, finish_one, 0)


GELU_A = 0.7978845608028654
GELU_B = 0.044715


def experts(n, collective_id, rows, cot, up, up_bias, down, other, other_bias, down_bias, router, hot):
    _, hr, width = rows.shape
    hidden = up.shape[1]
    shape = jax.ShapeDtypeStruct
    sems = pltpu.SemaphoreType.DMA((5, 2 * n))
    quarters = pltpu.VMEM((2 * n, hr, width // 2), BF16)
    return vmem_call(
        functools.partial(expert_kernel, n),
        [
            shape((2, n, 2 * hr, width), BF16),
            shape((2, width, hidden), F32),
            shape((2, width, hidden), BF16),
            shape((2, SUB, hidden), F32),
            shape((SUB, width), F32),
        ],
        [
            pltpu.VMEM((2, n, hr, width), BF16),
            pltpu.VMEM((2, n * hr, hidden), BF16),
            pltpu.VMEM((2, n * hr, hidden), F32),
            pltpu.VMEM((2, n * hr, hidden), BF16),
            pltpu.VMEM((n * hr, width), BF16),
            quarters,
            quarters,
            sems,
            sems,
        ],
        collective_id, rows, cot, up, up_bias, down, other, other_bias, down_bias, router, hot,
    )


def finish_kernel(
    n,
    count,
    cuts,
    layout,
    part_ref,
    select_ref,
    inner_ref,
    base_ref,
    pre_ref,
    both_ref,
    lead_ref,
    gate_ref,
    normed_ref,
    weight_ref,
    taps_ref,
    given_ref,
    tok_ref,
    resid_ref,
    gain_ref,
    grad_ref,
    gin_ref,
    small_ref,
    first_ref,
    conv_s,
    ext_s,
    both_s,
    got,
    part_s,
    sum_s,
    ra,
    sb,
    rb,
    blocks,
    pa,
    ps,
    pc,
    outs,
    tile_s,
    firsts,
    rows_s,
    fold_s,
    low_s,
    proj_ref,
    qa,
    qs,
    qr,
    send,
    recv,
):
    mh, sh = layout
    g = lax.axis_index("dp")
    j, near, far = mp_pair()
    near, far = {"mp": near}, {"mp": far}
    odd, z, m = g % 2, g // 2, n // 2
    pair = {"dp": g + 1 - 2 * odd}
    like = [{"dp": 2 * ((z + k) % m) + odd} for k in range(1, m)]
    others = [{"dp": (g + k) % n} for k in range(1, n)]
    greet([near, far] + others)
    rows, chans = inner_ref.shape
    width = normed_ref.shape[1]
    kernel = taps_ref.shape[0]
    edge = (kernel - 1) * SUB
    block = 256
    half = rows // 2
    size = half // count
    own = (j % 2) * half
    other = (1 - j % 2) * half

    def lower(b, _):
        value = part_ref[pl.ds(pl.multiple_of(b * block + SUB, SUB), block), :]
        low_s[ds(b * block, block), :] = value.astype(BF16)
        return 0

    lax.fori_loop(0, rows // block, lower, 0)
    pieces = half // block
    q_one, q_two, q_three = [], [], []
    for k in range(pieces):
        at = ds(other + k * block, block)
        q_one.append(sending(low_s.at[at], qa.at[k], send.at[9, k], recv.at[9, k], near))
    for k in range(pieces):
        q_one[k].wait_recv()
        qs[k] = (low_s[ds(own + k * block, block), :].astype(F32) + qa[k].astype(F32)).astype(BF16)
        q_two.append(sending(qs.at[k], qr.at[k], send.at[10, k], recv.at[10, k], far))
    ext_s[0:edge, :] = lead_ref[...]

    def past_rows(b, _):
        at = ds(b * block, block)
        ext_s[pl.ds(pl.multiple_of(b * block + edge, SUB), block), :] = both_ref[at, 0:chans].astype(F32)
        return 0

    lax.fori_loop(0, rows // block, past_rows, 0)
    for k in range(pieces):
        q_two[k].wait_recv()
        at = ds(own + k * block, block)
        proj_ref[at, :] = (qs[k].astype(F32) + qr[k].astype(F32)).astype(BF16)
        q_three.append(sending(proj_ref.at[at], proj_ref.at[at], send.at[11, k], recv.at[11, k], near))
    for copy in q_three:
        copy.wait_recv()

    def conv_block(b):
        at = ds(b * block, block)
        grad = base_ref[at, :] + dot(proj_ref[at, :], select_ref[...], NT)
        conv_s[at, :] = grad * silu_slope(pre_ref[at, :])

    conv_block(0)
    head = sending(conv_s.at[0:edge], got, send.at[8, 0], recv.at[8, 0], {"dp": (g + n - 1) % n})

    def rest(b, _):
        conv_block(b)
        return 0

    lax.fori_loop(1, rows // block, rest, 0)
    given = given_ref.shape[0]
    selects = select_ref.shape[1]
    rest_at = given + selects
    fold_s[0:given, :] = given_ref[...]
    fold_s[given:rest_at, :] = dot(proj_ref[...], inner_ref[...], TN)
    folded = lambda v: jnp.sum(v.reshape(block // SUB, SUB, chans), axis=0)

    def taps(b, sums):
        grad = conv_s[ds(b * block, block), :]
        past = [ext_s[pl.ds(pl.multiple_of(b * block + k * SUB, SUB), block), :] for k in range(kernel)]
        return tuple(v + folded(grad * p) for v, p in zip(sums, past)) + (sums[kernel] + folded(grad),)

    zero = tuple(jnp.zeros((SUB, chans), F32) for _ in range(kernel + 1))
    sums = lax.fori_loop(0, rows // block, taps, zero)
    for k in range(kernel + 1):
        fold_s[rest_at + k : rest_at + k + 1, :] = jnp.sum(sums[k], axis=0, keepdims=True)
    head.wait_recv()
    upper = lax.broadcasted_iota(jnp.int32, (SUB, chans), 0) >= SUB // 2
    some = jnp.where(g < n - 1, 1.0, 0.0)
    for k in range(kernel - 1):
        at = slice(k * SUB, (k + 1) * SUB)
        tail = half_turn(jnp.where(upper, conv_s[at, :], got[at, :] * some))
        conv_s[rows + k * SUB : rows + (k + 1) * SUB, :] = tail

    def back(b, _):
        at = ds(b * block, block)
        total = jnp.zeros((block, chans), F32)
        for k in range(kernel):
            later = conv_s[pl.ds(pl.multiple_of(b * block + (kernel - 1 - k) * SUB, SUB), block), :]
            total = total + taps_ref[k : k + 1, :] * later
        both_s[at, 0:chans] = total.astype(BF16)
        both_s[at, chans : 2 * chans] = gate_ref[at, :]
        return 0

    lax.fori_loop(0, rows // block, back, 0)

    rows_s[0:width, :] = dot(normed_ref[...], both_s[:, 0:chans], TN)
    for b in range(n):
        blocks[b, 0:mh, :] = rows_s[b * mh : (b + 1) * mh, :].astype(BF16)
        blocks[b, mh : mh + sh, :] = fold_s[b * sh : (b + 1) * sh, :].astype(BF16)
    order = [(z + k) % m for k in range(1, m)] + [z]
    first = [
        sending(blocks.at[2 * order[k] + 1 - odd], pa.at[k], send.at[3, k], recv.at[3, k], pair)
        for k in range(m)
    ]
    one, two, three, second = [], [], [], []

    def input_rows(start):
        at = ds(start, size)
        part_s[at, :] = dot(both_s[at, :], weight_ref[...], NT).astype(BF16)

    for k in range(count):
        input_rows(other + k * size)
        at = ds(other + k * size, size)
        one.append(sending(part_s.at[at], ra.at[k], send.at[0, k], recv.at[0, k], near))
    for k in range(count):
        input_rows(own + k * size)
        one[k].wait_recv()
        mine = part_s[ds(own + k * size, size), :].astype(F32)
        sb[k] = (mine + ra[k].astype(F32)).astype(BF16)
        two.append(sending(sb.at[k], rb.at[k], send.at[1, k], recv.at[1, k], far))
    for k in range(m):
        first[k].wait_recv()
        ps[k] = (blocks[2 * order[k] + odd].astype(F32) + pa[k].astype(F32)).astype(BF16)
        if k < m - 1:
            second.append(sending(ps.at[k], pc.at[k], send.at[4, k], recv.at[4, k], like[k]))

    def far_sum(k):
        two[k].wait_recv()
        at = ds(own + k * size, size)
        sum_s[at, :] = (sb[k].astype(F32) + rb[k].astype(F32)).astype(BF16)
        three.append(sending(sum_s.at[at], sum_s.at[at], send.at[2, k], recv.at[2, k], near))

    value = ps[m - 1].astype(F32)
    for copy in second:
        copy.wait_recv()
    for k in range(m - 1):
        value = value + pc[k].astype(F32)
    outs[g] = value.astype(BF16)
    third = [sending(outs.at[g], outs.at[g], send.at[5, k], recv.at[5, k], like[k]) for k in range(m - 1)]
    fourth = [sending(outs.at[g], outs.at[g], send.at[6, 0], recv.at[6, 0], pair)]
    firsts[0] = jnp.zeros(firsts.shape[1:], F32)
    gain = gain_ref[...]

    def norm_rows(start):
        at = ds(start, size)
        grad = sum_s[at, :].astype(F32)
        tok = tok_ref[at, :].astype(F32)
        inverse = lax.rsqrt(jnp.mean(tok * tok, axis=1, keepdims=True) + norm_eps)
        normed = tok * inverse
        firsts[0] += jnp.sum((grad * normed).reshape(size // SUB, SUB, width), axis=0)
        scaled = grad * gain
        mean = jnp.mean(scaled * normed, axis=1, keepdims=True)
        value = resid_ref[at, :] + inverse * (scaled - normed * mean)
        for ct in range(width // LANES):
            tile_s[ct, at, :] = value[:, ct * LANES : (ct + 1) * LANES]

    for k in range(count):
        far_sum(k)
        norm_rows(own + k * size)
    for k in range(m - 1):
        third[k].wait_recv()
        b = 2 * ((z + m - 1 - k) % m) + odd
        fourth.append(sending(outs.at[b], outs.at[b], send.at[6, k + 1], recv.at[6, k + 1], pair))
    for k in range(count):
        three[k].wait_recv()
        norm_rows(other + k * size)
    spread_first = [
        sending(firsts.at[0], firsts.at[k], send.at[7, k], recv.at[7, k], others[k - 1]) for k in range(1, n)
    ]
    restore(cuts, tile_s, grad_ref)
    for copy in spread_first:
        copy.wait_recv()

    def one_first(d, total):
        return total + firsts[(g + n - d) % n]

    first_ref[...] = lax.fori_loop(0, n, one_first, jnp.zeros(first_ref.shape, F32))
    for copy in fourth:
        copy.wait_recv()
    for b in range(n):
        gin_ref[b * mh : (b + 1) * mh, :] = outs[b, 0:mh, :].astype(F32)
        small_ref[b * sh : (b + 1) * sh, :] = outs[b, mh : mh + sh, :].astype(F32)
    mp_copies = q_one + q_two + q_three + one + two + three
    for copy in [head] + mp_copies + first + second + third + fourth + spread_first:
        copy.wait_send()


def finish(n, collective_id, cuts, *args, count=4):
    select, inner, normed, taps, given = args[1], args[2], args[8], args[10], args[11]
    wide = select.shape[1]
    rows, chans = inner.shape
    width = normed.shape[1]
    kernel = taps.shape[0]
    edge = (kernel - 1) * SUB
    m = n // 2
    over = lambda size: (size + 16 * n - 1) // (16 * n) * 16
    mh, sh = over(width), over(given.shape[0] + select.shape[1] + kernel + 1)
    slots = pltpu.VMEM((count, rows // 2 // count, width), BF16)
    part = lambda k: pltpu.VMEM((k, mh + sh, chans), BF16)
    few = pltpu.VMEM((rows // 512, 256, wide), BF16)
    low = pltpu.VMEM((rows, wide), BF16)
    sems = pltpu.SemaphoreType.DMA((12, max(n, count)))
    shape = jax.ShapeDtypeStruct
    return vmem_call(
        functools.partial(finish_kernel, n, count, cuts, (mh, sh)),
        [
            shape((rows, width), F32),
            shape((n * mh, chans), F32),
            shape((n * sh, chans), F32),
            shape((SUB, width), F32),
        ],
        [
            pltpu.VMEM((rows + edge, chans), F32),
            pltpu.VMEM((rows + edge, chans), F32),
            pltpu.VMEM((rows, 2 * chans), BF16),
            pltpu.VMEM((edge, chans), F32),
            pltpu.VMEM((rows, width), BF16),
            pltpu.VMEM((rows, width), BF16),
            slots,
            slots,
            slots,
            part(n),
            part(m),
            part(m),
            part(m),
            part(n),
            pltpu.VMEM((width // LANES, rows, LANES), F32),
            pltpu.VMEM((n, SUB, width), F32),
            pltpu.VMEM((n * mh, chans), F32),
            pltpu.VMEM((n * sh, chans), F32),
            low,
            low,
            few,
            few,
            few,
            sems,
            sems,
        ],
        collective_id, *args,
    )


def token_back_kernel(
    cuts,
    slot_ref,
    back_ref,
    residual_ref,
    hot_ref,
    cot_ref,
    valid_ref,
    gain_ref,
    router_ref,
    gated_ref,
    out_ref,
    scan_ref,
    both_ref,
    inner_ref,
    normed_in_ref,
    block_ref,
    resid_ref,
    gs_ref,
    gate_ref,
    early_ref,
    mixed_s,
    block_s,
    early_s,
    small_s,
    router_out,
    second_ref,
    skip_ref,
):
    rows, width = residual_ref.shape
    chans = inner_ref.shape[1]
    slots = back_ref.shape[1] * back_ref.shape[2]
    size = 256
    router_out[...] = jnp.zeros_like(router_out)
    second_ref[...] = jnp.zeros_like(second_ref)
    skip_ref[...] = jnp.zeros_like(skip_ref)

    def body(b, _):
        at = ds(b * size, size)
        folded = lambda v: jnp.sum(v.reshape(size // SUB, SUB, v.shape[1]), axis=0)
        iota = lax.broadcasted_iota(jnp.int32, (size, slots), 1)
        pick = jnp.where(iota == slot_ref[at, :], 1.0, 0.0).astype(BF16)
        result = dot(pick, back_ref[0].reshape(slots, width), NN)
        grad = dot(pick, back_ref[1].reshape(slots, width), NN)
        residual = residual_ref[at, :]
        inverse = lax.rsqrt(jnp.mean(residual * residual, axis=1, keepdims=True) + norm_eps)
        normed = residual * inverse
        normed_low = (normed * gain_ref[...]).astype(BF16)
        hot = hot_ref[at, :]
        probs = jax.nn.softmax(dot(normed_low, router_ref[...], NN), axis=-1)
        chosen = jnp.sum(probs * hot, axis=1, keepdims=True)
        block = residual + chosen * result
        for ct in range(width // LANES):
            block_s[ct, at, :] = block[:, ct * LANES : (ct + 1) * LANES]
        cot = cot_ref[at, :].astype(F32)
        gate = jnp.sum(cot * result, axis=1, keepdims=True)
        logit = (gate * probs * (hot - chosen)).astype(BF16)
        router_out[...] += dot(logit, normed_low, TN)
        grad = grad + dot(logit, router_ref[...], NT)
        second_ref[...] += folded(grad * normed)
        scaled = grad * gain_ref[...]
        mean = jnp.mean(scaled * normed, axis=1, keepdims=True)
        resid = cot + inverse * (scaled - normed * mean)
        resid_ref[at, :] = resid
        mixed = (valid_ref[at, :] * resid).astype(BF16)
        mixed_s[at, :] = mixed
        grad_gated = dot(mixed, out_ref[...], NT)
        pre = both_ref[at, chans : 2 * chans].astype(F32)
        sig = jax.nn.sigmoid(pre)
        act = pre * sig
        gs = grad_gated * act
        gs_ref[at, :] = gs
        skip_ref[...] += folded(gs * inner_ref[at, :].astype(F32))
        gate_ref[at, :] = (grad_gated * scan_ref[at, :] * (sig * (1.0 + pre * (1.0 - sig)))).astype(BF16)
        return 0

    lax.fori_loop(0, rows // size, body, 0)
    n, mh = early_ref.shape[0], early_s.shape[1] // early_ref.shape[0]
    sh = early_ref.shape[1] - 2 * mh
    some = router_out.shape[0]
    for k in range(width // chans):
        at = slice(k * chans, (k + 1) * chans)
        small_s[k * some : (k + 1) * some, :] = router_out[:, at]
        line = 2 * some + k
        small_s[line : line + 1, :] = jnp.sum(second_ref[:, at], axis=0, keepdims=True)
    small_s[2 * some + 2 : 2 * some + 3, :] = jnp.sum(skip_ref[...], axis=0, keepdims=True)
    early_s[0, 0:width, :] = dot(normed_in_ref[...], gate_ref[...], TN)
    value = dot(gated_ref[...], mixed_s[...], TN)
    for k in range(width // chans):
        early_s[1, k * chans : (k + 1) * chans, :] = value[:, k * chans : (k + 1) * chans]
    for b in range(n):
        for k in range(2):
            early_ref[b, k * mh : (k + 1) * mh, :] = early_s[k, b * mh : (b + 1) * mh, :].astype(BF16)
        early_ref[b, 2 * mh : 2 * mh + sh, :] = small_s[b * sh : (b + 1) * sh, :].astype(BF16)
    restore(cuts, block_s, block_ref)


def restore(cuts, tile_ref, out_ref):
    seqs, chunks, places = cuts
    for ct in range(tile_ref.shape[0]):
        for q in range(seqs):
            for k in range(chunks):
                picked = tile_ref[ct, pl.ds(k * seqs + q, places, stride=SUB), :]
                start = (q * chunks + k) * places
                out_ref[start : start + places, ct * LANES : (ct + 1) * LANES] = picked.astype(out_ref.dtype)


def token_back(n, cuts, *args):
    residual, router, inner = args[2], args[7], args[12]
    over = lambda size: (size + 16 * n - 1) // (16 * n) * 16
    mh, sh = over(residual.shape[1]), over(2 * router.shape[1] + 3)
    rows, width = residual.shape
    chans = inner.shape[1]
    shape = jax.ShapeDtypeStruct
    return pl.pallas_call(
        functools.partial(token_back_kernel, cuts),
        out_shape=[
            shape((rows, width), BF16),
            shape((rows, width), F32),
            shape((rows, chans), F32),
            shape((rows, chans), BF16),
            shape((n, 2 * mh + sh, chans), BF16),
        ],
        scratch_shapes=[
            pltpu.VMEM((rows, width), BF16),
            pltpu.VMEM((width // LANES, rows, LANES), F32),
            pltpu.VMEM((2, n * mh, chans), F32),
            pltpu.VMEM((n * sh, chans), F32),
            pltpu.VMEM((router.shape[1], width), F32),
            pltpu.VMEM((SUB, width), F32),
            pltpu.VMEM((SUB, chans), F32),
        ],
        compiler_params=pltpu.CompilerParams(vmem_limit_bytes=VMEM),
    )(*args)


def emit_kernel(
    layout,
    own_ref,
    far_ref,
    conv_ref,
    gate_ref,
    left_ref,
    right_ref,
    small_ref,
    few_ref,
    first_ref,
    ub_ref,
    far_bias_ref,
    db_ref,
    down_ref,
    up_ref,
    in_ref,
    out_ref,
    taps_ref,
    cb_ref,
    select_ref,
    sw_ref,
    sb_ref,
    decay_ref,
    skip_ref,
    second_ref,
    router_ref,
    norm_ref,
    gub_ref,
    gdb_ref,
):
    rank, states, select_at, taps_at = layout
    down_ref[...] = own_ref[0] + far_ref[0].astype(F32)
    up_ref[...] = own_ref[1] + far_ref[1].astype(F32)
    in_ref[:, 0, :] = conv_ref[...]
    in_ref[:, 1, :] = gate_ref[...]
    chans = conv_ref.shape[1]
    out_ref[:, 0:chans] = left_ref[...]
    out_ref[:, chans : 2 * chans] = right_ref[...]

    @pl.when(pl.program_id(0) == 0)
    def _():
        kernel = taps_ref.shape[0]
        taps_ref[...] = small_ref[taps_at : taps_at + kernel, :]
        cb_ref[...] = small_ref[taps_at + kernel : taps_at + kernel + 1, :]
        select_ref[...] = small_ref[select_at:taps_at, :].T
        sw_ref[...] = small_ref[0:rank, :]
        decay_ref[...] = small_ref[rank : rank + states, :]
        sb_ref[...] = small_ref[rank + states : rank + states + 1, :]
        some = router_ref.shape[1]
        line = 2 * some
        for k in range(2):
            at = slice(k * chans, (k + 1) * chans)
            router_ref[at, :] = few_ref[k * some : (k + 1) * some, :].T
            second_ref[:, at] = few_ref[line + k : line + k + 1, :]
        skip_ref[...] = few_ref[line + 2 : line + 3, :]
        total = lambda v: jnp.sum(v, axis=0, keepdims=True)
        norm_ref[...] = total(first_ref[...])
        bias = far_bias_ref[...].astype(F32)
        gub_ref[...] = total(ub_ref[0] + bias[0:SUB])
        gdb_ref[...] = total(db_ref[...].astype(F32) + bias[SUB : 2 * SUB])


def emit(layout, own, far, conv, gate, mixer, small, few, first, ub, far_bias, db, experts_all):
    width, chans = own.shape[1], conv.shape[1]
    hidden = own.shape[2]
    rank, states, select_at, taps_at = layout
    count = 6
    cut, part = width // count, chans // count
    shape = jax.ShapeDtypeStruct
    block = lambda size, wide: pl.BlockSpec((size, wide), lambda i: (i, 0))
    both = lambda size, wide: pl.BlockSpec((2, size, wide), lambda i: (0, i, 0))
    shapes = [
        (4, chans),
        (1, chans),
        (chans, taps_at - select_at),
        (rank, chans),
        (1, chans),
        (states, chans),
        (1, chans),
        (1, width),
        (width, experts_all),
        (1, width),
        (1, hidden),
        (1, width),
    ]
    return pl.pallas_call(
        functools.partial(emit_kernel, layout),
        grid=(count,),
        in_specs=[
            both(cut, hidden),
            both(cut, hidden),
            block(cut, chans),
            block(cut, chans),
            block(part, chans),
            pl.BlockSpec((part, chans), lambda i: (i + count, 0)),
            whole(*small.shape),
            whole(*few.shape),
            whole(*first.shape),
            whole(*ub.shape),
            whole(*far_bias.shape),
            whole(*db.shape),
        ],
        out_specs=[
            block(cut, hidden),
            block(cut, hidden),
            pl.BlockSpec((cut, 2, chans), lambda i: (i, 0, 0)),
            block(part, width),
            *[whole(*dims) for dims in shapes],
        ],
        out_shape=[
            shape((width, hidden), F32),
            shape((width, hidden), F32),
            shape((width, 2, chans), F32),
            shape((chans, width), F32),
            *[shape(dims, F32) for dims in shapes],
        ],
        compiler_params=pltpu.CompilerParams(vmem_limit_bytes=VMEM),
    )(own, far, conv, gate, mixer, mixer, small, few, first, ub, far_bias, db)


def silu_slope(values):
    sigmoid_vals = jax.nn.sigmoid(values)
    return sigmoid_vals * (1.0 + values * (1.0 - sigmoid_vals))


def per_device(
    tokens,
    routes,
    lengths,
    cotangent,
    first_gain,
    mixer_in,
    conv_weight,
    conv_bias,
    select_weight,
    step_weight,
    step_bias,
    decay_log,
    skip_gain,
    mixer_out,
    second_gain,
    router_weight,
    expert_up,
    up_bias,
    expert_down,
    down_bias,
):
    tok_count, model_width = tokens.shape
    kernel, chan_count = conv_weight.shape
    rank_size = step_weight.shape[0]
    state_size = decay_log.shape[0]
    expert_total = router_weight.shape[1]
    capacity = max(2, (5 * tok_count + 4 * expert_total - 1) // (4 * expert_total))
    room = (capacity + 31) // 32 * 32
    slot_dev = SLOT_DEV
    seq_count = tok_count // slot_dev
    chunks = SUB // seq_count
    places_dev = slot_dev // chunks
    cuts = (seq_count, chunks, places_dev)
    device = lax.axis_index("dp")
    dp_count = lax.axis_size("dp")

    mp_count = lax.axis_size("mp")
    to_far = [(i, (i + mp_count // 2) % mp_count) for i in range(mp_count)]
    swap_far = lambda values: lax.ppermute(values, "mp", to_far)
    own_bias = jnp.broadcast_to(up_bias, (16, up_bias.shape[1]))
    own_stack = jnp.concatenate([expert_up[0], expert_down[0], own_bias], axis=0)

    first_vals = first_gain.astype(F32)
    second_vals = second_gain.astype(F32)
    mixer_in_flat = mixer_in.reshape(model_width, 2 * chan_count)
    conv_taps = conv_weight.astype(F32)
    routes_cut = routes.reshape(seq_count, chunks, places_dev).transpose(2, 1, 0)
    (
        tok_low,
        cot_low,
        normed_in,
        both_in,
        conv_pre,
        inner_vals,
        lead_rows,
        projected,
        cot_rows,
        slot_ids,
        half_slots,
        valid_col,
        route_hot,
    ) = front(
        dp_count,
        0,
        cuts,
        capacity,
        room // 2,
        expert_total,
        tokens,
        cotangent,
        routes_cut.reshape(tok_count, 1),
        lengths[None],
        first_vals[None],
        mixer_in_flat,
        conv_taps,
        conv_bias.astype(F32)[None],
        select_weight,
    )
    own_stack, projected = lax.optimization_barrier((own_stack, projected))
    other_weights = swap_far(own_stack)
    decay_rates = -jnp.exp(decay_log.astype(F32))
    rates = decay_rates * LOG2E

    step_p, drive_p, step_slope, bin_p, cout_p, low_high, chunk_steps, state_in, totals = enter_forward(
        dp_count,
        2,
        projected,
        step_weight,
        step_bias.astype(F32)[None],
        inner_vals,
        valid_col,
        rates,
    )
    skip_vals = skip_gain.astype(F32)
    scan_out, gated_vals, mixer_part, states_before, last_states = forward(
        step_p,
        drive_p,
        bin_p,
        cout_p,
        rates,
        state_in,
        inner_vals,
        both_in,
        skip_vals[None],
        mixer_out,
    )
    residual, expert_rows = mixer_to_experts(
        dp_count, 3, room // 2, mixer_part, tok_low, valid_col, second_vals[None], half_slots
    )

    own_hot = (jnp.arange(expert_total) == device).astype(F32)[None]
    returned, grad_own, grad_other, up_bias_parts, down_bias_part = experts(
        dp_count,
        5,
        expert_rows,
        cot_rows,
        expert_up[0],
        up_bias.astype(F32),
        expert_down[0],
        other_weights,
        other_weights[-16:-15].astype(F32),
        down_bias.astype(F32),
        router_weight,
        own_hot,
    )
    down_bias_part = down_bias_part.astype(BF16)
    bias_rows = jnp.concatenate([up_bias_parts[1].astype(BF16), down_bias_part], axis=0)
    from_far = swap_far((grad_other, bias_rows))
    (
        block_out,
        grad_resid,
        grad_scan,
        grad_gate_low,
        early,
    ) = token_back(
        dp_count,
        cuts,
        slot_ids,
        returned,
        residual,
        route_hot,
        cot_low,
        valid_col,
        second_vals[None],
        router_weight,
        gated_vals,
        mixer_out,
        scan_out,
        both_in,
        inner_vals,
        normed_in,
    )
    gs_p = grad_scan.reshape(places_dev, SUB, chan_count)
    grad_in, early = enter_backward(
        dp_count, 6, step_p, gs_p, cout_p, chunk_steps, rates, totals, early
    )
    mixer_rows = (model_width + 16 * dp_count - 1) // (16 * dp_count) * 16
    grad_base, proj_part, given, grad_gate_in, grad_mixer_out, few = backward(
        dp_count,
        9,
        mixer_rows,
        step_p,
        drive_p,
        gs_p,
        bin_p,
        cout_p,
        rates,
        grad_in,
        last_states,
        states_before,
        inner_vals,
        step_slope,
        low_high,
        jnp.pad(step_weight, ((0, 2 * state_size), (0, 0))),
        skip_vals[None],
        early,
    )
    token_grad, grad_conv_half, small, grad_first = finish(
        dp_count,
        8,
        cuts,
        proj_part,
        select_weight,
        inner_vals,
        grad_base,
        conv_pre,
        both_in,
        lead_rows,
        grad_gate_low,
        normed_in,
        mixer_in_flat,
        conv_taps,
        given,
        tok_low,
        grad_resid,
        first_vals[None],
    )
    select_at = given.shape[0]
    taps_at = select_at + select_weight.shape[1]
    (
        grad_down,
        grad_up,
        grad_mixer_in,
        grad_mixer_full,
        grad_taps,
        grad_conv_bias,
        grad_select,
        grad_step_weight,
        grad_step_bias,
        grad_decay_log,
        grad_skip,
        grad_second,
        grad_router,
        grad_gain,
        grad_up_bias,
        grad_down_bias,
    ) = emit(
        (rank_size, state_size, select_at, taps_at),
        grad_own,
        from_far[0],
        grad_conv_half,
        grad_gate_in,
        grad_mixer_out,
        small,
        few,
        grad_first,
        up_bias_parts,
        from_far[1],
        down_bias_part,
        expert_total,
    )
    return (
        block_out,
        token_grad,
        grad_gain[0],
        grad_mixer_in,
        grad_taps,
        grad_conv_bias[0],
        grad_select,
        grad_step_weight,
        grad_step_bias[0],
        grad_decay_log,
        grad_skip[0],
        grad_mixer_full,
        grad_second[0],
        grad_router,
        grad_up[None],
        grad_up_bias,
        grad_down[None],
        grad_down_bias,
    )


def solution(mesh):
    return jax.shard_map(
        per_device,
        mesh=mesh,
        in_specs=(
            P("dp", None),
            P("dp", None),
            P(),
            P("dp", None),
            P(),
            P(None, None, "mp"),
            P(None, "mp"),
            P("mp"),
            P("mp", None),
            P(None, "mp"),
            P("mp"),
            P(None, "mp"),
            P("mp"),
            P("mp", None),
            P(),
            P(),
            P("dp", None, "mp"),
            P("dp", "mp"),
            P("dp", "mp", None),
            P("dp", None),
        ),
        out_specs=(
            P("dp", None),
            P("dp", None),
            P(),
            P(None, None, "mp"),
            P(None, "mp"),
            P("mp"),
            P("mp", None),
            P(None, "mp"),
            P("mp"),
            P(None, "mp"),
            P("mp"),
            P("mp", None),
            P(),
            P(),
            P("dp", None, "mp"),
            P("dp", "mp"),
            P("dp", "mp", None),
            P("dp", None),
        ),
        check_vma=False,
    )
```

```python
import functools

import jax
import jax.numpy as jnp
from jax import lax
from jax.experimental import pallas as pl
from jax.experimental.pallas import tpu as pltpu
from jax.sharding import PartitionSpec as P

F32 = jnp.float32
BF16 = jnp.bfloat16
SLOT_DEV = 256
LANES = 128
SUB = 8
LOG2E = 1.4426950408889634
LN2 = 0.6931471805599453
VMEM = 48 * 2**20
norm_eps = 1e-05
MESH = pl.DeviceIdType.MESH


NN = ((1,), (0,))
NT = ((1,), (1,))
TN = ((0,), (0,))


def dot(a, b, dims):
    return lax.dot_general(a, b, (dims, ((), ())), preferred_element_type=F32)


def lane(col):
    return jnp.broadcast_to(col, (SUB, LANES))


def row(ref, n, cs):
    return jnp.broadcast_to(ref[n : n + 1, cs], (SUB, LANES))


def tiles(count):
    return [slice(ct * LANES, (ct + 1) * LANES) for ct in range(count // LANES)]


def whole(*dims):
    return pl.BlockSpec(dims, lambda i: (0,) * len(dims))


def local_scan(step_ref, in_ref, map_ref, rates_ref, out_ref, nh, half, reverse):
    places, chans = step_ref.shape[0], step_ref.shape[2]
    cols = tiles(chans)
    ns = [nh * half + n for n in range(half)]

    def body(lap, st):
        i = places - 1 - lap if reverse else lap
        st = list(st)
        m = map_ref[i]
        mm = [lane(m[:, n : n + 1]) for n in ns]
        for ct, cs in enumerate(cols):
            s = step_ref[i, :, cs]
            x = in_ref[i, :, cs]
            for n in range(half):
                k = n * len(cols) + ct
                e = jnp.exp2(s * row(rates_ref, ns[n], cs))
                st[k] = e * (st[k] + x * mm[n]) if reverse else e * st[k] + x * mm[n]
        return tuple(st)

    zero = tuple(jnp.zeros((SUB, LANES), F32) for _ in range(half * len(cols)))
    st = lax.fori_loop(0, places, body, zero, unroll=8)
    for n in range(half):
        for ct, cs in enumerate(cols):
            out_ref[ns[n], :, cs] = st[n * len(cols) + ct]


def forward_kernel(
    step_ref,
    x_ref,
    bin_ref,
    cout_ref,
    rates_ref,
    h0_ref,
    inner_ref,
    gate_ref,
    skip_ref,
    weight_ref,
    quarter_ref,
    scan_ref,
    gated_ref,
    sum_ref,
    hb_ref,
    hf_ref,
    rows_ref,
    st_ref,
    y_ref,
    part_s,
    sum_s,
    rows_s,
    ra,
    sb,
    rb,
    send,
    recv,
    dsend,
    drecv,
    local,
):
    places, chans = step_ref.shape[0], step_ref.shape[2]
    states, half = rates_ref.shape[0], 8
    cols = tiles(chans)
    n = quarter_ref.shape[0]
    g = lax.axis_index("dp")
    j, near, far = mp_pair()
    c = j % 2
    i_block, count = pl.program_id(0), part_s.shape[0]
    size = places * SUB // 2

    def copy(kind, b, src, dst, to):
        return pltpu.make_async_remote_copy(
            src_ref=src,
            dst_ref=dst,
            send_sem=send.at[kind, b],
            recv_sem=recv.at[kind, b],
            device_id={"mp": to},
            device_id_type=MESH,
        )

    mine = lambda b: sum_s.at[b, ds(c * size, size)]
    one = lambda b: copy(0, b, part_s.at[b, ds((1 - c) * size, size)], ra.at[b], near)
    two = lambda b: copy(1, b, sb.at[b], rb.at[b], far)
    three = lambda b: copy(2, b, mine(b), mine(b), near)

    def pair_sum(b):
        one(b).wait_recv()
        sb[b] = (part_s[b, ds(c * size, size), :].astype(F32) + ra[b].astype(F32)).astype(BF16)
        two(b).start()

    def far_sum(b):
        two(b).wait_recv()
        sum_s[b, ds(c * size, size), :] = (sb[b].astype(F32) + rb[b].astype(F32)).astype(BF16)
        three(b).start()

    start, middle, end = dispatching(n, quarter_ref, rows_s, dsend, drecv, local)

    @pl.when(i_block == 0)
    def _():
        greet([{"mp": near}, {"mp": far}] + [{"dp": (g + k) % n} for k in range(1, n)])
        start()

    @pl.when(pl.program_id(0) == 0)
    def _():
        st_ref[...] = h0_ref[...]

    for nh in range(states // half):
        ns = [nh * half + n for n in range(half)]

        def body(i, st):
            st = list(st)
            b = bin_ref[i]
            c = cout_ref[i]
            bb = [lane(b[:, n : n + 1]) for n in ns]
            cc = [lane(c[:, n : n + 1]) for n in ns]
            for ct, cs in enumerate(cols):
                s = step_ref[i, :, cs]
                x = x_ref[i, :, cs]
                y = y_ref[i, :, cs] if nh else jnp.zeros((SUB, LANES), F32)
                for n in range(half):
                    k = n * len(cols) + ct
                    hb_ref[i, ns[n], :, cs] = st[k].astype(hb_ref.dtype)
                    e = jnp.exp2(s * row(rates_ref, ns[n], cs))
                    st[k] = e * st[k] + x * bb[n]
                    y = y + cc[n] * st[k]
                y_ref[i, :, cs] = y
            return tuple(st)

        st = tuple(st_ref[n, :, cs] for n in ns for cs in cols)
        st = lax.fori_loop(0, places, body, st, unroll=8)
        for n in range(half):
            for ct, cs in enumerate(cols):
                st_ref[ns[n], :, cs] = st[n * len(cols) + ct]
    hf_ref[...] = st_ref[...]
    scan = y_ref[...].reshape(places * SUB, chans) + skip_ref[...] * inner_ref[...].astype(F32)
    scan_ref[...] = scan
    gate = gate_ref[...].astype(F32)
    gated = (scan * (gate * jax.nn.sigmoid(gate))).astype(BF16)
    gated_ref[...] = gated
    part_s[i_block] = dot(gated, weight_ref[...], NN).astype(BF16)
    one(i_block).start()
    lag = 3

    @pl.when(i_block >= 1)
    def _():
        pair_sum(i_block - 1)

    @pl.when(i_block >= lag)
    def _():
        far_sum(i_block - lag)

    @pl.when(i_block == count // 2 + 1)
    def _():
        middle()

    @pl.when(i_block == count - 1)
    def _():
        pair_sum(count - 1)
        for b in range(count - lag, count):
            far_sum(b)
        end()
        rows_ref[...] = rows_s[...]
        for b in range(count):
            three(b).wait_recv()
        sum_ref[...] = sum_s[...].reshape(sum_ref.shape)
        for b in range(count):
            for made in (one, two, three):
                made(b).wait_send()


def forward(collective_id, step, x, bin_vals, cout, rates, h0, inner, both, skip, weight, quarter, block=16):
    places, _, chans = step.shape
    n, hr, hc = quarter.shape
    count = places // block
    sems = pltpu.SemaphoreType.DMA((3, count))
    dsems = pltpu.SemaphoreType.DMA((2, n))
    states = rates.shape[0]
    width = weight.shape[1]
    rows = places * SUB
    part = lambda size: pl.BlockSpec((block, SUB, size), lambda i: (i, 0, 0))
    flat = lambda size, col=0: pl.BlockSpec((block * SUB, size), lambda i: (i, col))
    shape = jax.ShapeDtypeStruct
    return pl.pallas_call(
        forward_kernel,
        grid=(count,),
        in_specs=[
            part(chans),
            part(chans),
            part(states),
            part(states),
            whole(states, chans),
            whole(states, SUB, chans),
            flat(chans),
            flat(chans, 1),
            whole(1, chans),
            whole(chans, width),
            whole(n, hr, hc),
        ],
        out_specs=[
            flat(chans),
            flat(chans),
            whole(rows, width),
            pl.BlockSpec((block, states, SUB, chans), lambda i: (i, 0, 0, 0)),
            whole(states, SUB, chans),
            whole(n, hr, 2 * hc),
        ],
        out_shape=[
            shape((rows, chans), F32),
            shape((rows, chans), BF16),
            shape((rows, width), BF16),
            shape((places, states, SUB, chans), BF16),
            shape((states, SUB, chans), F32),
            shape((n, hr, 2 * hc), BF16),
        ],
        scratch_shapes=[
            pltpu.VMEM((states, SUB, chans), F32),
            pltpu.VMEM((block, SUB, chans), F32),
            pltpu.VMEM((count, block * SUB, width), BF16),
            pltpu.VMEM((count, block * SUB, width), BF16),
            pltpu.VMEM((n, hr, 2 * hc), BF16),
            pltpu.VMEM((count, block * SUB // 2, width), BF16),
            pltpu.VMEM((count, block * SUB // 2, width), BF16),
            pltpu.VMEM((count, block * SUB // 2, width), BF16),
            sems,
            sems,
            dsems,
            dsems,
            pltpu.SemaphoreType.DMA,
        ],
        compiler_params=pltpu.CompilerParams(
            collective_id=collective_id, has_side_effects=True, vmem_limit_bytes=VMEM
        ),
    )(step, x, bin_vals, cout, rates, h0, inner, both, skip, weight, quarter)


def backward_kernel(
    n,
    step_ref,
    x_ref,
    gs_ref,
    past_ref,
    bin_ref,
    cout_ref,
    rates_ref,
    g0_ref,
    hf_ref,
    hb_ref,
    inner_ref,
    slope_ref,
    low_ref,
    weight_ref,
    skip_ref,
    early_ref,
    landed_ref,
    base_ref,
    proj_ref,
    given_ref,
    gin_ref,
    gout_ref,
    few_ref,
    result_ref,
    sbias_ref,
    gst_ref,
    rt_ref,
    q_ref,
    p_ref,
    sg_ref,
    sb_ref,
    gp_ref,
    sums,
    result_s,
    send,
    recv,
    rsend,
    rrecv,
):
    places, chans = step_ref.shape[0], step_ref.shape[2]
    states, some = rates_ref.shape[0], 4
    cols = tiles(chans)
    g = lax.axis_index("dp")
    j, near, far = mp_pair()
    y, c = j // 2, j % 2
    hr, hc = landed_ref.shape[1], landed_ref.shape[2]
    up, down, mine = ds(y * hr, hr), ds((1 - y) * hr, hr), ds(c * hc, hc)
    start, middle, end = gathering(n, sums, send, recv)

    def share(kind, src, dst, to):
        return pltpu.make_async_remote_copy(
            src_ref=src,
            dst_ref=dst,
            send_sem=rsend.at[kind],
            recv_sem=rrecv.at[kind],
            device_id={"mp": to},
            device_id_type=MESH,
        )

    place = lambda rows: result_s.at[:, rows, mine]
    to_far = share(0, landed_ref, place(up), far)
    to_near = share(1, landed_ref, place(up), near)
    pass_on = share(2, place(down), place(down), near)
    step_id, steps = pl.program_id(0), pl.num_programs(0)

    @pl.when(step_id == 0)
    def _():
        greet([{"mp": near}, {"mp": far}] + [{"dp": (g + k) % n} for k in range(1, n)])
        sums[g] = early_ref[...]
        start()
        to_far.start()
        to_near.start()
        result_s[:, up, mine] = landed_ref[...]

    @pl.when(step_id == steps // 2 - 1)
    def _():
        middle(0)

    @pl.when(step_id == steps // 2 + 1)
    def _():
        middle(1)

    @pl.when(step_id == steps - 2)
    def _():
        to_far.wait_recv()
        pass_on.start()

    @pl.when(pl.program_id(0) == 0)
    def _():
        gst_ref[...] = g0_ref[...]
        rt_ref[...] = jnp.zeros_like(rt_ref)
        given_ref[...] = jnp.zeros_like(given_ref)
        proj_ref[...] = jnp.zeros_like(proj_ref)
        sbias_ref[...] = jnp.zeros_like(sbias_ref)

    gp_ref[0] = past_ref[0]
    gp_ref[1:places] = gs_ref[0 : places - 1]

    for nq in range(states // some):
        ns = [nq * some + n for n in range(some)]
        size = some * len(cols)

        def body(lap, carry):
            i = places - 1 - lap
            st, rt = list(carry[:size]), list(carry[size:])
            b = bin_ref[i]
            c = cout_ref[i]
            bb = [lane(b[:, n : n + 1]) for n in ns]
            cc = [lane(c[:, n : n + 1]) for n in ns]
            qb, qc = [None] * some, [None] * some
            for ct, cs in enumerate(cols):
                s = step_ref[i, :, cs]
                x = x_ref[i, :, cs]
                g = gs_ref[i, :, cs]
                gp = gp_ref[i, :, cs]
                sg = sg_ref[i, :, cs] if nq else jnp.zeros((SUB, LANES), F32)
                sb = sb_ref[i, :, cs] if nq else jnp.zeros((SUB, LANES), F32)
                for n in range(some):
                    k = n * len(cols) + ct
                    rate = row(rates_ref, ns[n], cs)
                    e = jnp.exp2(s * rate)
                    h = hb_ref[i, ns[n], :, cs].astype(F32)
                    grad = st[k] + g * cc[n]
                    st[k] = e * grad
                    dg = st[k] * h
                    sg = sg + dg * rate
                    rt[k] = rt[k] + dg * s
                    sb = sb + grad * bb[n]
                    qb[n] = grad * x if ct == 0 else qb[n] + grad * x
                    qc[n] = gp * h if ct == 0 else qc[n] + gp * h
                sg_ref[i, :, cs] = sg
                sb_ref[i, :, cs] = sb
            rows = pl.ds(pl.multiple_of(i * SUB, SUB), SUB)
            for n in range(some):
                q_ref[rows, ns[n] * LANES : (ns[n] + 1) * LANES] = qb[n]
                p_ref[rows, ns[n] * LANES : (ns[n] + 1) * LANES] = qc[n]
            return tuple(st) + tuple(rt)

        at = [(ns[n], slice(None), cs) for n in range(some) for cs in cols]
        init = tuple(gst_ref[a] for a in at) + tuple(rt_ref[a] for a in at)
        out = lax.fori_loop(0, places, body, init, unroll=8)
        for j, a in enumerate(at):
            gst_ref[a] = out[j]
            rt_ref[a] = out[size + j]
    rank = low_ref.shape[1]
    wide = proj_ref.shape[1]
    dims = (states * LANES, wide)
    state = lax.broadcasted_iota(jnp.int32, dims, 0) // LANES
    column = lax.broadcasted_iota(jnp.int32, dims, 1)
    to_bin = jnp.where(column == state + rank, 1.0, 0.0).astype(BF16)
    to_cout = jnp.where(column == state + rank + states, 1.0, 0.0).astype(BF16)
    block_rows = places * SUB
    base = (pl.num_programs(0) - 1 - pl.program_id(0)) * block_rows
    here = pl.ds(pl.multiple_of(base + SUB, SUB), block_rows)
    late = pl.ds(pl.multiple_of(base, SUB), block_rows)

    @pl.when(pl.program_id(0) == 0)
    def _():
        end_rows = pl.ds(pl.multiple_of(base + block_rows, SUB), SUB)
        total_ = None
        for n_ in range(states):
            value = hf_ref[n_, :, cols[0]] * gs_ref[places - 1, :, cols[0]]
            for cs in cols[1:]:
                value = value + hf_ref[n_, :, cs] * gs_ref[places - 1, :, cs]
            term = jnp.dot(
                value.astype(BF16), to_cout[n_ * LANES : (n_ + 1) * LANES], preferred_element_type=F32
            )
            total_ = term if total_ is None else total_ + term
        proj_ref[end_rows, :] += total_

    proj_ref[late, :] += jnp.dot(p_ref[...].astype(BF16), to_cout, preferred_element_type=F32)
    flat = lambda ref: ref[...].reshape(places * SUB, chans)
    sb = flat(sb_ref)
    base_ref[...] = flat(gs_ref) * skip_ref[...] + flat(step_ref) * sb
    pre = (flat(sg_ref) * LN2 + inner_ref[...].astype(F32) * sb) * slope_ref[...]
    sbias_ref[...] += jnp.sum(pre.reshape(places, SUB, chans), axis=0)
    pre = pre.astype(BF16)
    given_ref[0:rank, :] += dot(low_ref[...], pre, TN)
    proj_ref[here, :] += dot(pre, weight_ref[...], NT) + jnp.dot(
        q_ref[...].astype(BF16), to_bin, preferred_element_type=F32
    )

    @pl.when(pl.program_id(0) == pl.num_programs(0) - 1)
    def _():
        end()
        to_near.wait_recv()
        pass_on.wait_recv()
        for made in (to_far, to_near, pass_on):
            made.wait_send()
        result_ref[...] = result_s[...]
        for n_ in range(states):
            line = rank + n_
            total_ = jnp.sum(rt_ref[n_], axis=0, keepdims=True)
            given_ref[line : line + 1, :] = total_ * rates_ref[n_ : n_ + 1, :] * LN2
        line = rank + states
        given_ref[line : line + 1, :] = jnp.sum(sbias_ref[...], axis=0, keepdims=True)
        mh = gin_ref.shape[0] // n
        sh = few_ref.shape[0] // n
        for b in range(n):
            few_ref[b * sh : (b + 1) * sh, :] = sums[b, 2 * mh : 2 * mh + sh, :].astype(F32)
            gin_ref[b * mh : (b + 1) * mh, :] = sums[b, 0:mh, :].astype(F32)
            gout_ref[b * mh : (b + 1) * mh, :] = sums[b, mh : 2 * mh, :].astype(F32)


def backward(
    n, collective_id, mh, step, x, gs, bin_vals, cout, rates, g0, hf, hb, inner, slope, low, weight, skip, early, quarter, block=16
):
    places, _, chans = step.shape
    states = rates.shape[0]
    rank, wide = low.shape[1], weight.shape[0]
    extra = (rank + states + SUB) // SUB * SUB
    count = places // block
    part = lambda width: pl.BlockSpec((block, SUB, width), lambda i: (count - 1 - i, 0, 0))
    flat = lambda width: pl.BlockSpec((block * SUB, width), lambda i: (count - 1 - i, 0))
    rows = places * SUB
    tall = n * mh
    few = n * (early.shape[0] - 2 * mh)
    sems = pltpu.SemaphoreType.DMA((2, PIECES * n // 2))
    return pl.pallas_call(
        functools.partial(backward_kernel, n),
        grid=(count,),
        in_specs=[
            part(chans),
            part(chans),
            part(chans),
            pl.BlockSpec((1, SUB, chans), lambda i: (jnp.maximum((count - 1 - i) * block - 1, 0), 0, 0)),
            part(states),
            part(states),
            whole(states, chans),
            whole(states, SUB, chans),
            whole(states, SUB, chans),
            pl.BlockSpec((block, states, SUB, chans), lambda i: (count - 1 - i, 0, 0, 0)),
            flat(chans),
            flat(chans),
            flat(rank),
            whole(wide, chans),
            whole(1, chans),
            whole(*early.shape),
            whole(*quarter.shape),
        ],
        out_specs=[
            flat(chans),
            whole(rows + SUB, wide),
            whole(extra, chans),
            whole(tall, chans),
            whole(tall, chans),
            whole(few, chans),
            whole(n, 2 * quarter.shape[1], 2 * quarter.shape[2]),
        ],
        out_shape=[
            jax.ShapeDtypeStruct((rows, chans), F32),
            jax.ShapeDtypeStruct((rows + SUB, wide), F32),
            jax.ShapeDtypeStruct((extra, chans), F32),
            jax.ShapeDtypeStruct((tall, chans), F32),
            jax.ShapeDtypeStruct((tall, chans), F32),
            jax.ShapeDtypeStruct((few, chans), F32),
            jax.ShapeDtypeStruct((n, 2 * quarter.shape[1], 2 * quarter.shape[2]), BF16),
        ],
        scratch_shapes=[
            pltpu.VMEM((SUB, chans), F32),
            pltpu.VMEM((states, SUB, chans), F32),
            pltpu.VMEM((states, SUB, chans), F32),
            pltpu.VMEM((block * SUB, states * LANES), F32),
            pltpu.VMEM((block * SUB, states * LANES), F32),
            pltpu.VMEM((block, SUB, chans), F32),
            pltpu.VMEM((block, SUB, chans), F32),
            pltpu.VMEM((block, SUB, chans), F32),
            pltpu.VMEM((n, *early.shape), BF16),
            pltpu.VMEM((n, 2 * quarter.shape[1], 2 * quarter.shape[2]), BF16),
            sems,
            sems,
            pltpu.SemaphoreType.DMA((3,)),
            pltpu.SemaphoreType.DMA((3,)),
        ],
        compiler_params=pltpu.CompilerParams(
            collective_id=collective_id, has_side_effects=True, vmem_limit_bytes=VMEM
        ),
    )(step, x, gs, gs, bin_vals, cout, rates, g0, hf, hb, inner, slope, low, weight, skip, early, quarter)


def mp_pair():
    j = lax.axis_index("mp")
    return j, j + 1 - 2 * (j % 2), (j + 2) % 4


def ds(start, size):
    return pl.ds(pl.multiple_of(start, size), size)


def greet(others):
    barrier = pltpu.get_barrier_semaphore()
    for other in others:
        pl.semaphore_signal(barrier, inc=1, device_id=other, device_id_type=MESH)
    pl.semaphore_wait(barrier, len(others))


def sending(src, dst, send, recv, device):
    copy = pltpu.make_async_remote_copy(
        src_ref=src, dst_ref=dst, send_sem=send, recv_sem=recv, device_id=device, device_id_type=MESH
    )
    copy.start()
    return copy


def vmem_call(kernel, out_shape, scratch, collective_id, *args, cost=0):
    space = pl.BlockSpec(memory_space=pltpu.VMEM)
    return pl.pallas_call(
        kernel,
        out_shape=out_shape,
        in_specs=[space] * len(args),
        out_specs=jax.tree.map(lambda _: space, out_shape),
        scratch_shapes=scratch,
        compiler_params=pltpu.CompilerParams(
            collective_id=collective_id, has_side_effects=True, vmem_limit_bytes=VMEM
        ),
    )(*args)


def half_turn(tile):
    return pltpu.roll(tile, SUB // 2, 0)


def send_totals(n, total_ref, all_ref, send, recv):
    g = lax.axis_index("dp")
    all_ref[0] = total_ref[...] + half_turn(total_ref[...])
    return [
        sending(all_ref.at[0], all_ref.at[k], send.at[1, k], recv.at[1, k], {"dp": (g + k) % n})
        for k in range(1, n)
    ]


def exchange_body(
    n, reverse, copies, part_ref, total_ref, rates_ref, packed_ref, all_ref, out_ref, sbuf, rbuf, send, recv
):
    g = lax.axis_index("dp")
    states, chans = rates_ref.shape
    pairs = states // 2
    upper = lax.broadcasted_iota(jnp.int32, (SUB, chans), 0) >= SUB // 2
    total = total_ref[...]
    decay = lambda m: jnp.exp2(jnp.broadcast_to(rates_ref[m : m + 1, :], (SUB, chans)) * total)

    def summary(m):
        part = part_ref[m]
        return part + decay(m) * half_turn(part)

    def packed(p):
        low, high = summary(p), summary(p + pairs)
        if reverse:
            return jnp.where(upper, half_turn(high), low)
        return jnp.where(upper, high, half_turn(low))

    for p in range(0, pairs, 2):
        sbuf[p * SUB : (p + 2) * SUB, :] = jnp.concatenate([packed(p), packed(p + 1)], axis=0).astype(BF16)
    copies = copies + [
        sending(sbuf, rbuf.at[k], send.at[0, k], recv.at[0, k], {"dp": (g + k) % n})
        for k in range(1, n)
    ]
    for copy in copies:
        copy.wait_recv()

    def one(lap, held):
        away = n - 1 - lap
        slot = n - away if reverse else away
        use = (g + away < n) if reverse else (away <= g)
        steps = all_ref[slot]
        new = []
        for p in range(0, pairs, 2):
            got = rbuf[slot, p * SUB : (p + 2) * SUB, :].astype(F32)
            for q in (p, p + 1):
                fall = jnp.exp2(packed_ref[q] * steps)
                value = fall * held[q] + got[(q - p) * SUB : (q - p + 1) * SUB]
                new.append(jnp.where(use, value, held[q]))
        return tuple(new)

    zero = tuple(jnp.zeros((SUB, chans), F32) for _ in range(pairs))
    held = lax.fori_loop(0, n - 1, one, zero)
    for m in range(states):
        state = held[m % pairs]
        if (m >= pairs) != reverse:
            state = half_turn(state)
        later = half_turn(decay(m) * state + part_ref[m])
        out_ref[m] = jnp.where(upper, state, later) if reverse else jnp.where(upper, later, state)
    for copy in copies:
        copy.wait_send()


def packed_rates(rates):
    states, chans = rates.shape
    pairs = states // 2
    wide = lambda r: jnp.broadcast_to(r[:, None, :], (pairs, SUB // 2, chans))
    return jnp.concatenate([wide(rates[:pairs]), wide(rates[pairs:])], axis=1)


def enter_forward_kernel(
    n, proj_ref, weight_ref, bias_ref, inner_ref, valid_ref, rates_ref, packed_ref,
    step_ref, drive_ref, slope_ref, bin_ref, cout_ref, low_ref, total_ref, h0_ref, all_ref,
    part, sbuf, rbuf, send, recv,
):
    places, _, chans = step_ref.shape
    states = rates_ref.shape[0]
    rank = weight_ref.shape[0]
    g = lax.axis_index("dp")
    greet([{"dp": (g + k) % n} for k in range(1, n)])
    size = 256
    total_ref[...] = jnp.zeros_like(total_ref)

    def block(b, _):
        at = ds(b * size, size)
        here = pl.ds(pl.multiple_of(b * (size // SUB), size // SUB), size // SUB)
        by_place = lambda v: v.reshape(size // SUB, SUB, v.shape[1])
        proj = proj_ref[at, :]
        low = proj[:, 0:rank]
        high = low.astype(BF16)
        rest = (low - high.astype(F32)).astype(BF16)
        low_ref[at, :] = high
        pre = dot(high, weight_ref[...], NN) + dot(rest, weight_ref[...], NN) + bias_ref[...]
        valid = valid_ref[at, :]
        steps = valid * (jnp.maximum(pre, 0.0) + jnp.log1p(jnp.exp(-jnp.abs(pre))))
        slope_ref[at, :] = valid * jax.nn.sigmoid(pre)
        step_ref[here] = by_place(steps)
        drive_ref[here] = by_place(steps * inner_ref[at, :].astype(F32))
        total_ref[...] += jnp.sum(by_place(steps), axis=0)
        bin_ref[here] = by_place(proj[:, rank : rank + states])
        cout_ref[here] = by_place(proj[:, rank + states : rank + 2 * states])
        return 0

    lax.fori_loop(0, places * SUB // size, block, 0)
    copies = send_totals(n, total_ref, all_ref, send, recv)
    half = 8
    for nh in range(states // half):
        local_scan(step_ref, drive_ref, bin_ref, rates_ref, part, nh, half, False)
    exchange_body(n, False, copies, part, total_ref, rates_ref, packed_ref, all_ref, h0_ref, sbuf, rbuf, send, recv)


def enter_forward(n, collective_id, proj, weight, bias, inner, valid, rates):
    rows, chans = inner.shape
    states = rates.shape[0]
    rank = weight.shape[0]
    shape = jax.ShapeDtypeStruct
    places = rows // SUB
    entering = shape((states, SUB, chans), F32)
    sems = pltpu.SemaphoreType.DMA((2, n))
    return vmem_call(
        functools.partial(enter_forward_kernel, n),
        [
            shape((places, SUB, chans), F32),
            shape((places, SUB, chans), F32),
            shape((rows, chans), F32),
            shape((places, SUB, states), F32),
            shape((places, SUB, states), F32),
            shape((rows, rank), BF16),
            shape((SUB, chans), F32),
            entering,
            shape((n, SUB, chans), F32),
        ],
        [
            pltpu.VMEM((states, SUB, chans), F32),
            pltpu.VMEM((states * SUB // 2, chans), BF16),
            pltpu.VMEM((n, states * SUB // 2, chans), BF16),
            sems,
            sems,
        ],
        collective_id, proj, weight, bias, inner, valid, rates, packed_rates(rates),
    )


def dp_pairs(n):
    g = lax.axis_index("dp")
    odd, z, m = g % 2, g // 2, n // 2
    return g, odd, {"dp": g + 1 - 2 * odd}, [{"dp": 2 * ((z + k) % m) + odd} for k in range(1, m)]


PIECES = 2


def gathering(n, sums, send, recv):
    g, odd, pair, like = dp_pairs(n)
    z, m = g // 2, n // 2
    rows = sums.shape[1]
    cut = (rows // 2 + 15) // 16 * 16
    parts = [pl.ds(0, cut), pl.ds(cut, rows - cut)]

    def copy(kind, k, p, b, to):
        return pltpu.make_async_remote_copy(
            src_ref=sums.at[b, parts[p]],
            dst_ref=sums.at[b, parts[p]],
            send_sem=send.at[kind, p * m + k],
            recv_sem=recv.at[kind, p * m + k],
            device_id=to,
            device_id_type=MESH,
        )

    third = lambda k, p: copy(0, k, p, g, like[k])
    fourth = lambda k, p: copy(1, k, p, 2 * ((z + m - k) % m) + odd, pair)

    def start():
        for p in range(PIECES):
            for k in range(m - 1):
                third(k, p).start()
            fourth(0, p).start()

    def middle(p):
        for k in range(m - 1):
            third(k, p).wait_recv()
            fourth(k + 1, p).start()

    def end():
        for p in range(PIECES):
            for k in range(m):
                fourth(k, p).wait_recv()
            for k in range(m - 1):
                third(k, p).wait_send()
            for k in range(m):
                fourth(k, p).wait_send()

    return start, middle, end


def enter_backward_kernel(
    n, step_ref, gs_ref, cout_ref, total_ref, rates_ref, packed_ref, all_ref, blocks_ref,
    g0_ref, own_ref, part, sbuf, rbuf, pa, ps, pc, send, recv, pair_send, pair_recv,
):
    states = rates_ref.shape[0]
    g, odd, pair, like = dp_pairs(n)
    z, m = g // 2, n // 2
    greet([{"dp": (g + k) % n} for k in range(1, n)])
    order = [(z + k) % m for k in range(1, m)] + [z]
    first = [
        sending(blocks_ref.at[2 * order[k] + 1 - odd], pa.at[k], pair_send.at[0, k], pair_recv.at[0, k], pair)
        for k in range(m)
    ]
    half = 8
    second = []
    for nh in range(states // half):
        local_scan(step_ref, gs_ref, cout_ref, rates_ref, part, nh, half, True)
        if nh == 0:
            few = range(0, m // 2)
        else:
            few = range(m // 2, m)
        for k in few:
            first[k].wait_recv()
            ps[k] = (blocks_ref[2 * order[k] + odd].astype(F32) + pa[k].astype(F32)).astype(BF16)
            if k < m - 1:
                second.append(sending(ps.at[k], pc.at[k], pair_send.at[1, k], pair_recv.at[1, k], like[k]))
    exchange_body(n, True, [], part, total_ref, rates_ref, packed_ref, all_ref, g0_ref, sbuf, rbuf, send, recv)
    value = ps[m - 1].astype(F32)
    for copy in second:
        copy.wait_recv()
    for k in range(m - 1):
        value = value + pc[k].astype(F32)
    own_ref[...] = value.astype(BF16)
    for copy in first + second:
        copy.wait_send()


def enter_backward(n, collective_id, step, gs, cout, total, rates, totals, blocks):
    _, _, chans = step.shape
    states = rates.shape[0]
    shape = jax.ShapeDtypeStruct
    m = n // 2
    sems = pltpu.SemaphoreType.DMA((2, n))
    some = pltpu.VMEM((m, *blocks.shape[1:]), BF16)
    return vmem_call(
        functools.partial(enter_backward_kernel, n),
        [shape((states, SUB, chans), F32), shape(blocks.shape[1:], BF16)],
        [
            pltpu.VMEM((states, SUB, chans), F32),
            pltpu.VMEM((states * SUB // 2, chans), BF16),
            pltpu.VMEM((n, states * SUB // 2, chans), BF16),
            some,
            some,
            some,
            sems,
            sems,
            sems,
            sems,
        ],
        collective_id, step, gs, cout, total, rates, packed_rates(rates), totals, blocks,
    )


def half_pick(ids, slots):
    iota = lax.broadcasted_iota(jnp.int32, (ids.shape[0], slots), 1)
    return jnp.where(iota == ids, 1.0, 0.0).astype(BF16)


def dispatching(n, x_ref, out_ref, send, recv, local):
    g = lax.axis_index("dp")
    j, near, _ = mp_pair()
    hc = x_ref.shape[2]
    cols = ds((j % 2) * hc, hc)

    def leave(k):
        return pltpu.make_async_remote_copy(
            src_ref=x_ref.at[(g + k) % n],
            dst_ref=out_ref.at[g, :, cols],
            send_sem=send.at[0, k],
            recv_sem=recv.at[0, k],
            device_id={"dp": (g + k) % n},
            device_id_type=MESH,
        )

    def share(k):
        place = out_ref.at[(g + n - k) % n, :, cols]
        return pltpu.make_async_remote_copy(
            src_ref=place,
            dst_ref=place,
            send_sem=send.at[1, k],
            recv_sem=recv.at[1, k],
            device_id={"mp": near},
            device_id_type=MESH,
        )

    own = pltpu.make_async_copy(x_ref.at[g], out_ref.at[g, :, cols], local)

    def start():
        own.start()
        for k in range(1, n):
            leave(k).start()

    def middle():
        for k in range(n):
            if k:
                leave(k).wait_recv()
            else:
                own.wait()
            share(k).start()

    def end():
        for k in range(n):
            share(k).wait_recv()
        for k in range(n):
            if k:
                leave(k).wait_send()
            share(k).wait_send()

    return start, middle, end


def arrange(cuts, in_ref, tile_ref):
    seqs, chunks, places = cuts
    for ct in range(tile_ref.shape[0]):
        for q in range(seqs):
            for k in range(chunks):
                start = (q * chunks + k) * places
                value = in_ref[start : start + places, ct * LANES : (ct + 1) * LANES]
                tile_ref[ct, pl.ds(k * seqs + q, places, stride=SUB), :] = value.astype(F32)


def front_kernel(
    n,
    cuts,
    capacity,
    tokens_ref,
    cot_ref,
    routes_ref,
    lengths_ref,
    gain_ref,
    weight_ref,
    taps_ref,
    bias_ref,
    select_ref,
    tok_ref,
    cot_low_ref,
    normed_ref,
    both_ref,
    pre_ref,
    inner_ref,
    lead_ref,
    proj_ref,
    quarter,
    slot_ref,
    half_ref,
    valid_ref,
    hot_ref,
    tile_s,
    ext_s,
    live_s,
    got,
    part_s,
    ra,
    sb,
    rb,
    send,
    recv,
):
    seqs, chunks, places = cuts
    g = lax.axis_index("dp")
    j, near, far = mp_pair()
    y, c = j // 2, j % 2
    near, far = {"mp": near}, {"mp": far}
    rows, width = tok_ref.shape
    chans = inner_ref.shape[1]
    kernel = taps_ref.shape[0]
    edge = (kernel - 1) * SUB
    slot_dev = chunks * places
    experts_all = hot_ref.shape[1]
    hr, hc = quarter.shape[1], quarter.shape[2]
    size = 256
    greet([near, far, {"dp": (g + 1) % n}, {"dp": (g + n - 1) % n}])

    arrange(cuts, tokens_ref, tile_s)

    def first(b, _):
        at = ds(b * size, size)
        tok = jnp.concatenate([tile_s[ct, at, :] for ct in range(width // LANES)], axis=1)
        tok_ref[at, :] = tok.astype(BF16)
        inverse = lax.rsqrt(jnp.mean(tok * tok, axis=1, keepdims=True) + norm_eps)
        normed = (tok * inverse * gain_ref[...]).astype(BF16)
        normed_ref[at, :] = normed
        both = dot(normed, weight_ref[...], NN).astype(BF16)
        both_ref[at, :] = both
        ext_s[pl.ds(pl.multiple_of(b * size + edge, SUB), size), :] = both[:, 0:chans].astype(F32)
        return 0

    lax.fori_loop(0, rows // size, first, 0)
    ends = sending(
        both_ref.at[rows - 32 : rows, 0:chans], got, send.at[3, 0], recv.at[3, 0], {"dp": (g + 1) % n}
    )

    at_row = lax.broadcasted_iota(jnp.int32, (rows, 1), 0)
    sub = at_row % SUB
    seq = sub % seqs
    local_place = (sub // seqs) * places + at_row // SUB
    limit = jnp.zeros((rows, 1), jnp.int32)
    for q in range(seqs):
        limit = jnp.where(seq == q, lengths_ref[0:1, q : q + 1], limit)
    valid = jnp.where(g * slot_dev + local_place < limit, 1.0, 0.0)
    valid_ref[...] = valid
    route = routes_ref[...]
    hot = jnp.where(lax.broadcasted_iota(jnp.int32, (rows, experts_all), 1) == route, 1.0, 0.0)
    hot_ref[...] = hot
    live_s[...] = hot * valid
    col = lax.broadcasted_iota(jnp.int32, (1, rows), 1)
    col_sub = col % SUB
    original = (col_sub % seqs) * slot_dev + (col_sub // seqs) * places + col // SUB
    room = 2 * hr

    def position(b, _):
        at = ds(b * size, size)
        here = b * size + lax.broadcasted_iota(jnp.int32, (size, 1), 0)
        here_sub = here % SUB
        mine = (here_sub % seqs) * slot_dev + (here_sub // seqs) * places + here // SUB
        before = jnp.where(original < mine, 1.0, 0.0).astype(BF16)
        live = live_s[at, :]
        earlier = dot(before, live_s[...].astype(BF16), NN)
        pos = jnp.sum(earlier * live, axis=1, keepdims=True)
        kept = jnp.where(pos < capacity, jnp.sum(live, axis=1, keepdims=True), 0.0) > 0.5
        pos = pos.astype(jnp.int32)
        to = routes_ref[at, :]
        slot_ref[at, :] = jnp.where(kept, to * room + pos, -1)
        lower = pos - y * hr
        inside = jnp.where(lower >= 0, 1, 0) * jnp.where(lower < hr, 1, 0)
        half_ref[at, :] = jnp.where(kept, jnp.where(inside > 0, to * hr + lower, -1), -1)
        return 0

    lax.fori_loop(0, rows // size, position, 0)

    ends.wait_recv()
    upper = lax.broadcasted_iota(jnp.int32, (SUB, chans), 0) >= SUB // 2
    some = jnp.where(g > 0, 1.0, 0.0)
    tails = got[...].astype(F32) * some
    for k in range(kernel - 1):
        at = slice(k * SUB, (k + 1) * SUB)
        tail = ext_s[rows + k * SUB : rows + (k + 1) * SUB, :]
        other_tail = tails[32 - edge + k * SUB : 32 - edge + (k + 1) * SUB, :]
        lead = half_turn(jnp.where(upper, other_tail, tail))
        ext_s[at, :] = lead
        lead_ref[at, :] = lead

    half = rows // 2
    count = half // size
    own = c * half
    other = (1 - c) * half

    def conv(start):
        at = ds(start, size)
        pre = jnp.broadcast_to(bias_ref[...], (size, chans))
        for k in range(kernel):
            past = ext_s[pl.ds(pl.multiple_of(start + k * SUB, SUB), size), :]
            pre = pre + taps_ref[k : k + 1, :] * past
        pre_ref[at, :] = pre
        inner = (pre * jax.nn.sigmoid(pre)).astype(BF16)
        inner_ref[at, :] = inner
        part_s[at, :] = dot(inner, select_ref[...], NN)

    one, two, three = [], [], []
    for k in range(count):
        conv(other + k * size)
        at = ds(other + k * size, size)
        one.append(sending(part_s.at[at], ra.at[k], send.at[0, k], recv.at[0, k], near))
    for k in range(count):
        conv(own + k * size)
        one[k].wait_recv()
        sb[k] = part_s[ds(own + k * size, size), :] + ra[k]
        two.append(sending(sb.at[k], rb.at[k], send.at[1, k], recv.at[1, k], far))

    arrange(cuts, cot_ref, tile_s)

    def second(b, _):
        at = ds(b * size, size)
        cot = jnp.concatenate([tile_s[ct, at, :] for ct in range(width // LANES)], axis=1)
        cot_low_ref[at, :] = cot.astype(BF16)
        return 0

    lax.fori_loop(0, rows // size, second, 0)
    pick = half_pick(half_ref[...], n * hr)
    sent = dot(pick, cot_low_ref[:, ds(c * hc, hc)], TN).astype(BF16)
    quarter[...] = sent.reshape(n, hr, hc)
    for k in range(count):
        two[k].wait_recv()
        at = ds(own + k * size, size)
        proj_ref[at, :] = sb[k] + rb[k]
        three.append(sending(proj_ref.at[at], proj_ref.at[at], send.at[2, k], recv.at[2, k], near))
    for copy in three:
        copy.wait_recv()
    for copy in [ends] + one + two + three:
        copy.wait_send()


def front(n, collective_id, cuts, capacity, hr, experts_all, *args):
    tokens, taps, select = args[0], args[6], args[8]
    rows, width = tokens.shape
    kernel, chans = taps.shape
    edge = (kernel - 1) * SUB
    wide = select.shape[1]
    count = rows // 512
    shape = jax.ShapeDtypeStruct
    sems = pltpu.SemaphoreType.DMA((4, count))
    sums = pltpu.VMEM((count, 256, wide), F32)
    return vmem_call(
        functools.partial(front_kernel, n, cuts, capacity),
        [
            shape((rows, width), BF16),
            shape((rows, width), BF16),
            shape((rows, width), BF16),
            shape((rows, 2 * chans), BF16),
            shape((rows, chans), F32),
            shape((rows, chans), BF16),
            shape((edge, chans), F32),
            shape((rows, wide), F32),
            shape((n, hr, width // 2), BF16),
            shape((rows, 1), jnp.int32),
            shape((rows, 1), jnp.int32),
            shape((rows, 1), F32),
            shape((rows, experts_all), F32),
        ],
        [
            pltpu.VMEM((width // LANES, rows, LANES), F32),
            pltpu.VMEM((rows + edge, chans), F32),
            pltpu.VMEM((rows, experts_all), F32),
            pltpu.VMEM((32, chans), BF16),
            pltpu.VMEM((rows, wide), F32),
            sums,
            sums,
            sums,
            sems,
            sems,
        ],
        collective_id, *args,
    )


def middle_kernel(
    n, sum_ref, tok_ref, valid_ref, gain_ref, half_ref, resid_ref, rows_ref, normed_s, quarter, dsend, drecv, local
):
    g = lax.axis_index("dp")
    j, near, _ = mp_pair()
    c = j % 2
    rows, width = tok_ref.shape
    hr, hc = rows_ref.shape[1], width // 2
    size = 256
    greet([{"mp": near}] + [{"dp": (g + k) % n} for k in range(1, n)])

    def norm(b, _):
        at = ds(b * size, size)
        resid = tok_ref[at, :].astype(F32) + valid_ref[at, :] * sum_ref[at, :].astype(F32)
        resid_ref[at, :] = resid
        inverse = lax.rsqrt(jnp.mean(resid * resid, axis=1, keepdims=True) + norm_eps)
        normed_s[at, :] = (resid * inverse * gain_ref[...]).astype(BF16)
        return 0

    lax.fori_loop(0, rows // size, norm, 0)
    pick = half_pick(half_ref[...], n * hr)
    sent = dot(pick, normed_s[:, ds(c * hc, hc)], TN).astype(BF16)
    quarter[...] = sent.reshape(n, hr, hc)
    start, middle, end = dispatching(n, quarter, rows_ref, dsend, drecv, local)
    start()
    middle()
    end()


def mixer_to_experts(n, collective_id, hr, mixed, tok, valid, gain, half_slots):
    rows, width = tok.shape
    shape = jax.ShapeDtypeStruct
    dsems = pltpu.SemaphoreType.DMA((2, n))
    return vmem_call(
        functools.partial(middle_kernel, n),
        [shape((rows, width), F32), shape((n, hr, width), BF16)],
        [
            pltpu.VMEM((rows, width), BF16),
            pltpu.VMEM((n, hr, width // 2), BF16),
            dsems,
            dsems,
            pltpu.SemaphoreType.DMA,
        ],
        collective_id, mixed, tok, valid, gain, half_slots,
    )


def returning(n, x_ref, out_ref, send, recv):
    g = lax.axis_index("dp")
    j, near, far = mp_pair()
    hr, hc = x_ref.shape[1], x_ref.shape[2]
    y, c = j // 2, j % 2
    mine = ds(c * hc, hc)
    up, down = ds(y * hr, hr), ds((1 - y) * hr, hr)

    def copy(kind, k, src, dst, to):
        return pltpu.make_async_remote_copy(
            src_ref=src,
            dst_ref=dst,
            send_sem=send.at[kind, k],
            recv_sem=recv.at[kind, k],
            device_id=to,
            device_id_type=MESH,
        )

    def place(k, rows):
        return out_ref.at[(g + n - k) % n, rows, mine]

    there = lambda k: copy(0, k, x_ref.at[(g + k) % n], out_ref.at[g, up, mine], {"dp": (g + k) % n})
    to_far = lambda k: copy(1, k, place(k, up), place(k, up), {"mp": far})
    to_near = lambda k: copy(2, k, place(k, up), place(k, up), {"mp": near})
    on = lambda k: copy(3, k, place(k, down), place(k, down), {"mp": near})

    def keep():
        out_ref[g, up, mine] = x_ref[g]

    def arrived(k):
        @pl.when(k > 0)
        def _():
            there(k).wait_recv()

        to_far(k).start()
        to_near(k).start()

    def passed(k):
        to_far(k).wait_recv()
        on(k).start()

    def end(k):
        to_near(k).wait_recv()
        on(k).wait_recv()
        for made in (to_far, to_near, on):
            made(k).wait_send()

        @pl.when(k > 0)
        def _():
            there(k).wait_send()

    return keep, there, arrived, passed, end


def each(act, start, count):
    def one(i, _):
        act(start + i)
        return 0

    lax.fori_loop(0, count, one, 0)


def expert_kernel(
    n,
    rows_ref,
    cot_ref,
    up_ref,
    ub_ref,
    down_ref,
    up2_ref,
    down2_ref,
    ub2_ref,
    db_ref,
    router_ref,
    hot_ref,
    out_ref,
    quarter_ref,
    gates_ref,
    gown_ref,
    gother_ref,
    gub_ref,
    gdb_ref,
    part,
    hid,
    slope,
    pre,
    grad,
    ra,
    qb,
    gate_part,
    gate_near,
    gate_sum,
    gate_in,
    send,
    recv,
    near_send,
    near_recv,
    gate_send,
    gate_recv,
):
    g = lax.axis_index("dp")
    j, near, far = mp_pair()
    near, far = {"mp": near}, {"mp": far}
    y, c = j // 2, j % 2
    hr, width = rows_ref.shape[1], rows_ref.shape[2]
    hidden = up_ref.shape[1]
    hc = width // 2
    half = n // 2
    size = half * hr
    others = [{"dp": (g + k) % n} for k in range(1, n)]
    greet([near, far] + others)
    mine, theirs = ds(c * hc, hc), ds((1 - c) * hc, hc)
    gub_ref[...] = jnp.zeros_like(gub_ref)
    gdb_ref[...] = jnp.zeros_like(gdb_ref)
    folded = lambda v: jnp.sum(v.reshape(v.shape[0] // SUB, SUB, v.shape[1]), axis=0)
    ups = (up_ref, up2_ref)
    downs = (down_ref, down2_ref)
    biases = (ub_ref, ub2_ref)

    def near_copy(t):
        return pltpu.make_async_remote_copy(
            src_ref=part.at[t // n, (g + t) % n, :, theirs],
            dst_ref=ra.at[t],
            send_sem=near_send.at[t],
            recv_sem=near_recv.at[t],
            device_id=near,
            device_id_type=MESH,
        )

    def wide(ref, base):
        return ref[pl.ds(base, half)].reshape(size, ref.shape[2])

    def activate(base):
        rows = wide(rows_ref, base)
        at = pl.ds(pl.multiple_of(base * hr, size), size)
        for k in range(2):
            v = dot(rows, ups[k][...], NN) + biases[k][...]
            sq = v * v
            th = jnp.tanh(v * (GELU_A + GELU_A * GELU_B * sq))
            hid[k, at, :] = (0.5 * v * (1.0 + th)).astype(BF16)
            slope[k, at, :] = 0.5 * (1.0 + th) + 0.5 * v * (1.0 - th * th) * (
                GELU_A + 3.0 * GELU_A * GELU_B * sq
            )

    def behind(base):
        at = pl.ds(pl.multiple_of(base * hr, size), size)
        probs = jax.nn.softmax(dot(wide(rows_ref, base), router_ref[...], NN), axis=-1)
        chosen = jnp.sum(probs * hot_ref[...], axis=1, keepdims=True)
        scaled = (chosen * wide(cot_ref, base).astype(F32)).astype(BF16)
        grad[at, :] = scaled
        gdb_ref[...] += folded(scaled.astype(F32))
        total = None
        for k in range(2):
            value = (dot(scaled, downs[k][...], NT) * slope[k, at, :]).astype(BF16)
            pre[k, at, :] = value
            gub_ref[k] += folded(value.astype(F32))
            term = dot(value, ups[k][...], NT)
            total = term if k == 0 else total + term
        part[0, pl.ds(base, half)] = total.astype(BF16).reshape(half, hr, width)

    def results(base):
        at = pl.ds(pl.multiple_of(base * hr, size), size)
        total = dot(hid[0, at, :], downs[0][...], NN) + dot(hid[1, at, :], downs[1][...], NN)
        part[1, pl.ds(base, half)] = total.astype(BF16).reshape(half, hr, width)

    keep, there, arrived, passed, end = returning(n, qb, out_ref, send, recv)

    def grad_sum(k):
        to = (g + k) % n
        near_copy(k).wait_recv()
        qb[to] = (part[0, to, :, mine].astype(F32) + ra[k].astype(F32)).astype(BF16)

        @pl.when(k > 0)
        def _():
            there(k).start()

    eye = lax.broadcasted_iota(jnp.int32, (hr, LANES), 0) == lax.broadcasted_iota(jnp.int32, (hr, LANES), 1)

    def result_sum(k):
        to = (g + k) % n
        near_copy(n + k).wait_recv()
        value = part[1, to, :, mine].astype(F32) + ra[n + k].astype(F32) + db_ref[:, mine]
        value = value.astype(BF16)
        quarter_ref[to] = value
        gate = jnp.sum(cot_ref[to, :, mine].astype(F32) * value.astype(F32), axis=1, keepdims=True)
        gate_part[pl.ds(to, 1), :] = jnp.sum(jnp.where(eye, gate, 0.0), axis=0, keepdims=True)

    activate(0)
    activate(half)
    behind(0)
    behind(half)
    each(lambda t: near_copy(t).start(), 0, n)
    each(grad_sum, 0, n)
    keep()
    results(0)
    results(half)
    each(lambda t: near_copy(t).start(), n, n)
    each(result_sum, 0, n)
    gate_copy = sending(gate_part, gate_near, gate_send.at[0], gate_recv.at[0], near)
    gate_copy.wait_recv()
    gate_sum[...] = gate_part[...] + gate_near[...]
    gate_in[g] = gate_sum[...]
    gate_out = [
        sending(gate_sum, gate_in.at[g], gate_send.at[k], gate_recv.at[k], others[k - 1]) for k in range(1, n)
    ]

    cut = 256
    pieces = width // cut

    def weights(q):
        at = ds(q % pieces * cut, cut)
        for kind in range(2):
            for k in range(2):

                @pl.when(q // pieces == 2 * kind + 1 - k)
                def _(kind=kind, k=k):
                    if kind == 0:
                        value = dot(hid[k], grad[:, at], TN)
                    else:
                        value = dot(rows_ref[...].reshape(n * hr, width), pre[k, :, at], TN)
                    if k == 0:
                        gown_ref[kind, :, at] = value
                    else:
                        gother_ref[kind, :, at] = value.astype(BF16)

    lag = 3

    def step(i, _):
        @pl.when(i < 4 * pieces)
        def _():
            weights(i)

        @pl.when(i < n)
        def _():
            arrived(i)

        @pl.when((i >= lag) & (i < n + lag))
        def _():
            passed(i - lag)

        return 0

    lax.fori_loop(0, max(4 * pieces, n + lag), step, 0)
    for copy in gate_out:
        copy.wait_recv()
    for e in range(n):
        gates_ref[y, e : e + 1, :] = gate_in[e, pl.ds(g, 1), :]
    gate_far = sending(gates_ref.at[y], gates_ref.at[y], gate_send.at[n], gate_recv.at[n], far)
    each(end, 0, n)
    each(lambda t: near_copy(t).wait_send(), 0, 2 * n)
    gate_far.wait_recv()
    for copy in [gate_copy, gate_far] + gate_out:
        copy.wait_send()


GELU_A = 0.7978845608028654
GELU_B = 0.044715


def experts(n, collective_id, rows, cot, up, up_bias, down, up2, down2, up_bias2, down_bias, router, hot):
    _, hr, width = rows.shape
    hidden = up.shape[1]
    shape = jax.ShapeDtypeStruct
    gate = pltpu.VMEM((n, LANES), F32)
    return vmem_call(
        functools.partial(expert_kernel, n),
        [
            shape((n, 2 * hr, width), BF16),
            shape((n, hr, width // 2), BF16),
            shape((2, n, LANES), F32),
            shape((2, width, hidden), F32),
            shape((2, width, hidden), BF16),
            shape((2, SUB, hidden), F32),
            shape((SUB, width), F32),
        ],
        [
            pltpu.VMEM((2, n, hr, width), BF16),
            pltpu.VMEM((2, n * hr, hidden), BF16),
            pltpu.VMEM((2, n * hr, hidden), F32),
            pltpu.VMEM((2, n * hr, hidden), BF16),
            pltpu.VMEM((n * hr, width), BF16),
            pltpu.VMEM((2 * n, hr, width // 2), BF16),
            pltpu.VMEM((n, hr, width // 2), BF16),
            gate,
            gate,
            gate,
            pltpu.VMEM((n, n, LANES), F32),
            pltpu.SemaphoreType.DMA((4, n)),
            pltpu.SemaphoreType.DMA((4, n)),
            pltpu.SemaphoreType.DMA((2 * n,)),
            pltpu.SemaphoreType.DMA((2 * n,)),
            pltpu.SemaphoreType.DMA((n + 1,)),
            pltpu.SemaphoreType.DMA((n + 1,)),
        ],
        collective_id, rows, cot, up, up_bias, down, up2, down2, up_bias2, down_bias, router, hot,
    )


def finish_kernel(
    n,
    count,
    cuts,
    layout,
    part_ref,
    select_ref,
    inner_ref,
    base_ref,
    pre_ref,
    both_ref,
    lead_ref,
    gate_ref,
    normed_ref,
    weight_ref,
    taps_ref,
    given_ref,
    tok_ref,
    resid_ref,
    gain_ref,
    slot_ref,
    result_ref,
    residual_ref,
    chosen_ref,
    grad_ref,
    gin_ref,
    small_ref,
    first_ref,
    block_ref,
    conv_s,
    ext_s,
    both_s,
    got,
    part_s,
    sum_s,
    ra,
    sb,
    rb,
    blocks,
    pa,
    ps,
    pc,
    outs,
    firsts,
    rows_s,
    fold_s,
    low_s,
    proj_ref,
    qa,
    qs,
    qr,
    block_s,
    send,
    recv,
    gsend,
    grecv,
):
    mh, sh = layout
    g = lax.axis_index("dp")
    j, near, far = mp_pair()
    near, far = {"mp": near}, {"mp": far}
    odd, z, m = g % 2, g // 2, n // 2
    pair = {"dp": g + 1 - 2 * odd}
    like = [{"dp": 2 * ((z + k) % m) + odd} for k in range(1, m)]
    others = [{"dp": (g + k) % n} for k in range(1, n)]
    greet([near, far] + others)
    rows, chans = inner_ref.shape
    width = normed_ref.shape[1]
    kernel = taps_ref.shape[0]
    edge = (kernel - 1) * SUB
    block = 256
    half = rows // 2
    size = half // count
    own = (j % 2) * half
    other = (1 - j % 2) * half

    def lower(b, _):
        value = part_ref[pl.ds(pl.multiple_of(b * block + SUB, SUB), block), :]
        low_s[ds(b * block, block), :] = value.astype(BF16)
        return 0

    lax.fori_loop(0, rows // block, lower, 0)
    pieces = half // block
    q_one, q_two, q_three = [], [], []
    for k in range(pieces):
        at = ds(other + k * block, block)
        q_one.append(sending(low_s.at[at], qa.at[k], send.at[9, k], recv.at[9, k], near))
    for k in range(pieces):
        q_one[k].wait_recv()
        qs[k] = (low_s[ds(own + k * block, block), :].astype(F32) + qa[k].astype(F32)).astype(BF16)
        q_two.append(sending(qs.at[k], qr.at[k], send.at[10, k], recv.at[10, k], far))
    ext_s[0:edge, :] = lead_ref[...]

    def past_rows(b, _):
        at = ds(b * block, block)
        ext_s[pl.ds(pl.multiple_of(b * block + edge, SUB), block), :] = both_ref[at, 0:chans].astype(F32)
        return 0

    lax.fori_loop(0, rows // block, past_rows, 0)
    for k in range(pieces):
        q_two[k].wait_recv()
        at = ds(own + k * block, block)
        proj_ref[at, :] = (qs[k].astype(F32) + qr[k].astype(F32)).astype(BF16)
        q_three.append(sending(proj_ref.at[at], proj_ref.at[at], send.at[11, k], recv.at[11, k], near))
    for copy in q_three:
        copy.wait_recv()

    def conv_block(b):
        at = ds(b * block, block)
        grad = base_ref[at, :] + dot(proj_ref[at, :], select_ref[...], NT)
        conv_s[at, :] = grad * silu_slope(pre_ref[at, :])

    conv_block(0)
    head = sending(conv_s.at[0:edge], got, send.at[8, 0], recv.at[8, 0], {"dp": (g + n - 1) % n})

    def rest(b, _):
        conv_block(b)
        return 0

    lax.fori_loop(1, rows // block, rest, 0)
    given = given_ref.shape[0]
    selects = select_ref.shape[1]
    rest_at = given + selects
    fold_s[0:given, :] = given_ref[...]
    fold_s[given:rest_at, :] = dot(proj_ref[...], inner_ref[...], TN)
    folded = lambda v: jnp.sum(v.reshape(block // SUB, SUB, chans), axis=0)

    def taps(b, sums):
        grad = conv_s[ds(b * block, block), :]
        past = [ext_s[pl.ds(pl.multiple_of(b * block + k * SUB, SUB), block), :] for k in range(kernel)]
        return tuple(v + folded(grad * p) for v, p in zip(sums, past)) + (sums[kernel] + folded(grad),)

    zero = tuple(jnp.zeros((SUB, chans), F32) for _ in range(kernel + 1))
    sums = lax.fori_loop(0, rows // block, taps, zero)
    for k in range(kernel + 1):
        fold_s[rest_at + k : rest_at + k + 1, :] = jnp.sum(sums[k], axis=0, keepdims=True)
    head.wait_recv()
    upper = lax.broadcasted_iota(jnp.int32, (SUB, chans), 0) >= SUB // 2
    some = jnp.where(g < n - 1, 1.0, 0.0)
    for k in range(kernel - 1):
        at = slice(k * SUB, (k + 1) * SUB)
        tail = half_turn(jnp.where(upper, conv_s[at, :], got[at, :] * some))
        conv_s[rows + k * SUB : rows + (k + 1) * SUB, :] = tail

    def back(b, _):
        at = ds(b * block, block)
        total = jnp.zeros((block, chans), F32)
        for k in range(kernel):
            later = conv_s[pl.ds(pl.multiple_of(b * block + (kernel - 1 - k) * SUB, SUB), block), :]
            total = total + taps_ref[k : k + 1, :] * later
        both_s[at, 0:chans] = total.astype(BF16)
        both_s[at, chans : 2 * chans] = gate_ref[at, :]
        return 0

    lax.fori_loop(0, rows // block, back, 0)

    rows_s[0:width, :] = dot(normed_ref[...], both_s[:, 0:chans], TN)
    for b in range(n):
        blocks[b, 0:mh, :] = rows_s[b * mh : (b + 1) * mh, :].astype(BF16)
        blocks[b, mh : mh + sh, :] = fold_s[b * sh : (b + 1) * sh, :].astype(BF16)
    order = [(z + k) % m for k in range(1, m)] + [z]
    first = [
        sending(blocks.at[2 * order[k] + 1 - odd], pa.at[k], send.at[3, k], recv.at[3, k], pair)
        for k in range(m)
    ]
    one, two, three, second = [], [], [], []

    def input_rows(start):
        at = ds(start, size)
        part_s[at, :] = dot(both_s[at, :], weight_ref[...], NT).astype(BF16)

    for k in range(count):
        input_rows(other + k * size)
        at = ds(other + k * size, size)
        one.append(sending(part_s.at[at], ra.at[k], send.at[0, k], recv.at[0, k], near))
    for k in range(count):
        input_rows(own + k * size)
        one[k].wait_recv()
        mine = part_s[ds(own + k * size, size), :].astype(F32)
        sb[k] = (mine + ra[k].astype(F32)).astype(BF16)
        two.append(sending(sb.at[k], rb.at[k], send.at[1, k], recv.at[1, k], far))
    slots = result_ref.shape[0] * result_ref.shape[1]

    def output(b):
        at = ds(b * block, block)
        iota = lax.broadcasted_iota(jnp.int32, (block, slots), 1)
        pick = jnp.where(iota == slot_ref[at, :], 1.0, 0.0).astype(BF16)
        result = dot(pick, result_ref[...].reshape(slots, width), NN)
        value = residual_ref[at, :] + chosen_ref[at, :] * result
        for ct in range(width // LANES):
            block_s[ct, at, :] = value[:, ct * LANES : (ct + 1) * LANES]

    for k in range(m):
        first[k].wait_recv()
        ps[k] = (blocks[2 * order[k] + odd].astype(F32) + pa[k].astype(F32)).astype(BF16)
        if k < m - 1:
            second.append(sending(ps.at[k], pc.at[k], send.at[4, k], recv.at[4, k], like[k]))

    def far_sum(k):
        two[k].wait_recv()
        at = ds(own + k * size, size)
        sum_s[at, :] = (sb[k].astype(F32) + rb[k].astype(F32)).astype(BF16)
        three.append(sending(sum_s.at[at], sum_s.at[at], send.at[2, k], recv.at[2, k], near))

    output_blocks = rows // block
    for b in range(output_blocks // 2):
        output(b)
    value = ps[m - 1].astype(F32)
    for copy in second:
        copy.wait_recv()
    for k in range(m - 1):
        value = value + pc[k].astype(F32)
    outs[g] = value.astype(BF16)
    start, middle, end = gathering(n, outs, gsend, grecv)
    start()
    for b in range(output_blocks // 2, output_blocks):
        output(b)
    firsts[0] = jnp.zeros(firsts.shape[1:], F32)
    gain = gain_ref[...]

    def norm_rows(start):
        at = ds(start, size)
        grad = sum_s[at, :].astype(F32)
        tok = tok_ref[at, :].astype(F32)
        inverse = lax.rsqrt(jnp.mean(tok * tok, axis=1, keepdims=True) + norm_eps)
        normed = tok * inverse
        firsts[0] += jnp.sum((grad * normed).reshape(size // SUB, SUB, width), axis=0)
        scaled = grad * gain
        mean = jnp.mean(scaled * normed, axis=1, keepdims=True)
        value = resid_ref[at, :] + inverse * (scaled - normed * mean)
        for ct in range(width // LANES):
            grad_ref[ct, at, :] = value[:, ct * LANES : (ct + 1) * LANES]

    for k in range(count):
        far_sum(k)
        norm_rows(own + k * size)
    for p in range(PIECES):
        middle(p)
    for k in range(count):
        three[k].wait_recv()
        norm_rows(other + k * size)
    spread_first = [
        sending(firsts.at[0], firsts.at[k], send.at[7, k], recv.at[7, k], others[k - 1]) for k in range(1, n)
    ]
    restore(cuts, block_s, block_ref)
    for copy in spread_first:
        copy.wait_recv()

    def one_first(d, total):
        return total + firsts[(g + n - d) % n]

    first_ref[...] = lax.fori_loop(0, n, one_first, jnp.zeros(first_ref.shape, F32))
    end()
    for b in range(n):
        gin_ref[b * mh : (b + 1) * mh, :] = outs[b, 0:mh, :].astype(F32)
        small_ref[b * sh : (b + 1) * sh, :] = outs[b, mh : mh + sh, :].astype(F32)
    mp_copies = q_one + q_two + q_three + one + two + three
    for copy in [head] + mp_copies + first + second + spread_first:
        copy.wait_send()


def finish(n, collective_id, cuts, *args, count=4):
    select, inner, normed, taps, given = args[1], args[2], args[8], args[10], args[11]
    wide = select.shape[1]
    rows, chans = inner.shape
    width = normed.shape[1]
    kernel = taps.shape[0]
    edge = (kernel - 1) * SUB
    m = n // 2
    over = lambda size: (size + 16 * n - 1) // (16 * n) * 16
    mh, sh = over(width), over(given.shape[0] + select.shape[1] + kernel + 1)
    slots = pltpu.VMEM((count, rows // 2 // count, width), BF16)
    part = lambda k: pltpu.VMEM((k, mh + sh, chans), BF16)
    few = pltpu.VMEM((rows // 512, 256, wide), BF16)
    low = pltpu.VMEM((rows, wide), BF16)
    sems = pltpu.SemaphoreType.DMA((12, max(n, count)))
    shape = jax.ShapeDtypeStruct
    return vmem_call(
        functools.partial(finish_kernel, n, count, cuts, (mh, sh)),
        [
            shape((width // LANES, rows, LANES), F32),
            shape((n * mh, chans), F32),
            shape((n * sh, chans), F32),
            shape((SUB, width), F32),
            shape((rows, width), BF16),
        ],
        [
            pltpu.VMEM((rows + edge, chans), F32),
            pltpu.VMEM((rows + edge, chans), F32),
            pltpu.VMEM((rows, 2 * chans), BF16),
            pltpu.VMEM((edge, chans), F32),
            pltpu.VMEM((rows, width), BF16),
            pltpu.VMEM((rows, width), BF16),
            slots,
            slots,
            slots,
            part(n),
            part(m),
            part(m),
            part(m),
            part(n),
            pltpu.VMEM((n, SUB, width), F32),
            pltpu.VMEM((n * mh, chans), F32),
            pltpu.VMEM((n * sh, chans), F32),
            low,
            low,
            few,
            few,
            few,
            pltpu.VMEM((width // LANES, rows, LANES), F32),
            sems,
            sems,
            pltpu.SemaphoreType.DMA((2, PIECES * m)),
            pltpu.SemaphoreType.DMA((2, PIECES * m)),
        ],
        collective_id, *args,
    )


def token_back_kernel(
    n,
    slot_ref,
    back_ref,
    gates_ref,
    quarter_ref,
    residual_ref,
    hot_ref,
    cot_ref,
    valid_ref,
    gain_ref,
    router_ref,
    gated_ref,
    out_ref,
    scan_ref,
    both_ref,
    inner_ref,
    normed_in_ref,
    chosen_ref,
    resid_ref,
    gs_ref,
    gate_ref,
    early_ref,
    landed_ref,
    mixed_s,
    early_s,
    small_s,
    router_out,
    second_ref,
    skip_ref,
    send,
    recv,
):
    rows, width = residual_ref.shape
    chans = inner_ref.shape[1]
    slots = back_ref.shape[0] * back_ref.shape[1]
    hr = back_ref.shape[1] // 2
    g = lax.axis_index("dp")
    others = [{"dp": (g + k) % n} for k in range(1, n)]
    greet(others)
    copies = [
        sending(quarter_ref.at[(g + k) % n], landed_ref.at[g], send.at[k], recv.at[k], others[k - 1])
        for k in range(1, n)
    ]
    landed_ref[g] = quarter_ref[g]
    size = 256
    lanes = lax.broadcasted_iota(jnp.int32, (1, LANES), 1)
    router_out[...] = jnp.zeros_like(router_out)
    second_ref[...] = jnp.zeros_like(second_ref)
    skip_ref[...] = jnp.zeros_like(skip_ref)

    def body(b, _):
        at = ds(b * size, size)
        folded = lambda v: jnp.sum(v.reshape(size // SUB, SUB, v.shape[1]), axis=0)
        iota = lax.broadcasted_iota(jnp.int32, (size, slots), 1)
        slot = slot_ref[at, :]
        pick = jnp.where(iota == slot, 1.0, 0.0).astype(BF16)
        grad = dot(pick, back_ref[...].reshape(slots, width), NN)
        gates = jnp.zeros((size, LANES), F32)
        for e in range(n):
            for k in range(2):
                hit = slot - (2 * e + k) * hr == lanes
                gates = gates + jnp.where(hit, gates_ref[k, e : e + 1, :], 0.0)
        gate = jnp.sum(gates, axis=1, keepdims=True)
        residual = residual_ref[at, :]
        inverse = lax.rsqrt(jnp.mean(residual * residual, axis=1, keepdims=True) + norm_eps)
        normed = residual * inverse
        normed_low = (normed * gain_ref[...]).astype(BF16)
        hot = hot_ref[at, :]
        probs = jax.nn.softmax(dot(normed_low, router_ref[...], NN), axis=-1)
        chosen = jnp.sum(probs * hot, axis=1, keepdims=True)
        chosen_ref[at, :] = chosen
        cot = cot_ref[at, :].astype(F32)
        logit = (gate * probs * (hot - chosen)).astype(BF16)
        router_out[...] += dot(logit, normed_low, TN)
        grad = grad + dot(logit, router_ref[...], NT)
        second_ref[...] += folded(grad * normed)
        scaled = grad * gain_ref[...]
        mean = jnp.mean(scaled * normed, axis=1, keepdims=True)
        resid = cot + inverse * (scaled - normed * mean)
        resid_ref[at, :] = resid
        mixed = (valid_ref[at, :] * resid).astype(BF16)
        mixed_s[at, :] = mixed
        grad_gated = dot(mixed, out_ref[...], NT)
        pre = both_ref[at, chans : 2 * chans].astype(F32)
        sig = jax.nn.sigmoid(pre)
        act = pre * sig
        gs = grad_gated * act
        gs_ref[at, :] = gs
        skip_ref[...] += folded(gs * inner_ref[at, :].astype(F32))
        gate_ref[at, :] = (grad_gated * scan_ref[at, :] * (sig * (1.0 + pre * (1.0 - sig)))).astype(BF16)
        return 0

    lax.fori_loop(0, rows // size, body, 0)
    mh = early_s.shape[1] // n
    sh = early_ref.shape[1] - 2 * mh
    some = router_out.shape[0]
    for k in range(width // chans):
        at = slice(k * chans, (k + 1) * chans)
        small_s[k * some : (k + 1) * some, :] = router_out[:, at]
        line = 2 * some + k
        small_s[line : line + 1, :] = jnp.sum(second_ref[:, at], axis=0, keepdims=True)
    small_s[2 * some + 2 : 2 * some + 3, :] = jnp.sum(skip_ref[...], axis=0, keepdims=True)
    early_s[0, 0:width, :] = dot(normed_in_ref[...], gate_ref[...], TN)
    value = dot(gated_ref[...], mixed_s[...], TN)
    for k in range(width // chans):
        early_s[1, k * chans : (k + 1) * chans, :] = value[:, k * chans : (k + 1) * chans]
    for b in range(n):
        for k in range(2):
            early_ref[b, k * mh : (k + 1) * mh, :] = early_s[k, b * mh : (b + 1) * mh, :].astype(BF16)
        early_ref[b, 2 * mh : 2 * mh + sh, :] = small_s[b * sh : (b + 1) * sh, :].astype(BF16)
    for copy in copies:
        copy.wait_recv()
    for copy in copies:
        copy.wait_send()


def restore(cuts, tile_ref, out_ref):
    seqs, chunks, places = cuts
    for ct in range(tile_ref.shape[0]):
        for q in range(seqs):
            for k in range(chunks):
                picked = tile_ref[ct, pl.ds(k * seqs + q, places, stride=SUB), :]
                start = (q * chunks + k) * places
                out_ref[start : start + places, ct * LANES : (ct + 1) * LANES] = picked.astype(out_ref.dtype)


def token_back(n, collective_id, *args):
    quarter, residual, router, inner = args[3], args[4], args[9], args[14]
    over = lambda size: (size + 16 * n - 1) // (16 * n) * 16
    mh, sh = over(residual.shape[1]), over(2 * router.shape[1] + 3)
    rows, width = residual.shape
    chans = inner.shape[1]
    shape = jax.ShapeDtypeStruct
    sems = pltpu.SemaphoreType.DMA((n,))
    return vmem_call(
        functools.partial(token_back_kernel, n),
        [
            shape((rows, 1), F32),
            shape((rows, width), F32),
            shape((rows, chans), F32),
            shape((rows, chans), BF16),
            shape((n, 2 * mh + sh, chans), BF16),
            shape(quarter.shape, BF16),
        ],
        [
            pltpu.VMEM((rows, width), BF16),
            pltpu.VMEM((2, n * mh, chans), F32),
            pltpu.VMEM((n * sh, chans), F32),
            pltpu.VMEM((router.shape[1], width), F32),
            pltpu.VMEM((SUB, width), F32),
            pltpu.VMEM((SUB, chans), F32),
            sems,
            sems,
        ],
        collective_id, *args,
    )


def emit_kernel(
    layout,
    cuts,
    tile_ref,
    own_ref,
    far_ref,
    conv_ref,
    gate_ref,
    left_ref,
    right_ref,
    small_ref,
    few_ref,
    first_ref,
    ub_ref,
    far_bias_ref,
    db_ref,
    token_ref,
    down_ref,
    up_ref,
    in_ref,
    out_ref,
    taps_ref,
    cb_ref,
    select_ref,
    sw_ref,
    sb_ref,
    decay_ref,
    skip_ref,
    second_ref,
    router_ref,
    norm_ref,
    gub_ref,
    gdb_ref,
):
    restore(cuts, tile_ref, token_ref)
    rank, states, select_at, taps_at = layout
    down_ref[...] = own_ref[0] + far_ref[0].astype(F32)
    up_ref[...] = own_ref[1] + far_ref[1].astype(F32)
    in_ref[:, 0, :] = conv_ref[...]
    in_ref[:, 1, :] = gate_ref[...]
    chans = conv_ref.shape[1]
    out_ref[:, 0:chans] = left_ref[...]
    out_ref[:, chans : 2 * chans] = right_ref[...]

    @pl.when(pl.program_id(0) == 0)
    def _():
        kernel = taps_ref.shape[0]
        taps_ref[...] = small_ref[taps_at : taps_at + kernel, :]
        cb_ref[...] = small_ref[taps_at + kernel : taps_at + kernel + 1, :]
        select_ref[...] = small_ref[select_at:taps_at, :]
        sw_ref[...] = small_ref[0:rank, :]
        decay_ref[...] = small_ref[rank : rank + states, :]
        sb_ref[...] = small_ref[rank + states : rank + states + 1, :]
        some = router_ref.shape[0]
        line = 2 * some
        for k in range(2):
            at = slice(k * chans, (k + 1) * chans)
            router_ref[:, at] = few_ref[k * some : (k + 1) * some, :]
            second_ref[:, at] = few_ref[line + k : line + k + 1, :]
        skip_ref[...] = few_ref[line + 2 : line + 3, :]
        total = lambda v: jnp.sum(v, axis=0, keepdims=True)
        norm_ref[...] = total(first_ref[...])
        bias = far_bias_ref[...].astype(F32)
        gub_ref[...] = total(ub_ref[0] + bias[0:SUB])
        gdb_ref[...] = total(db_ref[...].astype(F32) + bias[SUB : 2 * SUB])


def emit(layout, cuts, tiles_, own, far, conv, gate, mixer, small, few, first, ub, far_bias, db, experts_all):
    width, chans = own.shape[1], conv.shape[1]
    hidden = own.shape[2]
    rank, states, select_at, taps_at = layout
    count, rows = tiles_.shape[0], tiles_.shape[1]
    cut, part = width // count, chans // count
    shape = jax.ShapeDtypeStruct
    block = lambda size, wide: pl.BlockSpec((size, wide), lambda i: (i, 0))
    both = lambda size, wide: pl.BlockSpec((2, size, wide), lambda i: (0, i, 0))
    shapes = [
        (4, chans),
        (1, chans),
        (taps_at - select_at, chans),
        (rank, chans),
        (1, chans),
        (states, chans),
        (1, chans),
        (1, width),
        (experts_all, width),
        (1, width),
        (1, hidden),
        (1, width),
    ]
    return pl.pallas_call(
        functools.partial(emit_kernel, layout, cuts),
        grid=(count,),
        in_specs=[
            pl.BlockSpec((1, rows, LANES), lambda i: (i, 0, 0)),
            both(cut, hidden),
            both(cut, hidden),
            block(cut, chans),
            block(cut, chans),
            block(part, chans),
            pl.BlockSpec((part, chans), lambda i: (i + count, 0)),
            whole(*small.shape),
            whole(*few.shape),
            whole(*first.shape),
            whole(*ub.shape),
            whole(*far_bias.shape),
            whole(*db.shape),
        ],
        out_specs=[
            pl.BlockSpec((rows, LANES), lambda i: (0, i)),
            block(cut, hidden),
            block(cut, hidden),
            pl.BlockSpec((cut, 2, chans), lambda i: (i, 0, 0)),
            block(part, width),
            *[whole(*dims) for dims in shapes],
        ],
        out_shape=[
            shape((rows, count * LANES), F32),
            shape((width, hidden), F32),
            shape((width, hidden), F32),
            shape((width, 2, chans), F32),
            shape((chans, width), F32),
            *[shape(dims, F32) for dims in shapes],
        ],
        compiler_params=pltpu.CompilerParams(vmem_limit_bytes=VMEM),
    )(tiles_, own, far, conv, gate, mixer, mixer, small, few, first, ub, far_bias, db)


def silu_slope(values):
    sigmoid_vals = jax.nn.sigmoid(values)
    return sigmoid_vals * (1.0 + values * (1.0 - sigmoid_vals))


def per_device(
    tokens,
    routes,
    lengths,
    cotangent,
    first_gain,
    mixer_in,
    conv_weight,
    conv_bias,
    select_weight,
    step_weight,
    step_bias,
    decay_log,
    skip_gain,
    mixer_out,
    second_gain,
    router_weight,
    expert_up,
    up_bias,
    expert_down,
    down_bias,
):
    tok_count, model_width = tokens.shape
    kernel, chan_count = conv_weight.shape
    rank_size = step_weight.shape[0]
    state_size = decay_log.shape[0]
    expert_total = router_weight.shape[1]
    capacity = max(2, (5 * tok_count + 4 * expert_total - 1) // (4 * expert_total))
    room = (capacity + 31) // 32 * 32
    slot_dev = SLOT_DEV
    seq_count = tok_count // slot_dev
    chunks = SUB // seq_count
    places_dev = slot_dev // chunks
    cuts = (seq_count, chunks, places_dev)
    device = lax.axis_index("dp")
    dp_count = lax.axis_size("dp")

    mp_count = lax.axis_size("mp")
    to_far = [(i, (i + mp_count // 2) % mp_count) for i in range(mp_count)]
    swap_far = lambda values: lax.ppermute(values, "mp", to_far)
    far_up = swap_far(expert_up[0])

    first_vals = first_gain.astype(F32)
    second_vals = second_gain.astype(F32)
    mixer_in_flat = mixer_in.reshape(model_width, 2 * chan_count)
    conv_taps = conv_weight.astype(F32)
    routes_cut = routes.reshape(seq_count, chunks, places_dev).transpose(2, 1, 0)
    (
        tok_low,
        cot_low,
        normed_in,
        both_in,
        conv_pre,
        inner_vals,
        lead_rows,
        projected,
        cot_quarter,
        slot_ids,
        half_slots,
        valid_col,
        route_hot,
    ) = front(
        dp_count,
        0,
        cuts,
        capacity,
        room // 2,
        expert_total,
        tokens,
        cotangent,
        routes_cut.reshape(tok_count, 1),
        lengths[None],
        first_vals[None],
        mixer_in_flat,
        conv_taps,
        conv_bias.astype(F32)[None],
        select_weight,
    )
    own_down, own_bias, projected = lax.optimization_barrier(
        (expert_down[0], jnp.broadcast_to(up_bias, (16, up_bias.shape[1])), projected)
    )
    far_down, far_bias = swap_far((own_down, own_bias))
    decay_rates = -jnp.exp(decay_log.astype(F32))
    rates = decay_rates * LOG2E

    step_p, drive_p, step_slope, bin_p, cout_p, low_high, chunk_steps, state_in, totals = enter_forward(
        dp_count,
        2,
        projected,
        step_weight,
        step_bias.astype(F32)[None],
        inner_vals,
        valid_col,
        rates,
    )
    skip_vals = skip_gain.astype(F32)
    scan_out, gated_vals, mixed, states_before, last_states, cot_rows = forward(
        10,
        step_p,
        drive_p,
        bin_p,
        cout_p,
        rates,
        state_in,
        inner_vals,
        both_in,
        skip_vals[None],
        mixer_out,
        cot_quarter,
    )
    residual, expert_rows = mixer_to_experts(
        dp_count, 3, room // 2, mixed, tok_low, valid_col, second_vals[None], half_slots
    )

    own_hot = (jnp.arange(expert_total) == device).astype(F32)[None]
    returned, quarters, gates, grad_own, grad_other, up_bias_parts, down_bias_part = experts(
        dp_count,
        5,
        expert_rows,
        cot_rows,
        expert_up[0],
        up_bias.astype(F32),
        expert_down[0],
        far_up,
        far_down,
        far_bias[:1].astype(F32),
        down_bias.astype(F32),
        router_weight,
        own_hot,
    )
    down_bias_part = down_bias_part.astype(BF16)
    bias_rows = jnp.concatenate([up_bias_parts[1].astype(BF16), down_bias_part], axis=0)
    from_far = swap_far((grad_other, bias_rows))
    (
        chosen,
        grad_resid,
        grad_scan,
        grad_gate_low,
        early,
        landed,
    ) = token_back(
        dp_count,
        11,
        slot_ids,
        returned,
        gates,
        quarters,
        residual,
        route_hot,
        cot_low,
        valid_col,
        second_vals[None],
        router_weight,
        gated_vals,
        mixer_out,
        scan_out,
        both_in,
        inner_vals,
        normed_in,
    )
    gs_p = grad_scan.reshape(places_dev, SUB, chan_count)
    grad_in, early = enter_backward(
        dp_count, 6, step_p, gs_p, cout_p, chunk_steps, rates, totals, early
    )
    mixer_rows = (model_width + 16 * dp_count - 1) // (16 * dp_count) * 16
    grad_base, proj_part, given, grad_gate_in, grad_mixer_out, few, results = backward(
        dp_count,
        9,
        mixer_rows,
        step_p,
        drive_p,
        gs_p,
        bin_p,
        cout_p,
        rates,
        grad_in,
        last_states,
        states_before,
        inner_vals,
        step_slope,
        low_high,
        jnp.pad(step_weight, ((0, 2 * state_size), (0, 0))),
        skip_vals[None],
        early,
        landed,
    )
    grad_tiles, grad_conv_half, small, grad_first, block_out = finish(
        dp_count,
        8,
        cuts,
        proj_part,
        select_weight,
        inner_vals,
        grad_base,
        conv_pre,
        both_in,
        lead_rows,
        grad_gate_low,
        normed_in,
        mixer_in_flat,
        conv_taps,
        given,
        tok_low,
        grad_resid,
        first_vals[None],
        slot_ids,
        results,
        residual,
        chosen,
    )
    select_at = given.shape[0]
    taps_at = select_at + select_weight.shape[1]
    (
        token_grad,
        grad_down,
        grad_up,
        grad_mixer_in,
        grad_mixer_full,
        grad_taps,
        grad_conv_bias,
        grad_select,
        grad_step_weight,
        grad_step_bias,
        grad_decay_log,
        grad_skip,
        grad_second,
        grad_router,
        grad_gain,
        grad_up_bias,
        grad_down_bias,
    ) = emit(
        (rank_size, state_size, select_at, taps_at),
        cuts,
        grad_tiles,
        grad_own,
        from_far[0],
        grad_conv_half,
        grad_gate_in,
        grad_mixer_out,
        small,
        few,
        grad_first,
        up_bias_parts,
        from_far[1],
        down_bias_part,
        expert_total,
    )
    return (
        block_out,
        token_grad,
        grad_gain[0],
        grad_mixer_in,
        grad_taps,
        grad_conv_bias[0],
        grad_select.T,
        grad_step_weight,
        grad_step_bias[0],
        grad_decay_log,
        grad_skip[0],
        grad_mixer_full,
        grad_second[0],
        grad_router.T,
        grad_up[None],
        grad_up_bias,
        grad_down[None],
        grad_down_bias,
    )


def solution(mesh):
    return jax.shard_map(
        per_device,
        mesh=mesh,
        in_specs=(
            P("dp", None),
            P("dp", None),
            P(),
            P("dp", None),
            P(),
            P(None, None, "mp"),
            P(None, "mp"),
            P("mp"),
            P("mp", None),
            P(None, "mp"),
            P("mp"),
            P(None, "mp"),
            P("mp"),
            P("mp", None),
            P(),
            P(),
            P("dp", None, "mp"),
            P("dp", "mp"),
            P("dp", "mp", None),
            P("dp", None),
        ),
        out_specs=(
            P("dp", None),
            P("dp", None),
            P(),
            P(None, None, "mp"),
            P(None, "mp"),
            P("mp"),
            P("mp", None),
            P(None, "mp"),
            P("mp"),
            P(None, "mp"),
            P("mp"),
            P("mp", None),
            P(),
            P(),
            P("dp", None, "mp"),
            P("dp", "mp"),
            P("dp", "mp", None),
            P("dp", None),
        ),
        check_vma=False,
    )
```

```python
import functools

import jax
import jax.numpy as jnp
from jax import lax
from jax.experimental import pallas as pl
from jax.experimental.pallas import tpu as pltpu
from jax.sharding import PartitionSpec as P

F32 = jnp.float32
BF16 = jnp.bfloat16
SLOT_DEV = 256
LANES = 128
SUB = 8
LOG2E = 1.4426950408889634
LN2 = 0.6931471805599453
VMEM = 48 * 2**20
norm_eps = 1e-05
MESH = pl.DeviceIdType.MESH


NN = ((1,), (0,))
NT = ((1,), (1,))
TN = ((0,), (0,))


def dot(a, b, dims):
    return lax.dot_general(a, b, (dims, ((), ())), preferred_element_type=F32)


def lane(col):
    return jnp.broadcast_to(col, (SUB, LANES))


def row(ref, n, cs):
    return jnp.broadcast_to(ref[n : n + 1, cs], (SUB, LANES))


def tiles(count):
    return [slice(ct * LANES, (ct + 1) * LANES) for ct in range(count // LANES)]


def whole(*dims):
    return pl.BlockSpec(dims, lambda i: (0,) * len(dims))


def local_scan(step_ref, in_ref, map_ref, rates_ref, out_ref, nh, half, reverse):
    places, chans = step_ref.shape[0], step_ref.shape[2]
    cols = tiles(chans)
    ns = [nh * half + n for n in range(half)]

    def body(lap, st):
        i = places - 1 - lap if reverse else lap
        st = list(st)
        m = map_ref[i]
        mm = [lane(m[:, n : n + 1]) for n in ns]
        for ct, cs in enumerate(cols):
            s = step_ref[i, :, cs]
            x = in_ref[i, :, cs]
            for n in range(half):
                k = n * len(cols) + ct
                e = jnp.exp2(s * row(rates_ref, ns[n], cs))
                st[k] = e * (st[k] + x * mm[n]) if reverse else e * st[k] + x * mm[n]
        return tuple(st)

    zero = tuple(jnp.zeros((SUB, LANES), F32) for _ in range(half * len(cols)))
    st = lax.fori_loop(0, places, body, zero, unroll=8)
    for n in range(half):
        for ct, cs in enumerate(cols):
            out_ref[ns[n], :, cs] = st[n * len(cols) + ct]


def block_sums(part_s, sum_s, ra, sb, rb, send, recv):
    j, near, far = mp_pair()
    c = j % 2
    size = ra.shape[1]
    mine, theirs = ds(c * size, size), ds((1 - c) * size, size)

    def copy(kind, b, src, dst, to):
        return pltpu.make_async_remote_copy(
            src_ref=src,
            dst_ref=dst,
            send_sem=send.at[kind, b],
            recv_sem=recv.at[kind, b],
            device_id={"mp": to},
            device_id_type=MESH,
        )

    one = lambda b: copy(0, b, part_s.at[b, theirs], ra.at[b], near)
    two = lambda b: copy(1, b, sb.at[b], rb.at[b], far)
    three = lambda b: copy(2, b, sum_s.at[b, mine], sum_s.at[b, mine], near)

    def pair_sum(b):
        one(b).wait_recv()
        sb[b] = (part_s[b, mine, :].astype(F32) + ra[b].astype(F32)).astype(BF16)
        two(b).start()

    def far_sum(b):
        two(b).wait_recv()
        sum_s[b, mine, :] = (sb[b].astype(F32) + rb[b].astype(F32)).astype(BF16)
        three(b).start()

    def end(count):
        for b in range(count):
            three(b).wait_recv()
        for b in range(count):
            for made in (one, two, three):
                made(b).wait_send()

    return lambda b: one(b).start(), pair_sum, far_sum, end


def forward_kernel(
    step_ref,
    x_ref,
    bin_ref,
    cout_ref,
    rates_ref,
    h0_ref,
    inner_ref,
    gate_ref,
    skip_ref,
    weight_ref,
    quarter_ref,
    scan_ref,
    gated_ref,
    sum_ref,
    hb_ref,
    hf_ref,
    rows_ref,
    st_ref,
    y_ref,
    part_s,
    sum_s,
    rows_s,
    ra,
    sb,
    rb,
    send,
    recv,
    dsend,
    drecv,
    local,
):
    places, chans = step_ref.shape[0], step_ref.shape[2]
    states, half = rates_ref.shape[0], 8
    cols = tiles(chans)
    n = quarter_ref.shape[0]
    g = lax.axis_index("dp")
    _, near, far = mp_pair()
    i_block, count = pl.program_id(0), part_s.shape[0]
    leave, pair_sum, far_sum, sums_end = block_sums(part_s, sum_s, ra, sb, rb, send, recv)
    start, middle, end = dispatching(n, quarter_ref, rows_s, dsend, drecv, local)

    @pl.when(i_block == 0)
    def _():
        greet([{"mp": near}, {"mp": far}] + [{"dp": (g + k) % n} for k in range(1, n)])
        start()

    @pl.when(pl.program_id(0) == 0)
    def _():
        st_ref[...] = h0_ref[...]

    for nh in range(states // half):
        ns = [nh * half + n for n in range(half)]

        def body(i, st):
            st = list(st)
            b = bin_ref[i]
            c = cout_ref[i]
            bb = [lane(b[:, n : n + 1]) for n in ns]
            cc = [lane(c[:, n : n + 1]) for n in ns]
            for ct, cs in enumerate(cols):
                s = step_ref[i, :, cs]
                x = x_ref[i, :, cs]
                y = y_ref[i, :, cs] if nh else jnp.zeros((SUB, LANES), F32)
                for n in range(half):
                    k = n * len(cols) + ct
                    hb_ref[i, ns[n], :, cs] = st[k].astype(hb_ref.dtype)
                    e = jnp.exp2(s * row(rates_ref, ns[n], cs))
                    st[k] = e * st[k] + x * bb[n]
                    y = y + cc[n] * st[k]
                y_ref[i, :, cs] = y
            return tuple(st)

        st = tuple(st_ref[n, :, cs] for n in ns for cs in cols)
        st = lax.fori_loop(0, places, body, st, unroll=8)
        for n in range(half):
            for ct, cs in enumerate(cols):
                st_ref[ns[n], :, cs] = st[n * len(cols) + ct]
    hf_ref[...] = st_ref[...]
    scan = y_ref[...].reshape(places * SUB, chans) + skip_ref[...] * inner_ref[...].astype(F32)
    scan_ref[...] = scan
    gate = gate_ref[...].astype(F32)
    gated = (scan * (gate * jax.nn.sigmoid(gate))).astype(BF16)
    gated_ref[...] = gated
    part_s[i_block] = dot(gated, weight_ref[...], NN).astype(BF16)
    leave(i_block)
    lag = 5

    @pl.when(i_block >= 1)
    def _():
        pair_sum(i_block - 1)

    @pl.when(i_block >= lag)
    def _():
        far_sum(i_block - lag)

    @pl.when(i_block == count - 2)
    def _():
        middle()

    @pl.when(i_block == count - 1)
    def _():
        pair_sum(count - 1)
        for b in range(count - lag, count):
            far_sum(b)
        end()
        rows_ref[...] = rows_s[...]
        sums_end(count)
        sum_ref[...] = sum_s[...].reshape(sum_ref.shape)


def forward(collective_id, step, x, bin_vals, cout, rates, h0, inner, both, skip, weight, quarter, block=16):
    places, _, chans = step.shape
    n, hr, hc = quarter.shape
    count = places // block
    sems = pltpu.SemaphoreType.DMA((3, count))
    dsems = pltpu.SemaphoreType.DMA((2, n))
    states = rates.shape[0]
    width = weight.shape[1]
    rows = places * SUB
    part = lambda size: pl.BlockSpec((block, SUB, size), lambda i: (i, 0, 0))
    flat = lambda size, col=0: pl.BlockSpec((block * SUB, size), lambda i: (i, col))
    shape = jax.ShapeDtypeStruct
    return pl.pallas_call(
        forward_kernel,
        grid=(count,),
        in_specs=[
            part(chans),
            part(chans),
            part(states),
            part(states),
            whole(states, chans),
            whole(states, SUB, chans),
            flat(chans),
            flat(chans, 1),
            whole(1, chans),
            whole(chans, width),
            whole(n, hr, hc),
        ],
        out_specs=[
            flat(chans),
            flat(chans),
            whole(rows, width),
            pl.BlockSpec((block, states, SUB, chans), lambda i: (i, 0, 0, 0)),
            whole(states, SUB, chans),
            whole(n, hr, 2 * hc),
        ],
        out_shape=[
            shape((rows, chans), F32),
            shape((rows, chans), BF16),
            shape((rows, width), BF16),
            shape((places, states, SUB, chans), BF16),
            shape((states, SUB, chans), F32),
            shape((n, hr, 2 * hc), BF16),
        ],
        scratch_shapes=[
            pltpu.VMEM((states, SUB, chans), F32),
            pltpu.VMEM((block, SUB, chans), F32),
            pltpu.VMEM((count, block * SUB, width), BF16),
            pltpu.VMEM((count, block * SUB, width), BF16),
            pltpu.VMEM((n, hr, 2 * hc), BF16),
            pltpu.VMEM((count, block * SUB // 2, width), BF16),
            pltpu.VMEM((count, block * SUB // 2, width), BF16),
            pltpu.VMEM((count, block * SUB // 2, width), BF16),
            sems,
            sems,
            dsems,
            dsems,
            pltpu.SemaphoreType.DMA,
        ],
        compiler_params=pltpu.CompilerParams(
            collective_id=collective_id, has_side_effects=True, vmem_limit_bytes=VMEM
        ),
    )(step, x, bin_vals, cout, rates, h0, inner, both, skip, weight, quarter)


def backward_kernel(
    n,
    step_ref,
    x_ref,
    gs_ref,
    past_ref,
    bin_ref,
    cout_ref,
    rates_ref,
    g0_ref,
    hf_ref,
    hb_ref,
    inner_ref,
    slope_ref,
    low_ref,
    weight_ref,
    skip_ref,
    early_ref,
    landed_ref,
    base_ref,
    proj_out,
    given_ref,
    gin_ref,
    gout_ref,
    few_ref,
    result_ref,
    sbias_ref,
    gst_ref,
    rt_ref,
    q_ref,
    p_ref,
    sg_ref,
    sb_ref,
    gp_ref,
    sums,
    result_s,
    proj_ref,
    part_s,
    sum_s,
    qa,
    qs,
    qr,
    send,
    recv,
    rsend,
    rrecv,
    qsend,
    qrecv,
):
    places, chans = step_ref.shape[0], step_ref.shape[2]
    states, some = rates_ref.shape[0], 4
    cols = tiles(chans)
    g = lax.axis_index("dp")
    j, near, far = mp_pair()
    y, c = j // 2, j % 2
    hr, hc = landed_ref.shape[1], landed_ref.shape[2]
    up, down, mine = ds(y * hr, hr), ds((1 - y) * hr, hr), ds(c * hc, hc)
    start, middle, end = gathering(n, sums, send, recv)

    def share(kind, src, dst, to):
        return pltpu.make_async_remote_copy(
            src_ref=src,
            dst_ref=dst,
            send_sem=rsend.at[kind],
            recv_sem=rrecv.at[kind],
            device_id={"mp": to},
            device_id_type=MESH,
        )

    place = lambda rows: result_s.at[:, rows, mine]
    to_far = share(0, landed_ref, place(up), far)
    to_near = share(1, landed_ref, place(up), near)
    pass_on = share(2, place(down), place(down), near)
    step_id, steps = pl.program_id(0), pl.num_programs(0)

    @pl.when(step_id == 0)
    def _():
        greet([{"mp": near}, {"mp": far}] + [{"dp": (g + k) % n} for k in range(1, n)])
        sums[g] = early_ref[...]
        start()
        to_far.start()
        to_near.start()
        result_s[:, up, mine] = landed_ref[...]

    @pl.when(step_id == steps // 2 - 1)
    def _():
        middle(0)

    @pl.when(step_id == steps // 2 + 2)
    def _():
        middle(1)

    @pl.when(step_id == steps - 2)
    def _():
        to_far.wait_recv()
        pass_on.start()

    @pl.when(pl.program_id(0) == 0)
    def _():
        gst_ref[...] = g0_ref[...]
        rt_ref[...] = jnp.zeros_like(rt_ref)
        given_ref[...] = jnp.zeros_like(given_ref)
        proj_ref[...] = jnp.zeros_like(proj_ref)
        sbias_ref[...] = jnp.zeros_like(sbias_ref)

    gp_ref[0] = past_ref[0]
    gp_ref[1:places] = gs_ref[0 : places - 1]

    for nq in range(states // some):
        ns = [nq * some + n for n in range(some)]
        size = some * len(cols)

        def body(lap, carry):
            i = places - 1 - lap
            st, rt = list(carry[:size]), list(carry[size:])
            b = bin_ref[i]
            c = cout_ref[i]
            bb = [lane(b[:, n : n + 1]) for n in ns]
            cc = [lane(c[:, n : n + 1]) for n in ns]
            qb, qc = [None] * some, [None] * some
            for ct, cs in enumerate(cols):
                s = step_ref[i, :, cs]
                x = x_ref[i, :, cs]
                g = gs_ref[i, :, cs]
                gp = gp_ref[i, :, cs]
                sg = sg_ref[i, :, cs] if nq else jnp.zeros((SUB, LANES), F32)
                sb = sb_ref[i, :, cs] if nq else jnp.zeros((SUB, LANES), F32)
                for n in range(some):
                    k = n * len(cols) + ct
                    rate = row(rates_ref, ns[n], cs)
                    e = jnp.exp2(s * rate)
                    h = hb_ref[i, ns[n], :, cs].astype(F32)
                    grad = st[k] + g * cc[n]
                    st[k] = e * grad
                    dg = st[k] * h
                    sg = sg + dg * rate
                    rt[k] = rt[k] + dg * s
                    sb = sb + grad * bb[n]
                    qb[n] = grad * x if ct == 0 else qb[n] + grad * x
                    qc[n] = gp * h if ct == 0 else qc[n] + gp * h
                sg_ref[i, :, cs] = sg
                sb_ref[i, :, cs] = sb
            rows = pl.ds(pl.multiple_of(i * SUB, SUB), SUB)
            for n in range(some):
                q_ref[rows, ns[n] * LANES : (ns[n] + 1) * LANES] = qb[n]
                p_ref[rows, ns[n] * LANES : (ns[n] + 1) * LANES] = qc[n]
            return tuple(st) + tuple(rt)

        at = [(ns[n], slice(None), cs) for n in range(some) for cs in cols]
        init = tuple(gst_ref[a] for a in at) + tuple(rt_ref[a] for a in at)
        out = lax.fori_loop(0, places, body, init, unroll=8)
        for j, a in enumerate(at):
            gst_ref[a] = out[j]
            rt_ref[a] = out[size + j]
    rank = low_ref.shape[1]
    wide = proj_ref.shape[1]
    dims = (states * LANES, wide)
    state = lax.broadcasted_iota(jnp.int32, dims, 0) // LANES
    column = lax.broadcasted_iota(jnp.int32, dims, 1)
    to_bin = jnp.where(column == state + rank, 1.0, 0.0).astype(BF16)
    to_cout = jnp.where(column == state + rank + states, 1.0, 0.0).astype(BF16)
    block_rows = places * SUB
    base = (pl.num_programs(0) - 1 - pl.program_id(0)) * block_rows
    here = pl.ds(pl.multiple_of(base + SUB, SUB), block_rows)
    late = pl.ds(pl.multiple_of(base, SUB), block_rows)

    @pl.when(pl.program_id(0) == 0)
    def _():
        end_rows = pl.ds(pl.multiple_of(base + block_rows, SUB), SUB)
        total_ = None
        for n_ in range(states):
            value = hf_ref[n_, :, cols[0]] * gs_ref[places - 1, :, cols[0]]
            for cs in cols[1:]:
                value = value + hf_ref[n_, :, cs] * gs_ref[places - 1, :, cs]
            term = jnp.dot(
                value.astype(BF16), to_cout[n_ * LANES : (n_ + 1) * LANES], preferred_element_type=F32
            )
            total_ = term if total_ is None else total_ + term
        proj_ref[end_rows, :] += total_

    proj_ref[late, :] += jnp.dot(p_ref[...].astype(BF16), to_cout, preferred_element_type=F32)
    flat = lambda ref: ref[...].reshape(places * SUB, chans)
    sb = flat(sb_ref)
    base_ref[...] = flat(gs_ref) * skip_ref[...] + flat(step_ref) * sb
    pre = (flat(sg_ref) * LN2 + inner_ref[...].astype(F32) * sb) * slope_ref[...]
    sbias_ref[...] += jnp.sum(pre.reshape(places, SUB, chans), axis=0)
    pre = pre.astype(BF16)
    given_ref[0:rank, :] += dot(low_ref[...], pre, TN)
    proj_ref[here, :] += dot(pre, weight_ref[...], NT) + jnp.dot(
        q_ref[...].astype(BF16), to_bin, preferred_element_type=F32
    )

    blocks = part_s.shape[0]
    at_block = blocks - 1 - step_id
    leave, pair_sum, far_sum, sums_end = block_sums(part_s, sum_s, qa, qs, qr, qsend, qrecv)
    part_s[at_block] = proj_ref[here, :].astype(BF16)
    leave(at_block)

    @pl.when(step_id >= 1)
    def _():
        pair_sum(at_block + 1)

    @pl.when(step_id >= 5)
    def _():
        far_sum(at_block + 5)

    @pl.when(pl.program_id(0) == pl.num_programs(0) - 1)
    def _():
        pair_sum(0)
        for b in (4, 3, 2, 1, 0):
            far_sum(b)
        sums_end(blocks)
        proj_out[...] = sum_s[...].reshape(proj_out.shape)
        end()
        to_near.wait_recv()
        pass_on.wait_recv()
        for made in (to_far, to_near, pass_on):
            made.wait_send()
        result_ref[...] = result_s[...]
        for n_ in range(states):
            line = rank + n_
            total_ = jnp.sum(rt_ref[n_], axis=0, keepdims=True)
            given_ref[line : line + 1, :] = total_ * rates_ref[n_ : n_ + 1, :] * LN2
        line = rank + states
        given_ref[line : line + 1, :] = jnp.sum(sbias_ref[...], axis=0, keepdims=True)
        mh = gin_ref.shape[0] // n
        sh = few_ref.shape[0] // n
        for b in range(n):
            few_ref[b * sh : (b + 1) * sh, :] = sums[b, 2 * mh : 2 * mh + sh, :].astype(F32)
            gin_ref[b * mh : (b + 1) * mh, :] = sums[b, 0:mh, :].astype(F32)
            gout_ref[b * mh : (b + 1) * mh, :] = sums[b, mh : 2 * mh, :].astype(F32)


def backward(
    n, collective_id, mh, step, x, gs, bin_vals, cout, rates, g0, hf, hb, inner, slope, low, weight, skip, early, quarter, block=16
):
    places, _, chans = step.shape
    states = rates.shape[0]
    rank, wide = low.shape[1], weight.shape[0]
    extra = (rank + states + SUB) // SUB * SUB
    count = places // block
    part = lambda width: pl.BlockSpec((block, SUB, width), lambda i: (count - 1 - i, 0, 0))
    flat = lambda width: pl.BlockSpec((block * SUB, width), lambda i: (count - 1 - i, 0))
    rows = places * SUB
    tall = n * mh
    proj_blocks = pltpu.VMEM((count, block * SUB, wide), BF16)
    proj_halves = pltpu.VMEM((count, block * SUB // 2, wide), BF16)
    few = n * (early.shape[0] - 2 * mh)
    sems = pltpu.SemaphoreType.DMA((2, PIECES * n // 2))
    return pl.pallas_call(
        functools.partial(backward_kernel, n),
        grid=(count,),
        in_specs=[
            part(chans),
            part(chans),
            part(chans),
            pl.BlockSpec((1, SUB, chans), lambda i: (jnp.maximum((count - 1 - i) * block - 1, 0), 0, 0)),
            part(states),
            part(states),
            whole(states, chans),
            whole(states, SUB, chans),
            whole(states, SUB, chans),
            pl.BlockSpec((block, states, SUB, chans), lambda i: (count - 1 - i, 0, 0, 0)),
            flat(chans),
            flat(chans),
            flat(rank),
            whole(wide, chans),
            whole(1, chans),
            whole(*early.shape),
            whole(*quarter.shape),
        ],
        out_specs=[
            flat(chans),
            whole(rows, wide),
            whole(extra, chans),
            whole(tall, chans),
            whole(tall, chans),
            whole(few, chans),
            whole(n, 2 * quarter.shape[1], 2 * quarter.shape[2]),
        ],
        out_shape=[
            jax.ShapeDtypeStruct((rows, chans), F32),
            jax.ShapeDtypeStruct((rows, wide), BF16),
            jax.ShapeDtypeStruct((extra, chans), F32),
            jax.ShapeDtypeStruct((tall, chans), F32),
            jax.ShapeDtypeStruct((tall, chans), F32),
            jax.ShapeDtypeStruct((few, chans), F32),
            jax.ShapeDtypeStruct((n, 2 * quarter.shape[1], 2 * quarter.shape[2]), BF16),
        ],
        scratch_shapes=[
            pltpu.VMEM((SUB, chans), F32),
            pltpu.VMEM((states, SUB, chans), F32),
            pltpu.VMEM((states, SUB, chans), F32),
            pltpu.VMEM((block * SUB, states * LANES), F32),
            pltpu.VMEM((block * SUB, states * LANES), F32),
            pltpu.VMEM((block, SUB, chans), F32),
            pltpu.VMEM((block, SUB, chans), F32),
            pltpu.VMEM((block, SUB, chans), F32),
            pltpu.VMEM((n, *early.shape), BF16),
            pltpu.VMEM((n, 2 * quarter.shape[1], 2 * quarter.shape[2]), BF16),
            pltpu.VMEM((rows + SUB, wide), F32),
            proj_blocks,
            proj_blocks,
            proj_halves,
            proj_halves,
            proj_halves,
            sems,
            sems,
            pltpu.SemaphoreType.DMA((3,)),
            pltpu.SemaphoreType.DMA((3,)),
            pltpu.SemaphoreType.DMA((3, count)),
            pltpu.SemaphoreType.DMA((3, count)),
        ],
        compiler_params=pltpu.CompilerParams(
            collective_id=collective_id, has_side_effects=True, vmem_limit_bytes=VMEM
        ),
    )(step, x, gs, gs, bin_vals, cout, rates, g0, hf, hb, inner, slope, low, weight, skip, early, quarter)


def mp_pair():
    j = lax.axis_index("mp")
    return j, j + 1 - 2 * (j % 2), (j + 2) % 4


def ds(start, size):
    return pl.ds(pl.multiple_of(start, size), size)


def greet(others):
    barrier = pltpu.get_barrier_semaphore()
    for other in others:
        pl.semaphore_signal(barrier, inc=1, device_id=other, device_id_type=MESH)
    pl.semaphore_wait(barrier, len(others))


def sending(src, dst, send, recv, device):
    copy = pltpu.make_async_remote_copy(
        src_ref=src, dst_ref=dst, send_sem=send, recv_sem=recv, device_id=device, device_id_type=MESH
    )
    copy.start()
    return copy


def vmem_call(kernel, out_shape, scratch, collective_id, *args, cost=0):
    space = pl.BlockSpec(memory_space=pltpu.VMEM)
    return pl.pallas_call(
        kernel,
        out_shape=out_shape,
        in_specs=[space] * len(args),
        out_specs=jax.tree.map(lambda _: space, out_shape),
        scratch_shapes=scratch,
        compiler_params=pltpu.CompilerParams(
            collective_id=collective_id, has_side_effects=True, vmem_limit_bytes=VMEM
        ),
    )(*args)


def half_turn(tile):
    return pltpu.roll(tile, SUB // 2, 0)


def send_totals(n, total_ref, all_ref, send, recv):
    g = lax.axis_index("dp")
    all_ref[0] = total_ref[...] + half_turn(total_ref[...])
    return [
        sending(all_ref.at[0], all_ref.at[k], send.at[1, k], recv.at[1, k], {"dp": (g + k) % n})
        for k in range(1, n)
    ]


def exchange_body(
    n, reverse, copies, part_ref, total_ref, rates_ref, packed_ref, all_ref, out_ref, sbuf, rbuf, send, recv
):
    g = lax.axis_index("dp")
    states, chans = rates_ref.shape
    pairs = states // 2
    upper = lax.broadcasted_iota(jnp.int32, (SUB, chans), 0) >= SUB // 2
    total = total_ref[...]
    decay = lambda m: jnp.exp2(jnp.broadcast_to(rates_ref[m : m + 1, :], (SUB, chans)) * total)

    def summary(m):
        part = part_ref[m]
        return part + decay(m) * half_turn(part)

    def packed(p):
        low, high = summary(p), summary(p + pairs)
        if reverse:
            return jnp.where(upper, half_turn(high), low)
        return jnp.where(upper, high, half_turn(low))

    for p in range(0, pairs, 2):
        sbuf[p * SUB : (p + 2) * SUB, :] = jnp.concatenate([packed(p), packed(p + 1)], axis=0).astype(BF16)
    copies = copies + [
        sending(sbuf, rbuf.at[k], send.at[0, k], recv.at[0, k], {"dp": (g + k) % n})
        for k in range(1, n)
    ]
    for copy in copies:
        copy.wait_recv()

    def one(lap, held):
        away = n - 1 - lap
        slot = n - away if reverse else away
        use = (g + away < n) if reverse else (away <= g)
        steps = all_ref[slot]
        new = []
        for p in range(0, pairs, 2):
            got = rbuf[slot, p * SUB : (p + 2) * SUB, :].astype(F32)
            for q in (p, p + 1):
                fall = jnp.exp2(packed_ref[q] * steps)
                value = fall * held[q] + got[(q - p) * SUB : (q - p + 1) * SUB]
                new.append(jnp.where(use, value, held[q]))
        return tuple(new)

    zero = tuple(jnp.zeros((SUB, chans), F32) for _ in range(pairs))
    held = lax.fori_loop(0, n - 1, one, zero)
    for m in range(states):
        state = held[m % pairs]
        if (m >= pairs) != reverse:
            state = half_turn(state)
        later = half_turn(decay(m) * state + part_ref[m])
        out_ref[m] = jnp.where(upper, state, later) if reverse else jnp.where(upper, later, state)
    for copy in copies:
        copy.wait_send()


def packed_rates(rates):
    states, chans = rates.shape
    pairs = states // 2
    wide = lambda r: jnp.broadcast_to(r[:, None, :], (pairs, SUB // 2, chans))
    return jnp.concatenate([wide(rates[:pairs]), wide(rates[pairs:])], axis=1)


def enter_forward_kernel(
    n, proj_ref, weight_ref, bias_ref, inner_ref, valid_ref, rates_ref, packed_ref,
    step_ref, drive_ref, slope_ref, bin_ref, cout_ref, low_ref, total_ref, h0_ref, all_ref,
    part, sbuf, rbuf, send, recv,
):
    places, _, chans = step_ref.shape
    states = rates_ref.shape[0]
    rank = weight_ref.shape[0]
    g = lax.axis_index("dp")
    greet([{"dp": (g + k) % n} for k in range(1, n)])
    size = 256
    total_ref[...] = jnp.zeros_like(total_ref)

    def block(b, _):
        at = ds(b * size, size)
        here = pl.ds(pl.multiple_of(b * (size // SUB), size // SUB), size // SUB)
        by_place = lambda v: v.reshape(size // SUB, SUB, v.shape[1])
        proj = proj_ref[at, :]
        low = proj[:, 0:rank]
        high = low.astype(BF16)
        rest = (low - high.astype(F32)).astype(BF16)
        low_ref[at, :] = high
        pre = dot(high, weight_ref[...], NN) + dot(rest, weight_ref[...], NN) + bias_ref[...]
        valid = valid_ref[at, :]
        steps = valid * (jnp.maximum(pre, 0.0) + jnp.log1p(jnp.exp(-jnp.abs(pre))))
        slope_ref[at, :] = valid * jax.nn.sigmoid(pre)
        step_ref[here] = by_place(steps)
        drive_ref[here] = by_place(steps * inner_ref[at, :].astype(F32))
        total_ref[...] += jnp.sum(by_place(steps), axis=0)
        bin_ref[here] = by_place(proj[:, rank : rank + states])
        cout_ref[here] = by_place(proj[:, rank + states : rank + 2 * states])
        return 0

    lax.fori_loop(0, places * SUB // size, block, 0)
    copies = send_totals(n, total_ref, all_ref, send, recv)
    half = 8
    for nh in range(states // half):
        local_scan(step_ref, drive_ref, bin_ref, rates_ref, part, nh, half, False)
    exchange_body(n, False, copies, part, total_ref, rates_ref, packed_ref, all_ref, h0_ref, sbuf, rbuf, send, recv)


def enter_forward(n, collective_id, proj, weight, bias, inner, valid, rates):
    rows, chans = inner.shape
    states = rates.shape[0]
    rank = weight.shape[0]
    shape = jax.ShapeDtypeStruct
    places = rows // SUB
    entering = shape((states, SUB, chans), F32)
    sems = pltpu.SemaphoreType.DMA((2, n))
    return vmem_call(
        functools.partial(enter_forward_kernel, n),
        [
            shape((places, SUB, chans), F32),
            shape((places, SUB, chans), F32),
            shape((rows, chans), F32),
            shape((places, SUB, states), F32),
            shape((places, SUB, states), F32),
            shape((rows, rank), BF16),
            shape((SUB, chans), F32),
            entering,
            shape((n, SUB, chans), F32),
        ],
        [
            pltpu.VMEM((states, SUB, chans), F32),
            pltpu.VMEM((states * SUB // 2, chans), BF16),
            pltpu.VMEM((n, states * SUB // 2, chans), BF16),
            sems,
            sems,
        ],
        collective_id, proj, weight, bias, inner, valid, rates, packed_rates(rates),
    )


def dp_pairs(n):
    g = lax.axis_index("dp")
    odd, z, m = g % 2, g // 2, n // 2
    return g, odd, {"dp": g + 1 - 2 * odd}, [{"dp": 2 * ((z + k) % m) + odd} for k in range(1, m)]


PIECES = 2


def gathering(n, sums, send, recv):
    g, odd, pair, like = dp_pairs(n)
    z, m = g // 2, n // 2
    rows = sums.shape[1]
    cut = (rows // 2 + 15) // 16 * 16
    parts = [pl.ds(0, cut), pl.ds(cut, rows - cut)]

    def copy(kind, k, p, b, to):
        return pltpu.make_async_remote_copy(
            src_ref=sums.at[b, parts[p]],
            dst_ref=sums.at[b, parts[p]],
            send_sem=send.at[kind, p * m + k],
            recv_sem=recv.at[kind, p * m + k],
            device_id=to,
            device_id_type=MESH,
        )

    third = lambda k, p: copy(0, k, p, g, like[k])
    fourth = lambda k, p: copy(1, k, p, 2 * ((z + m - k) % m) + odd, pair)

    def start():
        for p in range(PIECES):
            for k in range(m - 1):
                third(k, p).start()
            fourth(0, p).start()

    def middle(p):
        for k in range(m - 1):
            third(k, p).wait_recv()
            fourth(k + 1, p).start()

    def end():
        for p in range(PIECES):
            for k in range(m):
                fourth(k, p).wait_recv()
            for k in range(m - 1):
                third(k, p).wait_send()
            for k in range(m):
                fourth(k, p).wait_send()

    return start, middle, end


def enter_backward_kernel(
    n, step_ref, gs_ref, cout_ref, total_ref, rates_ref, packed_ref, all_ref, blocks_ref,
    g0_ref, own_ref, part, sbuf, rbuf, pa, ps, pc, send, recv, pair_send, pair_recv,
):
    states = rates_ref.shape[0]
    g, odd, pair, like = dp_pairs(n)
    z, m = g // 2, n // 2
    greet([{"dp": (g + k) % n} for k in range(1, n)])
    order = [(z + k) % m for k in range(1, m)] + [z]
    first = [
        sending(blocks_ref.at[2 * order[k] + 1 - odd], pa.at[k], pair_send.at[0, k], pair_recv.at[0, k], pair)
        for k in range(m)
    ]
    half = 8
    second = []
    for nh in range(states // half):
        local_scan(step_ref, gs_ref, cout_ref, rates_ref, part, nh, half, True)
        if nh == 0:
            few = range(0, m // 2)
        else:
            few = range(m // 2, m)
        for k in few:
            first[k].wait_recv()
            ps[k] = (blocks_ref[2 * order[k] + odd].astype(F32) + pa[k].astype(F32)).astype(BF16)
            if k < m - 1:
                second.append(sending(ps.at[k], pc.at[k], pair_send.at[1, k], pair_recv.at[1, k], like[k]))
    exchange_body(n, True, [], part, total_ref, rates_ref, packed_ref, all_ref, g0_ref, sbuf, rbuf, send, recv)
    value = ps[m - 1].astype(F32)
    for copy in second:
        copy.wait_recv()
    for k in range(m - 1):
        value = value + pc[k].astype(F32)
    own_ref[...] = value.astype(BF16)
    for copy in first + second:
        copy.wait_send()


def enter_backward(n, collective_id, step, gs, cout, total, rates, totals, blocks):
    _, _, chans = step.shape
    states = rates.shape[0]
    shape = jax.ShapeDtypeStruct
    m = n // 2
    sems = pltpu.SemaphoreType.DMA((2, n))
    some = pltpu.VMEM((m, *blocks.shape[1:]), BF16)
    return vmem_call(
        functools.partial(enter_backward_kernel, n),
        [shape((states, SUB, chans), F32), shape(blocks.shape[1:], BF16)],
        [
            pltpu.VMEM((states, SUB, chans), F32),
            pltpu.VMEM((states * SUB // 2, chans), BF16),
            pltpu.VMEM((n, states * SUB // 2, chans), BF16),
            some,
            some,
            some,
            sems,
            sems,
            sems,
            sems,
        ],
        collective_id, step, gs, cout, total, rates, packed_rates(rates), totals, blocks,
    )


def half_pick(ids, slots):
    iota = lax.broadcasted_iota(jnp.int32, (ids.shape[0], slots), 1)
    return jnp.where(iota == ids, 1.0, 0.0).astype(BF16)


def dispatching(n, x_ref, out_ref, send, recv, local):
    g = lax.axis_index("dp")
    j, near, _ = mp_pair()
    hc = x_ref.shape[2]
    cols = ds((j % 2) * hc, hc)

    def leave(k):
        return pltpu.make_async_remote_copy(
            src_ref=x_ref.at[(g + k) % n],
            dst_ref=out_ref.at[g, :, cols],
            send_sem=send.at[0, k],
            recv_sem=recv.at[0, k],
            device_id={"dp": (g + k) % n},
            device_id_type=MESH,
        )

    def share(k):
        place = out_ref.at[(g + n - k) % n, :, cols]
        return pltpu.make_async_remote_copy(
            src_ref=place,
            dst_ref=place,
            send_sem=send.at[1, k],
            recv_sem=recv.at[1, k],
            device_id={"mp": near},
            device_id_type=MESH,
        )

    own = pltpu.make_async_copy(x_ref.at[g], out_ref.at[g, :, cols], local)

    def start():
        own.start()
        for k in range(1, n):
            leave(k).start()

    def middle():
        for k in range(n):
            if k:
                leave(k).wait_recv()
            else:
                own.wait()
            share(k).start()

    def end():
        for k in range(n):
            share(k).wait_recv()
        for k in range(n):
            if k:
                leave(k).wait_send()
            share(k).wait_send()

    return start, middle, end


def arrange(cuts, in_ref, tile_ref):
    seqs, chunks, places = cuts
    for ct in range(tile_ref.shape[0]):
        for q in range(seqs):
            for k in range(chunks):
                start = (q * chunks + k) * places
                value = in_ref[start : start + places, ct * LANES : (ct + 1) * LANES]
                tile_ref[ct, pl.ds(k * seqs + q, places, stride=SUB), :] = value.astype(F32)


def front_kernel(
    n,
    cuts,
    capacity,
    tokens_ref,
    cot_ref,
    routes_ref,
    lengths_ref,
    gain_ref,
    weight_ref,
    taps_ref,
    bias_ref,
    select_ref,
    tok_ref,
    cot_low_ref,
    normed_ref,
    both_ref,
    pre_ref,
    inner_ref,
    lead_ref,
    proj_ref,
    quarter,
    slot_ref,
    half_ref,
    valid_ref,
    hot_ref,
    tile_s,
    ext_s,
    live_s,
    got,
    part_s,
    ra,
    sb,
    rb,
    send,
    recv,
):
    seqs, chunks, places = cuts
    g = lax.axis_index("dp")
    j, near, far = mp_pair()
    y, c = j // 2, j % 2
    near, far = {"mp": near}, {"mp": far}
    rows, width = tok_ref.shape
    chans = inner_ref.shape[1]
    kernel = taps_ref.shape[0]
    edge = (kernel - 1) * SUB
    slot_dev = chunks * places
    experts_all = hot_ref.shape[1]
    hr, hc = quarter.shape[1], quarter.shape[2]
    size = 256
    greet([near, far, {"dp": (g + 1) % n}, {"dp": (g + n - 1) % n}])

    arrange(cuts, tokens_ref, tile_s)

    def first(b, _):
        at = ds(b * size, size)
        tok = jnp.concatenate([tile_s[ct, at, :] for ct in range(width // LANES)], axis=1)
        tok_ref[at, :] = tok.astype(BF16)
        inverse = lax.rsqrt(jnp.mean(tok * tok, axis=1, keepdims=True) + norm_eps)
        normed = (tok * inverse * gain_ref[...]).astype(BF16)
        normed_ref[at, :] = normed
        both = dot(normed, weight_ref[...], NN).astype(BF16)
        both_ref[at, :] = both
        ext_s[pl.ds(pl.multiple_of(b * size + edge, SUB), size), :] = both[:, 0:chans].astype(F32)
        return 0

    lax.fori_loop(0, rows // size, first, 0)
    ends = sending(
        both_ref.at[rows - 32 : rows, 0:chans], got, send.at[3, 0], recv.at[3, 0], {"dp": (g + 1) % n}
    )

    at_row = lax.broadcasted_iota(jnp.int32, (rows, 1), 0)
    sub = at_row % SUB
    seq = sub % seqs
    local_place = (sub // seqs) * places + at_row // SUB
    limit = jnp.zeros((rows, 1), jnp.int32)
    for q in range(seqs):
        limit = jnp.where(seq == q, lengths_ref[0:1, q : q + 1], limit)
    valid = jnp.where(g * slot_dev + local_place < limit, 1.0, 0.0)
    valid_ref[...] = valid
    route = routes_ref[...]
    hot = jnp.where(lax.broadcasted_iota(jnp.int32, (rows, experts_all), 1) == route, 1.0, 0.0)
    hot_ref[...] = hot
    live_s[...] = hot * valid
    col = lax.broadcasted_iota(jnp.int32, (1, rows), 1)
    col_sub = col % SUB
    original = (col_sub % seqs) * slot_dev + (col_sub // seqs) * places + col // SUB
    room = 2 * hr

    def position(b, _):
        at = ds(b * size, size)
        here = b * size + lax.broadcasted_iota(jnp.int32, (size, 1), 0)
        here_sub = here % SUB
        mine = (here_sub % seqs) * slot_dev + (here_sub // seqs) * places + here // SUB
        before = jnp.where(original < mine, 1.0, 0.0).astype(BF16)
        live = live_s[at, :]
        earlier = dot(before, live_s[...].astype(BF16), NN)
        pos = jnp.sum(earlier * live, axis=1, keepdims=True)
        kept = jnp.where(pos < capacity, jnp.sum(live, axis=1, keepdims=True), 0.0) > 0.5
        pos = pos.astype(jnp.int32)
        to = routes_ref[at, :]
        slot_ref[at, :] = jnp.where(kept, to * room + pos, -1)
        lower = pos - y * hr
        inside = jnp.where(lower >= 0, 1, 0) * jnp.where(lower < hr, 1, 0)
        half_ref[at, :] = jnp.where(kept, jnp.where(inside > 0, to * hr + lower, -1), -1)
        return 0

    lax.fori_loop(0, rows // size, position, 0)

    ends.wait_recv()
    upper = lax.broadcasted_iota(jnp.int32, (SUB, chans), 0) >= SUB // 2
    some = jnp.where(g > 0, 1.0, 0.0)
    tails = got[...].astype(F32) * some
    for k in range(kernel - 1):
        at = slice(k * SUB, (k + 1) * SUB)
        tail = ext_s[rows + k * SUB : rows + (k + 1) * SUB, :]
        other_tail = tails[32 - edge + k * SUB : 32 - edge + (k + 1) * SUB, :]
        lead = half_turn(jnp.where(upper, other_tail, tail))
        ext_s[at, :] = lead
        lead_ref[at, :] = lead

    half = rows // 2
    count = half // size
    own = c * half
    other = (1 - c) * half

    def conv(start):
        at = ds(start, size)
        pre = jnp.broadcast_to(bias_ref[...], (size, chans))
        for k in range(kernel):
            past = ext_s[pl.ds(pl.multiple_of(start + k * SUB, SUB), size), :]
            pre = pre + taps_ref[k : k + 1, :] * past
        pre_ref[at, :] = pre
        inner = (pre * jax.nn.sigmoid(pre)).astype(BF16)
        inner_ref[at, :] = inner
        part_s[at, :] = dot(inner, select_ref[...], NN)

    one, two, three = [], [], []
    for k in range(count):
        conv(other + k * size)
        at = ds(other + k * size, size)
        one.append(sending(part_s.at[at], ra.at[k], send.at[0, k], recv.at[0, k], near))
    for k in range(count):
        conv(own + k * size)
        one[k].wait_recv()
        sb[k] = part_s[ds(own + k * size, size), :] + ra[k]
        two.append(sending(sb.at[k], rb.at[k], send.at[1, k], recv.at[1, k], far))

    arrange(cuts, cot_ref, tile_s)

    def second(b, _):
        at = ds(b * size, size)
        cot = jnp.concatenate([tile_s[ct, at, :] for ct in range(width // LANES)], axis=1)
        cot_low_ref[at, :] = cot.astype(BF16)
        return 0

    lax.fori_loop(0, rows // size, second, 0)
    pick = half_pick(half_ref[...], n * hr)
    sent = dot(pick, cot_low_ref[:, ds(c * hc, hc)], TN).astype(BF16)
    quarter[...] = sent.reshape(n, hr, hc)
    for k in range(count):
        two[k].wait_recv()
        at = ds(own + k * size, size)
        proj_ref[at, :] = sb[k] + rb[k]
        three.append(sending(proj_ref.at[at], proj_ref.at[at], send.at[2, k], recv.at[2, k], near))
    for copy in three:
        copy.wait_recv()
    for copy in [ends] + one + two + three:
        copy.wait_send()


def front(n, collective_id, cuts, capacity, hr, experts_all, *args):
    tokens, taps, select = args[0], args[6], args[8]
    rows, width = tokens.shape
    kernel, chans = taps.shape
    edge = (kernel - 1) * SUB
    wide = select.shape[1]
    count = rows // 512
    shape = jax.ShapeDtypeStruct
    sems = pltpu.SemaphoreType.DMA((4, count))
    sums = pltpu.VMEM((count, 256, wide), F32)
    return vmem_call(
        functools.partial(front_kernel, n, cuts, capacity),
        [
            shape((rows, width), BF16),
            shape((rows, width), BF16),
            shape((rows, width), BF16),
            shape((rows, 2 * chans), BF16),
            shape((rows, chans), F32),
            shape((rows, chans), BF16),
            shape((edge, chans), F32),
            shape((rows, wide), F32),
            shape((n, hr, width // 2), BF16),
            shape((rows, 1), jnp.int32),
            shape((rows, 1), jnp.int32),
            shape((rows, 1), F32),
            shape((rows, experts_all), F32),
        ],
        [
            pltpu.VMEM((width // LANES, rows, LANES), F32),
            pltpu.VMEM((rows + edge, chans), F32),
            pltpu.VMEM((rows, experts_all), F32),
            pltpu.VMEM((32, chans), BF16),
            pltpu.VMEM((rows, wide), F32),
            sums,
            sums,
            sums,
            sems,
            sems,
        ],
        collective_id, *args,
    )


def middle_kernel(
    n, sum_ref, tok_ref, valid_ref, gain_ref, half_ref, resid_ref, rows_ref, normed_s, quarter, dsend, drecv, local
):
    g = lax.axis_index("dp")
    j, near, _ = mp_pair()
    c = j % 2
    rows, width = tok_ref.shape
    hr, hc = rows_ref.shape[1], width // 2
    size = 256
    greet([{"mp": near}] + [{"dp": (g + k) % n} for k in range(1, n)])

    def norm(b, _):
        at = ds(b * size, size)
        resid = tok_ref[at, :].astype(F32) + valid_ref[at, :] * sum_ref[at, :].astype(F32)
        resid_ref[at, :] = resid
        inverse = lax.rsqrt(jnp.mean(resid * resid, axis=1, keepdims=True) + norm_eps)
        normed_s[at, :] = (resid * inverse * gain_ref[...]).astype(BF16)
        return 0

    lax.fori_loop(0, rows // size, norm, 0)
    pick = half_pick(half_ref[...], n * hr)
    sent = dot(pick, normed_s[:, ds(c * hc, hc)], TN).astype(BF16)
    quarter[...] = sent.reshape(n, hr, hc)
    start, middle, end = dispatching(n, quarter, rows_ref, dsend, drecv, local)
    start()
    middle()
    end()


def mixer_to_experts(n, collective_id, hr, mixed, tok, valid, gain, half_slots):
    rows, width = tok.shape
    shape = jax.ShapeDtypeStruct
    dsems = pltpu.SemaphoreType.DMA((2, n))
    return vmem_call(
        functools.partial(middle_kernel, n),
        [shape((rows, width), F32), shape((n, hr, width), BF16)],
        [
            pltpu.VMEM((rows, width), BF16),
            pltpu.VMEM((n, hr, width // 2), BF16),
            dsems,
            dsems,
            pltpu.SemaphoreType.DMA,
        ],
        collective_id, mixed, tok, valid, gain, half_slots,
    )


def returning(n, x_ref, out_ref, send, recv):
    g = lax.axis_index("dp")
    j, near, far = mp_pair()
    hr, hc = x_ref.shape[1], x_ref.shape[2]
    y, c = j // 2, j % 2
    mine = ds(c * hc, hc)
    up, down = ds(y * hr, hr), ds((1 - y) * hr, hr)

    def copy(kind, k, src, dst, to):
        return pltpu.make_async_remote_copy(
            src_ref=src,
            dst_ref=dst,
            send_sem=send.at[kind, k],
            recv_sem=recv.at[kind, k],
            device_id=to,
            device_id_type=MESH,
        )

    def place(k, rows):
        return out_ref.at[(g + n - k) % n, rows, mine]

    there = lambda k: copy(0, k, x_ref.at[(g + k) % n], out_ref.at[g, up, mine], {"dp": (g + k) % n})
    to_far = lambda k: copy(1, k, place(k, up), place(k, up), {"mp": far})
    to_near = lambda k: copy(2, k, place(k, up), place(k, up), {"mp": near})
    on = lambda k: copy(3, k, place(k, down), place(k, down), {"mp": near})

    def keep():
        out_ref[g, up, mine] = x_ref[g]

    def arrived(k):
        @pl.when(k > 0)
        def _():
            there(k).wait_recv()

        to_far(k).start()
        to_near(k).start()

    def passed(k):
        to_far(k).wait_recv()
        on(k).start()

    def end(k):
        to_near(k).wait_recv()
        on(k).wait_recv()
        for made in (to_far, to_near, on):
            made(k).wait_send()

        @pl.when(k > 0)
        def _():
            there(k).wait_send()

    return keep, there, arrived, passed, end


def each(act, start, count):
    def one(i, _):
        act(start + i)
        return 0

    lax.fori_loop(0, count, one, 0)


def expert_kernel(
    n,
    rows_ref,
    cot_ref,
    up_ref,
    ub_ref,
    down_ref,
    up2_ref,
    down2_ref,
    ub2_ref,
    db_ref,
    router_ref,
    hot_ref,
    out_ref,
    quarter_ref,
    gates_ref,
    gown_ref,
    gother_ref,
    gub_ref,
    gdb_ref,
    part,
    hid,
    slope,
    pre,
    grad,
    ra,
    qb,
    gate_part,
    gate_near,
    gate_sum,
    gate_in,
    send,
    recv,
    near_send,
    near_recv,
    gate_send,
    gate_recv,
):
    g = lax.axis_index("dp")
    j, near, far = mp_pair()
    near, far = {"mp": near}, {"mp": far}
    y, c = j // 2, j % 2
    hr, width = rows_ref.shape[1], rows_ref.shape[2]
    hidden = up_ref.shape[1]
    hc = width // 2
    half = n // 2
    size = half * hr
    others = [{"dp": (g + k) % n} for k in range(1, n)]
    greet([near, far] + others)
    mine, theirs = ds(c * hc, hc), ds((1 - c) * hc, hc)
    gub_ref[...] = jnp.zeros_like(gub_ref)
    gdb_ref[...] = jnp.zeros_like(gdb_ref)
    folded = lambda v: jnp.sum(v.reshape(v.shape[0] // SUB, SUB, v.shape[1]), axis=0)
    ups = (up_ref, up2_ref)
    downs = (down_ref, down2_ref)
    biases = (ub_ref, ub2_ref)

    def near_copy(t):
        return pltpu.make_async_remote_copy(
            src_ref=part.at[t // n, (g + t) % n, :, theirs],
            dst_ref=ra.at[t],
            send_sem=near_send.at[t],
            recv_sem=near_recv.at[t],
            device_id=near,
            device_id_type=MESH,
        )

    def wide(ref, base):
        return ref[pl.ds(base, half)].reshape(size, ref.shape[2])

    def activate(base):
        rows = wide(rows_ref, base)
        at = pl.ds(pl.multiple_of(base * hr, size), size)
        for k in range(2):
            v = dot(rows, ups[k][...], NN) + biases[k][...]
            sq = v * v
            th = jnp.tanh(v * (GELU_A + GELU_A * GELU_B * sq))
            hid[k, at, :] = (0.5 * v * (1.0 + th)).astype(BF16)
            slope[k, at, :] = 0.5 * (1.0 + th) + 0.5 * v * (1.0 - th * th) * (
                GELU_A + 3.0 * GELU_A * GELU_B * sq
            )

    def behind(base):
        at = pl.ds(pl.multiple_of(base * hr, size), size)
        probs = jax.nn.softmax(dot(wide(rows_ref, base), router_ref[...], NN), axis=-1)
        chosen = jnp.sum(probs * hot_ref[...], axis=1, keepdims=True)
        scaled = (chosen * wide(cot_ref, base).astype(F32)).astype(BF16)
        grad[at, :] = scaled
        gdb_ref[...] += folded(scaled.astype(F32))
        total = None
        for k in range(2):
            value = (dot(scaled, downs[k][...], NT) * slope[k, at, :]).astype(BF16)
            pre[k, at, :] = value
            gub_ref[k] += folded(value.astype(F32))
            term = dot(value, ups[k][...], NT)
            total = term if k == 0 else total + term
        part[0, pl.ds(base, half)] = total.astype(BF16).reshape(half, hr, width)

    def results(base):
        at = pl.ds(pl.multiple_of(base * hr, size), size)
        total = dot(hid[0, at, :], downs[0][...], NN) + dot(hid[1, at, :], downs[1][...], NN)
        part[1, pl.ds(base, half)] = total.astype(BF16).reshape(half, hr, width)

    keep, there, arrived, passed, end = returning(n, qb, out_ref, send, recv)

    def grad_sum(k):
        to = (g + k) % n
        near_copy(k).wait_recv()
        qb[to] = (part[0, to, :, mine].astype(F32) + ra[k].astype(F32)).astype(BF16)

        @pl.when(k > 0)
        def _():
            there(k).start()

    eye = lax.broadcasted_iota(jnp.int32, (hr, LANES), 0) == lax.broadcasted_iota(jnp.int32, (hr, LANES), 1)

    def result_sum(k):
        to = (g + k) % n
        near_copy(n + k).wait_recv()
        value = part[1, to, :, mine].astype(F32) + ra[n + k].astype(F32) + db_ref[:, mine]
        value = value.astype(BF16)
        quarter_ref[to] = value
        gate = jnp.sum(cot_ref[to, :, mine].astype(F32) * value.astype(F32), axis=1, keepdims=True)
        gate_part[pl.ds(to, 1), :] = jnp.sum(jnp.where(eye, gate, 0.0), axis=0, keepdims=True)

    activate(0)
    activate(half)
    behind(0)
    behind(half)
    each(lambda t: near_copy(t).start(), 0, n)
    each(grad_sum, 0, n)
    keep()
    results(0)
    results(half)
    each(lambda t: near_copy(t).start(), n, n)
    each(result_sum, 0, n)
    gate_copy = sending(gate_part, gate_near, gate_send.at[0], gate_recv.at[0], near)
    gate_copy.wait_recv()
    gate_sum[...] = gate_part[...] + gate_near[...]
    gate_in[g] = gate_sum[...]
    gate_out = [
        sending(gate_sum, gate_in.at[g], gate_send.at[k], gate_recv.at[k], others[k - 1]) for k in range(1, n)
    ]

    cut = 256
    pieces = width // cut

    def weights(q):
        at = ds(q % pieces * cut, cut)
        for kind in range(2):
            for k in range(2):

                @pl.when(q // pieces == 2 * kind + 1 - k)
                def _(kind=kind, k=k):
                    if kind == 0:
                        value = dot(hid[k], grad[:, at], TN)
                    else:
                        value = dot(rows_ref[...].reshape(n * hr, width), pre[k, :, at], TN)
                    if k == 0:
                        gown_ref[kind, :, at] = value
                    else:
                        gother_ref[kind, :, at] = value.astype(BF16)

    lag = 3

    def step(i, _):
        @pl.when(i < 4 * pieces)
        def _():
            weights(i)

        @pl.when(i < n)
        def _():
            arrived(i)

        @pl.when((i >= lag) & (i < n + lag))
        def _():
            passed(i - lag)

        return 0

    lax.fori_loop(0, max(4 * pieces, n + lag), step, 0)
    for copy in gate_out:
        copy.wait_recv()
    for e in range(n):
        gates_ref[y, e : e + 1, :] = gate_in[e, pl.ds(g, 1), :]
    gate_far = sending(gates_ref.at[y], gates_ref.at[y], gate_send.at[n], gate_recv.at[n], far)
    each(end, 0, n)
    each(lambda t: near_copy(t).wait_send(), 0, 2 * n)
    gate_far.wait_recv()
    for copy in [gate_copy, gate_far] + gate_out:
        copy.wait_send()


GELU_A = 0.7978845608028654
GELU_B = 0.044715


def experts(n, collective_id, rows, cot, up, up_bias, down, up2, down2, up_bias2, down_bias, router, hot):
    _, hr, width = rows.shape
    hidden = up.shape[1]
    shape = jax.ShapeDtypeStruct
    gate = pltpu.VMEM((n, LANES), F32)
    return vmem_call(
        functools.partial(expert_kernel, n),
        [
            shape((n, 2 * hr, width), BF16),
            shape((n, hr, width // 2), BF16),
            shape((2, n, LANES), F32),
            shape((2, width, hidden), F32),
            shape((2, width, hidden), BF16),
            shape((2, SUB, hidden), F32),
            shape((SUB, width), F32),
        ],
        [
            pltpu.VMEM((2, n, hr, width), BF16),
            pltpu.VMEM((2, n * hr, hidden), BF16),
            pltpu.VMEM((2, n * hr, hidden), F32),
            pltpu.VMEM((2, n * hr, hidden), BF16),
            pltpu.VMEM((n * hr, width), BF16),
            pltpu.VMEM((2 * n, hr, width // 2), BF16),
            pltpu.VMEM((n, hr, width // 2), BF16),
            gate,
            gate,
            gate,
            pltpu.VMEM((n, n, LANES), F32),
            pltpu.SemaphoreType.DMA((4, n)),
            pltpu.SemaphoreType.DMA((4, n)),
            pltpu.SemaphoreType.DMA((2 * n,)),
            pltpu.SemaphoreType.DMA((2 * n,)),
            pltpu.SemaphoreType.DMA((n + 1,)),
            pltpu.SemaphoreType.DMA((n + 1,)),
        ],
        collective_id, rows, cot, up, up_bias, down, up2, down2, up_bias2, down_bias, router, hot,
    )


def finish_kernel(
    n,
    count,
    cuts,
    layout,
    proj_ref,
    select_ref,
    inner_ref,
    base_ref,
    pre_ref,
    both_ref,
    lead_ref,
    gate_ref,
    normed_ref,
    weight_ref,
    taps_ref,
    given_ref,
    tok_ref,
    resid_ref,
    gain_ref,
    slot_ref,
    result_ref,
    residual_ref,
    chosen_ref,
    grad_ref,
    gin_ref,
    small_ref,
    first_ref,
    block_ref,
    conv_s,
    ext_s,
    both_s,
    got,
    part_s,
    sum_s,
    ra,
    sb,
    rb,
    blocks,
    pa,
    ps,
    pc,
    outs,
    firsts,
    rows_s,
    fold_s,
    block_s,
    send,
    recv,
    gsend,
    grecv,
):
    mh, sh = layout
    g = lax.axis_index("dp")
    j, near, far = mp_pair()
    near, far = {"mp": near}, {"mp": far}
    odd, z, m = g % 2, g // 2, n // 2
    pair = {"dp": g + 1 - 2 * odd}
    like = [{"dp": 2 * ((z + k) % m) + odd} for k in range(1, m)]
    others = [{"dp": (g + k) % n} for k in range(1, n)]
    greet([near, far] + others)
    rows, chans = inner_ref.shape
    width = normed_ref.shape[1]
    kernel = taps_ref.shape[0]
    edge = (kernel - 1) * SUB
    block = 256
    half = rows // 2
    size = half // count
    own = (j % 2) * half
    other = (1 - j % 2) * half

    ext_s[0:edge, :] = lead_ref[...]

    def conv_block(b):
        at = ds(b * block, block)
        grad = base_ref[at, :] + dot(proj_ref[at, :], select_ref[...], NT)
        conv_s[at, :] = grad * silu_slope(pre_ref[at, :])
        ext_s[pl.ds(pl.multiple_of(b * block + edge, SUB), block), :] = both_ref[at, 0:chans].astype(F32)

    conv_block(0)
    head = sending(conv_s.at[0:edge], got, send.at[8, 0], recv.at[8, 0], {"dp": (g + n - 1) % n})

    def rest(b, _):
        conv_block(b)
        return 0

    lax.fori_loop(1, rows // block, rest, 0)
    given = given_ref.shape[0]
    selects = select_ref.shape[1]
    rest_at = given + selects
    fold_s[0:given, :] = given_ref[...]
    fold_s[given:rest_at, :] = dot(proj_ref[...], inner_ref[...], TN)
    folded = lambda v: jnp.sum(v.reshape(block // SUB, SUB, chans), axis=0)

    def taps(b, sums):
        grad = conv_s[ds(b * block, block), :]
        past = [ext_s[pl.ds(pl.multiple_of(b * block + k * SUB, SUB), block), :] for k in range(kernel)]
        return tuple(v + folded(grad * p) for v, p in zip(sums, past)) + (sums[kernel] + folded(grad),)

    zero = tuple(jnp.zeros((SUB, chans), F32) for _ in range(kernel + 1))
    sums = lax.fori_loop(0, rows // block, taps, zero)
    for k in range(kernel + 1):
        fold_s[rest_at + k : rest_at + k + 1, :] = jnp.sum(sums[k], axis=0, keepdims=True)
    head.wait_recv()
    upper = lax.broadcasted_iota(jnp.int32, (SUB, chans), 0) >= SUB // 2
    some = jnp.where(g < n - 1, 1.0, 0.0)
    for k in range(kernel - 1):
        at = slice(k * SUB, (k + 1) * SUB)
        tail = half_turn(jnp.where(upper, conv_s[at, :], got[at, :] * some))
        conv_s[rows + k * SUB : rows + (k + 1) * SUB, :] = tail

    def back(b, _):
        at = ds(b * block, block)
        total = jnp.zeros((block, chans), F32)
        for k in range(kernel):
            later = conv_s[pl.ds(pl.multiple_of(b * block + (kernel - 1 - k) * SUB, SUB), block), :]
            total = total + taps_ref[k : k + 1, :] * later
        both_s[at, 0:chans] = total.astype(BF16)
        both_s[at, chans : 2 * chans] = gate_ref[at, :]
        return 0

    lax.fori_loop(0, rows // block, back, 0)

    rows_s[0:width, :] = dot(normed_ref[...], both_s[:, 0:chans], TN)
    for b in range(n):
        blocks[b, 0:mh, :] = rows_s[b * mh : (b + 1) * mh, :].astype(BF16)
        blocks[b, mh : mh + sh, :] = fold_s[b * sh : (b + 1) * sh, :].astype(BF16)
    order = [(z + k) % m for k in range(1, m)] + [z]
    first = [
        sending(blocks.at[2 * order[k] + 1 - odd], pa.at[k], send.at[3, k], recv.at[3, k], pair)
        for k in range(m)
    ]
    one, two, three, second = [], [], [], []

    def input_rows(start):
        at = ds(start, size)
        part_s[at, :] = dot(both_s[at, :], weight_ref[...], NT).astype(BF16)

    for k in range(count):
        input_rows(other + k * size)
        at = ds(other + k * size, size)
        one.append(sending(part_s.at[at], ra.at[k], send.at[0, k], recv.at[0, k], near))
    for k in range(count):
        input_rows(own + k * size)
        one[k].wait_recv()
        mine = part_s[ds(own + k * size, size), :].astype(F32)
        sb[k] = (mine + ra[k].astype(F32)).astype(BF16)
        two.append(sending(sb.at[k], rb.at[k], send.at[1, k], recv.at[1, k], far))
    slots = result_ref.shape[0] * result_ref.shape[1]

    def output(b):
        at = ds(b * block, block)
        iota = lax.broadcasted_iota(jnp.int32, (block, slots), 1)
        pick = jnp.where(iota == slot_ref[at, :], 1.0, 0.0).astype(BF16)
        result = dot(pick, result_ref[...].reshape(slots, width), NN)
        value = residual_ref[at, :] + chosen_ref[at, :] * result
        for ct in range(width // LANES):
            block_s[ct, at, :] = value[:, ct * LANES : (ct + 1) * LANES]

    for k in range(m):
        first[k].wait_recv()
        ps[k] = (blocks[2 * order[k] + odd].astype(F32) + pa[k].astype(F32)).astype(BF16)
        if k < m - 1:
            second.append(sending(ps.at[k], pc.at[k], send.at[4, k], recv.at[4, k], like[k]))

    def far_sum(k):
        two[k].wait_recv()
        at = ds(own + k * size, size)
        sum_s[at, :] = (sb[k].astype(F32) + rb[k].astype(F32)).astype(BF16)
        three.append(sending(sum_s.at[at], sum_s.at[at], send.at[2, k], recv.at[2, k], near))

    output_blocks = rows // block
    for b in range(output_blocks // 2):
        output(b)
    value = ps[m - 1].astype(F32)
    for copy in second:
        copy.wait_recv()
    for k in range(m - 1):
        value = value + pc[k].astype(F32)
    outs[g] = value.astype(BF16)
    start, middle, end = gathering(n, outs, gsend, grecv)
    start()
    for b in range(output_blocks // 2, output_blocks):
        output(b)
    firsts[0] = jnp.zeros(firsts.shape[1:], F32)
    gain = gain_ref[...]

    def norm_rows(start):
        at = ds(start, size)
        grad = sum_s[at, :].astype(F32)
        tok = tok_ref[at, :].astype(F32)
        inverse = lax.rsqrt(jnp.mean(tok * tok, axis=1, keepdims=True) + norm_eps)
        normed = tok * inverse
        firsts[0] += jnp.sum((grad * normed).reshape(size // SUB, SUB, width), axis=0)
        scaled = grad * gain
        mean = jnp.mean(scaled * normed, axis=1, keepdims=True)
        value = resid_ref[at, :] + inverse * (scaled - normed * mean)
        for ct in range(width // LANES):
            grad_ref[ct, at, :] = value[:, ct * LANES : (ct + 1) * LANES]

    for k in range(count):
        far_sum(k)
        norm_rows(own + k * size)
    for p in range(PIECES):
        middle(p)
    for k in range(count):
        three[k].wait_recv()
        norm_rows(other + k * size)
    spread_first = [
        sending(firsts.at[0], firsts.at[k], send.at[7, k], recv.at[7, k], others[k - 1]) for k in range(1, n)
    ]
    restore(cuts, block_s, block_ref)
    for copy in spread_first:
        copy.wait_recv()

    def one_first(d, total):
        return total + firsts[(g + n - d) % n]

    first_ref[...] = lax.fori_loop(0, n, one_first, jnp.zeros(first_ref.shape, F32))
    end()
    for b in range(n):
        gin_ref[b * mh : (b + 1) * mh, :] = outs[b, 0:mh, :].astype(F32)
        small_ref[b * sh : (b + 1) * sh, :] = outs[b, mh : mh + sh, :].astype(F32)
    mp_copies = one + two + three
    for copy in [head] + mp_copies + first + second + spread_first:
        copy.wait_send()


def finish(n, collective_id, cuts, *args, count=4):
    select, inner, normed, taps, given = args[1], args[2], args[8], args[10], args[11]
    rows, chans = inner.shape
    width = normed.shape[1]
    kernel = taps.shape[0]
    edge = (kernel - 1) * SUB
    m = n // 2
    over = lambda size: (size + 16 * n - 1) // (16 * n) * 16
    mh, sh = over(width), over(given.shape[0] + select.shape[1] + kernel + 1)
    slots = pltpu.VMEM((count, rows // 2 // count, width), BF16)
    part = lambda k: pltpu.VMEM((k, mh + sh, chans), BF16)
    sems = pltpu.SemaphoreType.DMA((12, max(n, count)))
    shape = jax.ShapeDtypeStruct
    return vmem_call(
        functools.partial(finish_kernel, n, count, cuts, (mh, sh)),
        [
            shape((width // LANES, rows, LANES), F32),
            shape((n * mh, chans), F32),
            shape((n * sh, chans), F32),
            shape((SUB, width), F32),
            shape((rows, width), BF16),
        ],
        [
            pltpu.VMEM((rows + edge, chans), F32),
            pltpu.VMEM((rows + edge, chans), F32),
            pltpu.VMEM((rows, 2 * chans), BF16),
            pltpu.VMEM((edge, chans), F32),
            pltpu.VMEM((rows, width), BF16),
            pltpu.VMEM((rows, width), BF16),
            slots,
            slots,
            slots,
            part(n),
            part(m),
            part(m),
            part(m),
            part(n),
            pltpu.VMEM((n, SUB, width), F32),
            pltpu.VMEM((n * mh, chans), F32),
            pltpu.VMEM((n * sh, chans), F32),
            pltpu.VMEM((width // LANES, rows, LANES), F32),
            sems,
            sems,
            pltpu.SemaphoreType.DMA((2, PIECES * m)),
            pltpu.SemaphoreType.DMA((2, PIECES * m)),
        ],
        collective_id, *args,
    )


def token_back_kernel(
    n,
    slot_ref,
    back_ref,
    gates_ref,
    quarter_ref,
    residual_ref,
    hot_ref,
    cot_ref,
    valid_ref,
    gain_ref,
    router_ref,
    gated_ref,
    out_ref,
    scan_ref,
    both_ref,
    inner_ref,
    normed_in_ref,
    chosen_ref,
    resid_ref,
    gs_ref,
    gate_ref,
    early_ref,
    landed_ref,
    mixed_s,
    early_s,
    small_s,
    router_out,
    second_ref,
    skip_ref,
    send,
    recv,
):
    rows, width = residual_ref.shape
    chans = inner_ref.shape[1]
    slots = back_ref.shape[0] * back_ref.shape[1]
    hr = back_ref.shape[1] // 2
    g = lax.axis_index("dp")
    others = [{"dp": (g + k) % n} for k in range(1, n)]
    greet(others)
    copies = [
        sending(quarter_ref.at[(g + k) % n], landed_ref.at[g], send.at[k], recv.at[k], others[k - 1])
        for k in range(1, n)
    ]
    landed_ref[g] = quarter_ref[g]
    size = 256
    lanes = lax.broadcasted_iota(jnp.int32, (1, LANES), 1)
    router_out[...] = jnp.zeros_like(router_out)
    second_ref[...] = jnp.zeros_like(second_ref)
    skip_ref[...] = jnp.zeros_like(skip_ref)

    def body(b, _):
        at = ds(b * size, size)
        folded = lambda v: jnp.sum(v.reshape(size // SUB, SUB, v.shape[1]), axis=0)
        iota = lax.broadcasted_iota(jnp.int32, (size, slots), 1)
        slot = slot_ref[at, :]
        pick = jnp.where(iota == slot, 1.0, 0.0).astype(BF16)
        grad = dot(pick, back_ref[...].reshape(slots, width), NN)
        gates = jnp.zeros((size, LANES), F32)
        for e in range(n):
            for k in range(2):
                hit = slot - (2 * e + k) * hr == lanes
                gates = gates + jnp.where(hit, gates_ref[k, e : e + 1, :], 0.0)
        gate = jnp.sum(gates, axis=1, keepdims=True)
        residual = residual_ref[at, :]
        inverse = lax.rsqrt(jnp.mean(residual * residual, axis=1, keepdims=True) + norm_eps)
        normed = residual * inverse
        normed_low = (normed * gain_ref[...]).astype(BF16)
        hot = hot_ref[at, :]
        probs = jax.nn.softmax(dot(normed_low, router_ref[...], NN), axis=-1)
        chosen = jnp.sum(probs * hot, axis=1, keepdims=True)
        chosen_ref[at, :] = chosen
        cot = cot_ref[at, :].astype(F32)
        logit = (gate * probs * (hot - chosen)).astype(BF16)
        router_out[...] += dot(logit, normed_low, TN)
        grad = grad + dot(logit, router_ref[...], NT)
        second_ref[...] += folded(grad * normed)
        scaled = grad * gain_ref[...]
        mean = jnp.mean(scaled * normed, axis=1, keepdims=True)
        resid = cot + inverse * (scaled - normed * mean)
        resid_ref[at, :] = resid
        mixed = (valid_ref[at, :] * resid).astype(BF16)
        mixed_s[at, :] = mixed
        grad_gated = dot(mixed, out_ref[...], NT)
        pre = both_ref[at, chans : 2 * chans].astype(F32)
        sig = jax.nn.sigmoid(pre)
        act = pre * sig
        gs = grad_gated * act
        gs_ref[at, :] = gs
        skip_ref[...] += folded(gs * inner_ref[at, :].astype(F32))
        gate_ref[at, :] = (grad_gated * scan_ref[at, :] * (sig * (1.0 + pre * (1.0 - sig)))).astype(BF16)
        return 0

    lax.fori_loop(0, rows // size, body, 0)
    mh = early_s.shape[1] // n
    sh = early_ref.shape[1] - 2 * mh
    some = router_out.shape[0]
    for k in range(width // chans):
        at = slice(k * chans, (k + 1) * chans)
        small_s[k * some : (k + 1) * some, :] = router_out[:, at]
        line = 2 * some + k
        small_s[line : line + 1, :] = jnp.sum(second_ref[:, at], axis=0, keepdims=True)
    small_s[2 * some + 2 : 2 * some + 3, :] = jnp.sum(skip_ref[...], axis=0, keepdims=True)
    early_s[0, 0:width, :] = dot(normed_in_ref[...], gate_ref[...], TN)
    value = dot(gated_ref[...], mixed_s[...], TN)
    for k in range(width // chans):
        early_s[1, k * chans : (k + 1) * chans, :] = value[:, k * chans : (k + 1) * chans]
    for b in range(n):
        for k in range(2):
            early_ref[b, k * mh : (k + 1) * mh, :] = early_s[k, b * mh : (b + 1) * mh, :].astype(BF16)
        early_ref[b, 2 * mh : 2 * mh + sh, :] = small_s[b * sh : (b + 1) * sh, :].astype(BF16)
    for copy in copies:
        copy.wait_recv()
    for copy in copies:
        copy.wait_send()


def restore(cuts, tile_ref, out_ref):
    seqs, chunks, places = cuts
    for ct in range(tile_ref.shape[0]):
        for q in range(seqs):
            for k in range(chunks):
                picked = tile_ref[ct, pl.ds(k * seqs + q, places, stride=SUB), :]
                start = (q * chunks + k) * places
                out_ref[start : start + places, ct * LANES : (ct + 1) * LANES] = picked.astype(out_ref.dtype)


def token_back(n, collective_id, *args):
    quarter, residual, router, inner = args[3], args[4], args[9], args[14]
    over = lambda size: (size + 16 * n - 1) // (16 * n) * 16
    mh, sh = over(residual.shape[1]), over(2 * router.shape[1] + 3)
    rows, width = residual.shape
    chans = inner.shape[1]
    shape = jax.ShapeDtypeStruct
    sems = pltpu.SemaphoreType.DMA((n,))
    return vmem_call(
        functools.partial(token_back_kernel, n),
        [
            shape((rows, 1), F32),
            shape((rows, width), F32),
            shape((rows, chans), F32),
            shape((rows, chans), BF16),
            shape((n, 2 * mh + sh, chans), BF16),
            shape(quarter.shape, BF16),
        ],
        [
            pltpu.VMEM((rows, width), BF16),
            pltpu.VMEM((2, n * mh, chans), F32),
            pltpu.VMEM((n * sh, chans), F32),
            pltpu.VMEM((router.shape[1], width), F32),
            pltpu.VMEM((SUB, width), F32),
            pltpu.VMEM((SUB, chans), F32),
            sems,
            sems,
        ],
        collective_id, *args,
    )


def emit_kernel(
    layout,
    cuts,
    tile_ref,
    own_ref,
    far_ref,
    conv_ref,
    gate_ref,
    left_ref,
    right_ref,
    small_ref,
    few_ref,
    first_ref,
    ub_ref,
    far_bias_ref,
    db_ref,
    token_ref,
    down_ref,
    up_ref,
    in_ref,
    out_ref,
    taps_ref,
    cb_ref,
    select_ref,
    sw_ref,
    sb_ref,
    decay_ref,
    skip_ref,
    second_ref,
    router_ref,
    norm_ref,
    gub_ref,
    gdb_ref,
):
    restore(cuts, tile_ref, token_ref)
    rank, states, select_at, taps_at = layout
    down_ref[...] = own_ref[0] + far_ref[0].astype(F32)
    up_ref[...] = own_ref[1] + far_ref[1].astype(F32)
    in_ref[:, 0, :] = conv_ref[...]
    in_ref[:, 1, :] = gate_ref[...]
    chans = conv_ref.shape[1]
    out_ref[:, 0:chans] = left_ref[...]
    out_ref[:, chans : 2 * chans] = right_ref[...]

    @pl.when(pl.program_id(0) == 0)
    def _():
        kernel = taps_ref.shape[0]
        taps_ref[...] = small_ref[taps_at : taps_at + kernel, :]
        cb_ref[...] = small_ref[taps_at + kernel : taps_at + kernel + 1, :]
        select_ref[...] = small_ref[select_at:taps_at, :]
        sw_ref[...] = small_ref[0:rank, :]
        decay_ref[...] = small_ref[rank : rank + states, :]
        sb_ref[...] = small_ref[rank + states : rank + states + 1, :]
        some = router_ref.shape[0]
        line = 2 * some
        for k in range(2):
            at = slice(k * chans, (k + 1) * chans)
            router_ref[:, at] = few_ref[k * some : (k + 1) * some, :]
            second_ref[:, at] = few_ref[line + k : line + k + 1, :]
        skip_ref[...] = few_ref[line + 2 : line + 3, :]
        total = lambda v: jnp.sum(v, axis=0, keepdims=True)
        norm_ref[...] = total(first_ref[...])
        bias = far_bias_ref[...].astype(F32)
        gub_ref[...] = total(ub_ref[0] + bias[0:SUB])
        gdb_ref[...] = total(db_ref[...].astype(F32) + bias[SUB : 2 * SUB])


def emit(layout, cuts, tiles_, own, far, conv, gate, mixer, small, few, first, ub, far_bias, db, experts_all):
    width, chans = own.shape[1], conv.shape[1]
    hidden = own.shape[2]
    rank, states, select_at, taps_at = layout
    count, rows = tiles_.shape[0], tiles_.shape[1]
    cut, part = width // count, chans // count
    shape = jax.ShapeDtypeStruct
    block = lambda size, wide: pl.BlockSpec((size, wide), lambda i: (i, 0))
    both = lambda size, wide: pl.BlockSpec((2, size, wide), lambda i: (0, i, 0))
    shapes = [
        (4, chans),
        (1, chans),
        (taps_at - select_at, chans),
        (rank, chans),
        (1, chans),
        (states, chans),
        (1, chans),
        (1, width),
        (experts_all, width),
        (1, width),
        (1, hidden),
        (1, width),
    ]
    return pl.pallas_call(
        functools.partial(emit_kernel, layout, cuts),
        grid=(count,),
        in_specs=[
            pl.BlockSpec((1, rows, LANES), lambda i: (i, 0, 0)),
            both(cut, hidden),
            both(cut, hidden),
            block(cut, chans),
            block(cut, chans),
            block(part, chans),
            pl.BlockSpec((part, chans), lambda i: (i + count, 0)),
            whole(*small.shape),
            whole(*few.shape),
            whole(*first.shape),
            whole(*ub.shape),
            whole(*far_bias.shape),
            whole(*db.shape),
        ],
        out_specs=[
            pl.BlockSpec((rows, LANES), lambda i: (0, i)),
            block(cut, hidden),
            block(cut, hidden),
            pl.BlockSpec((cut, 2, chans), lambda i: (i, 0, 0)),
            block(part, width),
            *[whole(*dims) for dims in shapes],
        ],
        out_shape=[
            shape((rows, count * LANES), F32),
            shape((width, hidden), F32),
            shape((width, hidden), F32),
            shape((width, 2, chans), F32),
            shape((chans, width), F32),
            *[shape(dims, F32) for dims in shapes],
        ],
        compiler_params=pltpu.CompilerParams(vmem_limit_bytes=VMEM),
    )(tiles_, own, far, conv, gate, mixer, mixer, small, few, first, ub, far_bias, db)


def silu_slope(values):
    sigmoid_vals = jax.nn.sigmoid(values)
    return sigmoid_vals * (1.0 + values * (1.0 - sigmoid_vals))


def per_device(
    tokens,
    routes,
    lengths,
    cotangent,
    first_gain,
    mixer_in,
    conv_weight,
    conv_bias,
    select_weight,
    step_weight,
    step_bias,
    decay_log,
    skip_gain,
    mixer_out,
    second_gain,
    router_weight,
    expert_up,
    up_bias,
    expert_down,
    down_bias,
):
    tok_count, model_width = tokens.shape
    kernel, chan_count = conv_weight.shape
    rank_size = step_weight.shape[0]
    state_size = decay_log.shape[0]
    expert_total = router_weight.shape[1]
    capacity = max(2, (5 * tok_count + 4 * expert_total - 1) // (4 * expert_total))
    room = (capacity + 31) // 32 * 32
    slot_dev = SLOT_DEV
    seq_count = tok_count // slot_dev
    chunks = SUB // seq_count
    places_dev = slot_dev // chunks
    cuts = (seq_count, chunks, places_dev)
    device = lax.axis_index("dp")
    dp_count = lax.axis_size("dp")

    mp_count = lax.axis_size("mp")
    to_far = [(i, (i + mp_count // 2) % mp_count) for i in range(mp_count)]
    swap_far = lambda values: lax.ppermute(values, "mp", to_far)
    far_up = swap_far(expert_up[0])

    first_vals = first_gain.astype(F32)
    second_vals = second_gain.astype(F32)
    mixer_in_flat = mixer_in.reshape(model_width, 2 * chan_count)
    conv_taps = conv_weight.astype(F32)
    routes_cut = routes.reshape(seq_count, chunks, places_dev).transpose(2, 1, 0)
    (
        tok_low,
        cot_low,
        normed_in,
        both_in,
        conv_pre,
        inner_vals,
        lead_rows,
        projected,
        cot_quarter,
        slot_ids,
        half_slots,
        valid_col,
        route_hot,
    ) = front(
        dp_count,
        0,
        cuts,
        capacity,
        room // 2,
        expert_total,
        tokens,
        cotangent,
        routes_cut.reshape(tok_count, 1),
        lengths[None],
        first_vals[None],
        mixer_in_flat,
        conv_taps,
        conv_bias.astype(F32)[None],
        select_weight,
    )
    own_down, own_bias, projected = lax.optimization_barrier(
        (expert_down[0], jnp.broadcast_to(up_bias, (16, up_bias.shape[1])), projected)
    )
    far_down, far_bias = swap_far((own_down, own_bias))
    decay_rates = -jnp.exp(decay_log.astype(F32))
    rates = decay_rates * LOG2E

    step_p, drive_p, step_slope, bin_p, cout_p, low_high, chunk_steps, state_in, totals = enter_forward(
        dp_count,
        2,
        projected,
        step_weight,
        step_bias.astype(F32)[None],
        inner_vals,
        valid_col,
        rates,
    )
    skip_vals = skip_gain.astype(F32)
    scan_out, gated_vals, mixed, states_before, last_states, cot_rows = forward(
        10,
        step_p,
        drive_p,
        bin_p,
        cout_p,
        rates,
        state_in,
        inner_vals,
        both_in,
        skip_vals[None],
        mixer_out,
        cot_quarter,
    )
    residual, expert_rows = mixer_to_experts(
        dp_count, 3, room // 2, mixed, tok_low, valid_col, second_vals[None], half_slots
    )

    own_hot = (jnp.arange(expert_total) == device).astype(F32)[None]
    returned, quarters, gates, grad_own, grad_other, up_bias_parts, down_bias_part = experts(
        dp_count,
        5,
        expert_rows,
        cot_rows,
        expert_up[0],
        up_bias.astype(F32),
        expert_down[0],
        far_up,
        far_down,
        far_bias[:1].astype(F32),
        down_bias.astype(F32),
        router_weight,
        own_hot,
    )
    down_bias_part = down_bias_part.astype(BF16)
    bias_rows = jnp.concatenate([up_bias_parts[1].astype(BF16), down_bias_part], axis=0)
    from_far = swap_far((grad_other, bias_rows))
    (
        chosen,
        grad_resid,
        grad_scan,
        grad_gate_low,
        early,
        landed,
    ) = token_back(
        dp_count,
        11,
        slot_ids,
        returned,
        gates,
        quarters,
        residual,
        route_hot,
        cot_low,
        valid_col,
        second_vals[None],
        router_weight,
        gated_vals,
        mixer_out,
        scan_out,
        both_in,
        inner_vals,
        normed_in,
    )
    gs_p = grad_scan.reshape(places_dev, SUB, chan_count)
    grad_in, early = enter_backward(
        dp_count, 6, step_p, gs_p, cout_p, chunk_steps, rates, totals, early
    )
    mixer_rows = (model_width + 16 * dp_count - 1) // (16 * dp_count) * 16
    grad_base, proj_part, given, grad_gate_in, grad_mixer_out, few, results = backward(
        dp_count,
        9,
        mixer_rows,
        step_p,
        drive_p,
        gs_p,
        bin_p,
        cout_p,
        rates,
        grad_in,
        last_states,
        states_before,
        inner_vals,
        step_slope,
        low_high,
        jnp.pad(step_weight, ((0, 2 * state_size), (0, 0))),
        skip_vals[None],
        early,
        landed,
    )
    grad_tiles, grad_conv_half, small, grad_first, block_out = finish(
        dp_count,
        8,
        cuts,
        proj_part,
        select_weight,
        inner_vals,
        grad_base,
        conv_pre,
        both_in,
        lead_rows,
        grad_gate_low,
        normed_in,
        mixer_in_flat,
        conv_taps,
        given,
        tok_low,
        grad_resid,
        first_vals[None],
        slot_ids,
        results,
        residual,
        chosen,
    )
    select_at = given.shape[0]
    taps_at = select_at + select_weight.shape[1]
    (
        token_grad,
        grad_down,
        grad_up,
        grad_mixer_in,
        grad_mixer_full,
        grad_taps,
        grad_conv_bias,
        grad_select,
        grad_step_weight,
        grad_step_bias,
        grad_decay_log,
        grad_skip,
        grad_second,
        grad_router,
        grad_gain,
        grad_up_bias,
        grad_down_bias,
    ) = emit(
        (rank_size, state_size, select_at, taps_at),
        cuts,
        grad_tiles,
        grad_own,
        from_far[0],
        grad_conv_half,
        grad_gate_in,
        grad_mixer_out,
        small,
        few,
        grad_first,
        up_bias_parts,
        from_far[1],
        down_bias_part,
        expert_total,
    )
    return (
        block_out,
        token_grad,
        grad_gain[0],
        grad_mixer_in,
        grad_taps,
        grad_conv_bias[0],
        grad_select.T,
        grad_step_weight,
        grad_step_bias[0],
        grad_decay_log,
        grad_skip[0],
        grad_mixer_full,
        grad_second[0],
        grad_router.T,
        grad_up[None],
        grad_up_bias,
        grad_down[None],
        grad_down_bias,
    )


def solution(mesh):
    return jax.shard_map(
        per_device,
        mesh=mesh,
        in_specs=(
            P("dp", None),
            P("dp", None),
            P(),
            P("dp", None),
            P(),
            P(None, None, "mp"),
            P(None, "mp"),
            P("mp"),
            P("mp", None),
            P(None, "mp"),
            P("mp"),
            P(None, "mp"),
            P("mp"),
            P("mp", None),
            P(),
            P(),
            P("dp", None, "mp"),
            P("dp", "mp"),
            P("dp", "mp", None),
            P("dp", None),
        ),
        out_specs=(
            P("dp", None),
            P("dp", None),
            P(),
            P(None, None, "mp"),
            P(None, "mp"),
            P("mp"),
            P("mp", None),
            P(None, "mp"),
            P("mp"),
            P(None, "mp"),
            P("mp"),
            P("mp", None),
            P(),
            P(),
            P("dp", None, "mp"),
            P("dp", "mp"),
            P("dp", "mp", None),
            P("dp", None),
        ),
        check_vma=False,
    )
```

```python
import functools

import jax
import jax.numpy as jnp
from jax import lax
from jax.experimental import pallas as pl
from jax.experimental.pallas import tpu as pltpu
from jax.sharding import PartitionSpec as P

F32 = jnp.float32
BF16 = jnp.bfloat16
SLOT_DEV = 256
LANES = 128
SUB = 8
LOG2E = 1.4426950408889634
LN2 = 0.6931471805599453
VMEM = 48 * 2**20
norm_eps = 1e-05
MESH = pl.DeviceIdType.MESH


NN = ((1,), (0,))
NT = ((1,), (1,))
TN = ((0,), (0,))


def dot(a, b, dims):
    return lax.dot_general(a, b, (dims, ((), ())), preferred_element_type=F32)


def lane(col):
    return jnp.broadcast_to(col, (SUB, LANES))


def row(ref, n, cs):
    return jnp.broadcast_to(ref[n : n + 1, cs], (SUB, LANES))


def tiles(count):
    return [slice(ct * LANES, (ct + 1) * LANES) for ct in range(count // LANES)]


def whole(*dims):
    return pl.BlockSpec(dims, lambda i: (0,) * len(dims))


def local_scan(step_ref, in_ref, map_ref, rates_ref, out_ref, nh, half, reverse):
    places, chans = step_ref.shape[0], step_ref.shape[2]
    cols = tiles(chans)
    ns = [nh * half + n for n in range(half)]

    def body(lap, st):
        i = places - 1 - lap if reverse else lap
        st = list(st)
        m = map_ref[i]
        mm = [lane(m[:, n : n + 1]) for n in ns]
        for ct, cs in enumerate(cols):
            s = step_ref[i, :, cs]
            x = in_ref[i, :, cs]
            for n in range(half):
                k = n * len(cols) + ct
                e = jnp.exp2(s * row(rates_ref, ns[n], cs))
                st[k] = e * (st[k] + x * mm[n]) if reverse else e * st[k] + x * mm[n]
        return tuple(st)

    zero = tuple(jnp.zeros((SUB, LANES), F32) for _ in range(half * len(cols)))
    st = lax.fori_loop(0, places, body, zero, unroll=8)
    for n in range(half):
        for ct, cs in enumerate(cols):
            out_ref[ns[n], :, cs] = st[n * len(cols) + ct]


def block_sums(part_s, sum_s, ra, sb, rb, send, recv):
    j, near, far = mp_pair()
    c = j % 2
    size = ra.shape[1]
    mine, theirs = ds(c * size, size), ds((1 - c) * size, size)

    def copy(kind, b, src, dst, to):
        return pltpu.make_async_remote_copy(
            src_ref=src,
            dst_ref=dst,
            send_sem=send.at[kind, b],
            recv_sem=recv.at[kind, b],
            device_id={"mp": to},
            device_id_type=MESH,
        )

    one = lambda b: copy(0, b, part_s.at[b, theirs], ra.at[b], near)
    two = lambda b: copy(1, b, sb.at[b], rb.at[b], far)
    three = lambda b: copy(2, b, sum_s.at[b, mine], sum_s.at[b, mine], near)

    def pair_sum(b):
        one(b).wait_recv()
        sb[b] = (part_s[b, mine, :].astype(F32) + ra[b].astype(F32)).astype(BF16)
        two(b).start()

    def far_sum(b):
        two(b).wait_recv()
        sum_s[b, mine, :] = (sb[b].astype(F32) + rb[b].astype(F32)).astype(BF16)
        three(b).start()

    def end(count):
        for b in range(count):
            three(b).wait_recv()
        for b in range(count):
            for made in (one, two, three):
                made(b).wait_send()

    return lambda b: one(b).start(), pair_sum, far_sum, end


def forward_kernel(
    step_ref,
    x_ref,
    bin_ref,
    cout_ref,
    rates_ref,
    h0_ref,
    inner_ref,
    gate_ref,
    skip_ref,
    weight_ref,
    quarter_ref,
    scan_ref,
    gated_ref,
    sum_ref,
    hb_ref,
    hf_ref,
    rows_ref,
    st_ref,
    y_ref,
    part_s,
    sum_s,
    rows_s,
    ra,
    sb,
    rb,
    send,
    recv,
    dsend,
    drecv,
    local,
):
    places, chans = step_ref.shape[0], step_ref.shape[2]
    states, half = rates_ref.shape[0], 8
    cols = tiles(chans)
    n = quarter_ref.shape[0]
    g = lax.axis_index("dp")
    _, near, far = mp_pair()
    i_block, count = pl.program_id(0), part_s.shape[0]
    leave, pair_sum, far_sum, sums_end = block_sums(part_s, sum_s, ra, sb, rb, send, recv)
    start, middle, end = dispatching(n, quarter_ref, rows_s, dsend, drecv, local)

    @pl.when(i_block == 0)
    def _():
        greet([{"mp": near}, {"mp": far}] + [{"dp": (g + k) % n} for k in range(1, n)])
        start()

    @pl.when(pl.program_id(0) == 0)
    def _():
        st_ref[...] = h0_ref[...]

    for nh in range(states // half):
        ns = [nh * half + n for n in range(half)]

        def body(i, st):
            st = list(st)
            b = bin_ref[i]
            c = cout_ref[i]
            bb = [lane(b[:, n : n + 1]) for n in ns]
            cc = [lane(c[:, n : n + 1]) for n in ns]
            for ct, cs in enumerate(cols):
                s = step_ref[i, :, cs]
                x = x_ref[i, :, cs]
                y = y_ref[i, :, cs] if nh else jnp.zeros((SUB, LANES), F32)
                for n in range(half):
                    k = n * len(cols) + ct
                    hb_ref[i, ns[n], :, cs] = st[k].astype(hb_ref.dtype)
                    e = jnp.exp2(s * row(rates_ref, ns[n], cs))
                    st[k] = e * st[k] + x * bb[n]
                    y = y + cc[n] * st[k]
                y_ref[i, :, cs] = y
            return tuple(st)

        st = tuple(st_ref[n, :, cs] for n in ns for cs in cols)
        st = lax.fori_loop(0, places, body, st, unroll=8)
        for n in range(half):
            for ct, cs in enumerate(cols):
                st_ref[ns[n], :, cs] = st[n * len(cols) + ct]
    hf_ref[...] = st_ref[...]
    scan = y_ref[...].reshape(places * SUB, chans) + skip_ref[...] * inner_ref[...].astype(F32)
    scan_ref[...] = scan
    gate = gate_ref[...].astype(F32)
    gated = (scan * (gate * jax.nn.sigmoid(gate))).astype(BF16)
    gated_ref[...] = gated
    part_s[i_block] = dot(gated, weight_ref[...], NN).astype(BF16)
    leave(i_block)
    lag = 5

    @pl.when(i_block >= 1)
    def _():
        pair_sum(i_block - 1)

    @pl.when(i_block >= lag)
    def _():
        far_sum(i_block - lag)

    @pl.when(i_block == count - 2)
    def _():
        middle()

    @pl.when(i_block == count - 1)
    def _():
        pair_sum(count - 1)
        for b in range(count - lag, count):
            far_sum(b)
        end()
        rows_ref[...] = rows_s[...]
        sums_end(count)
        sum_ref[...] = sum_s[...].reshape(sum_ref.shape)


def forward(collective_id, step, x, bin_vals, cout, rates, h0, inner, both, skip, weight, quarter, block=16):
    places, _, chans = step.shape
    n, hr, hc = quarter.shape
    count = places // block
    sems = pltpu.SemaphoreType.DMA((3, count))
    dsems = pltpu.SemaphoreType.DMA((2, n))
    states = rates.shape[0]
    width = weight.shape[1]
    rows = places * SUB
    part = lambda size: pl.BlockSpec((block, SUB, size), lambda i: (i, 0, 0))
    flat = lambda size, col=0: pl.BlockSpec((block * SUB, size), lambda i: (i, col))
    shape = jax.ShapeDtypeStruct
    return pl.pallas_call(
        forward_kernel,
        grid=(count,),
        in_specs=[
            part(chans),
            part(chans),
            part(states),
            part(states),
            whole(states, chans),
            whole(states, SUB, chans),
            flat(chans),
            flat(chans, 1),
            whole(1, chans),
            whole(chans, width),
            whole(n, hr, hc),
        ],
        out_specs=[
            flat(chans),
            flat(chans),
            whole(rows, width),
            pl.BlockSpec((block, states, SUB, chans), lambda i: (i, 0, 0, 0)),
            whole(states, SUB, chans),
            whole(n, hr, 2 * hc),
        ],
        out_shape=[
            shape((rows, chans), F32),
            shape((rows, chans), BF16),
            shape((rows, width), BF16),
            shape((places, states, SUB, chans), BF16),
            shape((states, SUB, chans), F32),
            shape((n, hr, 2 * hc), BF16),
        ],
        scratch_shapes=[
            pltpu.VMEM((states, SUB, chans), F32),
            pltpu.VMEM((block, SUB, chans), F32),
            pltpu.VMEM((count, block * SUB, width), BF16),
            pltpu.VMEM((count, block * SUB, width), BF16),
            pltpu.VMEM((n, hr, 2 * hc), BF16),
            pltpu.VMEM((count, block * SUB // 2, width), BF16),
            pltpu.VMEM((count, block * SUB // 2, width), BF16),
            pltpu.VMEM((count, block * SUB // 2, width), BF16),
            sems,
            sems,
            dsems,
            dsems,
            pltpu.SemaphoreType.DMA,
        ],
        compiler_params=pltpu.CompilerParams(
            collective_id=collective_id, has_side_effects=True, vmem_limit_bytes=VMEM
        ),
    )(step, x, bin_vals, cout, rates, h0, inner, both, skip, weight, quarter)


def backward_kernel(
    n,
    step_ref,
    x_ref,
    gs_ref,
    past_ref,
    bin_ref,
    cout_ref,
    rates_ref,
    g0_ref,
    hf_ref,
    hb_ref,
    inner_ref,
    slope_ref,
    low_ref,
    weight_ref,
    skip_ref,
    early_ref,
    landed_ref,
    base_ref,
    proj_out,
    given_ref,
    gin_ref,
    gout_ref,
    few_ref,
    result_ref,
    sbias_ref,
    gst_ref,
    rt_ref,
    q_ref,
    p_ref,
    sg_ref,
    sb_ref,
    gp_ref,
    sums,
    result_s,
    proj_ref,
    part_s,
    sum_s,
    qa,
    qs,
    qr,
    send,
    recv,
    rsend,
    rrecv,
    qsend,
    qrecv,
):
    places, chans = step_ref.shape[0], step_ref.shape[2]
    states, some = rates_ref.shape[0], 4
    cols = tiles(chans)
    g = lax.axis_index("dp")
    j, near, far = mp_pair()
    y, c = j // 2, j % 2
    hr, hc = landed_ref.shape[1], landed_ref.shape[2]
    up, down, mine = ds(y * hr, hr), ds((1 - y) * hr, hr), ds(c * hc, hc)
    start, middle, end = gathering(n, sums, send, recv)

    def share(kind, src, dst, to):
        return pltpu.make_async_remote_copy(
            src_ref=src,
            dst_ref=dst,
            send_sem=rsend.at[kind],
            recv_sem=rrecv.at[kind],
            device_id={"mp": to},
            device_id_type=MESH,
        )

    place = lambda rows: result_s.at[:, rows, mine]
    to_far = share(0, landed_ref, place(up), far)
    to_near = share(1, landed_ref, place(up), near)
    pass_on = share(2, place(down), place(down), near)
    step_id, steps = pl.program_id(0), pl.num_programs(0)

    @pl.when(step_id == 0)
    def _():
        greet([{"mp": near}, {"mp": far}] + [{"dp": (g + k) % n} for k in range(1, n)])
        sums[g] = early_ref[...]
        start()
        to_far.start()
        to_near.start()
        result_s[:, up, mine] = landed_ref[...]

    @pl.when(step_id == steps // 2 - 1)
    def _():
        middle(0)

    @pl.when(step_id == steps // 2 + 2)
    def _():
        middle(1)

    @pl.when(step_id == steps - 2)
    def _():
        to_far.wait_recv()
        pass_on.start()

    @pl.when(pl.program_id(0) == 0)
    def _():
        gst_ref[...] = g0_ref[...]
        rt_ref[...] = jnp.zeros_like(rt_ref)
        given_ref[...] = jnp.zeros_like(given_ref)
        proj_ref[...] = jnp.zeros_like(proj_ref)
        sbias_ref[...] = jnp.zeros_like(sbias_ref)

    gp_ref[0] = past_ref[0]
    gp_ref[1:places] = gs_ref[0 : places - 1]

    for nq in range(states // some):
        ns = [nq * some + n for n in range(some)]
        size = some * len(cols)

        def body(lap, carry):
            i = places - 1 - lap
            st, rt = list(carry[:size]), list(carry[size:])
            b = bin_ref[i]
            c = cout_ref[i]
            bb = [lane(b[:, n : n + 1]) for n in ns]
            cc = [lane(c[:, n : n + 1]) for n in ns]
            qb, qc = [None] * some, [None] * some
            for ct, cs in enumerate(cols):
                s = step_ref[i, :, cs]
                x = x_ref[i, :, cs]
                g = gs_ref[i, :, cs]
                gp = gp_ref[i, :, cs]
                sg = sg_ref[i, :, cs] if nq else jnp.zeros((SUB, LANES), F32)
                sb = sb_ref[i, :, cs] if nq else jnp.zeros((SUB, LANES), F32)
                for n in range(some):
                    k = n * len(cols) + ct
                    rate = row(rates_ref, ns[n], cs)
                    e = jnp.exp2(s * rate)
                    h = hb_ref[i, ns[n], :, cs].astype(F32)
                    grad = st[k] + g * cc[n]
                    st[k] = e * grad
                    dg = st[k] * h
                    sg = sg + dg * rate
                    rt[k] = rt[k] + dg * s
                    sb = sb + grad * bb[n]
                    qb[n] = grad * x if ct == 0 else qb[n] + grad * x
                    qc[n] = gp * h if ct == 0 else qc[n] + gp * h
                sg_ref[i, :, cs] = sg
                sb_ref[i, :, cs] = sb
            rows = pl.ds(pl.multiple_of(i * SUB, SUB), SUB)
            for n in range(some):
                q_ref[rows, ns[n] * LANES : (ns[n] + 1) * LANES] = qb[n]
                p_ref[rows, ns[n] * LANES : (ns[n] + 1) * LANES] = qc[n]
            return tuple(st) + tuple(rt)

        at = [(ns[n], slice(None), cs) for n in range(some) for cs in cols]
        init = tuple(gst_ref[a] for a in at) + tuple(rt_ref[a] for a in at)
        out = lax.fori_loop(0, places, body, init, unroll=8)
        for j, a in enumerate(at):
            gst_ref[a] = out[j]
            rt_ref[a] = out[size + j]
    rank = low_ref.shape[1]
    wide = proj_ref.shape[1]
    dims = (states * LANES, wide)
    state = lax.broadcasted_iota(jnp.int32, dims, 0) // LANES
    column = lax.broadcasted_iota(jnp.int32, dims, 1)
    to_bin = jnp.where(column == state + rank, 1.0, 0.0).astype(BF16)
    to_cout = jnp.where(column == state + rank + states, 1.0, 0.0).astype(BF16)
    block_rows = places * SUB
    base = (pl.num_programs(0) - 1 - pl.program_id(0)) * block_rows
    here = pl.ds(pl.multiple_of(base + SUB, SUB), block_rows)
    late = pl.ds(pl.multiple_of(base, SUB), block_rows)

    @pl.when(pl.program_id(0) == 0)
    def _():
        end_rows = pl.ds(pl.multiple_of(base + block_rows, SUB), SUB)
        total_ = None
        for n_ in range(states):
            value = hf_ref[n_, :, cols[0]] * gs_ref[places - 1, :, cols[0]]
            for cs in cols[1:]:
                value = value + hf_ref[n_, :, cs] * gs_ref[places - 1, :, cs]
            term = jnp.dot(
                value.astype(BF16), to_cout[n_ * LANES : (n_ + 1) * LANES], preferred_element_type=F32
            )
            total_ = term if total_ is None else total_ + term
        proj_ref[end_rows, :] += total_

    proj_ref[late, :] += jnp.dot(p_ref[...].astype(BF16), to_cout, preferred_element_type=F32)
    flat = lambda ref: ref[...].reshape(places * SUB, chans)
    sb = flat(sb_ref)
    base_ref[...] = flat(gs_ref) * skip_ref[...] + flat(step_ref) * sb
    pre = (flat(sg_ref) * LN2 + inner_ref[...].astype(F32) * sb) * slope_ref[...]
    sbias_ref[...] += jnp.sum(pre.reshape(places, SUB, chans), axis=0)
    pre = pre.astype(BF16)
    given_ref[0:rank, :] += dot(low_ref[...], pre, TN)
    proj_ref[here, :] += dot(pre, weight_ref[...], NT) + jnp.dot(
        q_ref[...].astype(BF16), to_bin, preferred_element_type=F32
    )

    blocks = part_s.shape[0]
    at_block = blocks - 1 - step_id
    leave, pair_sum, far_sum, sums_end = block_sums(part_s, sum_s, qa, qs, qr, qsend, qrecv)
    part_s[at_block] = proj_ref[here, :].astype(BF16)
    leave(at_block)

    @pl.when(step_id >= 1)
    def _():
        pair_sum(at_block + 1)

    @pl.when(step_id >= 5)
    def _():
        far_sum(at_block + 5)

    @pl.when(pl.program_id(0) == pl.num_programs(0) - 1)
    def _():
        pair_sum(0)
        for b in (4, 3, 2, 1, 0):
            far_sum(b)
        sums_end(blocks)
        proj_out[...] = sum_s[...].reshape(proj_out.shape)
        end()
        to_near.wait_recv()
        pass_on.wait_recv()
        for made in (to_far, to_near, pass_on):
            made.wait_send()
        result_ref[...] = result_s[...]
        for n_ in range(states):
            line = rank + n_
            total_ = jnp.sum(rt_ref[n_], axis=0, keepdims=True)
            given_ref[line : line + 1, :] = total_ * rates_ref[n_ : n_ + 1, :] * LN2
        line = rank + states
        given_ref[line : line + 1, :] = jnp.sum(sbias_ref[...], axis=0, keepdims=True)
        mh = gin_ref.shape[0] // n
        sh = few_ref.shape[0] // n
        for b in range(n):
            few_ref[b * sh : (b + 1) * sh, :] = sums[b, 2 * mh : 2 * mh + sh, :].astype(F32)
            gin_ref[b * mh : (b + 1) * mh, :] = sums[b, 0:mh, :].astype(F32)
            gout_ref[b * mh : (b + 1) * mh, :] = sums[b, mh : 2 * mh, :].astype(F32)


def backward(
    n, collective_id, mh, step, x, gs, bin_vals, cout, rates, g0, hf, hb, inner, slope, low, weight, skip, early, quarter, block=16
):
    places, _, chans = step.shape
    states = rates.shape[0]
    rank, wide = low.shape[1], weight.shape[0]
    extra = (rank + states + SUB) // SUB * SUB
    count = places // block
    part = lambda width: pl.BlockSpec((block, SUB, width), lambda i: (count - 1 - i, 0, 0))
    flat = lambda width: pl.BlockSpec((block * SUB, width), lambda i: (count - 1 - i, 0))
    rows = places * SUB
    tall = n * mh
    proj_blocks = pltpu.VMEM((count, block * SUB, wide), BF16)
    proj_halves = pltpu.VMEM((count, block * SUB // 2, wide), BF16)
    few = n * (early.shape[0] - 2 * mh)
    sems = pltpu.SemaphoreType.DMA((2, PIECES * n // 2))
    return pl.pallas_call(
        functools.partial(backward_kernel, n),
        grid=(count,),
        in_specs=[
            part(chans),
            part(chans),
            part(chans),
            pl.BlockSpec((1, SUB, chans), lambda i: (jnp.maximum((count - 1 - i) * block - 1, 0), 0, 0)),
            part(states),
            part(states),
            whole(states, chans),
            whole(states, SUB, chans),
            whole(states, SUB, chans),
            pl.BlockSpec((block, states, SUB, chans), lambda i: (count - 1 - i, 0, 0, 0)),
            flat(chans),
            flat(chans),
            flat(rank),
            whole(wide, chans),
            whole(1, chans),
            whole(*early.shape),
            whole(*quarter.shape),
        ],
        out_specs=[
            flat(chans),
            whole(rows, wide),
            whole(extra, chans),
            whole(tall, chans),
            whole(tall, chans),
            whole(few, chans),
            whole(n, 2 * quarter.shape[1], 2 * quarter.shape[2]),
        ],
        out_shape=[
            jax.ShapeDtypeStruct((rows, chans), F32),
            jax.ShapeDtypeStruct((rows, wide), BF16),
            jax.ShapeDtypeStruct((extra, chans), F32),
            jax.ShapeDtypeStruct((tall, chans), F32),
            jax.ShapeDtypeStruct((tall, chans), F32),
            jax.ShapeDtypeStruct((few, chans), F32),
            jax.ShapeDtypeStruct((n, 2 * quarter.shape[1], 2 * quarter.shape[2]), BF16),
        ],
        scratch_shapes=[
            pltpu.VMEM((SUB, chans), F32),
            pltpu.VMEM((states, SUB, chans), F32),
            pltpu.VMEM((states, SUB, chans), F32),
            pltpu.VMEM((block * SUB, states * LANES), F32),
            pltpu.VMEM((block * SUB, states * LANES), F32),
            pltpu.VMEM((block, SUB, chans), F32),
            pltpu.VMEM((block, SUB, chans), F32),
            pltpu.VMEM((block, SUB, chans), F32),
            pltpu.VMEM((n, *early.shape), BF16),
            pltpu.VMEM((n, 2 * quarter.shape[1], 2 * quarter.shape[2]), BF16),
            pltpu.VMEM((rows + SUB, wide), F32),
            proj_blocks,
            proj_blocks,
            proj_halves,
            proj_halves,
            proj_halves,
            sems,
            sems,
            pltpu.SemaphoreType.DMA((3,)),
            pltpu.SemaphoreType.DMA((3,)),
            pltpu.SemaphoreType.DMA((3, count)),
            pltpu.SemaphoreType.DMA((3, count)),
        ],
        compiler_params=pltpu.CompilerParams(
            collective_id=collective_id, has_side_effects=True, vmem_limit_bytes=VMEM
        ),
    )(step, x, gs, gs, bin_vals, cout, rates, g0, hf, hb, inner, slope, low, weight, skip, early, quarter)


def mp_pair():
    j = lax.axis_index("mp")
    return j, j + 1 - 2 * (j % 2), (j + 2) % 4


def ds(start, size):
    return pl.ds(pl.multiple_of(start, size), size)


def greet(others):
    barrier = pltpu.get_barrier_semaphore()
    for other in others:
        pl.semaphore_signal(barrier, inc=1, device_id=other, device_id_type=MESH)
    pl.semaphore_wait(barrier, len(others))


def sending(src, dst, send, recv, device):
    copy = pltpu.make_async_remote_copy(
        src_ref=src, dst_ref=dst, send_sem=send, recv_sem=recv, device_id=device, device_id_type=MESH
    )
    copy.start()
    return copy


def vmem_call(kernel, out_shape, scratch, collective_id, *args, cost=0):
    space = pl.BlockSpec(memory_space=pltpu.VMEM)
    return pl.pallas_call(
        kernel,
        out_shape=out_shape,
        in_specs=[space] * len(args),
        out_specs=jax.tree.map(lambda _: space, out_shape),
        scratch_shapes=scratch,
        compiler_params=pltpu.CompilerParams(
            collective_id=collective_id, has_side_effects=True, vmem_limit_bytes=VMEM
        ),
    )(*args)


def half_turn(tile):
    return pltpu.roll(tile, SUB // 2, 0)


def send_totals(n, total_ref, all_ref, send, recv):
    g = lax.axis_index("dp")
    all_ref[0] = total_ref[...] + half_turn(total_ref[...])
    return [
        sending(all_ref.at[0], all_ref.at[k], send.at[1, k], recv.at[1, k], {"dp": (g + k) % n})
        for k in range(1, n)
    ]


def exchange_body(
    n, reverse, copies, part_ref, total_ref, rates_ref, packed_ref, all_ref, out_ref, sbuf, rbuf, send, recv
):
    g = lax.axis_index("dp")
    states, chans = rates_ref.shape
    pairs = states // 2
    upper = lax.broadcasted_iota(jnp.int32, (SUB, chans), 0) >= SUB // 2
    total = total_ref[...]
    decay = lambda m: jnp.exp2(jnp.broadcast_to(rates_ref[m : m + 1, :], (SUB, chans)) * total)

    def summary(m):
        part = part_ref[m]
        return part + decay(m) * half_turn(part)

    def packed(p):
        low, high = summary(p), summary(p + pairs)
        if reverse:
            return jnp.where(upper, half_turn(high), low)
        return jnp.where(upper, high, half_turn(low))

    for p in range(0, pairs, 2):
        sbuf[p * SUB : (p + 2) * SUB, :] = jnp.concatenate([packed(p), packed(p + 1)], axis=0).astype(BF16)
    copies = copies + [
        sending(sbuf, rbuf.at[k], send.at[0, k], recv.at[0, k], {"dp": (g + k) % n})
        for k in range(1, n)
    ]
    for copy in copies:
        copy.wait_recv()

    def one(lap, held):
        away = n - 1 - lap
        slot = n - away if reverse else away
        use = (g + away < n) if reverse else (away <= g)
        steps = all_ref[slot]
        new = []
        for p in range(0, pairs, 2):
            got = rbuf[slot, p * SUB : (p + 2) * SUB, :].astype(F32)
            for q in (p, p + 1):
                fall = jnp.exp2(packed_ref[q] * steps)
                value = fall * held[q] + got[(q - p) * SUB : (q - p + 1) * SUB]
                new.append(jnp.where(use, value, held[q]))
        return tuple(new)

    zero = tuple(jnp.zeros((SUB, chans), F32) for _ in range(pairs))
    held = lax.fori_loop(0, n - 1, one, zero)
    for m in range(states):
        state = held[m % pairs]
        if (m >= pairs) != reverse:
            state = half_turn(state)
        later = half_turn(decay(m) * state + part_ref[m])
        out_ref[m] = jnp.where(upper, state, later) if reverse else jnp.where(upper, later, state)
    for copy in copies:
        copy.wait_send()


def packed_rates(rates):
    states, chans = rates.shape
    pairs = states // 2
    wide = lambda r: jnp.broadcast_to(r[:, None, :], (pairs, SUB // 2, chans))
    return jnp.concatenate([wide(rates[:pairs]), wide(rates[pairs:])], axis=1)


def enter_forward_kernel(
    n, proj_ref, weight_ref, bias_ref, inner_ref, valid_ref, rates_ref, packed_ref,
    step_ref, drive_ref, slope_ref, bin_ref, cout_ref, low_ref, total_ref, h0_ref, all_ref,
    part, sbuf, rbuf, send, recv,
):
    places, _, chans = step_ref.shape
    states = rates_ref.shape[0]
    rank = weight_ref.shape[0]
    g = lax.axis_index("dp")
    greet([{"dp": (g + k) % n} for k in range(1, n)])
    size = 256
    total_ref[...] = jnp.zeros_like(total_ref)

    def block(b, _):
        at = ds(b * size, size)
        here = pl.ds(pl.multiple_of(b * (size // SUB), size // SUB), size // SUB)
        by_place = lambda v: v.reshape(size // SUB, SUB, v.shape[1])
        proj = proj_ref[at, :]
        low = proj[:, 0:rank]
        high = low.astype(BF16)
        rest = (low - high.astype(F32)).astype(BF16)
        low_ref[at, :] = high
        pre = dot(high, weight_ref[...], NN) + dot(rest, weight_ref[...], NN) + bias_ref[...]
        valid = valid_ref[at, :]
        steps = valid * (jnp.maximum(pre, 0.0) + jnp.log1p(jnp.exp(-jnp.abs(pre))))
        slope_ref[at, :] = valid * jax.nn.sigmoid(pre)
        step_ref[here] = by_place(steps)
        drive_ref[here] = by_place(steps * inner_ref[at, :].astype(F32))
        total_ref[...] += jnp.sum(by_place(steps), axis=0)
        bin_ref[here] = by_place(proj[:, rank : rank + states])
        cout_ref[here] = by_place(proj[:, rank + states : rank + 2 * states])
        return 0

    lax.fori_loop(0, places * SUB // size, block, 0)
    copies = send_totals(n, total_ref, all_ref, send, recv)
    half = 8
    for nh in range(states // half):
        local_scan(step_ref, drive_ref, bin_ref, rates_ref, part, nh, half, False)
    exchange_body(n, False, copies, part, total_ref, rates_ref, packed_ref, all_ref, h0_ref, sbuf, rbuf, send, recv)


def enter_forward(n, collective_id, proj, weight, bias, inner, valid, rates):
    rows, chans = inner.shape
    states = rates.shape[0]
    rank = weight.shape[0]
    shape = jax.ShapeDtypeStruct
    places = rows // SUB
    entering = shape((states, SUB, chans), F32)
    sems = pltpu.SemaphoreType.DMA((2, n))
    return vmem_call(
        functools.partial(enter_forward_kernel, n),
        [
            shape((places, SUB, chans), F32),
            shape((places, SUB, chans), F32),
            shape((rows, chans), F32),
            shape((places, SUB, states), F32),
            shape((places, SUB, states), F32),
            shape((rows, rank), BF16),
            shape((SUB, chans), F32),
            entering,
            shape((n, SUB, chans), F32),
        ],
        [
            pltpu.VMEM((states, SUB, chans), F32),
            pltpu.VMEM((states * SUB // 2, chans), BF16),
            pltpu.VMEM((n, states * SUB // 2, chans), BF16),
            sems,
            sems,
        ],
        collective_id, proj, weight, bias, inner, valid, rates, packed_rates(rates),
    )


def dp_pairs(n):
    g = lax.axis_index("dp")
    odd, z, m = g % 2, g // 2, n // 2
    return g, odd, {"dp": g + 1 - 2 * odd}, [{"dp": 2 * ((z + k) % m) + odd} for k in range(1, m)]


PIECES = 2


def gathering(n, sums, send, recv):
    g, odd, pair, like = dp_pairs(n)
    z, m = g // 2, n // 2
    rows = sums.shape[1]
    cut = (rows // 2 + 15) // 16 * 16
    parts = [pl.ds(0, cut), pl.ds(cut, rows - cut)]

    def copy(kind, k, p, b, to):
        return pltpu.make_async_remote_copy(
            src_ref=sums.at[b, parts[p]],
            dst_ref=sums.at[b, parts[p]],
            send_sem=send.at[kind, p * m + k],
            recv_sem=recv.at[kind, p * m + k],
            device_id=to,
            device_id_type=MESH,
        )

    third = lambda k, p: copy(0, k, p, g, like[k])
    fourth = lambda k, p: copy(1, k, p, 2 * ((z + m - k) % m) + odd, pair)

    def start():
        for p in range(PIECES):
            for k in range(m - 1):
                third(k, p).start()
            fourth(0, p).start()

    def middle(p):
        for k in range(m - 1):
            third(k, p).wait_recv()
            fourth(k + 1, p).start()

    def end():
        for p in range(PIECES):
            for k in range(m):
                fourth(k, p).wait_recv()
            for k in range(m - 1):
                third(k, p).wait_send()
            for k in range(m):
                fourth(k, p).wait_send()

    return start, middle, end


def enter_backward_kernel(
    n, step_ref, gs_ref, cout_ref, total_ref, rates_ref, packed_ref, all_ref, blocks_ref,
    g0_ref, own_ref, part, sbuf, rbuf, pa, ps, pc, send, recv, pair_send, pair_recv,
):
    states = rates_ref.shape[0]
    g, odd, pair, like = dp_pairs(n)
    z, m = g // 2, n // 2
    greet([{"dp": (g + k) % n} for k in range(1, n)])
    order = [(z + k) % m for k in range(1, m)] + [z]
    first = [
        sending(blocks_ref.at[2 * order[k] + 1 - odd], pa.at[k], pair_send.at[0, k], pair_recv.at[0, k], pair)
        for k in range(m)
    ]
    half = 8
    second = []
    for nh in range(states // half):
        local_scan(step_ref, gs_ref, cout_ref, rates_ref, part, nh, half, True)
        if nh == 0:
            few = range(0, m // 2)
        else:
            few = range(m // 2, m)
        for k in few:
            first[k].wait_recv()
            ps[k] = (blocks_ref[2 * order[k] + odd].astype(F32) + pa[k].astype(F32)).astype(BF16)
            if k < m - 1:
                second.append(sending(ps.at[k], pc.at[k], pair_send.at[1, k], pair_recv.at[1, k], like[k]))
    exchange_body(n, True, [], part, total_ref, rates_ref, packed_ref, all_ref, g0_ref, sbuf, rbuf, send, recv)
    value = ps[m - 1].astype(F32)
    for copy in second:
        copy.wait_recv()
    for k in range(m - 1):
        value = value + pc[k].astype(F32)
    own_ref[...] = value.astype(BF16)
    for copy in first + second:
        copy.wait_send()


def enter_backward(n, collective_id, step, gs, cout, total, rates, totals, blocks):
    _, _, chans = step.shape
    states = rates.shape[0]
    shape = jax.ShapeDtypeStruct
    m = n // 2
    sems = pltpu.SemaphoreType.DMA((2, n))
    some = pltpu.VMEM((m, *blocks.shape[1:]), BF16)
    return vmem_call(
        functools.partial(enter_backward_kernel, n),
        [shape((states, SUB, chans), F32), shape(blocks.shape[1:], BF16)],
        [
            pltpu.VMEM((states, SUB, chans), F32),
            pltpu.VMEM((states * SUB // 2, chans), BF16),
            pltpu.VMEM((n, states * SUB // 2, chans), BF16),
            some,
            some,
            some,
            sems,
            sems,
            sems,
            sems,
        ],
        collective_id, step, gs, cout, total, rates, packed_rates(rates), totals, blocks,
    )


def half_pick(ids, slots):
    iota = lax.broadcasted_iota(jnp.int32, (ids.shape[0], slots), 1)
    return jnp.where(iota == ids, 1.0, 0.0).astype(BF16)


def dispatching(n, x_ref, out_ref, send, recv, local):
    g = lax.axis_index("dp")
    j, near, _ = mp_pair()
    hc = x_ref.shape[2]
    cols = ds((j % 2) * hc, hc)

    def leave(k):
        return pltpu.make_async_remote_copy(
            src_ref=x_ref.at[(g + k) % n],
            dst_ref=out_ref.at[g, :, cols],
            send_sem=send.at[0, k],
            recv_sem=recv.at[0, k],
            device_id={"dp": (g + k) % n},
            device_id_type=MESH,
        )

    def share(k):
        place = out_ref.at[(g + n - k) % n, :, cols]
        return pltpu.make_async_remote_copy(
            src_ref=place,
            dst_ref=place,
            send_sem=send.at[1, k],
            recv_sem=recv.at[1, k],
            device_id={"mp": near},
            device_id_type=MESH,
        )

    own = pltpu.make_async_copy(x_ref.at[g], out_ref.at[g, :, cols], local)

    def start():
        own.start()
        for k in range(1, n):
            leave(k).start()

    def middle():
        for k in range(n):
            if k:
                leave(k).wait_recv()
            else:
                own.wait()
            share(k).start()

    def end():
        for k in range(n):
            share(k).wait_recv()
        for k in range(n):
            if k:
                leave(k).wait_send()
            share(k).wait_send()

    return start, middle, end


def arrange(cuts, in_ref, tile_ref):
    seqs, chunks, places = cuts
    for ct in range(tile_ref.shape[0]):
        for q in range(seqs):
            for k in range(chunks):
                start = (q * chunks + k) * places
                value = in_ref[start : start + places, ct * LANES : (ct + 1) * LANES]
                tile_ref[ct, pl.ds(k * seqs + q, places, stride=SUB), :] = value.astype(F32)


def front_kernel(
    n,
    cuts,
    capacity,
    tokens_ref,
    cot_ref,
    routes_ref,
    lengths_ref,
    gain_ref,
    weight_ref,
    taps_ref,
    bias_ref,
    select_ref,
    tok_ref,
    cot_low_ref,
    normed_ref,
    both_ref,
    pre_ref,
    inner_ref,
    lead_ref,
    proj_ref,
    quarter,
    slot_ref,
    half_ref,
    valid_ref,
    hot_ref,
    tile_s,
    ext_s,
    live_s,
    got,
    part_s,
    ra,
    sb,
    rb,
    send,
    recv,
):
    seqs, chunks, places = cuts
    g = lax.axis_index("dp")
    j, near, far = mp_pair()
    y, c = j // 2, j % 2
    near, far = {"mp": near}, {"mp": far}
    rows, width = tok_ref.shape
    chans = inner_ref.shape[1]
    kernel = taps_ref.shape[0]
    edge = (kernel - 1) * SUB
    slot_dev = chunks * places
    experts_all = hot_ref.shape[1]
    hr, hc = quarter.shape[1], quarter.shape[2]
    size = 256
    greet([near, far, {"dp": (g + 1) % n}, {"dp": (g + n - 1) % n}])

    arrange(cuts, tokens_ref, tile_s)

    def first(b, _):
        at = ds(b * size, size)
        tok = jnp.concatenate([tile_s[ct, at, :] for ct in range(width // LANES)], axis=1)
        tok_ref[at, :] = tok.astype(BF16)
        inverse = lax.rsqrt(jnp.mean(tok * tok, axis=1, keepdims=True) + norm_eps)
        normed = (tok * inverse * gain_ref[...]).astype(BF16)
        normed_ref[at, :] = normed
        both = dot(normed, weight_ref[...], NN).astype(BF16)
        both_ref[at, :] = both
        ext_s[pl.ds(pl.multiple_of(b * size + edge, SUB), size), :] = both[:, 0:chans].astype(F32)
        return 0

    lax.fori_loop(0, rows // size, first, 0)
    ends = sending(
        both_ref.at[rows - 32 : rows, 0:chans], got, send.at[3, 0], recv.at[3, 0], {"dp": (g + 1) % n}
    )

    at_row = lax.broadcasted_iota(jnp.int32, (rows, 1), 0)
    sub = at_row % SUB
    seq = sub % seqs
    local_place = (sub // seqs) * places + at_row // SUB
    limit = jnp.zeros((rows, 1), jnp.int32)
    for q in range(seqs):
        limit = jnp.where(seq == q, lengths_ref[0:1, q : q + 1], limit)
    valid = jnp.where(g * slot_dev + local_place < limit, 1.0, 0.0)
    valid_ref[...] = valid
    route = routes_ref[...]
    hot = jnp.where(lax.broadcasted_iota(jnp.int32, (rows, experts_all), 1) == route, 1.0, 0.0)
    hot_ref[...] = hot
    live_s[...] = hot * valid
    col = lax.broadcasted_iota(jnp.int32, (1, rows), 1)
    col_sub = col % SUB
    original = (col_sub % seqs) * slot_dev + (col_sub // seqs) * places + col // SUB
    room = 2 * hr

    def position(b, _):
        at = ds(b * size, size)
        here = b * size + lax.broadcasted_iota(jnp.int32, (size, 1), 0)
        here_sub = here % SUB
        mine = (here_sub % seqs) * slot_dev + (here_sub // seqs) * places + here // SUB
        before = jnp.where(original < mine, 1.0, 0.0).astype(BF16)
        live = live_s[at, :]
        earlier = dot(before, live_s[...].astype(BF16), NN)
        pos = jnp.sum(earlier * live, axis=1, keepdims=True)
        kept = jnp.where(pos < capacity, jnp.sum(live, axis=1, keepdims=True), 0.0) > 0.5
        pos = pos.astype(jnp.int32)
        to = routes_ref[at, :]
        slot_ref[at, :] = jnp.where(kept, to * room + pos, -1)
        lower = pos - y * hr
        inside = jnp.where(lower >= 0, 1, 0) * jnp.where(lower < hr, 1, 0)
        half_ref[at, :] = jnp.where(kept, jnp.where(inside > 0, to * hr + lower, -1), -1)
        return 0

    lax.fori_loop(0, rows // size, position, 0)

    ends.wait_recv()
    upper = lax.broadcasted_iota(jnp.int32, (SUB, chans), 0) >= SUB // 2
    some = jnp.where(g > 0, 1.0, 0.0)
    tails = got[...].astype(F32) * some
    for k in range(kernel - 1):
        at = slice(k * SUB, (k + 1) * SUB)
        tail = ext_s[rows + k * SUB : rows + (k + 1) * SUB, :]
        other_tail = tails[32 - edge + k * SUB : 32 - edge + (k + 1) * SUB, :]
        lead = half_turn(jnp.where(upper, other_tail, tail))
        ext_s[at, :] = lead
        lead_ref[at, :] = lead

    half = rows // 2
    count = half // size
    own = c * half
    other = (1 - c) * half

    def conv(start):
        at = ds(start, size)
        pre = jnp.broadcast_to(bias_ref[...], (size, chans))
        for k in range(kernel):
            past = ext_s[pl.ds(pl.multiple_of(start + k * SUB, SUB), size), :]
            pre = pre + taps_ref[k : k + 1, :] * past
        pre_ref[at, :] = pre
        inner = (pre * jax.nn.sigmoid(pre)).astype(BF16)
        inner_ref[at, :] = inner
        part_s[at, :] = dot(inner, select_ref[...], NN)

    one, two, three = [], [], []
    for k in range(count):
        conv(other + k * size)
        at = ds(other + k * size, size)
        one.append(sending(part_s.at[at], ra.at[k], send.at[0, k], recv.at[0, k], near))
    for k in range(count):
        conv(own + k * size)
        one[k].wait_recv()
        sb[k] = part_s[ds(own + k * size, size), :] + ra[k]
        two.append(sending(sb.at[k], rb.at[k], send.at[1, k], recv.at[1, k], far))

    arrange(cuts, cot_ref, tile_s)

    def second(b, _):
        at = ds(b * size, size)
        cot = jnp.concatenate([tile_s[ct, at, :] for ct in range(width // LANES)], axis=1)
        cot_low_ref[at, :] = cot.astype(BF16)
        return 0

    lax.fori_loop(0, rows // size, second, 0)
    pick = half_pick(half_ref[...], n * hr)
    sent = dot(pick, cot_low_ref[:, ds(c * hc, hc)], TN).astype(BF16)
    quarter[...] = sent.reshape(n, hr, hc)
    for k in range(count):
        two[k].wait_recv()
        at = ds(own + k * size, size)
        proj_ref[at, :] = sb[k] + rb[k]
        three.append(sending(proj_ref.at[at], proj_ref.at[at], send.at[2, k], recv.at[2, k], near))
    for copy in three:
        copy.wait_recv()
    for copy in [ends] + one + two + three:
        copy.wait_send()


def front(n, collective_id, cuts, capacity, hr, experts_all, *args):
    tokens, taps, select = args[0], args[6], args[8]
    rows, width = tokens.shape
    kernel, chans = taps.shape
    edge = (kernel - 1) * SUB
    wide = select.shape[1]
    count = rows // 512
    shape = jax.ShapeDtypeStruct
    sems = pltpu.SemaphoreType.DMA((4, count))
    sums = pltpu.VMEM((count, 256, wide), F32)
    return vmem_call(
        functools.partial(front_kernel, n, cuts, capacity),
        [
            shape((rows, width), BF16),
            shape((rows, width), BF16),
            shape((rows, width), BF16),
            shape((rows, 2 * chans), BF16),
            shape((rows, chans), F32),
            shape((rows, chans), BF16),
            shape((edge, chans), F32),
            shape((rows, wide), F32),
            shape((n, hr, width // 2), BF16),
            shape((rows, 1), jnp.int32),
            shape((rows, 1), jnp.int32),
            shape((rows, 1), F32),
            shape((rows, experts_all), F32),
        ],
        [
            pltpu.VMEM((width // LANES, rows, LANES), F32),
            pltpu.VMEM((rows + edge, chans), F32),
            pltpu.VMEM((rows, experts_all), F32),
            pltpu.VMEM((32, chans), BF16),
            pltpu.VMEM((rows, wide), F32),
            sums,
            sums,
            sums,
            sems,
            sems,
        ],
        collective_id, *args,
    )


def middle_kernel(
    n, sum_ref, tok_ref, valid_ref, gain_ref, half_ref, resid_ref, rows_ref, normed_s, quarter, dsend, drecv, local
):
    g = lax.axis_index("dp")
    j, near, _ = mp_pair()
    c = j % 2
    rows, width = tok_ref.shape
    hr, hc = rows_ref.shape[1], width // 2
    size = 256
    greet([{"mp": near}] + [{"dp": (g + k) % n} for k in range(1, n)])

    def norm(b, _):
        at = ds(b * size, size)
        resid = tok_ref[at, :].astype(F32) + valid_ref[at, :] * sum_ref[at, :].astype(F32)
        resid_ref[at, :] = resid
        inverse = lax.rsqrt(jnp.mean(resid * resid, axis=1, keepdims=True) + norm_eps)
        normed_s[at, :] = (resid * inverse * gain_ref[...]).astype(BF16)
        return 0

    lax.fori_loop(0, rows // size, norm, 0)
    pick = half_pick(half_ref[...], n * hr)
    sent = dot(pick, normed_s[:, ds(c * hc, hc)], TN).astype(BF16)
    quarter[...] = sent.reshape(n, hr, hc)
    start, middle, end = dispatching(n, quarter, rows_ref, dsend, drecv, local)
    start()
    middle()
    end()


def mixer_to_experts(n, collective_id, hr, mixed, tok, valid, gain, half_slots):
    rows, width = tok.shape
    shape = jax.ShapeDtypeStruct
    dsems = pltpu.SemaphoreType.DMA((2, n))
    return vmem_call(
        functools.partial(middle_kernel, n),
        [shape((rows, width), F32), shape((n, hr, width), BF16)],
        [
            pltpu.VMEM((rows, width), BF16),
            pltpu.VMEM((n, hr, width // 2), BF16),
            dsems,
            dsems,
            pltpu.SemaphoreType.DMA,
        ],
        collective_id, mixed, tok, valid, gain, half_slots,
    )


def returning(n, x_ref, out_ref, send, recv):
    g = lax.axis_index("dp")
    j, near, far = mp_pair()
    hr, hc = x_ref.shape[1], x_ref.shape[2]
    y, c = j // 2, j % 2
    mine = ds(c * hc, hc)
    up, down = ds(y * hr, hr), ds((1 - y) * hr, hr)

    def copy(kind, k, src, dst, to):
        return pltpu.make_async_remote_copy(
            src_ref=src,
            dst_ref=dst,
            send_sem=send.at[kind, k],
            recv_sem=recv.at[kind, k],
            device_id=to,
            device_id_type=MESH,
        )

    def place(k, rows):
        return out_ref.at[(g + n - k) % n, rows, mine]

    there = lambda k: copy(0, k, x_ref.at[(g + k) % n], out_ref.at[g, up, mine], {"dp": (g + k) % n})
    to_far = lambda k: copy(1, k, place(k, up), place(k, up), {"mp": far})
    to_near = lambda k: copy(2, k, place(k, up), place(k, up), {"mp": near})
    on = lambda k: copy(3, k, place(k, down), place(k, down), {"mp": near})

    def keep():
        out_ref[g, up, mine] = x_ref[g]

    def arrived(k):
        @pl.when(k > 0)
        def _():
            there(k).wait_recv()

        to_far(k).start()
        to_near(k).start()

    def passed(k):
        to_far(k).wait_recv()
        on(k).start()

    def end(k):
        to_near(k).wait_recv()
        on(k).wait_recv()
        for made in (to_far, to_near, on):
            made(k).wait_send()

        @pl.when(k > 0)
        def _():
            there(k).wait_send()

    return keep, there, arrived, passed, end


def each(act, start, count):
    def one(i, _):
        act(start + i)
        return 0

    lax.fori_loop(0, count, one, 0)


def expert_kernel(
    n,
    rows_ref,
    cot_ref,
    up_ref,
    ub_ref,
    down_ref,
    up2_ref,
    down2_ref,
    ub2_ref,
    db_ref,
    router_ref,
    hot_ref,
    out_ref,
    quarter_ref,
    gates_ref,
    gown_ref,
    gother_ref,
    gub_ref,
    gdb_ref,
    part,
    hid,
    slope,
    pre,
    grad,
    ra,
    qb,
    gate_part,
    gate_near,
    gate_sum,
    gate_in,
    send,
    recv,
    near_send,
    near_recv,
    gate_send,
    gate_recv,
):
    g = lax.axis_index("dp")
    j, near, far = mp_pair()
    near, far = {"mp": near}, {"mp": far}
    y, c = j // 2, j % 2
    hr, width = rows_ref.shape[1], rows_ref.shape[2]
    hidden = up_ref.shape[1]
    hc = width // 2
    half = n // 2
    size = half * hr
    others = [{"dp": (g + k) % n} for k in range(1, n)]
    greet([near, far] + others)
    mine, theirs = ds(c * hc, hc), ds((1 - c) * hc, hc)
    gub_ref[...] = jnp.zeros_like(gub_ref)
    gdb_ref[...] = jnp.zeros_like(gdb_ref)
    folded = lambda v: jnp.sum(v.reshape(v.shape[0] // SUB, SUB, v.shape[1]), axis=0)
    ups = (up_ref, up2_ref)
    downs = (down_ref, down2_ref)
    biases = (ub_ref, ub2_ref)

    def near_copy(t):
        return pltpu.make_async_remote_copy(
            src_ref=part.at[t // n, (g + t) % n, :, theirs],
            dst_ref=ra.at[t],
            send_sem=near_send.at[t],
            recv_sem=near_recv.at[t],
            device_id=near,
            device_id_type=MESH,
        )

    def wide(ref, base):
        return ref[pl.ds(base, half)].reshape(size, ref.shape[2])

    def activate(base):
        rows = wide(rows_ref, base)
        at = pl.ds(pl.multiple_of(base * hr, size), size)
        for k in range(2):
            v = dot(rows, ups[k][...], NN) + biases[k][...]
            sq = v * v
            th = jnp.tanh(v * (GELU_A + GELU_A * GELU_B * sq))
            hid[k, at, :] = (0.5 * v * (1.0 + th)).astype(BF16)
            slope[k, at, :] = 0.5 * (1.0 + th) + 0.5 * v * (1.0 - th * th) * (
                GELU_A + 3.0 * GELU_A * GELU_B * sq
            )

    def behind(base):
        at = pl.ds(pl.multiple_of(base * hr, size), size)
        probs = jax.nn.softmax(dot(wide(rows_ref, base), router_ref[...], NN), axis=-1)
        chosen = jnp.sum(probs * hot_ref[...], axis=1, keepdims=True)
        scaled = (chosen * wide(cot_ref, base).astype(F32)).astype(BF16)
        grad[at, :] = scaled
        gdb_ref[...] += folded(scaled.astype(F32))
        total = None
        for k in range(2):
            value = (dot(scaled, downs[k][...], NT) * slope[k, at, :]).astype(BF16)
            pre[k, at, :] = value
            gub_ref[k] += folded(value.astype(F32))
            term = dot(value, ups[k][...], NT)
            total = term if k == 0 else total + term
        part[0, pl.ds(base, half)] = total.astype(BF16).reshape(half, hr, width)

    def results(base):
        at = pl.ds(pl.multiple_of(base * hr, size), size)
        total = dot(hid[0, at, :], downs[0][...], NN) + dot(hid[1, at, :], downs[1][...], NN)
        part[1, pl.ds(base, half)] = total.astype(BF16).reshape(half, hr, width)

    keep, there, arrived, passed, end = returning(n, qb, out_ref, send, recv)

    def grad_sum(k):
        to = (g + k) % n
        near_copy(k).wait_recv()
        qb[to] = (part[0, to, :, mine].astype(F32) + ra[k].astype(F32)).astype(BF16)

        @pl.when(k > 0)
        def _():
            there(k).start()

    eye = lax.broadcasted_iota(jnp.int32, (hr, LANES), 0) == lax.broadcasted_iota(jnp.int32, (hr, LANES), 1)

    def result_sum(k):
        to = (g + k) % n
        near_copy(n + k).wait_recv()
        value = part[1, to, :, mine].astype(F32) + ra[n + k].astype(F32) + db_ref[:, mine]
        value = value.astype(BF16)
        quarter_ref[to] = value
        gate = jnp.sum(cot_ref[to, :, mine].astype(F32) * value.astype(F32), axis=1, keepdims=True)
        gate_part[pl.ds(to, 1), :] = jnp.sum(jnp.where(eye, gate, 0.0), axis=0, keepdims=True)

    activate(0)
    activate(half)
    behind(0)
    behind(half)
    each(lambda t: near_copy(t).start(), 0, n)
    each(grad_sum, 0, n)
    keep()
    results(0)
    results(half)
    each(lambda t: near_copy(t).start(), n, n)
    each(result_sum, 0, n)
    gate_copy = sending(gate_part, gate_near, gate_send.at[0], gate_recv.at[0], near)
    gate_copy.wait_recv()
    gate_sum[...] = gate_part[...] + gate_near[...]
    gate_in[g] = gate_sum[...]
    gate_out = [
        sending(gate_sum, gate_in.at[g], gate_send.at[k], gate_recv.at[k], others[k - 1]) for k in range(1, n)
    ]

    cut = 256
    pieces = width // cut

    def weights(q):
        at = ds(q % pieces * cut, cut)
        for kind in range(2):
            for k in range(2):

                @pl.when(q // pieces == 2 * kind + 1 - k)
                def _(kind=kind, k=k):
                    if kind == 0:
                        value = dot(hid[k], grad[:, at], TN)
                    else:
                        value = dot(rows_ref[...].reshape(n * hr, width), pre[k, :, at], TN)
                    if k == 0:
                        gown_ref[kind, :, at] = value
                    else:
                        gother_ref[kind, :, at] = value.astype(BF16)

    lag = 3

    def step(i, _):
        @pl.when(i < 4 * pieces)
        def _():
            weights(i)

        @pl.when(i < n)
        def _():
            arrived(i)

        @pl.when((i >= lag) & (i < n + lag))
        def _():
            passed(i - lag)

        return 0

    lax.fori_loop(0, max(4 * pieces, n + lag), step, 0)
    for copy in gate_out:
        copy.wait_recv()
    for e in range(n):
        gates_ref[y, e : e + 1, :] = gate_in[e, pl.ds(g, 1), :]
    gate_far = sending(gates_ref.at[y], gates_ref.at[y], gate_send.at[n], gate_recv.at[n], far)
    each(end, 0, n)
    each(lambda t: near_copy(t).wait_send(), 0, 2 * n)
    gate_far.wait_recv()
    for copy in [gate_copy, gate_far] + gate_out:
        copy.wait_send()


GELU_A = 0.7978845608028654
GELU_B = 0.044715


def experts(n, collective_id, rows, cot, up, up_bias, down, up2, down2, up_bias2, down_bias, router, hot):
    _, hr, width = rows.shape
    hidden = up.shape[1]
    shape = jax.ShapeDtypeStruct
    gate = pltpu.VMEM((n, LANES), F32)
    return vmem_call(
        functools.partial(expert_kernel, n),
        [
            shape((n, 2 * hr, width), BF16),
            shape((n, hr, width // 2), BF16),
            shape((2, n, LANES), F32),
            shape((2, width, hidden), F32),
            shape((2, width, hidden), BF16),
            shape((2, SUB, hidden), F32),
            shape((SUB, width), F32),
        ],
        [
            pltpu.VMEM((2, n, hr, width), BF16),
            pltpu.VMEM((2, n * hr, hidden), BF16),
            pltpu.VMEM((2, n * hr, hidden), F32),
            pltpu.VMEM((2, n * hr, hidden), BF16),
            pltpu.VMEM((n * hr, width), BF16),
            pltpu.VMEM((2 * n, hr, width // 2), BF16),
            pltpu.VMEM((n, hr, width // 2), BF16),
            gate,
            gate,
            gate,
            pltpu.VMEM((n, n, LANES), F32),
            pltpu.SemaphoreType.DMA((4, n)),
            pltpu.SemaphoreType.DMA((4, n)),
            pltpu.SemaphoreType.DMA((2 * n,)),
            pltpu.SemaphoreType.DMA((2 * n,)),
            pltpu.SemaphoreType.DMA((n + 1,)),
            pltpu.SemaphoreType.DMA((n + 1,)),
        ],
        collective_id, rows, cot, up, up_bias, down, up2, down2, up_bias2, down_bias, router, hot,
    )


def finish_kernel(
    n,
    count,
    cuts,
    layout,
    proj_ref,
    select_ref,
    inner_ref,
    base_ref,
    pre_ref,
    both_ref,
    lead_ref,
    gate_ref,
    normed_ref,
    weight_ref,
    taps_ref,
    given_ref,
    tok_ref,
    resid_ref,
    gain_ref,
    slot_ref,
    result_ref,
    residual_ref,
    chosen_ref,
    grad_ref,
    gin_ref,
    small_ref,
    first_ref,
    block_ref,
    conv_s,
    ext_s,
    both_s,
    got,
    part_s,
    sum_s,
    ra,
    sb,
    rb,
    blocks,
    pa,
    ps,
    pc,
    outs,
    firsts,
    rows_s,
    fold_s,
    block_s,
    send,
    recv,
    gsend,
    grecv,
):
    mh, sh = layout
    g = lax.axis_index("dp")
    j, near, far = mp_pair()
    near, far = {"mp": near}, {"mp": far}
    odd, z, m = g % 2, g // 2, n // 2
    pair = {"dp": g + 1 - 2 * odd}
    like = [{"dp": 2 * ((z + k) % m) + odd} for k in range(1, m)]
    others = [{"dp": (g + k) % n} for k in range(1, n)]
    greet([near, far] + others)
    rows, chans = inner_ref.shape
    width = normed_ref.shape[1]
    kernel = taps_ref.shape[0]
    edge = (kernel - 1) * SUB
    block = 256
    half = rows // 2
    size = half // count
    own = (j % 2) * half
    other = (1 - j % 2) * half

    ext_s[0:edge, :] = lead_ref[...]

    def conv_block(b):
        at = ds(b * block, block)
        grad = base_ref[at, :] + dot(proj_ref[at, :], select_ref[...], NT)
        conv_s[at, :] = grad * silu_slope(pre_ref[at, :])
        ext_s[pl.ds(pl.multiple_of(b * block + edge, SUB), block), :] = both_ref[at, 0:chans].astype(F32)

    conv_block(0)
    head = sending(conv_s.at[0:edge], got, send.at[8, 0], recv.at[8, 0], {"dp": (g + n - 1) % n})

    def rest(b, _):
        conv_block(b)
        return 0

    lax.fori_loop(1, rows // block, rest, 0)
    given = given_ref.shape[0]
    selects = select_ref.shape[1]
    rest_at = given + selects
    fold_s[0:given, :] = given_ref[...]
    fold_s[given:rest_at, :] = dot(proj_ref[...], inner_ref[...], TN)
    folded = lambda v: jnp.sum(v.reshape(block // SUB, SUB, chans), axis=0)

    def taps(b, sums):
        grad = conv_s[ds(b * block, block), :]
        past = [ext_s[pl.ds(pl.multiple_of(b * block + k * SUB, SUB), block), :] for k in range(kernel)]
        return tuple(v + folded(grad * p) for v, p in zip(sums, past)) + (sums[kernel] + folded(grad),)

    zero = tuple(jnp.zeros((SUB, chans), F32) for _ in range(kernel + 1))
    sums = lax.fori_loop(0, rows // block, taps, zero)
    for k in range(kernel + 1):
        fold_s[rest_at + k : rest_at + k + 1, :] = jnp.sum(sums[k], axis=0, keepdims=True)
    head.wait_recv()
    upper = lax.broadcasted_iota(jnp.int32, (SUB, chans), 0) >= SUB // 2
    some = jnp.where(g < n - 1, 1.0, 0.0)
    for k in range(kernel - 1):
        at = slice(k * SUB, (k + 1) * SUB)
        tail = half_turn(jnp.where(upper, conv_s[at, :], got[at, :] * some))
        conv_s[rows + k * SUB : rows + (k + 1) * SUB, :] = tail

    def back(b, _):
        at = ds(b * block, block)
        total = jnp.zeros((block, chans), F32)
        for k in range(kernel):
            later = conv_s[pl.ds(pl.multiple_of(b * block + (kernel - 1 - k) * SUB, SUB), block), :]
            total = total + taps_ref[k : k + 1, :] * later
        both_s[at, 0:chans] = total.astype(BF16)
        both_s[at, chans : 2 * chans] = gate_ref[at, :]
        return 0

    lax.fori_loop(0, rows // block, back, 0)

    rows_s[0:width, :] = dot(normed_ref[...], both_s[:, 0:chans], TN)
    for b in range(n):
        blocks[b, 0:mh, :] = rows_s[b * mh : (b + 1) * mh, :].astype(BF16)
        blocks[b, mh : mh + sh, :] = fold_s[b * sh : (b + 1) * sh, :].astype(BF16)
    order = [(z + k) % m for k in range(1, m)] + [z]
    first = [
        sending(blocks.at[2 * order[k] + 1 - odd], pa.at[k], send.at[3, k], recv.at[3, k], pair)
        for k in range(m)
    ]
    one, two, three, second = [], [], [], []

    def input_rows(start):
        at = ds(start, size)
        part_s[at, :] = dot(both_s[at, :], weight_ref[...], NT).astype(BF16)

    for k in range(count):
        input_rows(other + k * size)
        at = ds(other + k * size, size)
        one.append(sending(part_s.at[at], ra.at[k], send.at[0, k], recv.at[0, k], near))
    for k in range(count):
        input_rows(own + k * size)
        one[k].wait_recv()
        mine = part_s[ds(own + k * size, size), :].astype(F32)
        sb[k] = (mine + ra[k].astype(F32)).astype(BF16)
        two.append(sending(sb.at[k], rb.at[k], send.at[1, k], recv.at[1, k], far))
    slots = result_ref.shape[0] * result_ref.shape[1]

    def output(b):
        at = ds(b * block, block)
        iota = lax.broadcasted_iota(jnp.int32, (block, slots), 1)
        pick = jnp.where(iota == slot_ref[at, :], 1.0, 0.0).astype(BF16)
        result = dot(pick, result_ref[...].reshape(slots, width), NN)
        value = residual_ref[at, :] + chosen_ref[at, :] * result
        for ct in range(width // LANES):
            block_s[ct, at, :] = value[:, ct * LANES : (ct + 1) * LANES]

    for k in range(m):
        first[k].wait_recv()
        ps[k] = (blocks[2 * order[k] + odd].astype(F32) + pa[k].astype(F32)).astype(BF16)
        if k < m - 1:
            second.append(sending(ps.at[k], pc.at[k], send.at[4, k], recv.at[4, k], like[k]))

    def far_sum(k):
        two[k].wait_recv()
        at = ds(own + k * size, size)
        sum_s[at, :] = (sb[k].astype(F32) + rb[k].astype(F32)).astype(BF16)
        three.append(sending(sum_s.at[at], sum_s.at[at], send.at[2, k], recv.at[2, k], near))

    output_blocks = rows // block
    for b in range(output_blocks // 2):
        output(b)
    value = ps[m - 1].astype(F32)
    for copy in second:
        copy.wait_recv()
    for k in range(m - 1):
        value = value + pc[k].astype(F32)
    outs[g] = value.astype(BF16)
    start, middle, end = gathering(n, outs, gsend, grecv)
    start()
    for b in range(output_blocks // 2, output_blocks):
        output(b)
    firsts[0] = jnp.zeros(firsts.shape[1:], F32)
    gain = gain_ref[...]

    def norm_rows(start):
        at = ds(start, size)
        grad = sum_s[at, :].astype(F32)
        tok = tok_ref[at, :].astype(F32)
        inverse = lax.rsqrt(jnp.mean(tok * tok, axis=1, keepdims=True) + norm_eps)
        normed = tok * inverse
        firsts[0] += jnp.sum((grad * normed).reshape(size // SUB, SUB, width), axis=0)
        scaled = grad * gain
        mean = jnp.mean(scaled * normed, axis=1, keepdims=True)
        value = resid_ref[at, :] + inverse * (scaled - normed * mean)
        for ct in range(width // LANES):
            grad_ref[ct, at, :] = value[:, ct * LANES : (ct + 1) * LANES]

    for k in range(count):
        far_sum(k)
        norm_rows(own + k * size)
    for p in range(PIECES):
        middle(p)
    for k in range(count):
        three[k].wait_recv()
        norm_rows(other + k * size)
    spread_first = [
        sending(firsts.at[0], firsts.at[k], send.at[7, k], recv.at[7, k], others[k - 1]) for k in range(1, n)
    ]
    restore(cuts, block_s, block_ref)
    for copy in spread_first:
        copy.wait_recv()

    def one_first(d, total):
        return total + firsts[(g + n - d) % n]

    first_ref[...] = lax.fori_loop(0, n, one_first, jnp.zeros(first_ref.shape, F32))
    end()
    for b in range(n):
        gin_ref[b * mh : (b + 1) * mh, :] = outs[b, 0:mh, :].astype(F32)
        small_ref[b * sh : (b + 1) * sh, :] = outs[b, mh : mh + sh, :].astype(F32)
    mp_copies = one + two + three
    for copy in [head] + mp_copies + first + second + spread_first:
        copy.wait_send()


def finish(n, collective_id, cuts, *args, count=4):
    select, inner, normed, taps, given = args[1], args[2], args[8], args[10], args[11]
    rows, chans = inner.shape
    width = normed.shape[1]
    kernel = taps.shape[0]
    edge = (kernel - 1) * SUB
    m = n // 2
    over = lambda size: (size + 16 * n - 1) // (16 * n) * 16
    mh, sh = over(width), over(given.shape[0] + select.shape[1] + kernel + 1)
    slots = pltpu.VMEM((count, rows // 2 // count, width), BF16)
    part = lambda k: pltpu.VMEM((k, mh + sh, chans), BF16)
    sems = pltpu.SemaphoreType.DMA((12, max(n, count)))
    shape = jax.ShapeDtypeStruct
    return vmem_call(
        functools.partial(finish_kernel, n, count, cuts, (mh, sh)),
        [
            shape((width // LANES, rows, LANES), F32),
            shape((n * mh, chans), F32),
            shape((n * sh, chans), F32),
            shape((SUB, width), F32),
            shape((rows, width), BF16),
        ],
        [
            pltpu.VMEM((rows + edge, chans), F32),
            pltpu.VMEM((rows + edge, chans), F32),
            pltpu.VMEM((rows, 2 * chans), BF16),
            pltpu.VMEM((edge, chans), F32),
            pltpu.VMEM((rows, width), BF16),
            pltpu.VMEM((rows, width), BF16),
            slots,
            slots,
            slots,
            part(n),
            part(m),
            part(m),
            part(m),
            part(n),
            pltpu.VMEM((n, SUB, width), F32),
            pltpu.VMEM((n * mh, chans), F32),
            pltpu.VMEM((n * sh, chans), F32),
            pltpu.VMEM((width // LANES, rows, LANES), F32),
            sems,
            sems,
            pltpu.SemaphoreType.DMA((2, PIECES * m)),
            pltpu.SemaphoreType.DMA((2, PIECES * m)),
        ],
        collective_id, *args,
    )


def token_back_kernel(
    n,
    slot_ref,
    back_ref,
    gates_ref,
    quarter_ref,
    residual_ref,
    hot_ref,
    cot_ref,
    valid_ref,
    gain_ref,
    router_ref,
    gated_ref,
    out_ref,
    scan_ref,
    both_ref,
    inner_ref,
    normed_in_ref,
    chosen_ref,
    resid_ref,
    gs_ref,
    gate_ref,
    early_ref,
    landed_ref,
    mixed_s,
    early_s,
    small_s,
    router_out,
    second_ref,
    skip_ref,
    send,
    recv,
):
    rows, width = residual_ref.shape
    chans = inner_ref.shape[1]
    slots = back_ref.shape[0] * back_ref.shape[1]
    hr = back_ref.shape[1] // 2
    g = lax.axis_index("dp")
    others = [{"dp": (g + k) % n} for k in range(1, n)]
    greet(others)
    copies = [
        sending(quarter_ref.at[(g + k) % n], landed_ref.at[g], send.at[k], recv.at[k], others[k - 1])
        for k in range(1, n)
    ]
    landed_ref[g] = quarter_ref[g]
    size = 256
    lanes = lax.broadcasted_iota(jnp.int32, (1, LANES), 1)
    router_out[...] = jnp.zeros_like(router_out)
    second_ref[...] = jnp.zeros_like(second_ref)
    skip_ref[...] = jnp.zeros_like(skip_ref)

    def body(b, _):
        at = ds(b * size, size)
        folded = lambda v: jnp.sum(v.reshape(size // SUB, SUB, v.shape[1]), axis=0)
        iota = lax.broadcasted_iota(jnp.int32, (size, slots), 1)
        slot = slot_ref[at, :]
        pick = jnp.where(iota == slot, 1.0, 0.0).astype(BF16)
        grad = dot(pick, back_ref[...].reshape(slots, width), NN)
        gates = jnp.zeros((size, LANES), F32)
        for e in range(n):
            for k in range(2):
                hit = slot - (2 * e + k) * hr == lanes
                gates = gates + jnp.where(hit, gates_ref[k, e : e + 1, :], 0.0)
        gate = jnp.sum(gates, axis=1, keepdims=True)
        residual = residual_ref[at, :]
        inverse = lax.rsqrt(jnp.mean(residual * residual, axis=1, keepdims=True) + norm_eps)
        normed = residual * inverse
        normed_low = (normed * gain_ref[...]).astype(BF16)
        hot = hot_ref[at, :]
        probs = jax.nn.softmax(dot(normed_low, router_ref[...], NN), axis=-1)
        chosen = jnp.sum(probs * hot, axis=1, keepdims=True)
        chosen_ref[at, :] = chosen
        cot = cot_ref[at, :].astype(F32)
        logit = (gate * probs * (hot - chosen)).astype(BF16)
        router_out[...] += dot(logit, normed_low, TN)
        grad = grad + dot(logit, router_ref[...], NT)
        second_ref[...] += folded(grad * normed)
        scaled = grad * gain_ref[...]
        mean = jnp.mean(scaled * normed, axis=1, keepdims=True)
        resid = cot + inverse * (scaled - normed * mean)
        resid_ref[at, :] = resid
        mixed = (valid_ref[at, :] * resid).astype(BF16)
        mixed_s[at, :] = mixed
        grad_gated = dot(mixed, out_ref[...], NT)
        pre = both_ref[at, chans : 2 * chans].astype(F32)
        sig = jax.nn.sigmoid(pre)
        act = pre * sig
        gs = grad_gated * act
        gs_ref[at, :] = gs
        skip_ref[...] += folded(gs * inner_ref[at, :].astype(F32))
        gate_ref[at, :] = (grad_gated * scan_ref[at, :] * (sig * (1.0 + pre * (1.0 - sig)))).astype(BF16)
        return 0

    lax.fori_loop(0, rows // size, body, 0)
    mh = early_s.shape[1] // n
    sh = early_ref.shape[1] - 2 * mh
    some = router_out.shape[0]
    for k in range(width // chans):
        at = slice(k * chans, (k + 1) * chans)
        small_s[k * some : (k + 1) * some, :] = router_out[:, at]
        line = 2 * some + k
        small_s[line : line + 1, :] = jnp.sum(second_ref[:, at], axis=0, keepdims=True)
    small_s[2 * some + 2 : 2 * some + 3, :] = jnp.sum(skip_ref[...], axis=0, keepdims=True)
    early_s[0, 0:width, :] = dot(normed_in_ref[...], gate_ref[...], TN)
    value = dot(gated_ref[...], mixed_s[...], TN)
    for k in range(width // chans):
        early_s[1, k * chans : (k + 1) * chans, :] = value[:, k * chans : (k + 1) * chans]
    for b in range(n):
        for k in range(2):
            early_ref[b, k * mh : (k + 1) * mh, :] = early_s[k, b * mh : (b + 1) * mh, :].astype(BF16)
        early_ref[b, 2 * mh : 2 * mh + sh, :] = small_s[b * sh : (b + 1) * sh, :].astype(BF16)
    for copy in copies:
        copy.wait_recv()
    for copy in copies:
        copy.wait_send()


def restore(cuts, tile_ref, out_ref):
    seqs, chunks, places = cuts
    for ct in range(tile_ref.shape[0]):
        for q in range(seqs):
            for k in range(chunks):
                picked = tile_ref[ct, pl.ds(k * seqs + q, places, stride=SUB), :]
                start = (q * chunks + k) * places
                out_ref[start : start + places, ct * LANES : (ct + 1) * LANES] = picked.astype(out_ref.dtype)


def token_back(n, collective_id, *args):
    quarter, residual, router, inner = args[3], args[4], args[9], args[14]
    over = lambda size: (size + 16 * n - 1) // (16 * n) * 16
    mh, sh = over(residual.shape[1]), over(2 * router.shape[1] + 3)
    rows, width = residual.shape
    chans = inner.shape[1]
    shape = jax.ShapeDtypeStruct
    sems = pltpu.SemaphoreType.DMA((n,))
    return vmem_call(
        functools.partial(token_back_kernel, n),
        [
            shape((rows, 1), F32),
            shape((rows, width), F32),
            shape((rows, chans), F32),
            shape((rows, chans), BF16),
            shape((n, 2 * mh + sh, chans), BF16),
            shape(quarter.shape, BF16),
        ],
        [
            pltpu.VMEM((rows, width), BF16),
            pltpu.VMEM((2, n * mh, chans), F32),
            pltpu.VMEM((n * sh, chans), F32),
            pltpu.VMEM((router.shape[1], width), F32),
            pltpu.VMEM((SUB, width), F32),
            pltpu.VMEM((SUB, chans), F32),
            sems,
            sems,
        ],
        collective_id, *args,
    )


def emit_kernel(
    layout,
    cuts,
    tile_ref,
    own_ref,
    far_ref,
    conv_ref,
    gate_ref,
    left_ref,
    right_ref,
    small_ref,
    few_ref,
    first_ref,
    ub_ref,
    far_bias_ref,
    db_ref,
    token_ref,
    down_ref,
    up_ref,
    in_ref,
    out_ref,
    taps_ref,
    cb_ref,
    select_ref,
    sw_ref,
    sb_ref,
    decay_ref,
    skip_ref,
    second_ref,
    router_ref,
    norm_ref,
    gub_ref,
    gdb_ref,
):
    restore(cuts, tile_ref, token_ref)
    rank, states, select_at, taps_at = layout
    down_ref[...] = own_ref[0] + far_ref[0].astype(F32)
    up_ref[...] = own_ref[1] + far_ref[1].astype(F32)
    in_ref[:, 0, :] = conv_ref[...]
    in_ref[:, 1, :] = gate_ref[...]
    chans = conv_ref.shape[1]
    out_ref[:, 0:chans] = left_ref[...]
    out_ref[:, chans : 2 * chans] = right_ref[...]

    @pl.when(pl.program_id(0) == 0)
    def _():
        kernel = taps_ref.shape[0]
        taps_ref[...] = small_ref[taps_at : taps_at + kernel, :]
        cb_ref[...] = small_ref[taps_at + kernel, :]
        select_ref[...] = small_ref[select_at:taps_at, :]
        sw_ref[...] = small_ref[0:rank, :]
        decay_ref[...] = small_ref[rank : rank + states, :]
        sb_ref[...] = small_ref[rank + states, :]
        some = router_ref.shape[0]
        line = 2 * some
        for k in range(2):
            at = slice(k * chans, (k + 1) * chans)
            router_ref[:, at] = few_ref[k * some : (k + 1) * some, :]
            second_ref[at] = few_ref[line + k, :]
        skip_ref[...] = few_ref[line + 2, :]
        total = lambda v: jnp.sum(v, axis=0, keepdims=True)
        norm_ref[...] = jnp.sum(first_ref[...], axis=0)
        bias = far_bias_ref[...].astype(F32)
        gub_ref[...] = total(ub_ref[0] + bias[0:SUB])
        gdb_ref[...] = total(db_ref[...].astype(F32) + bias[SUB : 2 * SUB])


def emit(layout, cuts, tiles_, own, far, conv, gate, mixer, small, few, first, ub, far_bias, db, experts_all):
    width, chans = own.shape[1], conv.shape[1]
    hidden = own.shape[2]
    rank, states, select_at, taps_at = layout
    count, rows = tiles_.shape[0], tiles_.shape[1]
    cut, part = width // count, chans // count
    shape = jax.ShapeDtypeStruct
    block = lambda size, wide: pl.BlockSpec((size, wide), lambda i: (i, 0))
    both = lambda size, wide: pl.BlockSpec((2, size, wide), lambda i: (0, i, 0))
    shapes = [
        (4, chans),
        (chans,),
        (taps_at - select_at, chans),
        (rank, chans),
        (chans,),
        (states, chans),
        (chans,),
        (width,),
        (experts_all, width),
        (width,),
        (1, hidden),
        (1, width),
    ]
    return pl.pallas_call(
        functools.partial(emit_kernel, layout, cuts),
        grid=(count,),
        in_specs=[
            pl.BlockSpec((1, rows, LANES), lambda i: (i, 0, 0)),
            both(cut, hidden),
            both(cut, hidden),
            block(cut, chans),
            block(cut, chans),
            block(part, chans),
            pl.BlockSpec((part, chans), lambda i: (i + count, 0)),
            whole(*small.shape),
            whole(*few.shape),
            whole(*first.shape),
            whole(*ub.shape),
            whole(*far_bias.shape),
            whole(*db.shape),
        ],
        out_specs=[
            pl.BlockSpec((rows, LANES), lambda i: (0, i)),
            block(cut, hidden),
            block(cut, hidden),
            pl.BlockSpec((cut, 2, chans), lambda i: (i, 0, 0)),
            block(part, width),
            *[whole(*dims) for dims in shapes],
        ],
        out_shape=[
            shape((rows, count * LANES), F32),
            shape((width, hidden), F32),
            shape((width, hidden), F32),
            shape((width, 2, chans), F32),
            shape((chans, width), F32),
            *[shape(dims, F32) for dims in shapes],
        ],
        compiler_params=pltpu.CompilerParams(vmem_limit_bytes=VMEM),
    )(tiles_, own, far, conv, gate, mixer, mixer, small, few, first, ub, far_bias, db)


def silu_slope(values):
    sigmoid_vals = jax.nn.sigmoid(values)
    return sigmoid_vals * (1.0 + values * (1.0 - sigmoid_vals))


def per_device(
    tokens,
    routes,
    lengths,
    cotangent,
    first_gain,
    mixer_in,
    conv_weight,
    conv_bias,
    select_weight,
    step_weight,
    step_bias,
    decay_log,
    skip_gain,
    mixer_out,
    second_gain,
    router_weight,
    expert_up,
    up_bias,
    expert_down,
    down_bias,
):
    tok_count, model_width = tokens.shape
    kernel, chan_count = conv_weight.shape
    rank_size = step_weight.shape[0]
    state_size = decay_log.shape[0]
    expert_total = router_weight.shape[1]
    capacity = max(2, (5 * tok_count + 4 * expert_total - 1) // (4 * expert_total))
    room = (capacity + 31) // 32 * 32
    slot_dev = SLOT_DEV
    seq_count = tok_count // slot_dev
    chunks = SUB // seq_count
    places_dev = slot_dev // chunks
    cuts = (seq_count, chunks, places_dev)
    device = lax.axis_index("dp")
    dp_count = lax.axis_size("dp")

    mp_count = lax.axis_size("mp")
    to_far = [(i, (i + mp_count // 2) % mp_count) for i in range(mp_count)]
    swap_far = lambda values: lax.ppermute(values, "mp", to_far)
    far_up = swap_far(expert_up[0])

    first_vals = first_gain.astype(F32)
    second_vals = second_gain.astype(F32)
    mixer_in_flat = mixer_in.reshape(model_width, 2 * chan_count)
    conv_taps = conv_weight.astype(F32)
    routes_cut = routes.reshape(seq_count, chunks, places_dev).transpose(2, 1, 0)
    (
        tok_low,
        cot_low,
        normed_in,
        both_in,
        conv_pre,
        inner_vals,
        lead_rows,
        projected,
        cot_quarter,
        slot_ids,
        half_slots,
        valid_col,
        route_hot,
    ) = front(
        dp_count,
        0,
        cuts,
        capacity,
        room // 2,
        expert_total,
        tokens,
        cotangent,
        routes_cut.reshape(tok_count, 1),
        lengths[None],
        first_vals[None],
        mixer_in_flat,
        conv_taps,
        conv_bias.astype(F32)[None],
        select_weight,
    )
    own_down, own_bias, projected = lax.optimization_barrier(
        (expert_down[0], jnp.broadcast_to(up_bias, (16, up_bias.shape[1])), projected)
    )
    far_down, far_bias = swap_far((own_down, own_bias))
    decay_rates = -jnp.exp(decay_log.astype(F32))
    rates = decay_rates * LOG2E

    step_p, drive_p, step_slope, bin_p, cout_p, low_high, chunk_steps, state_in, totals = enter_forward(
        dp_count,
        2,
        projected,
        step_weight,
        step_bias.astype(F32)[None],
        inner_vals,
        valid_col,
        rates,
    )
    skip_vals = skip_gain.astype(F32)
    scan_out, gated_vals, mixed, states_before, last_states, cot_rows = forward(
        10,
        step_p,
        drive_p,
        bin_p,
        cout_p,
        rates,
        state_in,
        inner_vals,
        both_in,
        skip_vals[None],
        mixer_out,
        cot_quarter,
    )
    residual, expert_rows = mixer_to_experts(
        dp_count, 3, room // 2, mixed, tok_low, valid_col, second_vals[None], half_slots
    )

    own_hot = (jnp.arange(expert_total) == device).astype(F32)[None]
    returned, quarters, gates, grad_own, grad_other, up_bias_parts, down_bias_part = experts(
        dp_count,
        5,
        expert_rows,
        cot_rows,
        expert_up[0],
        up_bias.astype(F32),
        expert_down[0],
        far_up,
        far_down,
        far_bias[:1].astype(F32),
        down_bias.astype(F32),
        router_weight,
        own_hot,
    )
    down_bias_part = down_bias_part.astype(BF16)
    bias_rows = jnp.concatenate([up_bias_parts[1].astype(BF16), down_bias_part], axis=0)
    from_far = swap_far((grad_other, bias_rows))
    (
        chosen,
        grad_resid,
        grad_scan,
        grad_gate_low,
        early,
        landed,
    ) = token_back(
        dp_count,
        11,
        slot_ids,
        returned,
        gates,
        quarters,
        residual,
        route_hot,
        cot_low,
        valid_col,
        second_vals[None],
        router_weight,
        gated_vals,
        mixer_out,
        scan_out,
        both_in,
        inner_vals,
        normed_in,
    )
    gs_p = grad_scan.reshape(places_dev, SUB, chan_count)
    grad_in, early = enter_backward(
        dp_count, 6, step_p, gs_p, cout_p, chunk_steps, rates, totals, early
    )
    mixer_rows = (model_width + 16 * dp_count - 1) // (16 * dp_count) * 16
    grad_base, proj_part, given, grad_gate_in, grad_mixer_out, few, results = backward(
        dp_count,
        9,
        mixer_rows,
        step_p,
        drive_p,
        gs_p,
        bin_p,
        cout_p,
        rates,
        grad_in,
        last_states,
        states_before,
        inner_vals,
        step_slope,
        low_high,
        jnp.pad(step_weight, ((0, 2 * state_size), (0, 0))),
        skip_vals[None],
        early,
        landed,
    )
    grad_tiles, grad_conv_half, small, grad_first, block_out = finish(
        dp_count,
        8,
        cuts,
        proj_part,
        select_weight,
        inner_vals,
        grad_base,
        conv_pre,
        both_in,
        lead_rows,
        grad_gate_low,
        normed_in,
        mixer_in_flat,
        conv_taps,
        given,
        tok_low,
        grad_resid,
        first_vals[None],
        slot_ids,
        results,
        residual,
        chosen,
    )
    select_at = given.shape[0]
    taps_at = select_at + select_weight.shape[1]
    (
        token_grad,
        grad_down,
        grad_up,
        grad_mixer_in,
        grad_mixer_full,
        grad_taps,
        grad_conv_bias,
        grad_select,
        grad_step_weight,
        grad_step_bias,
        grad_decay_log,
        grad_skip,
        grad_second,
        grad_router,
        grad_gain,
        grad_up_bias,
        grad_down_bias,
    ) = emit(
        (rank_size, state_size, select_at, taps_at),
        cuts,
        grad_tiles,
        grad_own,
        from_far[0],
        grad_conv_half,
        grad_gate_in,
        grad_mixer_out,
        small,
        few,
        grad_first,
        up_bias_parts,
        from_far[1],
        down_bias_part,
        expert_total,
    )
    return (
        block_out,
        token_grad,
        grad_gain,
        grad_mixer_in,
        grad_taps,
        grad_conv_bias,
        grad_select.T,
        grad_step_weight,
        grad_step_bias,
        grad_decay_log,
        grad_skip,
        grad_mixer_full,
        grad_second,
        grad_router.T,
        grad_up[None],
        grad_up_bias,
        grad_down[None],
        grad_down_bias,
    )


def solution(mesh):
    return jax.shard_map(
        per_device,
        mesh=mesh,
        in_specs=(
            P("dp", None),
            P("dp", None),
            P(),
            P("dp", None),
            P(),
            P(None, None, "mp"),
            P(None, "mp"),
            P("mp"),
            P("mp", None),
            P(None, "mp"),
            P("mp"),
            P(None, "mp"),
            P("mp"),
            P("mp", None),
            P(),
            P(),
            P("dp", None, "mp"),
            P("dp", "mp"),
            P("dp", "mp", None),
            P("dp", None),
        ),
        out_specs=(
            P("dp", None),
            P("dp", None),
            P(),
            P(None, None, "mp"),
            P(None, "mp"),
            P("mp"),
            P("mp", None),
            P(None, "mp"),
            P("mp"),
            P(None, "mp"),
            P("mp"),
            P("mp", None),
            P(),
            P(),
            P("dp", None, "mp"),
            P("dp", "mp"),
            P("dp", "mp", None),
            P("dp", None),
        ),
        check_vma=False,
    )
```
